32 devices in a mesh: seq: 4 (over y, x), batch: 8 (over z, core).
Axes of the slice: x: 2, y: 2, z: 4, core: 2. Of those that a mesh axis runs over, the one named last changes fastest.
Arguments:
- tokens: bfloat16 [32, 1024, 768], P('batch', 'seq'), may hold values from -6 to 6
- cotangent: bfloat16 [32, 1024, 768], P('batch', 'seq'), may hold values from -6 to 6
- doc_lengths: int32 [32, 8], P('batch'), may hold values from 1 to 1017, as said below
- w_query: bfloat16 [768, 768], replicated, may hold values from -0.21875 to 0.21875
- w_key: bfloat16 [768, 768], replicated, may hold values from -0.21875 to 0.21875
- w_value: bfloat16 [768, 768], replicated, may hold values from -0.21875 to 0.21875
- w_out: bfloat16 [768, 768], replicated, may hold values from -1.25 to 1.25
- w_in: bfloat16 [768, 3072], replicated, may hold values from -0.21875 to 0.21875
- w_back: bfloat16 [3072, 768], replicated, may hold values from -0.109375 to 0.109375
- gain_one: float32 [768], replicated, may hold values from 0.5 to 1.5
- shift_one: float32 [768], replicated, may hold values from -1.8 to 1.8
- gain_two: float32 [768], replicated, may hold values from 0.5 to 1.5
- shift_two: float32 [768], replicated, may hold values from -1.8 to 1.8
Outputs:
- layer_out: bfloat16 [32, 1024, 768], P('batch', 'seq')
- grad_tokens: float32 [32, 1024, 768], P('batch', 'seq')
- grad_query: float32 [768, 768], P('seq')
- grad_key: float32 [768, 768], P('seq')
- grad_value: float32 [768, 768], P('seq')
- grad_out: float32 [768, 768], P('seq')
- grad_in: float32 [768, 3072], P('seq')
- grad_back: float32 [3072, 768], P('seq')
- grad_gain_one: float32 [768], P('seq')
- grad_shift_one: float32 [768], P('seq')
- grad_gain_two: float32 [768], P('seq')
- grad_shift_two: float32 [768], P('seq')
The draws below stay inside these ranges and needn't reach their ends.
Inputs may be any that keep to these rules, and one draw needn't show every extreme that they name: `doc_lengths`: each row holds the lengths of its 8 documents in order, each 1 or more, summing to 1024. Among the 4 rows of each index of batch, one holds a document of 1017 positions followed by documents of one position; the other rows are cut at distinct places drawn evenly.
All inputs are finite; a program needn't handle non-finite values.
Results may differ from the reference program's by a relative error of at most 0.0085.
Values sent between devices are 32-bit elements; how exact they have to be, the bound alone decides.
No kernel may reach another device: no remote copies, remote signals or barrier semaphores. Data moves between devices by JAX's collectives and lax.ppermute only.
A program may use at most 256 MiB of HBM per device.

```python
import jax
import jax.numpy as jnp
from jax import lax

D = 768
HEADS = 12
HEAD_DIM = 64
FF = 3072
ROWS_DEV = 4
DOCS = 8
LENGTH = 1024
ROWS = 32


def draw_doc_lengths(key, part):
    key = jax.random.fold_in(key, 7)
    cut_key, pick_key = jax.random.split(key)

    def row_lengths(row_key):
        chosen = jax.random.permutation(row_key, LENGTH - 1)[:DOCS - 1] + 1
        bounds = jnp.concatenate([jnp.zeros((1,), jnp.int32), jnp.sort(chosen).astype(jnp.int32), jnp.full((1,), LENGTH, jnp.int32)])
        return bounds[1:] - bounds[:-1]
    spread = jax.vmap(row_lengths)(jax.random.split(cut_key, ROWS))
    single = jnp.concatenate([jnp.full((1,), LENGTH - DOCS + 1, jnp.int32), jnp.ones((DOCS - 1,), jnp.int32)])
    picked = jax.random.randint(pick_key, (ROWS // ROWS_DEV,), 0, ROWS_DEV)
    longest = jnp.arange(ROWS) % ROWS_DEV == jnp.repeat(picked, ROWS_DEV)
    return jnp.where(longest[:, None], single[None, :], spread).astype(jnp.int32)


def with_spikes(values, key, source, target, parts, factor):
    owner, partner = [(jnp.arange(values.shape[dim]) // (values.shape[dim] // parts)).reshape([-1 if axis == dim else 1 for axis in range(values.ndim)]) for dim in (source, target)]
    chosen = jax.random.permutation(key, parts)[partner]
    strong = (owner == chosen) | (owner == (partner + parts // 2) % parts)
    return jnp.where(strong, factor * values, values)


def steps_of(own_key, shape, cuts, smallest, top_value):
    level = 1.0
    for dim, shards_of in cuts:
        heights = jax.random.uniform(jax.random.fold_in(jax.random.fold_in(own_key, 6), dim), (shards_of,), jnp.float32, smallest / len(cuts), top_value / len(cuts))
        level = level * jnp.repeat(jnp.exp(heights), shape[dim] // shards_of).reshape((-1,) + (1,) * (len(shape) - 1 - dim))
    return level


def bell_draw(own_key, shape, deviation, limit, shards=(), kind=jnp.bfloat16):
    entries = deviation * jax.random.normal(own_key, shape, jnp.float32)
    if shards:
        entries = entries * steps_of(own_key, shape, shards, -0.22, 0.18)
    return jnp.clip(entries, -limit, limit).astype(kind)


def bell_draw_with(key, extent, scale, reach, shards, heavy, kind=jnp.bfloat16):
    values = scale * jax.random.normal(key, extent, jnp.float32)
    if shards:
        values = values * steps_of(key, extent, shards, -0.22, 0.18)
    return jnp.clip(with_spikes(values, jax.random.fold_in(key, 3), *heavy), -reach, reach).astype(kind)


def setup_inputs(seed: int = 0) -> dict:
    splits = jax.random.split(jax.random.key(seed), 14)
    tokens = bell_draw(splits[0], (ROWS, LENGTH, D), 1.0, 6.0, ((0, 8), (1, 4)))
    cotangent = bell_draw_with(splits[1], (ROWS, LENGTH, D), 1.0, 6.0, ((0, 8), (1, 4)), (0, 2, 8, 2.0))
    doc_lengths = draw_doc_lengths(jax.random.fold_in(splits[13], 71), 0)
    w_query = bell_draw(splits[3], (D, D), D ** -0.5, 0.21875)
    w_key = bell_draw(splits[4], (D, D), D ** -0.5, 0.21875)
    w_value = bell_draw(splits[5], (D, D), D ** -0.5, 0.21875)
    w_out = bell_draw(splits[6], (D, D), (D // 32) ** -0.5, 1.25)
    w_in = bell_draw(splits[7], (D, FF), D ** -0.5, 0.21875)
    w_back = bell_draw(splits[8], (FF, D), FF ** -0.5, 0.109375)
    gain_one = jnp.clip(1.0 + 0.1 * jax.random.normal(splits[9], (D,), jnp.float32), 0.5, 1.5)
    shift_one = bell_draw(splits[10], (D,), 0.3, 1.8, (), jnp.float32)
    gain_two = jnp.clip(1.0 + 0.1 * jax.random.normal(splits[11], (D,), jnp.float32), 0.5, 1.5)
    shift_two = bell_draw(splits[12], (D,), 0.3, 1.8, (), jnp.float32)
    return {"tokens": tokens, "cotangent": cotangent, "doc_lengths": doc_lengths, "w_query": w_query, "w_key": w_key, "w_value": w_value, "w_out": w_out, "w_in": w_in, "w_back": w_back, "gain_one": gain_one, "shift_one": shift_one, "gain_two": gain_two, "shift_two": shift_two}


@jax.custom_vjp
def low(v):
    return lax.optimization_barrier(v.astype(jnp.bfloat16)).astype(jnp.float32)

@jax.custom_vjp
def low_back(v):
    return v

def low_keep(v):
    return (low(v), None)

def low_pass(kept, grad):
    return (grad,)

def back_keep(v):
    return (v, None)

def back_low(kept, grad):
    return (low(grad),)
low.defvjp(low_keep, low_pass)
low_back.defvjp(back_keep, back_low)
half_pi = 1.5707963267948966
norm_eps = 1e-05

def exact_dot(left_side, right_side):
    return jnp.dot(left_side, right_side, precision=lax.Precision.HIGHEST)

def layer_norm(summed, gain_vec, shift_vec):
    centered = summed - lax.optimization_barrier(jnp.mean(summed, axis=-1, keepdims=True))
    inv_scale = lax.rsqrt(lax.optimization_barrier(jnp.mean(centered * centered, axis=-1, keepdims=True)) + norm_eps)
    return centered * inv_scale * gain_vec + shift_vec

def doc_tables(lengths, positions):
    doc_ends = jnp.cumsum(lengths, axis=-1).astype(jnp.int32)
    starts = (doc_ends - lengths).astype(jnp.int32)
    inside = ((positions[None, :, None] >= starts[:, None, :]) & (positions[None, :, None] < doc_ends[:, None, :])).astype(jnp.int32)
    doc_begin = lax.optimization_barrier(jnp.sum(inside * starts[:, None, :], axis=-1)).astype(jnp.int32)
    doc_span = lax.optimization_barrier(jnp.sum(inside * lengths[:, None, :], axis=-1)).astype(jnp.int32)
    return (doc_begin, doc_span)

def row_attention(pieces):
    query_rows, key_rows, value_rows, doc_begin, doc_pos, doc_span = pieces
    length_here = query_rows.shape[0]
    step_index = jnp.arange(length_here, dtype=jnp.int32)
    same_doc = (doc_begin[:, None] == doc_begin[None, :]) & (step_index[:, None] >= step_index[None, :])
    angles = half_pi * (doc_pos[:, None] - doc_pos[None, :]).astype(jnp.float32) / doc_span[:, None].astype(jnp.float32)
    weight = jnp.where(same_doc, jnp.cos(angles), 0.0)

    def one_head(head_pieces):
        query_head, key_head, value_head = head_pieces
        scores = exact_dot(query_head, key_head.T) * weight
        return exact_dot(scores, value_head) / lax.optimization_barrier(jnp.sum(scores, axis=-1, keepdims=True))

    def split_heads(matrix):
        return matrix.reshape(length_here, HEADS, HEAD_DIM).transpose(1, 0, 2)
    result = lax.map(jax.checkpoint(one_head), (split_heads(query_rows), split_heads(key_rows), split_heads(value_rows)))
    return result.transpose(1, 0, 2).reshape(length_here, HEADS * HEAD_DIM)

def forward(tokens, w_query, w_key, w_value, w_out, w_in, w_back, gain_one, shift_one, gain_two, shift_two, doc_begin, doc_pos, doc_span):
    row_count, tok_count, model_width = tokens.shape
    flat_tokens = tokens.reshape(row_count * tok_count, model_width)
    query_rows = low(jax.nn.softplus(low_back(exact_dot(flat_tokens, w_query))))
    key_rows = low(jax.nn.softplus(low_back(exact_dot(flat_tokens, w_key))))
    value_rows = low(low_back(exact_dot(flat_tokens, w_value)))
    row_shape = (row_count, tok_count, model_width)
    attended = lax.map(jax.checkpoint(row_attention), (query_rows.reshape(row_shape), key_rows.reshape(row_shape), value_rows.reshape(row_shape), doc_begin, doc_pos, doc_span))
    att_low = low(attended.reshape(row_count * tok_count, model_width))
    branch = low_back(exact_dot(att_low, w_out))
    first_out = layer_norm(flat_tokens + branch, gain_one, shift_one)
    hidden = low_back(exact_dot(low(first_out), w_in))
    active = low(jax.nn.gelu(hidden, approximate=False))
    second = low_back(exact_dot(active, w_back))
    return layer_norm(first_out + second, gain_two, shift_two).reshape(row_shape)

def reference(tokens, cotangent, doc_lengths, w_query, w_key, w_value, w_out, w_in, w_back, gain_one, shift_one, gain_two, shift_two):
    tok_count = tokens.shape[1]
    positions = jnp.arange(tok_count, dtype=jnp.int32)
    doc_begin, doc_span = doc_tables(doc_lengths, positions)
    doc_pos = (positions[None, :] - doc_begin).astype(jnp.int32)

    def run(token_values, *params):
        return forward(token_values, *params, doc_begin, doc_pos, doc_span)
    weights = (w_query.astype(jnp.float32), w_key.astype(jnp.float32), w_value.astype(jnp.float32), w_out.astype(jnp.float32), w_in.astype(jnp.float32), w_back.astype(jnp.float32), gain_one, shift_one, gain_two, shift_two)
    layer_out, pull_back = jax.vjp(run, tokens.astype(jnp.float32), *weights)
    grads_all = pull_back(cotangent.astype(jnp.float32))
    return (layer_out.astype(jnp.bfloat16), grads_all[0], grads_all[1], grads_all[2], grads_all[3], grads_all[4], grads_all[5], grads_all[6], grads_all[7], grads_all[8], grads_all[9], grads_all[10])
```

```python
from functools import partial

import jax
import jax.numpy as jnp
from jax import lax
from jax.sharding import PartitionSpec as P

HEADS = 12
HEAD_DIM = 64


half_pi = 1.5707963267948966
norm_eps = 1e-05
highest = lax.Precision.HIGHEST


def entering(part, axis, combine, identity, reverse):
    count = lax.axis_size(axis)
    place = lax.axis_index(axis)
    ahead = count - 1 - place if reverse else place
    gathered = jax.tree.map(lambda a: lax.all_gather(a, axis), part)
    state = jax.tree.map(lambda a, e: jnp.zeros_like(a) + jnp.asarray(e, a.dtype), part, identity)

    def one(step, state):
        source = count - 1 - step if reverse else step
        return combine(
            state, jax.tree.map(lambda a: lax.dynamic_index_in_dim(a, source, 0, False), gathered)
        )

    return lax.fori_loop(0, ahead, one, state)


def doc_tables(lengths, positions):
    order = jnp.arange(lengths.shape[-1])
    upto = (order[:, None] >= order[None, :]).astype(jnp.int32)
    doc_ends = jnp.sum(lengths[:, None, :] * upto[None], axis=-1)
    starts = doc_ends - lengths
    inside = (
        (positions[None, :, None] >= starts[:, None, :])
        & (positions[None, :, None] < doc_ends[:, None, :])
    ).astype(jnp.int32)
    doc_begin = jnp.sum(inside * starts[:, None, :], axis=-1)
    doc_span = jnp.sum(inside * lengths[:, None, :], axis=-1)
    return (doc_begin, doc_span)


def norm_parts(summed):
    centered = summed - jnp.mean(summed, axis=-1, keepdims=True)
    inv_scale = lax.rsqrt(jnp.mean(centered * centered, axis=-1, keepdims=True) + norm_eps)
    return (centered * inv_scale, inv_scale)


def norm_back(grad_norm, normed, inv_scale):
    return inv_scale * (
        grad_norm
        - jnp.mean(grad_norm, axis=-1, keepdims=True)
        - normed * jnp.mean(grad_norm * normed, axis=-1, keepdims=True)
    )


def combine_state(earlier, latter):
    factor = latter[2]
    return (
        latter[0] + factor[:, None, None] * earlier[0],
        latter[1] + factor[:, None] * earlier[1],
        earlier[2] * latter[2],
    )


def body(
    tokens,
    cotangent,
    doc_lengths,
    w_query,
    w_key,
    w_value,
    w_out,
    w_in,
    w_back,
    gain_one,
    shift_one,
    gain_two,
    shift_two,
):
    row_count, tok_count, model_width = tokens.shape
    head_count = HEADS
    head_size = HEAD_DIM
    flat_count = row_count * tok_count
    first_place = lax.axis_index("seq") * tok_count
    positions = first_place + jnp.arange(tok_count, dtype=jnp.int32)
    doc_begin, doc_span = doc_tables(doc_lengths, positions)
    doc_pos = positions[None, :] - doc_begin
    angles = half_pi * doc_pos.astype(jnp.float32) / doc_span.astype(jnp.float32)
    trig_pair = jnp.stack([jnp.cos(angles), jnp.sin(angles)], axis=1)
    reader = (doc_begin < first_place).astype(jnp.float32)
    last_begin = doc_begin[:, -1:]
    tail_mask = (doc_begin == last_begin).astype(jnp.float32)
    keep_flag = (last_begin[:, 0] < first_place).astype(jnp.float32)
    causal = jnp.arange(tok_count)[:, None] >= jnp.arange(tok_count)[None, :]
    same_doc = (doc_begin[:, :, None] == doc_begin[:, None, :]) & causal[None]
    blend = jnp.where(
        same_doc, jnp.einsum("rti,rtj->rij", trig_pair, trig_pair, precision=highest), 0.0
    )
    trig_read = trig_pair * reader[:, None, :]
    trig_tail = trig_pair * tail_mask[:, None, :]
    flat_tokens = tokens.reshape(flat_count, model_width)
    query_pre = jnp.dot(flat_tokens, w_query, preferred_element_type=jnp.float32)
    key_pre = jnp.dot(flat_tokens, w_key, preferred_element_type=jnp.float32)
    value_pre = jnp.dot(flat_tokens, w_value, preferred_element_type=jnp.float32)
    head_shape = (row_count, tok_count, head_count, head_size)
    query_heads = (
        jax.nn.softplus(query_pre).astype(jnp.bfloat16).astype(jnp.float32).reshape(head_shape)
    )
    key_heads = (
        jax.nn.softplus(key_pre).astype(jnp.bfloat16).astype(jnp.float32).reshape(head_shape)
    )
    value_heads = value_pre.astype(jnp.bfloat16).astype(jnp.float32).reshape(head_shape)
    scores = (
        jnp.einsum("rihd,rjhd->rhij", query_heads, key_heads, precision=highest) * blend[:, None]
    )
    numer = jnp.einsum("rhij,rjhd->rihd", scores, value_heads, precision=highest)
    denom = jnp.swapaxes(jnp.sum(scores, axis=-1), 1, 2)
    weighted_keys = trig_tail[:, :, :, None, None] * key_heads[:, None]
    local_mats = jnp.einsum("rtjhk,rjhv->rthkv", weighted_keys, value_heads, precision=highest)
    local_sums = jnp.sum(weighted_keys, axis=2)
    pair_shape = (row_count, 2 * head_count, head_size * head_size)
    sums_shape = (row_count, 2 * head_count * head_size)
    outgoing = (local_mats.reshape(pair_shape), local_sums.reshape(sums_shape), keep_flag)
    identity = (
        jnp.zeros(pair_shape, jnp.float32),
        jnp.zeros(sums_shape, jnp.float32),
        jnp.ones((row_count,), jnp.float32),
    )
    in_mats, in_sums, unused = entering(outgoing, "seq", combine_state, identity, False)
    in_mats = in_mats.reshape(row_count, 2, head_count, head_size, head_size)
    in_sums = in_sums.reshape(row_count, 2, head_count, head_size)
    query_read = trig_read[:, :, :, None, None] * query_heads[:, None]
    numer = numer + jnp.einsum("rtihk,rthkv->rihv", query_read, in_mats, precision=highest)
    denom = denom + jnp.einsum("rtihk,rthk->rih", query_read, in_sums, precision=highest)
    attended = numer / denom[..., None]
    att_low = attended.reshape(flat_count, model_width).astype(jnp.bfloat16)
    branch = jnp.dot(att_low, w_out, preferred_element_type=jnp.float32)
    normed_one, scale_one = norm_parts(flat_tokens.astype(jnp.float32) + branch)
    first_out = normed_one * gain_one + shift_one
    first_low = first_out.astype(jnp.bfloat16)
    hidden = jnp.dot(first_low, w_in, preferred_element_type=jnp.float32)
    active, gelu_pull = jax.vjp(partial(jax.nn.gelu, approximate=False), hidden)
    active_low = active.astype(jnp.bfloat16)
    second = jnp.dot(active_low, w_back, preferred_element_type=jnp.float32)
    normed_two, scale_two = norm_parts(first_out + second)
    layer_out = (normed_two * gain_two + shift_two).astype(jnp.bfloat16).reshape(tokens.shape)
    grad_top = cotangent.reshape(flat_count, model_width).astype(jnp.float32)
    grad_gain_two = jnp.sum(grad_top * normed_two, axis=0)
    grad_shift_two = jnp.sum(grad_top, axis=0)
    grad_mid = norm_back(grad_top * gain_two, normed_two, scale_two)
    grad_second = grad_mid.astype(jnp.bfloat16)
    grad_back = jnp.dot(active_low.T, grad_second, preferred_element_type=jnp.float32)
    grad_active = jnp.dot(grad_second, w_back.T, preferred_element_type=jnp.float32)
    grad_hidden = gelu_pull(grad_active)[0].astype(jnp.bfloat16)
    grad_in = jnp.dot(first_low.T, grad_hidden, preferred_element_type=jnp.float32)
    grad_first = grad_mid + jnp.dot(grad_hidden, w_in.T, preferred_element_type=jnp.float32)
    grad_gain_one = jnp.sum(grad_first * normed_one, axis=0)
    grad_shift_one = jnp.sum(grad_first, axis=0)
    grad_base = norm_back(grad_first * gain_one, normed_one, scale_one)
    grad_branch = grad_base.astype(jnp.bfloat16)
    grad_out = jnp.dot(att_low.T, grad_branch, preferred_element_type=jnp.float32)
    grad_att = jnp.dot(grad_branch, w_out.T, preferred_element_type=jnp.float32).reshape(head_shape)
    grad_numer = grad_att / denom[..., None]
    grad_denom = -jnp.sum(grad_att * attended, axis=-1) / denom
    grad_scores = (
        jnp.einsum("rihv,rjhv->rhij", grad_numer, value_heads, precision=highest)
        + jnp.swapaxes(grad_denom, 1, 2)[..., None]
    ) * blend[:, None]
    grad_vheads = jnp.einsum("rhij,rihv->rjhv", scores, grad_numer, precision=highest)
    grad_qheads = jnp.einsum("rhij,rjhk->rihk", grad_scores, key_heads, precision=highest)
    grad_kheads = jnp.einsum("rhij,rihk->rjhk", grad_scores, query_heads, precision=highest)
    read_inner = (
        jnp.einsum("rthkv,rihv->rtihk", in_mats, grad_numer, precision=highest)
        + grad_denom[:, None, :, :, None] * in_sums[:, :, None]
    )
    grad_qheads = grad_qheads + jnp.sum(trig_read[:, :, :, None, None] * read_inner, axis=1)
    read_mats = jnp.einsum("rtihk,rihv->rthkv", query_read, grad_numer, precision=highest)
    read_sums = jnp.einsum("rtihk,rih->rthk", query_read, grad_denom, precision=highest)
    incoming_grad = (read_mats.reshape(pair_shape), read_sums.reshape(sums_shape), keep_flag)
    out_mats, out_sums, unused_two = entering(incoming_grad, "seq", combine_state, identity, True)
    out_mats = out_mats.reshape(row_count, 2, head_count, head_size, head_size)
    out_sums = out_sums.reshape(row_count, 2, head_count, head_size)
    tail_inner = (
        jnp.einsum("rthkv,rjhv->rtjhk", out_mats, value_heads, precision=highest)
        + out_sums[:, :, None]
    )
    grad_kheads = grad_kheads + jnp.sum(trig_tail[:, :, :, None, None] * tail_inner, axis=1)
    grad_vheads = grad_vheads + jnp.einsum(
        "rtjhk,rthkv->rjhv", weighted_keys, out_mats, precision=highest
    )
    grad_qpre = (grad_qheads.reshape(flat_count, model_width) * jax.nn.sigmoid(query_pre)).astype(
        jnp.bfloat16
    )
    grad_kpre = (grad_kheads.reshape(flat_count, model_width) * jax.nn.sigmoid(key_pre)).astype(
        jnp.bfloat16
    )
    grad_vpre = grad_vheads.reshape(flat_count, model_width).astype(jnp.bfloat16)
    grad_query = jnp.dot(flat_tokens.T, grad_qpre, preferred_element_type=jnp.float32)
    grad_key = jnp.dot(flat_tokens.T, grad_kpre, preferred_element_type=jnp.float32)
    grad_value = jnp.dot(flat_tokens.T, grad_vpre, preferred_element_type=jnp.float32)
    grad_tokens = grad_base + jnp.dot(grad_qpre, w_query.T, preferred_element_type=jnp.float32)
    grad_tokens = grad_tokens + jnp.dot(grad_kpre, w_key.T, preferred_element_type=jnp.float32)
    grad_tokens = grad_tokens + jnp.dot(grad_vpre, w_value.T, preferred_element_type=jnp.float32)
    grad_tokens = grad_tokens.reshape(tokens.shape)
    shards = (
        lax.psum_scatter(grad_query, "seq", scatter_dimension=0, tiled=True),
        lax.psum_scatter(grad_key, "seq", scatter_dimension=0, tiled=True),
        lax.psum_scatter(grad_value, "seq", scatter_dimension=0, tiled=True),
        lax.psum_scatter(grad_out, "seq", scatter_dimension=0, tiled=True),
        lax.psum_scatter(grad_in, "seq", scatter_dimension=0, tiled=True),
        lax.psum_scatter(grad_back, "seq", scatter_dimension=0, tiled=True),
        lax.psum_scatter(grad_gain_one, "seq", scatter_dimension=0, tiled=True),
        lax.psum_scatter(grad_shift_one, "seq", scatter_dimension=0, tiled=True),
        lax.psum_scatter(grad_gain_two, "seq", scatter_dimension=0, tiled=True),
        lax.psum_scatter(grad_shift_two, "seq", scatter_dimension=0, tiled=True),
    )
    totals = lax.psum(
        (
            shards[0],
            shards[1],
            shards[2],
            shards[3],
            shards[4],
            shards[5],
            shards[6],
            shards[7],
            shards[8],
            shards[9],
        ),
        "batch",
    )
    return (
        layer_out,
        grad_tokens,
        totals[0],
        totals[1],
        totals[2],
        totals[3],
        totals[4],
        totals[5],
        totals[6],
        totals[7],
        totals[8],
        totals[9],
    )


def solution(mesh):
    in_specs = (
        P("batch", "seq", None),
        P("batch", "seq", None),
        P("batch", None),
        P(),
        P(),
        P(),
        P(),
        P(),
        P(),
        P(),
        P(),
        P(),
        P(),
    )
    out_specs = (
        P("batch", "seq", None),
        P("batch", "seq", None),
        P("seq", None),
        P("seq", None),
        P("seq", None),
        P("seq", None),
        P("seq", None),
        P("seq", None),
        P("seq"),
        P("seq"),
        P("seq"),
        P("seq"),
    )
    return jax.shard_map(body, mesh=mesh, in_specs=in_specs, out_specs=out_specs, check_vma=False)
```

```python
import jax
import jax.numpy as jnp
from jax import lax
from jax.experimental import pallas as pl
from jax.experimental.pallas import tpu as pltpu
from jax.sharding import PartitionSpec as P

HEADS = 12
HEAD_DIM = 64
PAIRS = HEADS // 2
HALF_HEADS = HEADS // 2
STATE_ROWS = HALF_HEADS * HEAD_DIM + 8

f32 = jnp.float32
bf16 = jnp.bfloat16
half_pi = 1.5707963267948966
norm_eps = 1e-05
VMEM_LIMIT = 58 * 1024 * 1024

NN = (((1,), (0,)), ((), ()))
NT = (((1,), (1,)), ((), ()))
TN = (((0,), (0,)), ((), ()))


def mm(a, b, dims=NN):
    return lax.dot_general(a, b, dims, preferred_element_type=f32)


COS, SIN, BEGIN, COS_READ, SIN_READ, COS_TAIL, SIN_TAIL = range(7)


def make_table(place, lens_ref, row, tok_count):
    pos = place + lax.broadcasted_iota(jnp.int32, (8, tok_count), 1)
    last = place + tok_count - 1
    start = jnp.int32(0)
    begin = jnp.zeros((8, tok_count), jnp.int32)
    span = jnp.ones((8, tok_count), jnp.int32)
    last_begin = jnp.int32(0)
    for d in range(lens_ref.shape[1]):
        length = lens_ref[row, d]
        inside = pos >= start
        begin = jnp.where(inside, start, begin)
        span = jnp.where(inside, length, span)
        last_begin = jnp.where(start <= last, start, last_begin)
        start = start + length
    angle = half_pi * (pos - begin).astype(f32) / span.astype(f32)
    cos, sin = jnp.cos(angle), jnp.sin(angle)
    reader = (begin < place).astype(f32)
    tail = (begin == last_begin).astype(f32)
    which = lax.broadcasted_iota(jnp.int32, (8, tok_count), 0)
    table = jnp.zeros((8, tok_count), f32)
    for index, value in (
        (COS, cos),
        (SIN, sin),
        (BEGIN, begin.astype(f32)),
        (COS_READ, cos * reader),
        (SIN_READ, sin * reader),
        (COS_TAIL, cos * tail),
        (SIN_TAIL, sin * tail),
    ):
        table = jnp.where(which == index, value, table)
    return table


def blend_of(table):
    columns = table.T
    tok_count = table.shape[1]
    source = lax.broadcasted_iota(jnp.int32, (tok_count, tok_count), 0)
    reader = lax.broadcasted_iota(jnp.int32, (tok_count, tok_count), 1)
    same = (columns[:, BEGIN : BEGIN + 1] == table[BEGIN : BEGIN + 1]) & (source <= reader)
    value = (
        columns[:, COS : COS + 1] * table[COS : COS + 1]
        + columns[:, SIN : SIN + 1] * table[SIN : SIN + 1]
    )
    return jnp.where(same, value, 0.0)


def trig_rows(head_rows, cos, sin):
    wide = head_rows.astype(f32)
    return jnp.concatenate([(wide * cos).astype(bf16), (wide * sin).astype(bf16)], axis=0)


def with_row(rows, extra):
    which = lax.broadcasted_iota(jnp.int32, (16, rows.shape[1]), 0)
    return jnp.concatenate([rows, jnp.where(which == 0, extra, 0.0).astype(bf16)], axis=0)


def head_slice(h):
    return slice(h * HEAD_DIM, (h + 1) * HEAD_DIM)


def put_state(state_refs, h, value):
    ref = state_refs[h // HALF_HEADS]
    place = h % HALF_HEADS
    ref[0, head_slice(place), :] = value[:HEAD_DIM]
    ref[0, HALF_HEADS * HEAD_DIM + place : HALF_HEADS * HEAD_DIM + place + 1, :] = value[
        HEAD_DIM : HEAD_DIM + 1
    ]


def take_state(state_refs, h):
    ref = state_refs[h // HALF_HEADS]
    place = h % HALF_HEADS
    mats = ref[0, head_slice(place), :].astype(bf16)
    sums = ref[0, HALF_HEADS * HEAD_DIM + place : HALF_HEADS * HEAD_DIM + place + 1, :]
    return with_row(mats, sums)


def clear_pad(state_refs):
    for ref in state_refs:
        ref[0, HALF_HEADS * HEAD_DIM :, :] = jnp.zeros((8, 2 * HEAD_DIM), f32)


def softplus_sigmoid(v):
    small = jnp.exp(-jnp.abs(v))
    soft = jnp.maximum(v, 0.0) + jnp.log1p(small)
    inverse = 1.0 / (1.0 + small)
    return soft, jnp.where(v >= 0, inverse, small * inverse)


def project_kernel(
    place_ref,
    lens_ref,
    tok_ref,
    wk_ref,
    wv_ref,
    tab_ref,
    tok_t_ref,
    k_t_ref,
    v_t_ref,
    k_ref,
    v_ref,
    sig_k_ref,
    state_a,
    state_b,
    w_t,
):
    row = pl.program_id(0)

    @pl.when(row == 0)
    def _():
        w_t[0] = wk_ref[...].T
        w_t[1] = wv_ref[...].T

    tok_t = tok_ref[0].T
    tok_t_ref[...] = tok_t
    table = make_table(place_ref[0], lens_ref, row, tok_t.shape[1])
    tab_ref[0] = table
    soft, sig = softplus_sigmoid(mm(w_t[0], tok_t))
    key_t = soft.astype(bf16)
    k_t_ref[...] = key_t
    k_ref[0] = key_t.T
    sig_k_ref[...] = sig.astype(bf16)
    value_t = mm(w_t[1], tok_t).astype(bf16)
    v_t_ref[...] = value_t
    v_ref[0] = value_t.T
    states = (state_a, state_b)
    clear_pad(states)
    cos, sin = table[COS_TAIL : COS_TAIL + 1], table[SIN_TAIL : SIN_TAIL + 1]
    for h in range(HEADS):
        keys = trig_rows(k_t_ref[head_slice(h), :], cos, sin)
        values = with_row(v_t_ref[head_slice(h), :], 1.0)
        put_state(states, h, mm(values, keys, NT))


def pair_rows(ref, pair):
    first = ref[head_slice(2 * pair), :]
    second = ref[head_slice(2 * pair + 1), :]
    nothing = jnp.zeros_like(first)
    return jnp.concatenate(
        [
            jnp.concatenate([first, nothing], axis=1),
            jnp.concatenate([nothing, second], axis=1),
        ],
        axis=0,
    )


def two_parts(v):
    high = v.astype(bf16)
    return high, (v - high.astype(f32)).astype(bf16)


def local_kernel(
    tab_ref,
    tok_t_ref,
    k_ref,
    v_t_ref,
    wq_ref,
    w_out_ref,
    w_in_ref,
    w_back_ref,
    q_t_ref,
    sig_q_ref,
    numer_ref,
    denom_ref,
    w_out_t,
    w_in_t,
    w_back_t,
    w_t,
):
    @pl.when(pl.program_id(0) == 0)
    def _():
        w_t[...] = wq_ref[...].T
        w_out_t[...] = w_out_ref[...].T

    w_in_t[...] = w_in_ref[...].T
    w_back_t[...] = w_back_ref[...].T

    soft, sig = softplus_sigmoid(mm(w_t[...], tok_t_ref[...]))
    q_t_ref[...] = soft.astype(bf16)
    sig_q_ref[...] = sig.astype(bf16)
    blend = blend_of(tab_ref[0])
    tok_count = blend.shape[0]
    denom_ref[...] = jnp.zeros_like(denom_ref)
    for pair in range(PAIRS):
        lanes = slice(pair * 2 * HEAD_DIM, (pair + 1) * 2 * HEAD_DIM)
        both = mm(k_ref[0, :, lanes], pair_rows(q_t_ref, pair))
        for side in range(2):
            h = 2 * pair + side
            high, low = two_parts(both[:, side * tok_count : (side + 1) * tok_count] * blend)
            values = with_row(v_t_ref[head_slice(h), :], 1.0)
            out = mm(values, high) + mm(values, low)
            numer_ref[head_slice(h), :] = out[:HEAD_DIM]
            denom_ref[h : h + 1, :] = out[HEAD_DIM : HEAD_DIM + 1]


def mean_rows(v):
    return jnp.sum(v, axis=0, keepdims=True) * (1.0 / v.shape[0])


def fold_lanes(v):
    total = v[:, :128]
    for at in range(128, v.shape[1], 128):
        total = total + v[:, at : at + 128]
    return total


def add_to(ref, value):
    first = pl.program_id(0) == 0

    @pl.when(first)
    def _():
        ref[...] = value

    @pl.when(jnp.logical_not(first))
    def _():
        ref[...] += value


def norm_back(grad_norm, normed, inv_scale):
    return inv_scale * (grad_norm - mean_rows(grad_norm) - normed * mean_rows(grad_norm * normed))


def forward_kernel(
    tab_ref,
    q_t_ref,
    numer_ref,
    denom_loc_ref,
    state_a,
    state_b,
    tok_t_ref,
    cot_ref,
    w_out_t,
    w_in_t,
    w_back_t,
    gain_one_ref,
    shift_one_ref,
    gain_two_ref,
    shift_two_ref,
    layer_ref,
    denom_ref,
    att_t_ref,
    att_low_ref,
    first_t_ref,
    normed_t_ref,
    scale_ref,
    active_t_ref,
    slope_t_ref,
    grad_mid_ref,
    grad_second_ref,
    grad_gain_ref,
    grad_shift_ref,
    second,
):
    table = tab_ref[0]
    cos, sin = table[COS_READ : COS_READ + 1], table[SIN_READ : SIN_READ + 1]
    states = (state_a, state_b)
    denom_ref[...] = denom_loc_ref[...]
    for h in range(HEADS):
        reads = trig_rows(q_t_ref[head_slice(h), :], cos, sin)
        more = mm(take_state(states, h), reads)
        numer = numer_ref[head_slice(h), :] + more[:HEAD_DIM]
        denom = denom_loc_ref[h : h + 1, :] + more[HEAD_DIM : HEAD_DIM + 1]
        denom_ref[h : h + 1, :] = denom
        high, low = two_parts(numer * (1.0 / denom))
        att_t_ref[head_slice(h), :] = high
        att_low_ref[head_slice(h), :] = low
    summed = tok_t_ref[...].astype(f32) + mm(w_out_t[...], att_t_ref[...])
    centered = summed - mean_rows(summed)
    inv_scale = lax.rsqrt(mean_rows(centered * centered) + norm_eps)
    scale_ref[...] = jnp.broadcast_to(inv_scale, scale_ref.shape)
    normed = centered * inv_scale
    normed_t_ref[...] = normed
    first_out = normed * gain_one_ref[...] + shift_one_ref[...]
    first_low = first_out.astype(bf16)
    first_t_ref[...] = first_low
    for at in range(0, w_in_t.shape[0], 768):
        hidden = mm(w_in_t[at : at + 768, :], first_low)
        half = 0.5 * (1.0 + lax.erf(hidden * 0.7071067811865476))
        bell = jnp.exp(hidden * hidden * -0.5) * 0.3989422804014327
        active = (hidden * half).astype(bf16)
        active_t_ref[at : at + 768, :] = active
        slope_t_ref[at : at + 768, :] = (half + hidden * bell).astype(bf16)
        part = mm(w_back_t[:, at : at + 768], active)
        if at == 0:
            second[...] = part
        else:
            second[...] += part
    summed = normed_t_ref[...] * gain_one_ref[...] + shift_one_ref[...] + second[...]
    centered = summed - mean_rows(summed)
    inv_scale = lax.rsqrt(mean_rows(centered * centered) + norm_eps)
    normed = centered * inv_scale
    layer_ref[0] = (normed * gain_two_ref[...] + shift_two_ref[...]).T.astype(bf16)
    grad_top = cot_ref[0].T.astype(f32)
    add_to(grad_gain_ref, fold_lanes(grad_top * normed))
    add_to(grad_shift_ref, fold_lanes(grad_top))
    grad_mid = norm_back(grad_top * gain_two_ref[...], normed, inv_scale)
    grad_mid_ref[...] = grad_mid
    grad_second_ref[...] = grad_mid.astype(bf16)


def backward_kernel(
    tab_ref,
    q_t_ref,
    denom_ref,
    att_t_ref,
    att_low_ref,
    normed_t_ref,
    scale_ref,
    slope_t_ref,
    grad_mid_ref,
    grad_second_ref,
    w_out_ref,
    w_in_ref,
    w_back_ref,
    gain_one_ref,
    grad_hidden_ref,
    grad_base_ref,
    grad_branch_ref,
    grad_numer_ref,
    grad_denom_ref,
    grad_gain_ref,
    grad_shift_ref,
    state_a,
    state_b,
    total,
):
    total[...] = grad_mid_ref[...]
    grad_second = grad_second_ref[...]
    for at in range(0, w_in_ref.shape[1], 768):
        grad_active = mm(w_back_ref[at : at + 768, :], grad_second)
        low = (grad_active * slope_t_ref[at : at + 768, :].astype(f32)).astype(bf16)
        grad_hidden_ref[at : at + 768, :] = low
        total[...] += mm(w_in_ref[:, at : at + 768], low)
    grad_first = total[...]
    normed = normed_t_ref[...]
    add_to(grad_gain_ref, fold_lanes(grad_first * normed))
    add_to(grad_shift_ref, fold_lanes(grad_first))
    grad_base = norm_back(grad_first * gain_one_ref[...], normed, scale_ref[0:1, :])
    grad_base_ref[...] = grad_base
    grad_branch = grad_base.astype(bf16)
    grad_branch_ref[...] = grad_branch
    total[...] = mm(w_out_ref[...], grad_branch)
    table = tab_ref[0]
    cos, sin = table[COS_READ : COS_READ + 1], table[SIN_READ : SIN_READ + 1]
    states = (state_a, state_b)
    clear_pad(states)
    grad_denom_ref[...] = jnp.zeros_like(grad_denom_ref)
    for h in range(HEADS):
        inverse = 1.0 / denom_ref[h : h + 1, :]
        grad_att = total[head_slice(h), :]
        grad_numer = (grad_att * inverse).astype(bf16)
        attended = att_t_ref[head_slice(h), :].astype(f32) + att_low_ref[head_slice(h), :].astype(f32)
        grad_denom = -jnp.sum(grad_numer.astype(f32) * attended, axis=0, keepdims=True)
        grad_denom_ref[h : h + 1, :] = grad_denom
        grad_numer_ref[head_slice(h), :] = grad_numer
        reads = trig_rows(q_t_ref[head_slice(h), :], cos, sin)
        put_state(states, h, mm(with_row(grad_numer, grad_denom), reads, NT))


def local_back_kernel(
    tab_ref,
    q_t_ref,
    k_t_ref,
    k_ref,
    v_ref,
    sig_q_ref,
    grad_numer_ref,
    grad_denom_ref,
    state_a,
    state_b,
    grad_q_ref,
    grad_k_ref,
    grad_v_ref,
):
    table = tab_ref[0]
    blend = blend_of(table)
    tok_count = blend.shape[0]
    cos, sin = table[COS_READ : COS_READ + 1], table[SIN_READ : SIN_READ + 1]
    states = (state_a, state_b)
    for pair in range(PAIRS):
        lanes = slice(pair * 2 * HEAD_DIM, (pair + 1) * 2 * HEAD_DIM)
        both = mm(k_ref[0, :, lanes], pair_rows(q_t_ref, pair))
        grads = mm(v_ref[0, :, lanes], pair_rows(grad_numer_ref, pair))
        for side in range(2):
            h = 2 * pair + side
            rows = head_slice(h)
            part = slice(side * tok_count, (side + 1) * tok_count)
            grad_denom = grad_denom_ref[h : h + 1, :]
            scores = (both[:, part] * blend).astype(bf16)
            grad_scores, rest = two_parts((grads[:, part] + grad_denom) * blend)
            grad_numer = grad_numer_ref[rows, :]
            grad_v_ref[rows, :] = mm(grad_numer, scores, NT)
            grad_k_ref[rows, :] = mm(q_t_ref[rows, :], grad_scores, NT)
            reads = mm(take_state(states, h), with_row(grad_numer, grad_denom), TN)
            grad_q = (
                mm(k_t_ref[rows, :], grad_scores)
                + mm(k_t_ref[rows, :], rest)
                + cos * reads[:HEAD_DIM]
                + sin * reads[HEAD_DIM:]
            )
            grad_q_ref[rows, :] = (grad_q * sig_q_ref[rows, :].astype(f32)).astype(bf16)


def tail_kernel(
    tab_ref,
    k_t_ref,
    v_t_ref,
    sig_k_ref,
    state_a,
    state_b,
    grad_k_in,
    grad_v_in,
    grad_kv_ref,
):
    table = tab_ref[0]
    cos, sin = table[COS_TAIL : COS_TAIL + 1], table[SIN_TAIL : SIN_TAIL + 1]
    states = (state_a, state_b)
    for h in range(HEADS):
        rows = head_slice(h)
        state = take_state(states, h)
        inner = mm(state, with_row(v_t_ref[rows, :], 1.0), TN)
        grad_k = grad_k_in[rows, :] + cos * inner[:HEAD_DIM] + sin * inner[HEAD_DIM:]
        grad_kv_ref[0, rows, :] = (grad_k * sig_k_ref[rows, :].astype(f32)).astype(bf16)
        keys = trig_rows(k_t_ref[rows, :], cos, sin)
        grad_kv_ref[1, rows, :] = (grad_v_in[rows, :] + mm(state[:HEAD_DIM], keys)).astype(bf16)


def token_kernel(gq_ref, gkv_ref, base_ref, wq_ref, wk_ref, wv_ref, out_ref):
    total = base_ref[...] + mm(wq_ref[...], gq_ref[...])
    total = total + mm(wk_ref[...], gkv_ref[0])
    total = total + mm(wv_ref[...], gkv_ref[1])
    out_ref[0] = total.T


def first_begins(lengths, count, tok_count):
    slots = lengths.shape[1]
    order = jnp.arange(slots)
    before = (order[:, None] > order[None, :]).astype(jnp.int32)
    starts = jnp.sum(lengths[:, None, :] * before[None], axis=-1)
    firsts = jnp.arange(count, dtype=jnp.int32) * tok_count
    reached = starts[:, None, :] <= firsts[None, :, None]
    return jnp.max(jnp.where(reached, starts[:, None, :], 0), axis=-1)


def pick(index, values):
    out = values[0]
    for i in range(1, len(values)):
        out = jnp.where(index == i, values[i], out)
    return out[:, None, None]


class Order:
    def __init__(self):
        self.last = None

    def tie(self, value):
        if self.last is None:
            return value
        return lax.optimization_barrier((value, self.last))[0]

    def done(self, value):
        self.last = value
        return value


def entering(order, parts, begin_first, tok_count, reverse):
    count = lax.axis_size("seq")
    place = lax.axis_index("seq")
    part_a, part_b = parts

    def covers(i, j):
        low, high = (count - 1 - j, count - 1 - i) if reverse else (i, j)
        return (begin_first[:, high] < (low + 1) * tok_count).astype(f32)

    if count != 4:
        spots = jnp.arange(count)
        mine = begin_first.T if reverse else begin_first[:, place][None]
        reach = (place if reverse else spots[:, None]) + 1
        ahead = (spots > place) if reverse else (spots < place)
        weight = ((mine < reach * tok_count) & ahead[:, None]).astype(f32)
        gathered = [lax.all_gather(p, "seq") for p in parts]
        yield
        yield
        yield tuple(jnp.sum(g * weight[:, :, None, None], axis=0) for g in gathered)
    index = count - 1 - place if reverse else place

    zero = jnp.zeros_like(begin_first[:, 0], f32)
    one = zero + 1.0
    m02, m03, m13 = covers(0, 2), covers(0, 3), covers(1, 3)
    own_a, first_a = pick(index, [m02, m13, zero, zero]), pick(index, [one, m03, zero, zero])
    own_b, first_b = pick(index, [one, zero, one, zero]), pick(index, [zero, zero, m03, one])
    end_a, then_a = pick(index, [zero, one, zero, one]), pick(index, [zero, zero, one, one])
    end_b, then_b = pick(index, [zero, zero, m02, m13]), pick(index, [zero, one, one, one])
    got_a = swap(part_a, "seq", 1)
    got_b = swap(part_b, "seq", 2)
    yield
    got_a, got_b = order.tie((got_a, got_b))
    next_a = own_a * part_a + first_a * got_a
    next_b = own_b * part_b + first_b * got_b
    order.done((next_a, next_b))
    last_a = swap(next_a, "seq", 2)
    last_b = swap(next_b, "seq", 1)
    yield
    last_a, last_b = order.tie((last_a, last_b))
    full = (end_a * got_a + then_a * last_a, end_b * got_b + then_b * last_b)
    yield order.done(full)


def take(value, index, dim):
    return lax.dynamic_index_in_dim(value, index, dim, False)


def swap(value, axis, distance):
    count = lax.axis_size(axis)
    return lax.ppermute(value, axis, [(i, i ^ distance) for i in range(count)])


def reduced(order, away, keep):
    shards, rows, columns = keep.shape
    place = lax.axis_index("seq")
    batch_place = lax.axis_index("batch")
    count = lax.axis_size("batch")
    bits = shards.bit_length() - 1
    got = swap(away, "batch", 1)
    yield
    summed = keep + order.tie(got)
    shape = (2,) * bits + (rows // 2, columns)
    parts = [summed[:, : rows // 2].reshape(shape), summed[:, rows // 2 :].reshape(shape)]
    left = [list(range(bits - 1, -1, -1)) for _ in parts]
    orders = [list(range(bits)), list(range(bits - 1, -1, -1))]
    for step in range(bits):
        aways, keeps = [], []
        for side, part in enumerate(parts):
            bit = orders[side][step]
            dim = left[side].index(bit)
            left[side].pop(dim)
            mine = (place >> bit) & 1
            aways.append(take(part, 1 - mine, dim))
            keeps.append(take(part, mine, dim))
        aways, keeps = order.done((aways, keeps))
        gots = [swap(a, "seq", 1 << orders[side][step]) for side, a in enumerate(aways)]
        yield
        parts = [k + g for k, g in zip(keeps, order.tie(gots))]
    odd = (batch_place >> 1) & 1 == 1
    away = jnp.where(odd, parts[0], parts[1])
    part = jnp.where(odd, parts[1], parts[0])
    away, part = order.done((away, part))
    got = swap(away, "batch", 2)
    yield
    part = order.done(part + order.tie(got))
    distance = 4
    while distance < count:
        got = swap(part, "batch", distance)
        yield
        part = order.done(part + order.tie(got))
        distance *= 2
    got = swap(part, "batch", 2)
    yield
    got = order.tie(got)
    mine = order.done(
        jnp.concatenate([jnp.where(odd, got, part), jnp.where(odd, part, got)], axis=0)
    )
    other = swap(mine, "batch", 1)
    yield
    other = order.tie(other)
    first = batch_place & 1 == 0
    yield order.done((jnp.where(first, mine, other), jnp.where(first, other, mine)))


def call(kernel, grid, ins, outs, scratch, flops, moved, *args):
    return pl.pallas_call(
        kernel,
        grid=grid,
        in_specs=[s for s in ins],
        out_specs=[s for s, _ in outs],
        out_shape=[jax.ShapeDtypeStruct(shape, kind) for _, (shape, kind) in outs],
        scratch_shapes=scratch,
        compiler_params=pltpu.CompilerParams(
            dimension_semantics=("arbitrary",) * len(grid), vmem_limit_bytes=VMEM_LIMIT
        ),
        cost_estimate=pl.CostEstimate(flops=flops, bytes_accessed=moved, transcendentals=0),
    )(*args)


def body(
    tokens,
    cotangent,
    doc_lengths,
    w_query,
    w_key,
    w_value,
    w_out,
    w_in,
    w_back,
    gain_one,
    shift_one,
    gain_two,
    shift_two,
):
    rows, toks, width = tokens.shape
    ff = w_in.shape[1]
    flat = rows * toks
    shards = lax.axis_size("seq")
    place = (lax.axis_index("seq") * toks).astype(jnp.int32)
    begin_first = first_begins(doc_lengths, shards, toks)
    smem = pl.BlockSpec(memory_space=pltpu.SMEM)
    whole = pl.BlockSpec(memory_space=pltpu.VMEM)
    token_major = pl.BlockSpec((1, toks, width), lambda r: (r, 0, 0))
    table_spec = pl.BlockSpec((1, 8, toks), lambda r: (r, 0, 0))
    state_spec = pl.BlockSpec((1, STATE_ROWS, 2 * HEAD_DIM), lambda r: (r, 0, 0))
    fold_spec = pl.BlockSpec((width, 128), lambda r: (0, 0))

    def feature(count):
        return pl.BlockSpec((count, toks), lambda r: (0, r))

    tok_low = (token_major, ((rows, toks, width), bf16))
    wide_low = (feature(width), ((width, flat), bf16))
    wide_full = (feature(width), ((width, flat), f32))
    ff_low = (feature(ff), ((ff, flat), bf16))
    head_rows = (feature(16), ((16, flat), f32))
    one_row = (feature(8), ((8, flat), f32))
    fold = (fold_spec, ((width, 128), f32))
    state = (state_spec, ((rows, STATE_ROWS, 2 * HEAD_DIM), f32))
    cell = 2 * flat * toks * 256
    grid = (rows,)

    order = Order()
    core = (lax.axis_index("batch") % 2).astype(jnp.int32)

    def run(kernel, ins, outs, scratch, flops, first, *args):
        return order.done(call(kernel, grid, ins, outs, scratch, flops // 4, 1_000_000, order.tie(first), *args))

    def halves(b):
        split = b.reshape(b.shape[0], 2, b.shape[1] // 2, flat)
        return [take(split, c, 1).reshape(-1, flat) for c in (1 - core, core)]

    def product(a, b):
        grad = lax.dot_general(order.tie(a), b, NT, preferred_element_type=f32)
        return order.done(grad.reshape(shards, a.shape[0] // shards, b.shape[0]))

    def reduction(a, b):
        away, keep = halves(b)
        away = product(a, away)
        return reduced(order, away, product(a, keep))

    def column(v):
        return v[:, None]

    table, tok_t, k_t, v_t, key, value, sig_k, state_a, state_b = run(
        project_kernel,
        [smem, smem, token_major, whole, whole],
        [(table_spec, ((rows, 8, toks), f32))]
        + [wide_low] * 3
        + [tok_low] * 2
        + [wide_low]
        + [state] * 2,
        [pltpu.VMEM((2, width, width), bf16)],
        4 * flat * width * width,
        place[None],
        doc_lengths,
        tokens,
        w_key,
        w_value,
    )
    states = entering(order, (state_a, state_b), begin_first, toks, False)
    next(states)
    part = ff // rows
    q_t, sig_q, numer, denom_loc, w_out_t, w_in_t, w_back_t = run(
        local_kernel,
        [
            table_spec,
            feature(width),
            token_major,
            feature(width),
            whole,
            whole,
            pl.BlockSpec((width, part), lambda r: (0, r)),
            pl.BlockSpec((part, width), lambda r: (r, 0)),
        ],
        [
            wide_low,
            wide_low,
            wide_full,
            head_rows,
            (pl.BlockSpec((width, width), lambda r: (0, 0)), ((width, width), bf16)),
            (pl.BlockSpec((part, width), lambda r: (r, 0)), ((ff, width), bf16)),
            (pl.BlockSpec((width, part), lambda r: (0, r)), ((width, ff), bf16)),
        ],
        [pltpu.VMEM((width, width), bf16)],
        2 * cell * HEADS,
        table,
        tok_t,
        key,
        v_t,
        w_query,
        w_out,
        w_in,
        w_back,
    )
    next(states)
    in_a, in_b = next(states)
    (
        layer_out,
        denom,
        att_t,
        att_low,
        first_t,
        normed_t,
        scale_one,
        active_t,
        slope_t,
        grad_mid,
        grad_second,
        fold_gain_two,
        fold_shift_two,
    ) = run(
        forward_kernel,
        [
            table_spec,
            feature(width),
            feature(width),
            feature(16),
            state_spec,
            state_spec,
            feature(width),
            token_major,
        ]
        + [whole] * 7,
        [
            tok_low,
            head_rows,
            wide_low,
            wide_low,
            wide_low,
            wide_full,
            one_row,
            ff_low,
            ff_low,
            wide_full,
            wide_low,
            fold,
            fold,
        ],
        [pltpu.VMEM((width, toks), f32)],
        2 * flat * width * (width + 2 * ff),
        table,
        q_t,
        numer,
        denom_loc,
        in_a,
        in_b,
        tok_t,
        cotangent,
        w_out_t,
        w_in_t,
        w_back_t,
        column(gain_one),
        column(shift_one),
        column(gain_two),
        column(shift_two),
    )

    back = reduction(active_t, grad_second[None])
    next(back)
    next(back)
    (
        grad_hidden,
        grad_base,
        grad_branch,
        grad_numer,
        grad_denom,
        fold_gain_one,
        fold_shift_one,
        out_a,
        out_b,
    ) = run(
        backward_kernel,
        [
            table_spec,
            feature(width),
            feature(16),
            feature(width),
            feature(width),
            feature(width),
            feature(8),
            feature(ff),
            feature(width),
            feature(width),
        ]
        + [whole] * 4,
        [ff_low, wide_full, wide_low, wide_low, head_rows, fold, fold, state, state],
        [pltpu.VMEM((width, toks), f32)],
        2 * flat * width * (width + 2 * ff),
        table,
        q_t,
        denom,
        att_t,
        att_low,
        normed_t,
        scale_one,
        slope_t,
        grad_mid,
        grad_second,
        w_out,
        w_in,
        w_back,
        column(gain_one),
    )
    back_states = entering(order, (out_a, out_b), begin_first, toks, True)
    next(back_states)
    into = reduction(first_t, grad_hidden[None])
    next(into)
    next(back)
    next(back_states)
    grad_qpre, grad_k_loc, grad_v_loc = run(
        local_back_kernel,
        [
            table_spec,
            feature(width),
            feature(width),
            token_major,
            token_major,
            feature(width),
            feature(width),
            feature(16),
            state_spec,
            state_spec,
        ],
        [wide_low, wide_full, wide_full],
        [],
        5 * cell * HEADS,
        table,
        q_t,
        k_t,
        key,
        value,
        sig_q,
        grad_numer,
        grad_denom,
        in_a,
        in_b,
    )
    share = width // shards
    small = jnp.stack(
        [
            jnp.sum(v, axis=1)
            for v in order.tie((fold_gain_one, fold_shift_one, fold_gain_two, fold_shift_two))
        ]
    )
    small = small.reshape(4, shards, share).transpose(1, 0, 2).reshape(shards, 1, 4 * share)
    small = order.done(jnp.pad(small, ((0, 0), (0, 15), (0, width - 4 * share))))

    def mixed_part(half, out_rows, query_rows):
        columns = jnp.concatenate(
            [
                lax.dot_general(a, b, NT, preferred_element_type=f32)
                for a, b in ((order.tie(att_t), out_rows), (tok_t, query_rows))
            ],
            axis=1,
        )
        cut = width // 2
        extra = lax.dynamic_slice_in_dim(small, half * cut, cut, 2)
        extra = jnp.pad(extra, ((0, 0), (0, 0), (0, cut)))
        return order.done(
            jnp.concatenate([columns.reshape(shards, share, width), extra], axis=1)
        )

    out_halves, query_halves = halves(grad_branch[None]), halves(grad_qpre[None])
    away = mixed_part(1 - core, out_halves[0], query_halves[0])
    mixed = reduced(order, away, mixed_part(core, out_halves[1], query_halves[1]))
    next(mixed)
    next(back)
    next(into)
    back_a, back_b = next(back_states)
    (grad_kv,) = run(
        tail_kernel,
        [table_spec]
        + [feature(width)] * 3
        + [state_spec] * 2
        + [feature(width)] * 2,
        [(pl.BlockSpec((2, width, toks), lambda r: (0, 0, r)), ((2, width, flat), bf16))],
        [],
        2 * cell * HEADS,
        table,
        k_t,
        v_t,
        sig_k,
        back_a,
        back_b,
        grad_k_loc,
        grad_v_loc,
    )
    last = reduction(tok_t, grad_kv)
    next(last)
    next(back)
    next(mixed)
    next(into)
    next(last)
    (grad_tokens,) = run(
        token_kernel,
        [
            feature(width),
            pl.BlockSpec((2, width, toks), lambda r: (0, 0, r)),
            feature(width),
        ]
        + [whole] * 3,
        [(token_major, ((rows, toks, width), f32))],
        [],
        6 * flat * width * width,
        grad_qpre,
        grad_kv,
        grad_base,
        w_query,
        w_key,
        w_value,
    )
    pending = [mixed, into, back, last]
    ends = {}
    while pending:
        for steps in list(pending):
            value = next(steps)
            if value is not None:
                ends[id(steps)] = value
                pending.remove(steps)

    def joined(steps, groups):
        low, high = ends[id(steps)]
        size = low.shape[1] // groups
        return [
            jnp.concatenate([v[:, g * size : (g + 1) * size] for v in (low, high)], axis=1)
            for g in range(groups)
        ]

    (total_back,), (total_in,) = joined(back, 1), joined(into, 1)
    total_out, total_query = joined(mixed, 2)
    total_key, total_value = joined(last, 2)
    vectors = total_out[share, : 4 * share].reshape(4, share)
    return (
        layer_out,
        grad_tokens,
        total_query[:share],
        total_key,
        total_value,
        total_out[:share],
        total_in,
        total_back,
        vectors[0],
        vectors[1],
        vectors[2],
        vectors[3],
    )


def solution(mesh):
    in_specs = (
        P("batch", "seq", None),
        P("batch", "seq", None),
        P("batch", None),
        P(),
        P(),
        P(),
        P(),
        P(),
        P(),
        P(),
        P(),
        P(),
        P(),
    )
    out_specs = (
        P("batch", "seq", None),
        P("batch", "seq", None),
        P("seq", None),
        P("seq", None),
        P("seq", None),
        P("seq", None),
        P("seq", None),
        P("seq", None),
        P("seq"),
        P("seq"),
        P("seq"),
        P("seq"),
    )
    return jax.shard_map(body, mesh=mesh, in_specs=in_specs, out_specs=out_specs, check_vma=False)
```

```python
import jax
import jax.numpy as jnp
from jax import lax
from jax.experimental import pallas as pl
from jax.experimental.pallas import tpu as pltpu
from jax.sharding import PartitionSpec as P

HEADS = 12
HEAD_DIM = 64
PAIRS = HEADS // 2
HALF_HEADS = HEADS // 2
STATE_ROWS = HALF_HEADS * HEAD_DIM + 8

f32 = jnp.float32
bf16 = jnp.bfloat16
half_pi = 1.5707963267948966
norm_eps = 1e-05
VMEM_LIMIT = 60 * 1024 * 1024
LIGHT_LIMIT = 32 * 1024 * 1024

NN = (((1,), (0,)), ((), ()))
NT = (((1,), (1,)), ((), ()))
TN = (((0,), (0,)), ((), ()))


def mm(a, b, dims=NN):
    return lax.dot_general(a, b, dims, preferred_element_type=f32)


COS, SIN, BEGIN, COS_READ, SIN_READ, COS_TAIL, SIN_TAIL = range(7)


def make_table(place, lens_ref, row, tok_count):
    pos = place + lax.broadcasted_iota(jnp.int32, (8, tok_count), 1)
    last = place + tok_count - 1
    start = jnp.int32(0)
    begin = jnp.zeros((8, tok_count), jnp.int32)
    span = jnp.ones((8, tok_count), jnp.int32)
    last_begin = jnp.int32(0)
    for d in range(lens_ref.shape[1]):
        length = lens_ref[row, d]
        inside = pos >= start
        begin = jnp.where(inside, start, begin)
        span = jnp.where(inside, length, span)
        last_begin = jnp.where(start <= last, start, last_begin)
        start = start + length
    angle = half_pi * (pos - begin).astype(f32) / span.astype(f32)
    cos, sin = jnp.cos(angle), jnp.sin(angle)
    reader = (begin < place).astype(f32)
    tail = (begin == last_begin).astype(f32)
    which = lax.broadcasted_iota(jnp.int32, (8, tok_count), 0)
    table = jnp.zeros((8, tok_count), f32)
    for index, value in (
        (COS, cos),
        (SIN, sin),
        (BEGIN, begin.astype(f32)),
        (COS_READ, cos * reader),
        (SIN_READ, sin * reader),
        (COS_TAIL, cos * tail),
        (SIN_TAIL, sin * tail),
    ):
        table = jnp.where(which == index, value, table)
    return table


def blend_of(table):
    columns = table.T
    tok_count = table.shape[1]
    source = lax.broadcasted_iota(jnp.int32, (tok_count, tok_count), 0)
    reader = lax.broadcasted_iota(jnp.int32, (tok_count, tok_count), 1)
    same = (columns[:, BEGIN : BEGIN + 1] == table[BEGIN : BEGIN + 1]) & (source <= reader)
    value = (
        columns[:, COS : COS + 1] * table[COS : COS + 1]
        + columns[:, SIN : SIN + 1] * table[SIN : SIN + 1]
    )
    return jnp.where(same, value, 0.0)


def trig_rows(head_rows, cos, sin):
    wide = head_rows.astype(f32)
    return jnp.concatenate([(wide * cos).astype(bf16), (wide * sin).astype(bf16)], axis=0)


def with_row(rows, extra):
    which = lax.broadcasted_iota(jnp.int32, (16, rows.shape[1]), 0)
    return jnp.concatenate([rows, jnp.where(which == 0, extra, 0.0).astype(bf16)], axis=0)


def head_slice(h):
    return slice(h * HEAD_DIM, (h + 1) * HEAD_DIM)


def put_state(state_refs, h, value):
    ref = state_refs[h // HALF_HEADS]
    place = h % HALF_HEADS
    ref[0, head_slice(place), :] = value[:HEAD_DIM]
    ref[0, HALF_HEADS * HEAD_DIM + place : HALF_HEADS * HEAD_DIM + place + 1, :] = value[
        HEAD_DIM : HEAD_DIM + 1
    ]


def take_state(state_refs, h):
    ref = state_refs[h // HALF_HEADS]
    place = h % HALF_HEADS
    mats = ref[0, head_slice(place), :].astype(bf16)
    sums = ref[0, HALF_HEADS * HEAD_DIM + place : HALF_HEADS * HEAD_DIM + place + 1, :]
    return with_row(mats, sums)


def clear_pad(state_refs):
    for ref in state_refs:
        ref[0, HALF_HEADS * HEAD_DIM :, :] = jnp.zeros((8, 2 * HEAD_DIM), f32)


def softplus_sigmoid(v):
    small = jnp.exp(-jnp.abs(v))
    soft = jnp.maximum(v, 0.0) + jnp.log1p(small)
    inverse = 1.0 / (1.0 + small)
    return soft, jnp.where(v >= 0, inverse, small * inverse)


def project_kernel(
    place_ref,
    lens_ref,
    tok_ref,
    wk_ref,
    wv_ref,
    tab_ref,
    tok_t_ref,
    k_t_ref,
    v_t_ref,
    k_ref,
    v_ref,
    sig_k_ref,
    state_a,
    state_b,
    w_t,
):
    row = pl.program_id(0)

    @pl.when(row == 0)
    def _():
        w_t[0] = wk_ref[...].T
        w_t[1] = wv_ref[...].T

    tok_t = tok_ref[0].T
    tok_t_ref[...] = tok_t
    table = make_table(place_ref[0], lens_ref, row, tok_t.shape[1])
    tab_ref[0] = table
    soft, sig = softplus_sigmoid(mm(w_t[0], tok_t))
    key_t = soft.astype(bf16)
    k_t_ref[...] = key_t
    k_ref[0] = key_t.T
    sig_k_ref[...] = sig.astype(bf16)
    value_t = mm(w_t[1], tok_t).astype(bf16)
    v_t_ref[...] = value_t
    v_ref[0] = value_t.T
    states = (state_a, state_b)
    clear_pad(states)
    cos, sin = table[COS_TAIL : COS_TAIL + 1], table[SIN_TAIL : SIN_TAIL + 1]
    for h in range(HEADS):
        keys = trig_rows(k_t_ref[head_slice(h), :], cos, sin)
        values = with_row(v_t_ref[head_slice(h), :], 1.0)
        put_state(states, h, mm(values, keys, NT))


def pair_rows(ref, pair):
    first = ref[head_slice(2 * pair), :]
    second = ref[head_slice(2 * pair + 1), :]
    nothing = jnp.zeros_like(first)
    return jnp.concatenate(
        [
            jnp.concatenate([first, nothing], axis=1),
            jnp.concatenate([nothing, second], axis=1),
        ],
        axis=0,
    )


def two_parts(v):
    high = v.astype(bf16)
    return high, (v - high.astype(f32)).astype(bf16)


def local_kernel(
    tab_ref,
    tok_t_ref,
    k_ref,
    v_t_ref,
    wq_ref,
    w_out_ref,
    w_in_ref,
    w_back_ref,
    q_t_ref,
    sig_q_ref,
    numer_ref,
    denom_ref,
    w_out_t,
    w_in_t,
    w_back_t,
    w_t,
):
    @pl.when(pl.program_id(0) == 0)
    def _():
        w_t[...] = wq_ref[...].T
        w_out_t[...] = w_out_ref[...].T

    w_in_t[...] = w_in_ref[...].T
    w_back_t[...] = w_back_ref[...].T

    soft, sig = softplus_sigmoid(mm(w_t[...], tok_t_ref[...]))
    q_t_ref[...] = soft.astype(bf16)
    sig_q_ref[...] = sig.astype(bf16)
    blend = blend_of(tab_ref[0])
    tok_count = blend.shape[0]
    denom_ref[...] = jnp.zeros_like(denom_ref)
    for pair in range(PAIRS):
        lanes = slice(pair * 2 * HEAD_DIM, (pair + 1) * 2 * HEAD_DIM)
        both = mm(k_ref[0, :, lanes], pair_rows(q_t_ref, pair))
        for side in range(2):
            h = 2 * pair + side
            high, low = two_parts(both[:, side * tok_count : (side + 1) * tok_count] * blend)
            values = with_row(v_t_ref[head_slice(h), :], 1.0)
            out = mm(values, high) + mm(values, low)
            numer_ref[head_slice(h), :] = out[:HEAD_DIM]
            denom_ref[h : h + 1, :] = out[HEAD_DIM : HEAD_DIM + 1]


def mean_rows(v):
    return jnp.sum(v, axis=0, keepdims=True) * (1.0 / v.shape[0])


def fold_lanes(v):
    total = v[:, :128]
    for at in range(128, v.shape[1], 128):
        total = total + v[:, at : at + 128]
    return total


def add_to(ref, value):
    first = pl.program_id(0) == 0

    @pl.when(first)
    def _():
        ref[...] = value

    @pl.when(jnp.logical_not(first))
    def _():
        ref[...] += value


def norm_back(grad_norm, normed, inv_scale):
    return inv_scale * (grad_norm - mean_rows(grad_norm) - normed * mean_rows(grad_norm * normed))


def lane_total(ref):
    return jnp.sum(ref[...], axis=1, keepdims=True)


def layer_kernel(
    tab_ref,
    q_t_ref,
    numer_ref,
    denom_loc_ref,
    state_a,
    state_b,
    tok_t_ref,
    cot_ref,
    w_out_t,
    w_in_t,
    w_back_t,
    w_out_ref,
    w_in_ref,
    w_back_ref,
    gain_one_ref,
    shift_one_ref,
    gain_two_ref,
    shift_two_ref,
    layer_ref,
    att_t_ref,
    first_t_ref,
    active_t_ref,
    grad_second_ref,
    grad_hidden_ref,
    grad_base_ref,
    grad_branch_ref,
    grad_numer_ref,
    grad_denom_ref,
    small_ref,
    out_a,
    out_b,
    slope,
    normed_one,
    attended,
    inverse_denom,
    total,
    fold_gain_one,
    fold_shift_one,
    fold_gain_two,
    fold_shift_two,
):
    ff = w_in_ref.shape[1]
    step = 768
    table = tab_ref[0]
    cos, sin = table[COS_READ : COS_READ + 1], table[SIN_READ : SIN_READ + 1]
    states = (state_a, state_b)
    for h in range(HEADS):
        reads = trig_rows(q_t_ref[head_slice(h), :], cos, sin)
        more = mm(take_state(states, h), reads)
        numer = numer_ref[head_slice(h), :] + more[:HEAD_DIM]
        inverse = 1.0 / (denom_loc_ref[h : h + 1, :] + more[HEAD_DIM : HEAD_DIM + 1])
        inverse_denom[h : h + 1, :] = inverse
        value = numer * inverse
        attended[head_slice(h), :] = value
        att_t_ref[head_slice(h), :] = value.astype(bf16)
    summed = tok_t_ref[...].astype(f32) + mm(w_out_t[...], att_t_ref[...])
    centered = summed - mean_rows(summed)
    scale_one = lax.rsqrt(mean_rows(centered * centered) + norm_eps)
    normed = centered * scale_one
    normed_one[...] = normed
    first_out = normed * gain_one_ref[...] + shift_one_ref[...]
    total[...] = first_out
    first_low = first_out.astype(bf16)
    first_t_ref[...] = first_low
    for at in range(0, ff, step):
        hidden = mm(w_in_t[at : at + step, :], first_low)
        half = 0.5 * (1.0 + lax.erf(hidden * 0.7071067811865476))
        bell = jnp.exp(hidden * hidden * -0.5) * 0.3989422804014327
        active = (hidden * half).astype(bf16)
        active_t_ref[at : at + step, :] = active
        slope[at : at + step, :] = (half + hidden * bell).astype(bf16)
        total[...] += mm(w_back_t[:, at : at + step], active)
    summed = total[...]
    centered = summed - mean_rows(summed)
    scale_two = lax.rsqrt(mean_rows(centered * centered) + norm_eps)
    normed = centered * scale_two
    layer_ref[0] = (normed * gain_two_ref[...] + shift_two_ref[...]).T.astype(bf16)
    grad_top = cot_ref[0].T.astype(f32)
    add_to(fold_gain_two, fold_lanes(grad_top * normed))
    add_to(fold_shift_two, fold_lanes(grad_top))
    grad_mid = norm_back(grad_top * gain_two_ref[...], normed, scale_two)
    total[...] = grad_mid
    grad_second = grad_mid.astype(bf16)
    grad_second_ref[...] = grad_second
    for at in range(0, ff, step):
        grad_active = mm(w_back_ref[at : at + step, :], grad_second)
        low = (grad_active * slope[at : at + step, :].astype(f32)).astype(bf16)
        grad_hidden_ref[at : at + step, :] = low
        total[...] += mm(w_in_ref[:, at : at + step], low)
    grad_first = total[...]
    normed = normed_one[...]
    add_to(fold_gain_one, fold_lanes(grad_first * normed))
    add_to(fold_shift_one, fold_lanes(grad_first))
    grad_base = norm_back(grad_first * gain_one_ref[...], normed, scale_one)
    grad_base_ref[...] = grad_base
    grad_branch = grad_base.astype(bf16)
    grad_branch_ref[...] = grad_branch
    total[...] = mm(w_out_ref[...], grad_branch)
    outs = (out_a, out_b)
    clear_pad(outs)
    grad_denom_ref[...] = jnp.zeros_like(grad_denom_ref)
    for h in range(HEADS):
        rows = head_slice(h)
        grad_numer = (total[rows, :] * inverse_denom[h : h + 1, :]).astype(bf16)
        grad_denom = -jnp.sum(grad_numer.astype(f32) * attended[rows, :], axis=0, keepdims=True)
        grad_denom_ref[h : h + 1, :] = grad_denom
        grad_numer_ref[rows, :] = grad_numer
        reads = trig_rows(q_t_ref[rows, :], cos, sin)
        put_state(outs, h, mm(with_row(grad_numer, grad_denom), reads, NT))

    @pl.when(pl.program_id(0) == pl.num_programs(0) - 1)
    def _():
        lane = lax.broadcasted_iota(jnp.int32, small_ref.shape, 1)
        value = jnp.zeros(small_ref.shape, f32)
        for i, ref in enumerate((fold_gain_one, fold_shift_one, fold_gain_two, fold_shift_two)):
            value = jnp.where(lane == i, lane_total(ref), value)
        small_ref[...] = value


def local_back_kernel(
    tab_ref,
    q_t_ref,
    k_t_ref,
    k_ref,
    v_ref,
    sig_q_ref,
    grad_numer_ref,
    grad_denom_ref,
    state_a,
    state_b,
    grad_q_ref,
    grad_k_ref,
    grad_v_ref,
):
    table = tab_ref[0]
    blend = blend_of(table)
    tok_count = blend.shape[0]
    cos, sin = table[COS_READ : COS_READ + 1], table[SIN_READ : SIN_READ + 1]
    states = (state_a, state_b)
    for pair in range(PAIRS):
        lanes = slice(pair * 2 * HEAD_DIM, (pair + 1) * 2 * HEAD_DIM)
        both = mm(k_ref[0, :, lanes], pair_rows(q_t_ref, pair))
        grads = mm(v_ref[0, :, lanes], pair_rows(grad_numer_ref, pair))
        for side in range(2):
            h = 2 * pair + side
            rows = head_slice(h)
            part = slice(side * tok_count, (side + 1) * tok_count)
            grad_denom = grad_denom_ref[h : h + 1, :]
            scores = (both[:, part] * blend).astype(bf16)
            grad_scores, rest = two_parts((grads[:, part] + grad_denom) * blend)
            grad_numer = grad_numer_ref[rows, :]
            grad_v_ref[rows, :] = mm(grad_numer, scores, NT)
            grad_k_ref[rows, :] = mm(q_t_ref[rows, :], grad_scores, NT)
            reads = mm(take_state(states, h), with_row(grad_numer, grad_denom), TN)
            grad_q = (
                mm(k_t_ref[rows, :], grad_scores)
                + mm(k_t_ref[rows, :], rest)
                + cos * reads[:HEAD_DIM]
                + sin * reads[HEAD_DIM:]
            )
            grad_q_ref[rows, :] = (grad_q * sig_q_ref[rows, :].astype(f32)).astype(bf16)


def tail_kernel(
    tab_ref,
    k_t_ref,
    v_t_ref,
    sig_k_ref,
    state_a,
    state_b,
    grad_k_in,
    grad_v_in,
    grad_kv_ref,
):
    table = tab_ref[0]
    cos, sin = table[COS_TAIL : COS_TAIL + 1], table[SIN_TAIL : SIN_TAIL + 1]
    states = (state_a, state_b)
    for h in range(HEADS):
        rows = head_slice(h)
        state = take_state(states, h)
        inner = mm(state, with_row(v_t_ref[rows, :], 1.0), TN)
        grad_k = grad_k_in[rows, :] + cos * inner[:HEAD_DIM] + sin * inner[HEAD_DIM:]
        grad_kv_ref[0, rows, :] = (grad_k * sig_k_ref[rows, :].astype(f32)).astype(bf16)
        keys = trig_rows(k_t_ref[rows, :], cos, sin)
        grad_kv_ref[1, rows, :] = (grad_v_in[rows, :] + mm(state[:HEAD_DIM], keys)).astype(bf16)


def token_kernel(gq_ref, gkv_ref, base_ref, wq_ref, wk_ref, wv_ref, out_ref):
    total = base_ref[...] + mm(wq_ref[...], gq_ref[...])
    total = total + mm(wk_ref[...], gkv_ref[0])
    total = total + mm(wv_ref[...], gkv_ref[1])
    out_ref[0] = total.T


def spec(block, index):
    return pl.BlockSpec(block, index)


def light(kernel, grid, ins, outs, scalars, *args):
    return pl.pallas_call(
        kernel,
        grid_spec=pltpu.PrefetchScalarGridSpec(
            num_scalar_prefetch=1,
            grid=grid,
            in_specs=ins,
            out_specs=[o for o, _ in outs],
        ),
        out_shape=[jax.ShapeDtypeStruct(shape, f32) for _, shape in outs],
        compiler_params=pltpu.CompilerParams(
            dimension_semantics=("arbitrary",) * len(grid), vmem_limit_bytes=LIGHT_LIMIT
        ),
        cost_estimate=pl.CostEstimate(flops=1, bytes_accessed=1, transcendentals=0),
    )(scalars, *args)


def pick_halves(core, value):
    cut = value.shape[1] // 2
    low, high = value[:, :cut], value[:, cut:]
    return jnp.where(core == 0, high, low), jnp.where(core == 0, low, high)


def tall_kernel(s_ref, a_ref, b_ref, away_ref, keep_ref):
    away_ref[0], keep_ref[0] = pick_halves(s_ref[0], mm(a_ref[...], b_ref[...], NT))


def tall_product(core, shards, a, b):
    count, flat = a.shape
    rows, cut = count // shards, b.shape[0] // 2
    out = (spec((1, rows, cut), lambda i, s: (i, 0, 0)), (shards, rows, cut))
    return light(
        tall_kernel,
        (shards,),
        [spec((rows, flat), lambda i, s: (i, 0)), spec(b.shape, lambda i, s: (0, 0))],
        [out, out],
        core[None],
        a,
        b,
    )


def wide_kernel(s_ref, a_ref, b_ref, away_ref, keep_ref):
    value = mm(a_ref[...], b_ref[...], NT)
    first = pl.program_id(0) < pl.num_programs(0) // 2

    @pl.when(first)
    def _():
        away_ref[...] = value

    @pl.when(jnp.logical_not(first))
    def _():
        keep_ref[...] = value


def wide_product(core, shards, a, b):
    count, flat = a.shape
    cut = b.shape[0] // 2
    tile = 512
    half = cut // tile

    def source(i, s):
        return jnp.where(i < half, (1 - s[0]) * half + i, s[0] * half + i - half), 0

    outs = [
        (spec((count, tile), lambda i, s: (0, jnp.minimum(i, half - 1))), (count, cut)),
        (spec((count, tile), lambda i, s: (0, jnp.maximum(i - half, 0))), (count, cut)),
    ]
    return [
        v.reshape(shards, count // shards, cut)
        for v in light(
            wide_kernel,
            (2 * half,),
            [spec(a.shape, lambda i, s: (0, 0)), spec((tile, flat), source)],
            outs,
            core[None],
            a,
            b,
        )
    ]


def twin_kernel(s_ref, a_ref, b_ref, c_ref, d_ref, *refs):
    away_ref, keep_ref = refs[-2:]
    core = s_ref[0]
    at = 0
    for left, right in ((a_ref, b_ref), (c_ref, d_ref)):
        away, keep = pick_halves(core, mm(left[...], right[...].reshape(right.shape[-2:]), NT))
        away_ref[:, at : at + away.shape[1]] = away
        keep_ref[:, at : at + keep.shape[1]] = keep
        at += away.shape[1]
    if len(refs) == 3:
        value = refs[0][...]
        away_ref[:, at:] = jnp.where(core == 0, 0.0, value)
        keep_ref[:, at:] = jnp.where(core == 0, value, 0.0)


def twin_product(core, shards, a, b, c, d, small=None):
    count, flat = a.shape
    tile = count // 2

    def full(v):
        if isinstance(v, tuple):
            return spec((1,) + v[0].shape[1:], lambda i, s, g=v[1]: (g, 0, 0)), v[0]
        return spec(v.shape, lambda i, s: (0, 0)), v

    rows = spec((tile, flat), lambda i, s: (i, 0))
    (b_spec, b), (d_spec, d) = full(b), full(d)
    ins, args = [rows, b_spec, rows, d_spec], [a, b, c, d]
    columns = (b.shape[-2] + d.shape[-2]) // 2
    if small is not None:
        ins.append(spec((tile, small.shape[1]), lambda i, s: (i, 0)))
        args.append(small)
        columns += small.shape[1]
    out = (spec((tile, columns), lambda i, s: (i, 0)), (count, columns))
    return [
        v.reshape(shards, count // shards, columns)
        for v in light(twin_kernel, (2,), ins, [out, out], core[None], *args)
    ]


def route_kernel(s_ref, *refs):
    for i in range(4):
        refs[8 + i][...] = refs[2 * i][...] + refs[2 * i + 1][...]


def route(left, right, low_bit, high_bit):
    (a, b), (c, d) = left, right
    shards, rows, columns = a.shape
    same = a is c
    if same:
        rows //= 2
    lower = 1 if same else 0
    half = shards // 2

    def by_low(flip):
        def index(i, s):
            mine = s[0]
            return 2 * i + ((1 - mine) if flip else mine), 0, 0

        return index

    def by_high(flip):
        def index(i, s):
            mine = s[1]
            return i + ((1 - mine) if flip else mine) * half, lower, 0

        return index

    block = (1, rows, columns)
    maps = [by_low(True), by_low(False), by_high(True), by_high(False)]
    ins = [spec(block, m) for m in maps for _ in range(2)]
    out = (spec(block, lambda i, s: (i, 0, 0)), (half, rows, columns))
    return light(
        route_kernel,
        (half,),
        ins,
        [out] * 4,
        jnp.stack([low_bit, high_bit]),
        a,
        b,
        a,
        b,
        c,
        d,
        c,
        d,
    )


def choose_kernel(s_ref, a_ref, b_ref, c_ref, d_ref, away_ref, keep_ref):
    upper, lower = a_ref[...] + b_ref[...], c_ref[...] + d_ref[...]
    odd = s_ref[0] == 1
    away_ref[...] = jnp.where(odd, upper, lower)
    keep_ref[...] = jnp.where(odd, lower, upper)


def choose(left, right, odd):
    shape = left[0].shape
    whole = spec(shape, lambda i, s: (0, 0, 0))
    return light(choose_kernel, (1,), [whole] * 4, [(whole, shape)] * 2, odd[None], *left, *right)


def add_kernel(s_ref, a_ref, b_ref, out_ref):
    out_ref[...] = a_ref[...] + b_ref[...]


def add(a, b):
    whole = spec(a.shape, lambda i, s: (0,) * a.ndim)
    return light(add_kernel, (1,), [whole] * 2, [(whole, a.shape)], jnp.zeros((1,), jnp.int32), a, b)[0]


def join_kernel(s_ref, part_ref, got_ref, other_part_ref, other_got_ref, *outs):
    odd, first = s_ref[0] == 1, s_ref[1] == 0
    rows = part_ref.shape[1]
    for upper in (True, False):
        swapped = odd if upper else jnp.logical_not(odd)
        mine = jnp.where(swapped, got_ref[0], part_ref[0])
        other = jnp.where(swapped, other_got_ref[0], other_part_ref[0])
        low, high = jnp.where(first, mine, other), jnp.where(first, other, mine)
        lines = slice(0, rows) if upper else slice(rows, 2 * rows)
        at = 0
        for out in outs:
            cut = out.shape[1] // 2
            if cut < 128:
                out[lines, :] = low[:, at:]
            else:
                out[lines, :cut] = low[:, at : at + cut]
                out[lines, cut:] = high[:, at : at + cut]
            at += cut


def join(odd, core, part, got, other_part, other_got, widths):
    rows = 2 * part.shape[1]
    whole = spec(part.shape, lambda i, s: (0, 0, 0))
    outs = [(spec((rows, w), lambda i, s: (0, 0)), (rows, w)) for w in widths]
    return light(
        join_kernel,
        (1,),
        [whole] * 4,
        outs,
        jnp.stack([odd, core]),
        part,
        got,
        other_part,
        other_got,
    )


def mix_kernel(s_ref, *refs):
    row = pl.program_id(0)
    for i in range(2):
        refs[4 + i][...] = s_ref[2 * i, row] * refs[2 * i][...] + s_ref[2 * i + 1, row] * refs[2 * i + 1][...]


def mix(weights, a, b, c, d):
    block = spec((1,) + a.shape[1:], lambda r, s: (r, 0, 0))
    return light(mix_kernel, (a.shape[0],), [block] * 4, [(block, a.shape)] * 2, weights, a, b, c, d)


def first_begins(lengths, count, tok_count):
    slots = lengths.shape[1]
    order = jnp.arange(slots)
    before = (order[:, None] > order[None, :]).astype(jnp.int32)
    starts = jnp.sum(lengths[:, None, :] * before[None], axis=-1)
    firsts = jnp.arange(count, dtype=jnp.int32) * tok_count
    reached = starts[:, None, :] <= firsts[None, :, None]
    return jnp.max(jnp.where(reached, starts[:, None, :], 0), axis=-1)


def pick(index, values):
    out = values[0]
    for i in range(1, len(values)):
        out = jnp.where(index == i, values[i], out)
    return out


class Order:
    def __init__(self):
        self.last = None

    def tie(self, value):
        if self.last is None:
            return value
        return lax.optimization_barrier((value, self.last))[0]

    def done(self, value):
        self.last = value
        return value


def entering(order, parts, begin_first, tok_count, reverse):
    count = lax.axis_size("seq")
    place = lax.axis_index("seq")
    part_a, part_b = parts

    def covers(i, j):
        low, high = (count - 1 - j, count - 1 - i) if reverse else (i, j)
        return (begin_first[:, high] < (low + 1) * tok_count).astype(f32)

    if count != 4:
        spots = jnp.arange(count)
        mine = begin_first.T if reverse else begin_first[:, place][None]
        reach = (place if reverse else spots[:, None]) + 1
        ahead = (spots > place) if reverse else (spots < place)
        weight = ((mine < reach * tok_count) & ahead[:, None]).astype(f32)
        gathered = [lax.all_gather(p, "seq") for p in parts]
        yield
        yield
        yield tuple(jnp.sum(g * weight[:, :, None, None], axis=0) for g in gathered)
    index = count - 1 - place if reverse else place

    zero = jnp.zeros_like(begin_first[:, 0], f32)
    one = zero + 1.0
    m02, m03, m13 = covers(0, 2), covers(0, 3), covers(1, 3)
    onward = jnp.stack(
        [
            pick(index, [m02, m13, zero, zero]),
            pick(index, [one, m03, zero, zero]),
            pick(index, [one, zero, one, zero]),
            pick(index, [zero, zero, m03, one]),
        ]
    )
    final = jnp.stack(
        [
            pick(index, [zero, one, zero, one]),
            pick(index, [zero, zero, one, one]),
            pick(index, [zero, zero, m02, m13]),
            pick(index, [zero, one, one, one]),
        ]
    )
    got_a = swap(part_a, "seq", 1)
    got_b = swap(part_b, "seq", 2)
    yield
    got_a, got_b = order.tie((got_a, got_b))
    next_a, next_b = order.done(mix(onward, part_a, got_a, part_b, got_b))
    last_a = swap(next_a, "seq", 2)
    last_b = swap(next_b, "seq", 1)
    yield
    last_a, last_b = order.tie((last_a, last_b))
    yield order.done(mix(final, got_a, last_a, got_b, last_b))


def swap(value, axis, distance):
    count = lax.axis_size(axis)
    return lax.ppermute(value, axis, [(i, i ^ distance) for i in range(count)])


def reduced(order, core, away, keep, widths):
    place = lax.axis_index("seq").astype(jnp.int32)
    odd = ((lax.axis_index("batch") >> 1) & 1).astype(jnp.int32)
    count = lax.axis_size("batch")
    bits = keep.shape[0].bit_length() - 1
    got = swap(away, "batch", 1)
    yield
    left = right = (keep, order.tie(got))
    for step in range(bits):
        high = bits - 1 - step
        away_l, keep_l, away_r, keep_r = order.done(
            route(left, right, (place >> step) & 1, (place >> high) & 1)
        )
        got_l, got_r = swap(away_l, "seq", 1 << step), swap(away_r, "seq", 1 << high)
        yield
        got_l, got_r = order.tie((got_l, got_r))
        left, right = (keep_l, got_l), (keep_r, got_r)
    away, part = order.done(choose(left, right, odd))
    got = swap(away, "batch", 2)
    distance = 4
    yield
    part = order.done(add(part, order.tie(got)))
    while distance < count:
        got = swap(part, "batch", distance)
        yield
        part = order.done(add(part, order.tie(got)))
        distance *= 2
    got = swap(part, "batch", 2)
    other_part = swap(part, "batch", 1)
    yield
    got = order.done(order.tie(got))
    other_got = swap(got, "batch", 1)
    yield
    yield order.done(join(odd, core, part, got, order.tie(other_part), other_got, widths))


def call(kernel, grid, ins, outs, scratch, *args):
    return pl.pallas_call(
        kernel,
        grid=grid,
        in_specs=[s for s in ins],
        out_specs=[s for s, _ in outs],
        out_shape=[jax.ShapeDtypeStruct(shape, kind) for _, (shape, kind) in outs],
        scratch_shapes=scratch,
        compiler_params=pltpu.CompilerParams(
            dimension_semantics=("arbitrary",) * len(grid), vmem_limit_bytes=VMEM_LIMIT
        ),
        cost_estimate=pl.CostEstimate(flops=1, bytes_accessed=1, transcendentals=0),
    )(*args)


def body(
    tokens,
    cotangent,
    doc_lengths,
    w_query,
    w_key,
    w_value,
    w_out,
    w_in,
    w_back,
    gain_one,
    shift_one,
    gain_two,
    shift_two,
):
    rows, toks, width = tokens.shape
    ff = w_in.shape[1]
    flat = rows * toks
    shards = lax.axis_size("seq")
    place = (lax.axis_index("seq") * toks).astype(jnp.int32)
    begin_first = first_begins(doc_lengths, shards, toks)
    smem = pl.BlockSpec(memory_space=pltpu.SMEM)
    whole = pl.BlockSpec(memory_space=pltpu.VMEM)
    token_major = pl.BlockSpec((1, toks, width), lambda r: (r, 0, 0))
    table_spec = pl.BlockSpec((1, 8, toks), lambda r: (r, 0, 0))
    state_spec = pl.BlockSpec((1, STATE_ROWS, 2 * HEAD_DIM), lambda r: (r, 0, 0))

    def feature(count):
        return pl.BlockSpec((count, toks), lambda r: (0, r))

    tok_low = (token_major, ((rows, toks, width), bf16))
    wide_low = (feature(width), ((width, flat), bf16))
    wide_full = (feature(width), ((width, flat), f32))
    ff_low = (feature(ff), ((ff, flat), bf16))
    head_rows = (feature(16), ((16, flat), f32))
    fold = (pl.BlockSpec((width, 128), lambda r: (0, 0)), ((width, 128), f32))
    state = (state_spec, ((rows, STATE_ROWS, 2 * HEAD_DIM), f32))
    grid = (rows,)

    order = Order()
    core = (lax.axis_index("batch") % 2).astype(jnp.int32)

    def run(kernel, ins, outs, scratch, first, *args):
        return order.done(call(kernel, grid, ins, outs, scratch, order.tie(first), *args))

    def column(v):
        return v[:, None]

    table, tok_t, k_t, v_t, key, value, sig_k, state_a, state_b = run(
        project_kernel,
        [smem, smem, token_major, whole, whole],
        [(table_spec, ((rows, 8, toks), f32))]
        + [wide_low] * 3
        + [tok_low] * 2
        + [wide_low]
        + [state] * 2,
        [pltpu.VMEM((2, width, width), bf16)],
        place[None],
        doc_lengths,
        tokens,
        w_key,
        w_value,
    )
    states = entering(order, (state_a, state_b), begin_first, toks, False)
    next(states)
    part = ff // rows
    q_t, sig_q, numer, denom_loc, w_out_t, w_in_t, w_back_t = run(
        local_kernel,
        [
            table_spec,
            feature(width),
            token_major,
            feature(width),
            whole,
            whole,
            pl.BlockSpec((width, part), lambda r: (0, r)),
            pl.BlockSpec((part, width), lambda r: (r, 0)),
        ],
        [
            wide_low,
            wide_low,
            wide_full,
            head_rows,
            (pl.BlockSpec((width, width), lambda r: (0, 0)), ((width, width), bf16)),
            (pl.BlockSpec((part, width), lambda r: (r, 0)), ((ff, width), bf16)),
            (pl.BlockSpec((width, part), lambda r: (0, r)), ((width, ff), bf16)),
        ],
        [pltpu.VMEM((width, width), bf16)],
        table,
        tok_t,
        key,
        v_t,
        w_query,
        w_out,
        w_in,
        w_back,
    )
    next(states)
    in_a, in_b = next(states)
    (
        layer_out,
        att_t,
        first_t,
        active_t,
        grad_second,
        grad_hidden,
        grad_base,
        grad_branch,
        grad_numer,
        grad_denom,
        small,
        out_a,
        out_b,
    ) = run(
        layer_kernel,
        [
            table_spec,
            feature(width),
            feature(width),
            feature(16),
            state_spec,
            state_spec,
            feature(width),
            token_major,
        ]
        + [whole] * 10,
        [
            tok_low,
            wide_low,
            wide_low,
            ff_low,
            wide_low,
            ff_low,
            wide_full,
            wide_low,
            wide_low,
            head_rows,
            fold,
            state,
            state,
        ],
        [
            pltpu.VMEM((ff, toks), bf16),
            pltpu.VMEM((width, toks), f32),
            pltpu.VMEM((width, toks), f32),
            pltpu.VMEM((16, toks), f32),
            pltpu.VMEM((width, toks), f32),
        ]
        + [pltpu.VMEM((width, 128), f32)] * 4,
        table,
        q_t,
        numer,
        denom_loc,
        in_a,
        in_b,
        tok_t,
        cotangent,
        w_out_t,
        w_in_t,
        w_back_t,
        w_out,
        w_in,
        w_back,
        column(gain_one),
        column(shift_one),
        column(gain_two),
        column(shift_two),
    )

    def reduction(product, widths, first, *rest):
        away, keep = order.done(product(core, shards, order.tie(first), *rest))
        steps = reduced(order, core, away, keep, widths)
        next(steps)
        return steps

    back_states = entering(order, (out_a, out_b), begin_first, toks, True)
    next(back_states)
    back = reduction(tall_product, (width,), active_t, grad_second)
    into = reduction(wide_product, (ff,), first_t, grad_hidden)
    next(back_states)
    next(back)
    grad_qpre, grad_k_loc, grad_v_loc = run(
        local_back_kernel,
        [
            table_spec,
            feature(width),
            feature(width),
            token_major,
            token_major,
            feature(width),
            feature(width),
            feature(16),
            state_spec,
            state_spec,
        ],
        [wide_low, wide_full, wide_full],
        [],
        table,
        q_t,
        k_t,
        key,
        value,
        sig_q,
        grad_numer,
        grad_denom,
        in_a,
        in_b,
    )
    mixed = reduction(
        twin_product, (width, width, 128), att_t, grad_branch, tok_t, grad_qpre, small
    )
    next(into)
    back_a, back_b = next(back_states)
    (grad_kv,) = run(
        tail_kernel,
        [table_spec]
        + [feature(width)] * 3
        + [state_spec] * 2
        + [feature(width)] * 2,
        [(pl.BlockSpec((2, width, toks), lambda r: (0, 0, r)), ((2, width, flat), bf16))],
        [],
        table,
        k_t,
        v_t,
        sig_k,
        back_a,
        back_b,
        grad_k_loc,
        grad_v_loc,
    )
    next(back)
    last = reduction(twin_product, (width, width), tok_t, (grad_kv, 0), tok_t, (grad_kv, 1))
    next(mixed)
    next(back)
    next(into)
    next(last)
    (grad_tokens,) = run(
        token_kernel,
        [
            feature(width),
            pl.BlockSpec((2, width, toks), lambda r: (0, 0, r)),
            feature(width),
        ]
        + [whole] * 3,
        [(token_major, ((rows, toks, width), f32))],
        [],
        grad_qpre,
        grad_kv,
        grad_base,
        w_query,
        w_key,
        w_value,
    )
    pending = [back, mixed, into, last]
    ends = {}
    while pending:
        for steps in list(pending):
            value = next(steps)
            if value is not None:
                ends[id(steps)] = value
                pending.remove(steps)
    (total_back,), (total_in,) = ends[id(back)], ends[id(into)]
    total_out, total_query, vectors = ends[id(mixed)]
    total_key, total_value = ends[id(last)]
    return (
        layer_out,
        grad_tokens,
        total_query,
        total_key,
        total_value,
        total_out,
        total_in,
        total_back,
        vectors[:, 0],
        vectors[:, 1],
        vectors[:, 2],
        vectors[:, 3],
    )


def solution(mesh):
    in_specs = (
        P("batch", "seq", None),
        P("batch", "seq", None),
        P("batch", None),
        P(),
        P(),
        P(),
        P(),
        P(),
        P(),
        P(),
        P(),
        P(),
        P(),
    )
    out_specs = (
        P("batch", "seq", None),
        P("batch", "seq", None),
        P("seq", None),
        P("seq", None),
        P("seq", None),
        P("seq", None),
        P("seq", None),
        P("seq", None),
        P("seq"),
        P("seq"),
        P("seq"),
        P("seq"),
    )
    return jax.shard_map(body, mesh=mesh, in_specs=in_specs, out_specs=out_specs, check_vma=False)
```

```python
from functools import partial

import jax
import jax.numpy as jnp
from jax import lax
from jax.experimental import pallas as pl
from jax.experimental.pallas import tpu as pltpu
from jax.sharding import PartitionSpec as P

HEADS = 12
HEAD_DIM = 64
PAIRS = HEADS // 2
HALF_HEADS = HEADS // 2
STATE_ROWS = HALF_HEADS * HEAD_DIM + 8

f32 = jnp.float32
bf16 = jnp.bfloat16
half_pi = 1.5707963267948966
norm_eps = 1e-05
VMEM_LIMIT = 60 * 1024 * 1024
SMALL_LIMIT = 20 * 1024 * 1024

NN = (((1,), (0,)), ((), ()))
NT = (((1,), (1,)), ((), ()))
TN = (((0,), (0,)), ((), ()))


def mm(a, b, dims=NN):
    return lax.dot_general(a, b, dims, preferred_element_type=f32)


COS, SIN, BEGIN, COS_READ, SIN_READ, COS_TAIL, SIN_TAIL = range(7)


def make_table(place, lens_ref, row, tok_count):
    pos = place + lax.broadcasted_iota(jnp.int32, (8, tok_count), 1)
    last = place + tok_count - 1
    start = jnp.int32(0)
    begin = jnp.zeros((8, tok_count), jnp.int32)
    span = jnp.ones((8, tok_count), jnp.int32)
    last_begin = jnp.int32(0)
    for d in range(lens_ref.shape[1]):
        length = lens_ref[row, d]
        inside = pos >= start
        begin = jnp.where(inside, start, begin)
        span = jnp.where(inside, length, span)
        last_begin = jnp.where(start <= last, start, last_begin)
        start = start + length
    angle = half_pi * (pos - begin).astype(f32) / span.astype(f32)
    cos, sin = jnp.cos(angle), jnp.sin(angle)
    reader = (begin < place).astype(f32)
    tail = (begin == last_begin).astype(f32)
    which = lax.broadcasted_iota(jnp.int32, (8, tok_count), 0)
    table = jnp.zeros((8, tok_count), f32)
    for index, value in (
        (COS, cos),
        (SIN, sin),
        (BEGIN, begin.astype(f32)),
        (COS_READ, cos * reader),
        (SIN_READ, sin * reader),
        (COS_TAIL, cos * tail),
        (SIN_TAIL, sin * tail),
    ):
        table = jnp.where(which == index, value, table)
    return table


def blend_of(table):
    columns = table.T
    tok_count = table.shape[1]
    source = lax.broadcasted_iota(jnp.int32, (tok_count, tok_count), 0)
    reader = lax.broadcasted_iota(jnp.int32, (tok_count, tok_count), 1)
    same = (columns[:, BEGIN : BEGIN + 1] == table[BEGIN : BEGIN + 1]) & (source <= reader)
    value = (
        columns[:, COS : COS + 1] * table[COS : COS + 1]
        + columns[:, SIN : SIN + 1] * table[SIN : SIN + 1]
    )
    return jnp.where(same, value, 0.0)


def trig_rows(head_rows, cos, sin):
    wide = head_rows.astype(f32)
    return jnp.concatenate([(wide * cos).astype(bf16), (wide * sin).astype(bf16)], axis=0)


def with_row(rows, extra):
    which = lax.broadcasted_iota(jnp.int32, (16, rows.shape[1]), 0)
    return jnp.concatenate([rows, jnp.where(which == 0, extra, 0.0).astype(bf16)], axis=0)


def head_slice(h):
    return slice(h * HEAD_DIM, (h + 1) * HEAD_DIM)


def put_state(state_refs, h, value):
    ref = state_refs[h // HALF_HEADS]
    place = h % HALF_HEADS
    ref[0, head_slice(place), :] = value[:HEAD_DIM]
    ref[0, HALF_HEADS * HEAD_DIM + place : HALF_HEADS * HEAD_DIM + place + 1, :] = value[
        HEAD_DIM : HEAD_DIM + 1
    ]


def take_state(state_refs, h):
    ref = state_refs[h // HALF_HEADS]
    place = h % HALF_HEADS
    mats = ref[0, head_slice(place), :].astype(bf16)
    sums = ref[0, HALF_HEADS * HEAD_DIM + place : HALF_HEADS * HEAD_DIM + place + 1, :]
    return with_row(mats, sums)


def clear_pad(state_refs):
    for ref in state_refs:
        ref[0, HALF_HEADS * HEAD_DIM :, :] = jnp.zeros((8, 2 * HEAD_DIM), f32)


def softplus_sigmoid(v):
    small = jnp.exp(-jnp.abs(v))
    soft = jnp.maximum(v, 0.0) + jnp.log1p(small)
    inverse = 1.0 / (1.0 + small)
    return soft, jnp.where(v >= 0, inverse, small * inverse)


def project_kernel(
    s_ref,
    lens_ref,
    tok_ref,
    wk_ref,
    wv_ref,
    tab_ref,
    tok_t_ref,
    k_t_ref,
    v_t_ref,
    k_ref,
    v_ref,
    sig_k_ref,
    state_a,
    state_b,
    w_t,
):
    row = pl.program_id(0)

    @pl.when(row == 0)
    def _():
        w_t[0] = wk_ref[...].T
        w_t[1] = wv_ref[...].T

    tok_t = tok_ref[0].T
    tok_t_ref[...] = tok_t
    table = make_table(s_ref[PLACE] * tok_t.shape[1], lens_ref, row, tok_t.shape[1])
    tab_ref[0] = table
    soft, sig = softplus_sigmoid(mm(w_t[0], tok_t))
    key_t = soft.astype(bf16)
    k_t_ref[...] = key_t
    k_ref[0] = key_t.T
    sig_k_ref[...] = sig.astype(bf16)
    value_t = mm(w_t[1], tok_t).astype(bf16)
    v_t_ref[...] = value_t
    v_ref[0] = value_t.T
    states = (state_a, state_b)
    clear_pad(states)
    cos, sin = table[COS_TAIL : COS_TAIL + 1], table[SIN_TAIL : SIN_TAIL + 1]
    for h in range(HEADS):
        keys = trig_rows(k_t_ref[head_slice(h), :], cos, sin)
        values = with_row(v_t_ref[head_slice(h), :], 1.0)
        put_state(states, h, mm(values, keys, NT))


def pair_rows(ref, pair):
    first = ref[head_slice(2 * pair), :]
    second = ref[head_slice(2 * pair + 1), :]
    nothing = jnp.zeros_like(first)
    return jnp.concatenate(
        [
            jnp.concatenate([first, nothing], axis=1),
            jnp.concatenate([nothing, second], axis=1),
        ],
        axis=0,
    )


def two_parts(v):
    high = v.astype(bf16)
    return high, (v - high.astype(f32)).astype(bf16)


def local_kernel(
    s_ref,
    tab_ref,
    tok_t_ref,
    k_ref,
    v_t_ref,
    wq_ref,
    w_out_ref,
    w_in_ref,
    w_back_ref,
    q_t_ref,
    sig_q_ref,
    numer_ref,
    denom_ref,
    w_out_t,
    w_in_t,
    w_back_t,
    w_t,
):
    @pl.when(pl.program_id(0) == 0)
    def _():
        w_t[...] = wq_ref[...].T
        w_out_t[...] = w_out_ref[...].T

    w_in_t[...] = w_in_ref[...].T
    w_back_t[...] = w_back_ref[...].T

    soft, sig = softplus_sigmoid(mm(w_t[...], tok_t_ref[...]))
    q_t_ref[...] = soft.astype(bf16)
    sig_q_ref[...] = sig.astype(bf16)
    blend = blend_of(tab_ref[0])
    tok_count = blend.shape[0]
    denom_ref[...] = jnp.zeros_like(denom_ref)
    for pair in range(PAIRS):
        lanes = slice(pair * 2 * HEAD_DIM, (pair + 1) * 2 * HEAD_DIM)
        both = mm(k_ref[0, :, lanes], pair_rows(q_t_ref, pair))
        for side in range(2):
            h = 2 * pair + side
            high, low = two_parts(both[:, side * tok_count : (side + 1) * tok_count] * blend)
            values = with_row(v_t_ref[head_slice(h), :], 1.0)
            out = mm(values, high) + mm(values, low)
            numer_ref[head_slice(h), :] = out[:HEAD_DIM]
            denom_ref[h : h + 1, :] = out[HEAD_DIM : HEAD_DIM + 1]


def mean_rows(v):
    return jnp.sum(v, axis=0, keepdims=True) * (1.0 / v.shape[0])


def fold_lanes(v):
    total = v[:, :128]
    for at in range(128, v.shape[1], 128):
        total = total + v[:, at : at + 128]
    return total


def add_to(ref, value):
    first = pl.program_id(0) == 0

    @pl.when(first)
    def _():
        ref[...] = value

    @pl.when(jnp.logical_not(first))
    def _():
        ref[...] += value


def norm_back(grad_norm, normed, inv_scale):
    return inv_scale * (grad_norm - mean_rows(grad_norm) - normed * mean_rows(grad_norm * normed))


def lane_total(ref):
    return jnp.sum(ref[...], axis=1, keepdims=True)


def layer_kernel(
    s_ref,
    tab_ref,
    q_t_ref,
    numer_ref,
    denom_loc_ref,
    state_a,
    state_b,
    tok_t_ref,
    cot_ref,
    w_out_t,
    w_in_t,
    w_back_t,
    w_out_ref,
    w_in_ref,
    w_back_ref,
    gain_one_ref,
    shift_one_ref,
    gain_two_ref,
    shift_two_ref,
    layer_ref,
    att_t_ref,
    first_t_ref,
    active_t_ref,
    grad_second_ref,
    grad_hidden_ref,
    grad_base_ref,
    grad_branch_ref,
    grad_numer_ref,
    grad_denom_ref,
    small_ref,
    out_a,
    out_b,
    slope,
    normed_one,
    attended,
    inverse_denom,
    total,
    fold_gain_one,
    fold_shift_one,
    fold_gain_two,
    fold_shift_two,
):
    ff = w_in_ref.shape[1]
    step = 768
    table = tab_ref[0]
    cos, sin = table[COS_READ : COS_READ + 1], table[SIN_READ : SIN_READ + 1]
    states = (state_a, state_b)
    for h in range(HEADS):
        reads = trig_rows(q_t_ref[head_slice(h), :], cos, sin)
        more = mm(take_state(states, h), reads)
        numer = numer_ref[head_slice(h), :] + more[:HEAD_DIM]
        inverse = 1.0 / (denom_loc_ref[h : h + 1, :] + more[HEAD_DIM : HEAD_DIM + 1])
        inverse_denom[h : h + 1, :] = inverse
        value = numer * inverse
        attended[head_slice(h), :] = value
        att_t_ref[head_slice(h), :] = value.astype(bf16)
    summed = tok_t_ref[...].astype(f32) + mm(w_out_t[...], att_t_ref[...])
    centered = summed - mean_rows(summed)
    scale_one = lax.rsqrt(mean_rows(centered * centered) + norm_eps)
    normed = centered * scale_one
    normed_one[...] = normed
    first_out = normed * gain_one_ref[...] + shift_one_ref[...]
    total[...] = first_out
    first_low = first_out.astype(bf16)
    first_t_ref[...] = first_low
    for at in range(0, ff, step):
        hidden = mm(w_in_t[at : at + step, :], first_low)
        half = 0.5 * (1.0 + lax.erf(hidden * 0.7071067811865476))
        bell = jnp.exp(hidden * hidden * -0.5) * 0.3989422804014327
        active = (hidden * half).astype(bf16)
        active_t_ref[at : at + step, :] = active
        slope[at : at + step, :] = (half + hidden * bell).astype(bf16)
        total[...] += mm(w_back_t[:, at : at + step], active)
    summed = total[...]
    centered = summed - mean_rows(summed)
    scale_two = lax.rsqrt(mean_rows(centered * centered) + norm_eps)
    normed = centered * scale_two
    layer_ref[0] = (normed * gain_two_ref[...] + shift_two_ref[...]).T.astype(bf16)
    grad_top = cot_ref[0].T.astype(f32)
    add_to(fold_gain_two, fold_lanes(grad_top * normed))
    add_to(fold_shift_two, fold_lanes(grad_top))
    grad_mid = norm_back(grad_top * gain_two_ref[...], normed, scale_two)
    total[...] = grad_mid
    grad_second = grad_mid.astype(bf16)
    grad_second_ref[...] = grad_second
    for at in range(0, ff, step):
        grad_active = mm(w_back_ref[at : at + step, :], grad_second)
        low = (grad_active * slope[at : at + step, :].astype(f32)).astype(bf16)
        grad_hidden_ref[at : at + step, :] = low
        total[...] += mm(w_in_ref[:, at : at + step], low)
    grad_first = total[...]
    normed = normed_one[...]
    add_to(fold_gain_one, fold_lanes(grad_first * normed))
    add_to(fold_shift_one, fold_lanes(grad_first))
    grad_base = norm_back(grad_first * gain_one_ref[...], normed, scale_one)
    grad_base_ref[...] = grad_base
    grad_branch = grad_base.astype(bf16)
    grad_branch_ref[...] = grad_branch
    total[...] = mm(w_out_ref[...], grad_branch)
    outs = (out_a, out_b)
    clear_pad(outs)
    grad_denom_ref[...] = jnp.zeros_like(grad_denom_ref)
    for h in range(HEADS):
        rows = head_slice(h)
        grad_numer = (total[rows, :] * inverse_denom[h : h + 1, :]).astype(bf16)
        grad_denom = -jnp.sum(grad_numer.astype(f32) * attended[rows, :], axis=0, keepdims=True)
        grad_denom_ref[h : h + 1, :] = grad_denom
        grad_numer_ref[rows, :] = grad_numer
        reads = trig_rows(q_t_ref[rows, :], cos, sin)
        put_state(outs, h, mm(with_row(grad_numer, grad_denom), reads, NT))

    @pl.when(pl.program_id(0) == pl.num_programs(0) - 1)
    def _():
        lane = lax.broadcasted_iota(jnp.int32, small_ref.shape, 1)
        value = jnp.zeros(small_ref.shape, f32)
        for i, ref in enumerate((fold_gain_one, fold_shift_one, fold_gain_two, fold_shift_two)):
            value = jnp.where(lane == i, lane_total(ref), value)
        small_ref[...] = value


def local_back_kernel(
    s_ref,
    tab_ref,
    q_t_ref,
    k_t_ref,
    k_ref,
    v_ref,
    sig_q_ref,
    grad_numer_ref,
    grad_denom_ref,
    state_a,
    state_b,
    grad_q_ref,
    grad_k_ref,
    grad_v_ref,
):
    table = tab_ref[0]
    blend = blend_of(table)
    tok_count = blend.shape[0]
    cos, sin = table[COS_READ : COS_READ + 1], table[SIN_READ : SIN_READ + 1]
    states = (state_a, state_b)
    for pair in range(PAIRS):
        lanes = slice(pair * 2 * HEAD_DIM, (pair + 1) * 2 * HEAD_DIM)
        both = mm(k_ref[0, :, lanes], pair_rows(q_t_ref, pair))
        grads = mm(v_ref[0, :, lanes], pair_rows(grad_numer_ref, pair))
        for side in range(2):
            h = 2 * pair + side
            rows = head_slice(h)
            part = slice(side * tok_count, (side + 1) * tok_count)
            grad_denom = grad_denom_ref[h : h + 1, :]
            scores = (both[:, part] * blend).astype(bf16)
            grad_scores, rest = two_parts((grads[:, part] + grad_denom) * blend)
            grad_numer = grad_numer_ref[rows, :]
            grad_v_ref[rows, :] = mm(grad_numer, scores, NT)
            grad_k_ref[rows, :] = mm(q_t_ref[rows, :], grad_scores, NT)
            reads = mm(take_state(states, h), with_row(grad_numer, grad_denom), TN)
            grad_q = (
                mm(k_t_ref[rows, :], grad_scores)
                + mm(k_t_ref[rows, :], rest)
                + cos * reads[:HEAD_DIM]
                + sin * reads[HEAD_DIM:]
            )
            grad_q_ref[rows, :] = (grad_q * sig_q_ref[rows, :].astype(f32)).astype(bf16)


def tail_kernel(
    s_ref,
    tab_ref,
    k_t_ref,
    v_t_ref,
    sig_k_ref,
    state_a,
    state_b,
    grad_k_in,
    grad_v_in,
    grad_kv_ref,
):
    table = tab_ref[0]
    cos, sin = table[COS_TAIL : COS_TAIL + 1], table[SIN_TAIL : SIN_TAIL + 1]
    states = (state_a, state_b)
    for h in range(HEADS):
        rows = head_slice(h)
        state = take_state(states, h)
        inner = mm(state, with_row(v_t_ref[rows, :], 1.0), TN)
        grad_k = grad_k_in[rows, :] + cos * inner[:HEAD_DIM] + sin * inner[HEAD_DIM:]
        grad_kv_ref[0, rows, :] = (grad_k * sig_k_ref[rows, :].astype(f32)).astype(bf16)
        keys = trig_rows(k_t_ref[rows, :], cos, sin)
        grad_kv_ref[1, rows, :] = (grad_v_in[rows, :] + mm(state[:HEAD_DIM], keys)).astype(bf16)


def token_kernel(s_ref, gq_ref, gkv_ref, base_ref, wq_ref, wk_ref, wv_ref, out_ref):
    total = base_ref[...] + mm(wq_ref[...], gq_ref[...])
    total = total + mm(wk_ref[...], gkv_ref[0])
    total = total + mm(wv_ref[...], gkv_ref[1])
    out_ref[0] = total.T


def in_hbm(v):
    return pltpu.with_memory_space_constraint(v, pltpu.HBM)


def spec(block, index):
    return pl.BlockSpec(block, index)


CORE, ODD, PLACE = range(3)


class Order:
    def __init__(self, scalars):
        self.scalars = scalars

    def call(self, kernel, grid, ins, outs, scratch, args, extra=(), free=(), limit=VMEM_LIMIT):
        count = 1 + len(extra)
        placed = len(scratch)

        def stepped(*refs):
            s_ref, handed = refs[0], refs[len(refs) - placed - 1]
            rest = refs[: len(refs) - placed - 1] + refs[len(refs) - placed :]
            kernel(*rest)
            for i in range(s_ref.shape[0]):
                handed[i] = s_ref[i]

        *values, self.scalars = pl.pallas_call(
            stepped,
            grid_spec=pltpu.PrefetchScalarGridSpec(
                num_scalar_prefetch=count,
                grid=grid,
                in_specs=ins,
                out_specs=[o for o, _ in outs] + [pl.BlockSpec(memory_space=pltpu.SMEM)],
                scratch_shapes=scratch,
            ),
            out_shape=[pltpu.HBM(shape, kind) for _, (shape, kind) in outs]
            + [jax.ShapeDtypeStruct(self.scalars.shape, jnp.int32)],
            compiler_params=pltpu.CompilerParams(
                dimension_semantics=("arbitrary",) * len(grid), vmem_limit_bytes=limit
            ),
            cost_estimate=pl.CostEstimate(flops=1000000000000, bytes_accessed=1, transcendentals=0),
        )(self.scalars, *extra, *[v if i in free else in_hbm(v) for i, v in enumerate(args)])
        return values


def pick_halves(core, value):
    cut = value.shape[1] // 2
    low, high = value[:, :cut], value[:, cut:]
    return jnp.where(core == 0, high, low), jnp.where(core == 0, low, high)


def tall_kernel(s_ref, a_ref, b_ref, away_ref, keep_ref):
    away_ref[...], keep_ref[...] = pick_halves(s_ref[CORE], mm(a_ref[...], b_ref[...], NT))


def tall_product(order, a, b):
    count, flat = a.shape
    tile, cut = count // 4, b.shape[0] // 2
    out = (spec((tile, cut), lambda i, *s: (i, 0)), ((count, cut), f32))
    ins = [spec((tile, flat), lambda i, *s: (i, 0)), spec(b.shape, lambda i, *s: (0, 0))]
    return order.call(tall_kernel, (4,), ins, [out, out], [], (a, b))


def wide_kernel(s_ref, a_ref, b_ref, away_ref, keep_ref):
    value = mm(a_ref[...], b_ref[...], NT)
    first = pl.program_id(0) < pl.num_programs(0) // 2

    @pl.when(first)
    def _():
        away_ref[...] = value

    @pl.when(jnp.logical_not(first))
    def _():
        keep_ref[...] = value


def wide_product(order, a, b):
    count, flat = a.shape
    cut = b.shape[0] // 2
    tile = 512
    half = cut // tile

    def source(i, s):
        return jnp.where(i < half, (1 - s[CORE]) * half + i, s[CORE] * half + i - half), 0

    outs = [
        (spec((count, tile), lambda i, s: (0, jnp.minimum(i, half - 1))), ((count, cut), f32)),
        (spec((count, tile), lambda i, s: (0, jnp.maximum(i - half, 0))), ((count, cut), f32)),
    ]
    ins = [spec(a.shape, lambda i, s: (0, 0)), spec((tile, flat), source)]
    return order.call(wide_kernel, (2 * half,), ins, outs, [], (a, b))


def twin_kernel(s_ref, a_ref, b_ref, c_ref, d_ref, *refs):
    core = s_ref[CORE]
    away_ref, keep_ref = refs[-2:]
    at = 0
    for left, right in ((a_ref, b_ref[0]), (c_ref, d_ref[0])):
        away, keep = pick_halves(core, mm(left[...], right, NT))
        away_ref[:, at : at + away.shape[1]] = away
        keep_ref[:, at : at + keep.shape[1]] = keep
        at += away.shape[1]
    if len(refs) == 3:
        value = refs[0][...]
        away_ref[:, at:] = jnp.where(core == 0, 0.0, value)
        keep_ref[:, at:] = jnp.where(core == 0, value, 0.0)


def twin_product(order, a, b, c, d, small=None):
    count, flat = a.shape
    tile = count // 2
    columns = count + (0 if small is None else small.shape[1])
    rows = spec((tile, flat), lambda i, s: (i, 0))
    ins, args = [], []
    for left, (right, group) in ((a, b), (c, d)):
        ins += [rows, spec((1, count, flat), lambda i, s, g=group: (g, 0, 0))]
        args += [left, right]
    if small is not None:
        ins.append(spec((tile, small.shape[1]), lambda i, s: (i, 0)))
        args.append(small)
    out = (spec((tile, columns), lambda i, s: (i, 0)), ((count, columns), f32))
    return order.call(twin_kernel, (2,), ins, [out, out], [], args)


def route_kernel(s_ref, *refs):
    for i in range(4):
        refs[8 + i][...] = refs[2 * i][...] + refs[2 * i + 1][...]


def route(order, left, right, low_bit, high_bit):
    (a, b), (c, d) = left, right
    shards, rows, columns = a.shape
    same = a is c
    if same:
        rows //= 2
    lower = 1 if same else 0
    half = shards // 2

    def by_low(flip):
        def index(i, s):
            mine = (s[PLACE] >> low_bit) & 1
            return 2 * i + ((1 - mine) if flip else mine), 0, 0

        return index

    def by_high(flip):
        def index(i, s):
            mine = (s[PLACE] >> high_bit) & 1
            return i + ((1 - mine) if flip else mine) * half, lower, 0

        return index

    block = (1, rows, columns)
    maps = [by_low(True), by_low(False), by_high(True), by_high(False)]
    ins = [spec(block, m) for m in maps for _ in range(2)]
    out = (spec(block, lambda i, s: (i, 0, 0)), ((half, rows, columns), f32))
    return order.call(route_kernel, (half,), ins, [out] * 4, [], (a, b, a, b, c, d, c, d))


def choose_kernel(s_ref, a_ref, b_ref, c_ref, d_ref, away_ref, kept_ref):
    upper, lower = a_ref[0] + b_ref[0], c_ref[0] + d_ref[0]
    odd = s_ref[ODD] == 1
    away_ref[...] = jnp.where(odd, upper, lower)
    kept_ref[...] = jnp.where(odd, lower, upper)


def choose(order, left, right):
    shape = left[0].shape[1:]
    whole = spec((1,) + shape, lambda i, s: (0, 0, 0))
    out = (spec(shape, lambda i, s: (0, 0)), (shape, f32))
    return order.call(
        choose_kernel,
        (1,),
        [whole] * 4,
        [out] * 2,
        [],
        (*left, *right),
        free=(1, 3),
        limit=SMALL_LIMIT,
    )


def add_kernel(s_ref, a_ref, b_ref, out_ref):
    out_ref[...] = a_ref[...] + b_ref[...]


def add(order, a, b):
    whole = spec(a.shape, lambda i, s: (0, 0))
    return order.call(
        add_kernel, (1,), [whole] * 2, [(whole, (a.shape, f32))], [], (a, b), free=(1,), limit=SMALL_LIMIT
    )[0]


def merge_kernel(s_ref, kept_ref, got_ref, out_ref):
    odd = s_ref[ODD] == 1
    rows = kept_ref.shape[0]
    kept, got = kept_ref[...], got_ref[...]
    out_ref[:rows, :] = jnp.where(odd, got, kept)
    out_ref[rows:, :] = jnp.where(odd, kept, got)


def merge(order, kept, got):
    rows, columns = kept.shape
    whole = spec((rows, columns), lambda i, s: (0, 0))
    out = (spec((2 * rows, columns), lambda i, s: (0, 0)), ((2 * rows, columns), f32))
    return order.call(
        merge_kernel, (1,), [whole] * 2, [out], [], (kept, got), free=(1,), limit=SMALL_LIMIT
    )[0]


def side_kernel(s_ref, mine_ref, other_ref, *outs):
    first = s_ref[CORE] == 0
    at = 0
    for out in outs:
        cut = out.shape[1] // 2
        if cut < 128:
            out[...] = jnp.where(first, mine_ref[:, at:], other_ref[:, at:])
            break
        mine, other = mine_ref[:, at : at + cut], other_ref[:, at : at + cut]
        out[:, :cut] = jnp.where(first, mine, other)
        out[:, cut:] = jnp.where(first, other, mine)
        at += cut


def side(order, mine, other, widths):
    whole = spec(mine.shape, lambda i, s: (0, 0))
    outs = [(spec((mine.shape[0], w), lambda i, s: (0, 0)), ((mine.shape[0], w), f32)) for w in widths]
    return order.call(
        side_kernel, (1,), [whole] * 2, outs, [], (mine, other), free=(1,), limit=SMALL_LIMIT
    )


def mix_kernel(first, s_ref, w_ref, *refs):
    row = pl.program_id(0)
    for i in range(2):
        own, other = (w_ref[first + 2 * i + j, row] for j in range(2))
        refs[4 + i][...] = own * refs[2 * i][...] + other * refs[2 * i + 1][...]


def mix(order, weights, first, *parts):
    shape = parts[0].shape
    block = spec((1,) + shape[1:], lambda r, *s: (r, 0, 0))
    return order.call(
        partial(mix_kernel, first),
        (shape[0],),
        [block] * 4,
        [(block, (shape, f32))] * 2,
        [],
        parts,
        (weights,),
        free=range(4),
        limit=SMALL_LIMIT,
    )


def first_begins(lengths, count, tok_count):
    slots = lengths.shape[1]
    order = jnp.arange(slots)
    before = (order[:, None] > order[None, :]).astype(jnp.int32)
    starts = jnp.sum(lengths[:, None, :] * before[None], axis=-1)
    firsts = jnp.arange(count, dtype=jnp.int32) * tok_count
    reached = starts[:, None, :] <= firsts[None, :, None]
    return jnp.max(jnp.where(reached, starts[:, None, :], 0), axis=-1)


def pick(index, values):
    out = values[0]
    for i in range(1, len(values)):
        out = jnp.where(index == i, values[i], out)
    return out


def weights_of(begin_first, tok_count, reverse):
    count = lax.axis_size("seq")
    place = lax.axis_index("seq")

    def covers(i, j):
        low, high = (count - 1 - j, count - 1 - i) if reverse else (i, j)
        return (begin_first[:, high] < (low + 1) * tok_count).astype(f32)

    if count != 4:
        spots = jnp.arange(count)
        mine = begin_first.T if reverse else begin_first[:, place][None]
        reach = (place if reverse else spots[:, None]) + 1
        ahead = (spots > place) if reverse else (spots < place)
        return ((mine < reach * tok_count) & ahead[:, None]).astype(f32)
    index = count - 1 - place if reverse else place
    zero = jnp.zeros_like(begin_first[:, 0], f32)
    one = zero + 1.0
    m02, m03, m13 = covers(0, 2), covers(0, 3), covers(1, 3)
    onward = [
        pick(index, [m02, m13, zero, zero]),
        pick(index, [one, m03, zero, zero]),
        pick(index, [one, zero, one, zero]),
        pick(index, [zero, zero, m03, one]),
    ]
    final = [
        pick(index, [zero, one, zero, one]),
        pick(index, [zero, zero, one, one]),
        pick(index, [zero, zero, m02, m13]),
        pick(index, [zero, one, one, one]),
    ]
    return onward + final


def entering(order, parts, weights, first):
    if lax.axis_size("seq") != 4:
        gathered = [lax.all_gather(p, "seq") for p in parts]
        yield
        yield
        yield tuple(jnp.sum(g * weights[first][:, :, None, None], axis=0) for g in gathered)
    part_a, part_b = parts
    got_a, got_b = swap(part_a, "seq", 1), swap(part_b, "seq", 2)
    yield
    next_a, next_b = mix(order, weights, first, part_a, got_a, part_b, got_b)
    last_a, last_b = swap(next_a, "seq", 2), swap(next_b, "seq", 1)
    yield
    yield mix(order, weights, first + 4, got_a, last_a, got_b, last_b)


def swap(value, axis, distance):
    count = lax.axis_size(axis)
    return lax.ppermute(value, axis, [(i, i ^ distance) for i in range(count)])


def reduced(order, away, keep, widths):
    count = lax.axis_size("batch")
    shards = lax.axis_size("seq")
    bits = shards.bit_length() - 1
    shape = (shards, keep.shape[0] // shards, keep.shape[1])
    got = swap(away, "batch", 1).reshape(shape)
    yield
    left = right = (keep.reshape(shape), got)
    for step in range(bits):
        high = bits - 1 - step
        away_l, keep_l, away_r, keep_r = route(order, left, right, step, high)
        left = keep_l, swap(away_l, "seq", 1 << step)
        right = keep_r, swap(away_r, "seq", 1 << high)
        yield
    away, kept = choose(order, left, right)
    got = swap(away, "batch", 2)
    distance = 4
    while distance < count:
        yield
        kept = add(order, kept, got)
        got = swap(kept, "batch", distance)
        distance *= 2
    yield
    kept = add(order, kept, got)
    got = swap(kept, "batch", 2)
    yield
    merged = merge(order, kept, got)
    other = swap(merged, "batch", 1)
    yield
    yield side(order, merged, other, widths)


SCHEDULE = (
    "in_product", "states", "back_product", "in", "states", "back",
    "local", "mixed_product", "tail", "in", "back", "in",
    "mixed", "back", "mixed", "back", "last_product", "mixed",
    "last", "in", "back", "last", "mixed", "last",
    "in", "back", "last", "tokens", "mixed", "back",
    "last", "in", "mixed", "last", "in", "mixed",
    "last",
)


def body(
    tokens,
    cotangent,
    doc_lengths,
    w_query,
    w_key,
    w_value,
    w_out,
    w_in,
    w_back,
    gain_one,
    shift_one,
    gain_two,
    shift_two,
):
    rows, toks, width = tokens.shape
    ff = w_in.shape[1]
    flat = rows * toks
    shards = lax.axis_size("seq")
    whole = pl.BlockSpec(memory_space=pltpu.VMEM)
    token_major = pl.BlockSpec((1, toks, width), lambda r, *s: (r, 0, 0))
    table_spec = pl.BlockSpec((1, 8, toks), lambda r, *s: (r, 0, 0))
    state_spec = pl.BlockSpec((1, STATE_ROWS, 2 * HEAD_DIM), lambda r, *s: (r, 0, 0))

    def feature(count):
        return pl.BlockSpec((count, toks), lambda r, *s: (0, r))

    tok_low = (token_major, ((rows, toks, width), bf16))
    wide_low = (feature(width), ((width, flat), bf16))
    wide_full = (feature(width), ((width, flat), f32))
    ff_low = (feature(ff), ((ff, flat), bf16))
    head_rows = (feature(16), ((16, flat), f32))
    fold = (pl.BlockSpec((width, 128), lambda r, *s: (0, 0)), ((width, 128), f32))
    state = (state_spec, ((rows, STATE_ROWS, 2 * HEAD_DIM), f32))
    grid = (rows,)

    batch_place = lax.axis_index("batch").astype(jnp.int32)
    scalars = jnp.stack(
        [batch_place & 1, (batch_place >> 1) & 1, lax.axis_index("seq").astype(jnp.int32)]
    )
    order = Order(scalars)

    def run(kernel, ins, outs, scratch, *args, extra=()):
        return order.call(kernel, grid, ins, outs, scratch, args, extra)

    def column(v):
        return v[:, None]

    table, tok_t, k_t, v_t, key, value, sig_k, state_a, state_b = run(
        project_kernel,
        [token_major, whole, whole],
        [(table_spec, ((rows, 8, toks), f32))]
        + [wide_low] * 3
        + [tok_low] * 2
        + [wide_low]
        + [state] * 2,
        [pltpu.VMEM((2, width, width), bf16)],
        tokens,
        w_key,
        w_value,
        extra=(doc_lengths,),
    )
    begins = first_begins(doc_lengths, shards, toks)
    if shards == 4:
        weights = jnp.stack(weights_of(begins, toks, False) + weights_of(begins, toks, True))
        later = 8
    else:
        weights = [weights_of(begins, toks, False), weights_of(begins, toks, True)]
        later = 1
    states = entering(order, (state_a, state_b), weights, 0)
    next(states)
    part = ff // rows
    q_t, sig_q, numer, denom_loc, w_out_t, w_in_t, w_back_t = run(
        local_kernel,
        [
            table_spec,
            feature(width),
            token_major,
            feature(width),
            whole,
            whole,
            pl.BlockSpec((width, part), lambda r, *s: (0, r)),
            pl.BlockSpec((part, width), lambda r, *s: (r, 0)),
        ],
        [
            wide_low,
            wide_low,
            wide_full,
            head_rows,
            (pl.BlockSpec((width, width), lambda r, *s: (0, 0)), ((width, width), bf16)),
            (pl.BlockSpec((part, width), lambda r, *s: (r, 0)), ((ff, width), bf16)),
            (pl.BlockSpec((width, part), lambda r, *s: (0, r)), ((width, ff), bf16)),
        ],
        [pltpu.VMEM((width, width), bf16)],
        table,
        tok_t,
        key,
        v_t,
        w_query,
        w_out,
        w_in,
        w_back,
    )
    next(states)
    in_a, in_b = next(states)
    (
        layer_out,
        att_t,
        first_t,
        active_t,
        grad_second,
        grad_hidden,
        grad_base,
        grad_branch,
        grad_numer,
        grad_denom,
        small,
        out_a,
        out_b,
    ) = run(
        layer_kernel,
        [
            table_spec,
            feature(width),
            feature(width),
            feature(16),
            state_spec,
            state_spec,
            feature(width),
            token_major,
        ]
        + [whole] * 10,
        [
            tok_low,
            wide_low,
            wide_low,
            ff_low,
            wide_low,
            ff_low,
            wide_full,
            wide_low,
            wide_low,
            head_rows,
            fold,
            state,
            state,
        ],
        [
            pltpu.VMEM((ff, toks), bf16),
            pltpu.VMEM((width, toks), f32),
            pltpu.VMEM((width, toks), f32),
            pltpu.VMEM((16, toks), f32),
            pltpu.VMEM((width, toks), f32),
        ]
        + [pltpu.VMEM((width, 128), f32)] * 4,
        table,
        q_t,
        numer,
        denom_loc,
        in_a,
        in_b,
        tok_t,
        cotangent,
        w_out_t,
        w_in_t,
        w_back_t,
        w_out,
        w_in,
        w_back,
        column(gain_one),
        column(shift_one),
        column(gain_two),
        column(shift_two),
    )

    back_states = entering(order, (out_a, out_b), weights, later)
    next(back_states)
    pieces, made = {}, {}

    def begin(name, product, widths):
        pieces[name] = reduced(order, *product, widths)
        next(pieces[name])

    def local_back():
        made["query"], made["key"], made["value"] = run(
            local_back_kernel,
            [
                table_spec,
                feature(width),
                feature(width),
                token_major,
                token_major,
                feature(width),
                feature(width),
                feature(16),
                state_spec,
                state_spec,
            ],
            [wide_low, wide_full, wide_full],
            [],
            table,
            q_t,
            k_t,
            key,
            value,
            sig_q,
            grad_numer,
            grad_denom,
            in_a,
            in_b,
        )

    def tail():
        back_a, back_b = made["states"]
        (made["kv"],) = run(
            tail_kernel,
            [table_spec]
            + [feature(width)] * 3
            + [state_spec] * 2
            + [feature(width)] * 2,
            [(pl.BlockSpec((2, width, toks), lambda r, *s: (0, 0, r)), ((2, width, flat), bf16))],
            [],
            table,
            k_t,
            v_t,
            sig_k,
            back_a,
            back_b,
            made["key"],
            made["value"],
        )

    def token_grads():
        (made["tokens"],) = run(
            token_kernel,
            [
                feature(width),
                pl.BlockSpec((2, width, toks), lambda r, *s: (0, 0, r)),
                feature(width),
            ]
            + [whole] * 3,
            [(token_major, ((rows, toks, width), f32))],
            [],
            made["query"],
            made["kv"],
            grad_base,
            w_query,
            w_key,
            w_value,
        )

    def states_on():
        made["states"] = next(back_states)

    steps = {
        "back_product": lambda: begin("back", tall_product(order, active_t, grad_second), (width,)),
        "in_product": lambda: begin("in", wide_product(order, first_t, grad_hidden), (ff,)),
        "mixed_product": lambda: begin(
            "mixed",
            twin_product(order, att_t, (grad_branch[None], 0), tok_t, (made["query"][None], 0), small),
            (width, width, 128),
        ),
        "last_product": lambda: begin(
            "last",
            twin_product(order, tok_t, (made["kv"], 0), tok_t, (made["kv"], 1)),
            (width, width),
        ),
        "states": states_on,
        "local": local_back,
        "tail": tail,
        "tokens": token_grads,
    }
    ends = {}

    def step(name):
        value = next(pieces[name])
        if value is not None:
            ends[name] = value

    for name in SCHEDULE:
        if name in steps:
            steps[name]()
        elif name not in ends:
            step(name)
    while len(ends) < len(pieces):
        for name in pieces:
            if name not in ends:
                step(name)
    (total_back,), (total_in,) = ends["back"], ends["in"]
    total_out, total_query, vectors = ends["mixed"]
    total_key, total_value = ends["last"]
    grad_tokens = made["tokens"]
    return (
        layer_out,
        grad_tokens,
        total_query,
        total_key,
        total_value,
        total_out,
        total_in,
        total_back,
        vectors[:, 0],
        vectors[:, 1],
        vectors[:, 2],
        vectors[:, 3],
    )


def solution(mesh):
    in_specs = (
        P("batch", "seq", None),
        P("batch", "seq", None),
        P("batch", None),
        P(),
        P(),
        P(),
        P(),
        P(),
        P(),
        P(),
        P(),
        P(),
        P(),
    )
    out_specs = (
        P("batch", "seq", None),
        P("batch", "seq", None),
        P("seq", None),
        P("seq", None),
        P("seq", None),
        P("seq", None),
        P("seq", None),
        P("seq", None),
        P("seq"),
        P("seq"),
        P("seq"),
        P("seq"),
    )
    return jax.shard_map(body, mesh=mesh, in_specs=in_specs, out_specs=out_specs, check_vma=False)
```

```python
from functools import partial

import jax
import jax.numpy as jnp
from jax import lax
from jax.experimental import pallas as pl
from jax.experimental.pallas import tpu as pltpu
from jax.sharding import PartitionSpec as P

HEADS = 12
HEAD_DIM = 64
PAIRS = HEADS // 2
HALF_HEADS = HEADS // 2
STATE_ROWS = HALF_HEADS * HEAD_DIM + 8

f32 = jnp.float32
bf16 = jnp.bfloat16
half_pi = 1.5707963267948966
norm_eps = 1e-05
VMEM_LIMIT = 30 * 1024 * 1024
SMALL_LIMIT = 16 * 1024 * 1024
LAYER_LIMIT = 38 * 1024 * 1024

NN = (((1,), (0,)), ((), ()))
NT = (((1,), (1,)), ((), ()))
TN = (((0,), (0,)), ((), ()))


def mm(a, b, dims=NN):
    return lax.dot_general(a, b, dims, preferred_element_type=f32)


COS, SIN, BEGIN, COS_READ, SIN_READ, COS_TAIL, SIN_TAIL = range(7)


def make_table(place, lens_ref, row, tok_count):
    pos = place + lax.broadcasted_iota(jnp.int32, (8, tok_count), 1)
    last = place + tok_count - 1
    start = jnp.int32(0)
    begin = jnp.zeros((8, tok_count), jnp.int32)
    span = jnp.ones((8, tok_count), jnp.int32)
    last_begin = jnp.int32(0)
    for d in range(lens_ref.shape[1]):
        length = lens_ref[row, d]
        inside = pos >= start
        begin = jnp.where(inside, start, begin)
        span = jnp.where(inside, length, span)
        last_begin = jnp.where(start <= last, start, last_begin)
        start = start + length
    angle = half_pi * (pos - begin).astype(f32) / span.astype(f32)
    cos, sin = jnp.cos(angle), jnp.sin(angle)
    reader = (begin < place).astype(f32)
    tail = (begin == last_begin).astype(f32)
    which = lax.broadcasted_iota(jnp.int32, (8, tok_count), 0)
    table = jnp.zeros((8, tok_count), f32)
    for index, value in (
        (COS, cos),
        (SIN, sin),
        (BEGIN, begin.astype(f32)),
        (COS_READ, cos * reader),
        (SIN_READ, sin * reader),
        (COS_TAIL, cos * tail),
        (SIN_TAIL, sin * tail),
    ):
        table = jnp.where(which == index, value, table)
    return table


def blend_of(table):
    columns = table.T
    tok_count = table.shape[1]
    source = lax.broadcasted_iota(jnp.int32, (tok_count, tok_count), 0)
    reader = lax.broadcasted_iota(jnp.int32, (tok_count, tok_count), 1)
    same = (columns[:, BEGIN : BEGIN + 1] == table[BEGIN : BEGIN + 1]) & (source <= reader)
    value = (
        columns[:, COS : COS + 1] * table[COS : COS + 1]
        + columns[:, SIN : SIN + 1] * table[SIN : SIN + 1]
    )
    return jnp.where(same, value, 0.0)


def trig_rows(head_rows, cos, sin):
    wide = head_rows.astype(f32)
    return jnp.concatenate([(wide * cos).astype(bf16), (wide * sin).astype(bf16)], axis=0)


def with_row(rows, extra):
    which = lax.broadcasted_iota(jnp.int32, (16, rows.shape[1]), 0)
    return jnp.concatenate([rows, jnp.where(which == 0, extra, 0.0).astype(bf16)], axis=0)


def head_slice(h):
    return slice(h * HEAD_DIM, (h + 1) * HEAD_DIM)


def put_state(state_refs, h, value):
    ref = state_refs[h // HALF_HEADS]
    place = h % HALF_HEADS
    ref[0, head_slice(place), :] = value[:HEAD_DIM]
    ref[0, HALF_HEADS * HEAD_DIM + place : HALF_HEADS * HEAD_DIM + place + 1, :] = value[
        HEAD_DIM : HEAD_DIM + 1
    ]


def take_state(state_refs, h):
    ref = state_refs[h // HALF_HEADS]
    place = h % HALF_HEADS
    mats = ref[0, head_slice(place), :].astype(bf16)
    sums = ref[0, HALF_HEADS * HEAD_DIM + place : HALF_HEADS * HEAD_DIM + place + 1, :]
    return with_row(mats, sums)


def clear_pad(state_refs):
    for ref in state_refs:
        ref[0, HALF_HEADS * HEAD_DIM :, :] = jnp.zeros((8, 2 * HEAD_DIM), f32)


def softplus_sigmoid(v):
    small = jnp.exp(-jnp.abs(v))
    soft = jnp.maximum(v, 0.0) + jnp.log1p(small)
    inverse = 1.0 / (1.0 + small)
    return soft, jnp.where(v >= 0, inverse, small * inverse)


def project_kernel(
    s_ref,
    lens_ref,
    tok_ref,
    wk_ref,
    wv_ref,
    tab_ref,
    tok_t_ref,
    k_t_ref,
    v_t_ref,
    k_ref,
    v_ref,
    sig_k_ref,
    state_a,
    state_b,
    w_t,
):
    row = pl.program_id(0)

    @pl.when(row == 0)
    def _():
        w_t[0] = wk_ref[...].T
        w_t[1] = wv_ref[...].T

    tok_t = tok_ref[0].T
    tok_t_ref[...] = tok_t
    table = make_table(s_ref[PLACE] * tok_t.shape[1], lens_ref, row, tok_t.shape[1])
    tab_ref[0] = table
    soft, sig = softplus_sigmoid(mm(w_t[0], tok_t))
    key_t = soft.astype(bf16)
    k_t_ref[...] = key_t
    k_ref[0] = key_t.T
    sig_k_ref[...] = sig.astype(bf16)
    value_t = mm(w_t[1], tok_t).astype(bf16)
    v_t_ref[...] = value_t
    v_ref[0] = value_t.T
    states = (state_a, state_b)
    clear_pad(states)
    cos, sin = table[COS_TAIL : COS_TAIL + 1], table[SIN_TAIL : SIN_TAIL + 1]
    for h in range(HEADS):
        keys = trig_rows(k_t_ref[head_slice(h), :], cos, sin)
        values = with_row(v_t_ref[head_slice(h), :], 1.0)
        put_state(states, h, mm(values, keys, NT))


def pair_rows(ref, pair):
    first = ref[head_slice(2 * pair), :]
    second = ref[head_slice(2 * pair + 1), :]
    nothing = jnp.zeros_like(first)
    return jnp.concatenate(
        [
            jnp.concatenate([first, nothing], axis=1),
            jnp.concatenate([nothing, second], axis=1),
        ],
        axis=0,
    )


def two_parts(v):
    high = v.astype(bf16)
    return high, (v - high.astype(f32)).astype(bf16)


def local_kernel(
    s_ref,
    tab_ref,
    tok_t_ref,
    k_ref,
    v_t_ref,
    wq_ref,
    w_out_ref,
    w_in_ref,
    w_back_ref,
    q_t_ref,
    sig_q_ref,
    numer_ref,
    denom_ref,
    w_out_t,
    w_in_t,
    w_back_t,
    w_t,
):
    @pl.when(pl.program_id(0) == 0)
    def _():
        w_t[...] = wq_ref[...].T
        w_out_t[...] = w_out_ref[...].T

    w_in_t[...] = w_in_ref[...].T
    w_back_t[...] = w_back_ref[...].T

    soft, sig = softplus_sigmoid(mm(w_t[...], tok_t_ref[...]))
    q_t_ref[...] = soft.astype(bf16)
    sig_q_ref[...] = sig.astype(bf16)
    blend = blend_of(tab_ref[0])
    tok_count = blend.shape[0]
    denom_ref[...] = jnp.zeros_like(denom_ref)
    for pair in range(PAIRS):
        lanes = slice(pair * 2 * HEAD_DIM, (pair + 1) * 2 * HEAD_DIM)
        both = mm(k_ref[0, :, lanes], pair_rows(q_t_ref, pair))
        for side in range(2):
            h = 2 * pair + side
            high, low = two_parts(both[:, side * tok_count : (side + 1) * tok_count] * blend)
            values = with_row(v_t_ref[head_slice(h), :], 1.0)
            out = mm(values, high) + mm(values, low)
            numer_ref[head_slice(h), :] = out[:HEAD_DIM]
            denom_ref[h : h + 1, :] = out[HEAD_DIM : HEAD_DIM + 1]


def mean_rows(v):
    return jnp.sum(v, axis=0, keepdims=True) * (1.0 / v.shape[0])


def fold_lanes(v):
    total = v[:, :128]
    for at in range(128, v.shape[1], 128):
        total = total + v[:, at : at + 128]
    return total


def add_to(ref, value):
    first = pl.program_id(0) == 0

    @pl.when(first)
    def _():
        ref[...] = value

    @pl.when(jnp.logical_not(first))
    def _():
        ref[...] += value


def norm_back(grad_norm, normed, inv_scale):
    return inv_scale * (grad_norm - mean_rows(grad_norm) - normed * mean_rows(grad_norm * normed))


def lane_total(ref):
    return jnp.sum(ref[...], axis=1, keepdims=True)


def layer_kernel(
    s_ref,
    tab_ref,
    q_t_ref,
    numer_ref,
    denom_loc_ref,
    state_a,
    state_b,
    tok_t_ref,
    cot_ref,
    w_out_t,
    w_in_t,
    w_back_t,
    w_out_ref,
    w_in_ref,
    w_back_ref,
    gain_one_ref,
    shift_one_ref,
    gain_two_ref,
    shift_two_ref,
    layer_ref,
    att_t_ref,
    first_t_ref,
    active_t_ref,
    grad_second_ref,
    grad_hidden_ref,
    grad_base_ref,
    grad_branch_ref,
    grad_numer_ref,
    grad_denom_ref,
    small_ref,
    out_a,
    out_b,
    slope,
    normed_one,
    attended,
    inverse_denom,
    total,
    fold_gain_one,
    fold_shift_one,
    fold_gain_two,
    fold_shift_two,
):
    ff = w_in_ref.shape[1]
    step = 768
    table = tab_ref[0]
    cos, sin = table[COS_READ : COS_READ + 1], table[SIN_READ : SIN_READ + 1]
    states = (state_a, state_b)
    for h in range(HEADS):
        reads = trig_rows(q_t_ref[head_slice(h), :], cos, sin)
        more = mm(take_state(states, h), reads)
        numer = numer_ref[head_slice(h), :] + more[:HEAD_DIM]
        inverse = 1.0 / (denom_loc_ref[h : h + 1, :] + more[HEAD_DIM : HEAD_DIM + 1])
        inverse_denom[h : h + 1, :] = inverse
        value = numer * inverse
        attended[head_slice(h), :] = value
        att_t_ref[head_slice(h), :] = value.astype(bf16)
    summed = tok_t_ref[...].astype(f32) + mm(w_out_t[...], att_t_ref[...])
    centered = summed - mean_rows(summed)
    scale_one = lax.rsqrt(mean_rows(centered * centered) + norm_eps)
    normed = centered * scale_one
    normed_one[...] = normed
    first_out = normed * gain_one_ref[...] + shift_one_ref[...]
    total[...] = first_out
    first_low = first_out.astype(bf16)
    first_t_ref[...] = first_low
    for at in range(0, ff, step):
        hidden = mm(w_in_t[at : at + step, :], first_low)
        half = 0.5 * (1.0 + lax.erf(hidden * 0.7071067811865476))
        bell = jnp.exp(hidden * hidden * -0.5) * 0.3989422804014327
        active = (hidden * half).astype(bf16)
        active_t_ref[at : at + step, :] = active
        slope[at : at + step, :] = (half + hidden * bell).astype(bf16)
        total[...] += mm(w_back_t[:, at : at + step], active)
    summed = total[...]
    centered = summed - mean_rows(summed)
    scale_two = lax.rsqrt(mean_rows(centered * centered) + norm_eps)
    normed = centered * scale_two
    layer_ref[0] = (normed * gain_two_ref[...] + shift_two_ref[...]).T.astype(bf16)
    grad_top = cot_ref[0].T.astype(f32)
    add_to(fold_gain_two, fold_lanes(grad_top * normed))
    add_to(fold_shift_two, fold_lanes(grad_top))
    grad_mid = norm_back(grad_top * gain_two_ref[...], normed, scale_two)
    total[...] = grad_mid
    grad_second = grad_mid.astype(bf16)
    grad_second_ref[...] = grad_second
    for at in range(0, ff, step):
        grad_active = mm(w_back_ref[at : at + step, :], grad_second)
        low = (grad_active * slope[at : at + step, :].astype(f32)).astype(bf16)
        grad_hidden_ref[at : at + step, :] = low
        total[...] += mm(w_in_ref[:, at : at + step], low)
    grad_first = total[...]
    normed = normed_one[...]
    add_to(fold_gain_one, fold_lanes(grad_first * normed))
    add_to(fold_shift_one, fold_lanes(grad_first))
    grad_base = norm_back(grad_first * gain_one_ref[...], normed, scale_one)
    grad_base_ref[...] = grad_base
    grad_branch = grad_base.astype(bf16)
    grad_branch_ref[...] = grad_branch
    total[...] = mm(w_out_ref[...], grad_branch)
    outs = (out_a, out_b)
    clear_pad(outs)
    grad_denom_ref[...] = jnp.zeros_like(grad_denom_ref)
    for h in range(HEADS):
        rows = head_slice(h)
        grad_numer = (total[rows, :] * inverse_denom[h : h + 1, :]).astype(bf16)
        grad_denom = -jnp.sum(grad_numer.astype(f32) * attended[rows, :], axis=0, keepdims=True)
        grad_denom_ref[h : h + 1, :] = grad_denom
        grad_numer_ref[rows, :] = grad_numer
        reads = trig_rows(q_t_ref[rows, :], cos, sin)
        put_state(outs, h, mm(with_row(grad_numer, grad_denom), reads, NT))

    @pl.when(pl.program_id(0) == pl.num_programs(0) - 1)
    def _():
        lane = lax.broadcasted_iota(jnp.int32, small_ref.shape, 1)
        value = jnp.zeros(small_ref.shape, f32)
        for i, ref in enumerate((fold_gain_one, fold_shift_one, fold_gain_two, fold_shift_two)):
            value = jnp.where(lane == i, lane_total(ref), value)
        small_ref[...] = value


def local_back_kernel(
    s_ref,
    tab_ref,
    q_t_ref,
    k_t_ref,
    k_ref,
    v_ref,
    sig_q_ref,
    grad_numer_ref,
    grad_denom_ref,
    state_a,
    state_b,
    grad_q_ref,
    grad_k_ref,
    grad_v_ref,
):
    table = tab_ref[0]
    blend = blend_of(table)
    tok_count = blend.shape[0]
    cos, sin = table[COS_READ : COS_READ + 1], table[SIN_READ : SIN_READ + 1]
    states = (state_a, state_b)
    for pair in range(PAIRS):
        lanes = slice(pair * 2 * HEAD_DIM, (pair + 1) * 2 * HEAD_DIM)
        both = mm(k_ref[0, :, lanes], pair_rows(q_t_ref, pair))
        grads = mm(v_ref[0, :, lanes], pair_rows(grad_numer_ref, pair))
        for side in range(2):
            h = 2 * pair + side
            rows = head_slice(h)
            part = slice(side * tok_count, (side + 1) * tok_count)
            grad_denom = grad_denom_ref[h : h + 1, :]
            scores = (both[:, part] * blend).astype(bf16)
            grad_scores, rest = two_parts((grads[:, part] + grad_denom) * blend)
            grad_numer = grad_numer_ref[rows, :]
            grad_v_ref[rows, :] = mm(grad_numer, scores, NT)
            grad_k_ref[rows, :] = mm(q_t_ref[rows, :], grad_scores, NT)
            reads = mm(take_state(states, h), with_row(grad_numer, grad_denom), TN)
            grad_q = (
                mm(k_t_ref[rows, :], grad_scores)
                + mm(k_t_ref[rows, :], rest)
                + cos * reads[:HEAD_DIM]
                + sin * reads[HEAD_DIM:]
            )
            grad_q_ref[rows, :] = (grad_q * sig_q_ref[rows, :].astype(f32)).astype(bf16)


def tail_kernel(
    s_ref,
    tab_ref,
    k_t_ref,
    v_t_ref,
    sig_k_ref,
    state_a,
    state_b,
    grad_k_in,
    grad_v_in,
    grad_kv_ref,
):
    table = tab_ref[0]
    cos, sin = table[COS_TAIL : COS_TAIL + 1], table[SIN_TAIL : SIN_TAIL + 1]
    states = (state_a, state_b)
    for h in range(HEADS):
        rows = head_slice(h)
        state = take_state(states, h)
        inner = mm(state, with_row(v_t_ref[rows, :], 1.0), TN)
        grad_k = grad_k_in[rows, :] + cos * inner[:HEAD_DIM] + sin * inner[HEAD_DIM:]
        grad_kv_ref[0, rows, :] = (grad_k * sig_k_ref[rows, :].astype(f32)).astype(bf16)
        keys = trig_rows(k_t_ref[rows, :], cos, sin)
        grad_kv_ref[1, rows, :] = (grad_v_in[rows, :] + mm(state[:HEAD_DIM], keys)).astype(bf16)


def token_kernel(s_ref, gq_ref, gkv_ref, base_ref, wq_ref, wk_ref, wv_ref, out_ref):
    total = base_ref[...] + mm(wq_ref[...], gq_ref[...])
    total = total + mm(wk_ref[...], gkv_ref[0])
    total = total + mm(wv_ref[...], gkv_ref[1])
    out_ref[0] = total.T


def spec(block, index):
    return pl.BlockSpec(block, index)


NEAR = pl.BlockSpec(memory_space=pltpu.VMEM)

CORE, ODD, PLACE = range(3)


class Order:
    def __init__(self, scalars):
        self.scalars = scalars

    def call(
        self, kernel, grid, ins, outs, scratch, args, extra=(), free=(), near=(), near_out=(), limit=VMEM_LIMIT
    ):
        count = 1 + len(extra)
        placed = len(scratch)

        def stepped(*refs):
            s_ref, handed = refs[0], refs[len(refs) - placed - 1]
            rest = refs[: len(refs) - placed - 1] + refs[len(refs) - placed :]
            kernel(*rest)
            for i in range(s_ref.shape[0]):
                handed[i] = s_ref[i]

        *values, self.scalars = pl.pallas_call(
            stepped,
            grid_spec=pltpu.PrefetchScalarGridSpec(
                num_scalar_prefetch=count,
                grid=grid,
                in_specs=ins,
                out_specs=[o for o, _ in outs] + [pl.BlockSpec(memory_space=pltpu.SMEM)],
                scratch_shapes=scratch,
            ),
            out_shape=[
                (pltpu.VMEM if i in near_out else pltpu.HBM)(shape, kind)
                for i, (_, (shape, kind)) in enumerate(outs)
            ]
            + [jax.ShapeDtypeStruct(self.scalars.shape, jnp.int32)],
            compiler_params=pltpu.CompilerParams(
                dimension_semantics=("arbitrary",) * len(grid), vmem_limit_bytes=limit
            ),
            cost_estimate=pl.CostEstimate(flops=1000000000000, bytes_accessed=1, transcendentals=0),
        )(
            self.scalars,
            *extra,
            *[
                v
                if i in free
                else pltpu.with_memory_space_constraint(v, pltpu.VMEM if i in near else pltpu.HBM)
                for i, v in enumerate(args)
            ],
        )
        return values


def pick_halves(core, value):
    cut = value.shape[1] // 2
    low, high = value[:, :cut], value[:, cut:]
    return jnp.where(core == 0, high, low), jnp.where(core == 0, low, high)


def tall_kernel(s_ref, a_ref, b_ref, away_ref, keep_ref):
    away_ref[...], keep_ref[...] = pick_halves(s_ref[CORE], mm(a_ref[...], b_ref[...], NT))


def tall_product(order, a, b):
    count, flat = a.shape
    tile, cut = count // 4, b.shape[0] // 2
    out = (spec((tile, cut), lambda i, *s: (i, 0)), ((count, cut), f32))
    ins = [spec((tile, flat), lambda i, *s: (i, 0)), spec(b.shape, lambda i, *s: (0, 0))]
    return order.call(tall_kernel, (4,), ins, [out, out], [], (a, b))


def wide_kernel(s_ref, a_ref, b_ref, away_ref, keep_ref):
    value = mm(a_ref[...], b_ref[...], NT)
    first = pl.program_id(0) < pl.num_programs(0) // 2

    @pl.when(first)
    def _():
        away_ref[...] = value

    @pl.when(jnp.logical_not(first))
    def _():
        keep_ref[...] = value


def wide_product(order, a, b):
    count, flat = a.shape
    cut = b.shape[0] // 2
    tile = 512
    half = cut // tile

    def source(i, s):
        return jnp.where(i < half, (1 - s[CORE]) * half + i, s[CORE] * half + i - half), 0

    outs = [
        (spec((count, tile), lambda i, s: (0, jnp.minimum(i, half - 1))), ((count, cut), f32)),
        (spec((count, tile), lambda i, s: (0, jnp.maximum(i - half, 0))), ((count, cut), f32)),
    ]
    ins = [spec(a.shape, lambda i, s: (0, 0)), spec((tile, flat), source)]
    return order.call(wide_kernel, (2 * half,), ins, outs, [], (a, b))


def twin_kernel(s_ref, a_ref, b_ref, c_ref, d_ref, *refs):
    core = s_ref[CORE]
    away_ref, keep_ref = refs[-2:]
    at = 0
    for left, right in ((a_ref, b_ref[0]), (c_ref, d_ref[0])):
        away, keep = pick_halves(core, mm(left[...], right, NT))
        away_ref[:, at : at + away.shape[1]] = away
        keep_ref[:, at : at + keep.shape[1]] = keep
        at += away.shape[1]
    if len(refs) == 3:
        value = refs[0][...]
        away_ref[:, at:] = jnp.where(core == 0, 0.0, value)
        keep_ref[:, at:] = jnp.where(core == 0, value, 0.0)


def twin_product(order, a, b, c, d, small=None):
    count, flat = a.shape
    tile = count // 2
    columns = count + (0 if small is None else small.shape[1])
    rows = spec((tile, flat), lambda i, s: (i, 0))
    ins, args = [], []
    for left, (right, group) in ((a, b), (c, d)):
        ins += [rows, spec((1, count, flat), lambda i, s, g=group: (g, 0, 0))]
        args += [left, right]
    if small is not None:
        ins.append(spec((tile, small.shape[1]), lambda i, s: (i, 0)))
        args.append(small)
    out = (spec((tile, columns), lambda i, s: (i, 0)), ((count, columns), f32))
    return order.call(twin_kernel, (2,), ins, [out, out], [], args)


def route_kernel(s_ref, *refs):
    for i in range(4):
        refs[8 + i][...] = refs[2 * i][...] + refs[2 * i + 1][...]


def route(order, left, right, low_bit, high_bit):
    (a, b), (c, d) = left, right
    shards, rows, columns = a.shape
    same = a is c
    if same:
        rows //= 2
    lower = 1 if same else 0
    half = shards // 2

    def by_low(flip):
        def index(i, s):
            mine = (s[PLACE] >> low_bit) & 1
            return 2 * i + ((1 - mine) if flip else mine), 0, 0

        return index

    def by_high(flip):
        def index(i, s):
            mine = (s[PLACE] >> high_bit) & 1
            return i + ((1 - mine) if flip else mine) * half, lower, 0

        return index

    block = (1, rows, columns)
    maps = [by_low(True), by_low(False), by_high(True), by_high(False)]
    ins = [spec(block, m) for m in maps for _ in range(2)]
    out = (spec(block, lambda i, s: (i, 0, 0)), ((half, rows, columns), f32))
    return order.call(route_kernel, (half,), ins, [out] * 4, [], (a, b, a, b, c, d, c, d))


def choose_kernel(s_ref, a_ref, b_ref, c_ref, d_ref, away_ref, kept_ref):
    upper, lower = a_ref[0] + b_ref[0], c_ref[0] + d_ref[0]
    odd = s_ref[ODD] == 1
    away_ref[...] = jnp.where(odd, upper, lower)
    kept_ref[...] = jnp.where(odd, lower, upper)


def choose(order, left, right):
    shape = left[0].shape[1:]
    return order.call(
        choose_kernel,
        (1,),
        [NEAR] * 4,
        [(NEAR, (shape, f32))] * 2,
        [],
        (*left, *right),
        free=range(4),
        near_out=range(2),
        limit=SMALL_LIMIT,
    )


def add_kernel(s_ref, a_ref, b_ref, out_ref):
    out_ref[...] = a_ref[...] + b_ref[...]


def add(order, a, b):
    outs = [(NEAR, (a.shape, f32))]
    return order.call(
        add_kernel, (1,), [NEAR] * 2, outs, [], (a, b), near=range(2), near_out=range(1), limit=SMALL_LIMIT
    )[0]


def merge_kernel(s_ref, kept_ref, got_ref, out_ref):
    odd = s_ref[ODD] == 1
    rows = kept_ref.shape[0]
    kept, got = kept_ref[...], got_ref[...]
    out_ref[:rows, :] = jnp.where(odd, got, kept)
    out_ref[rows:, :] = jnp.where(odd, kept, got)


def merge(order, kept, got):
    rows, columns = kept.shape
    outs = [(NEAR, ((2 * rows, columns), f32))]
    return order.call(
        merge_kernel,
        (1,),
        [NEAR] * 2,
        outs,
        [],
        (kept, got),
        near=range(2),
        near_out=range(1),
        limit=SMALL_LIMIT,
    )[0]


def side_kernel(s_ref, mine_ref, other_ref, *outs):
    first = s_ref[CORE] == 0
    at = 0
    for out in outs:
        cut = out.shape[1] // 2
        if cut < 128:
            out[...] = jnp.where(first, mine_ref[:, at:], other_ref[:, at:])
            break
        mine, other = mine_ref[:, at : at + cut], other_ref[:, at : at + cut]
        out[:, :cut] = jnp.where(first, mine, other)
        out[:, cut:] = jnp.where(first, other, mine)
        at += cut


def side(order, mine, other, widths):
    rows = mine.shape[0]
    outs = [(spec((rows, w), lambda i, s: (0, 0)), ((rows, w), f32)) for w in widths]
    return order.call(
        side_kernel, (1,), [NEAR] * 2, outs, [], (mine, other), near=range(2), limit=SMALL_LIMIT
    )


def mix_kernel(first, s_ref, w_ref, *refs):
    row = pl.program_id(0)
    for i in range(2):
        own, other = (w_ref[first + 2 * i + j, row] for j in range(2))
        refs[4 + i][...] = own * refs[2 * i][...] + other * refs[2 * i + 1][...]


def mix(order, weights, first, *parts):
    shape = parts[0].shape
    block = spec((1,) + shape[1:], lambda r, *s: (r, 0, 0))
    return order.call(
        partial(mix_kernel, first),
        (shape[0],),
        [block] * 4,
        [(block, (shape, f32))] * 2,
        [],
        parts,
        (weights,),
        free=range(4),
        limit=SMALL_LIMIT,
    )


def first_begins(lengths, count, tok_count):
    slots = lengths.shape[1]
    order = jnp.arange(slots)
    before = (order[:, None] > order[None, :]).astype(jnp.int32)
    starts = jnp.sum(lengths[:, None, :] * before[None], axis=-1)
    firsts = jnp.arange(count, dtype=jnp.int32) * tok_count
    reached = starts[:, None, :] <= firsts[None, :, None]
    return jnp.max(jnp.where(reached, starts[:, None, :], 0), axis=-1)


def pick(index, values):
    out = values[0]
    for i in range(1, len(values)):
        out = jnp.where(index == i, values[i], out)
    return out


def weights_of(begin_first, tok_count, reverse):
    count = lax.axis_size("seq")
    place = lax.axis_index("seq")

    def covers(i, j):
        low, high = (count - 1 - j, count - 1 - i) if reverse else (i, j)
        return (begin_first[:, high] < (low + 1) * tok_count).astype(f32)

    if count != 4:
        spots = jnp.arange(count)
        mine = begin_first.T if reverse else begin_first[:, place][None]
        reach = (place if reverse else spots[:, None]) + 1
        ahead = (spots > place) if reverse else (spots < place)
        return ((mine < reach * tok_count) & ahead[:, None]).astype(f32)
    index = count - 1 - place if reverse else place
    zero = jnp.zeros_like(begin_first[:, 0], f32)
    one = zero + 1.0
    m02, m03, m13 = covers(0, 2), covers(0, 3), covers(1, 3)
    onward = [
        pick(index, [m02, m13, zero, zero]),
        pick(index, [one, m03, zero, zero]),
        pick(index, [one, zero, one, zero]),
        pick(index, [zero, zero, m03, one]),
    ]
    final = [
        pick(index, [zero, one, zero, one]),
        pick(index, [zero, zero, one, one]),
        pick(index, [zero, zero, m02, m13]),
        pick(index, [zero, one, one, one]),
    ]
    return onward + final


def entering(order, parts, weights, first):
    if lax.axis_size("seq") != 4:
        gathered = [lax.all_gather(p, "seq") for p in parts]
        yield
        yield
        yield tuple(jnp.sum(g * weights[first][:, :, None, None], axis=0) for g in gathered)
    part_a, part_b = parts
    got_a, got_b = swap(part_a, "seq", 1), swap(part_b, "seq", 2)
    yield
    next_a, next_b = mix(order, weights, first, part_a, got_a, part_b, got_b)
    last_a, last_b = swap(next_a, "seq", 2), swap(next_b, "seq", 1)
    yield
    yield mix(order, weights, first + 4, got_a, last_a, got_b, last_b)


def swap(value, axis, distance):
    count = lax.axis_size(axis)
    return lax.ppermute(value, axis, [(i, i ^ distance) for i in range(count)])


def reduced(order, away, keep, widths):
    count = lax.axis_size("batch")
    shards = lax.axis_size("seq")
    bits = shards.bit_length() - 1
    shape = (shards, keep.shape[0] // shards, keep.shape[1])
    got = swap(away, "batch", 1).reshape(shape)
    yield
    left = right = (keep.reshape(shape), got)
    for step in range(bits):
        high = bits - 1 - step
        away_l, keep_l, away_r, keep_r = route(order, left, right, step, high)
        left = keep_l, swap(away_l, "seq", 1 << step)
        right = keep_r, swap(away_r, "seq", 1 << high)
        yield
    away, kept = choose(order, left, right)
    got = swap(away, "batch", 2)
    distance = 4
    while distance < count:
        yield
        kept = add(order, kept, got)
        got = swap(kept, "batch", distance)
        distance *= 2
    yield
    kept = add(order, kept, got)
    got = swap(kept, "batch", 2)
    yield
    merged = merge(order, kept, got)
    other = swap(merged, "batch", 1)
    yield
    yield side(order, merged, other, widths)


SCHEDULE = (
    "in_product", "states", "back_product", "in", "states", "back",
    "local", "mixed_product", "tail", "in", "back", "in",
    "mixed", "back", "mixed", "back", "last_product", "mixed",
    "last", "in", "back", "last", "mixed", "last",
    "in", "back", "last", "tokens", "mixed", "back",
    "last", "in", "mixed", "last", "in", "mixed",
    "last",
)


def body(
    tokens,
    cotangent,
    doc_lengths,
    w_query,
    w_key,
    w_value,
    w_out,
    w_in,
    w_back,
    gain_one,
    shift_one,
    gain_two,
    shift_two,
):
    rows, toks, width = tokens.shape
    ff = w_in.shape[1]
    flat = rows * toks
    shards = lax.axis_size("seq")
    whole = pl.BlockSpec(memory_space=pltpu.VMEM)
    token_major = pl.BlockSpec((1, toks, width), lambda r, *s: (r, 0, 0))
    table_spec = pl.BlockSpec((1, 8, toks), lambda r, *s: (r, 0, 0))
    state_spec = pl.BlockSpec((1, STATE_ROWS, 2 * HEAD_DIM), lambda r, *s: (r, 0, 0))

    def feature(count):
        return pl.BlockSpec((count, toks), lambda r, *s: (0, r))

    tok_low = (token_major, ((rows, toks, width), bf16))
    wide_low = (feature(width), ((width, flat), bf16))
    wide_full = (feature(width), ((width, flat), f32))
    ff_low = (feature(ff), ((ff, flat), bf16))
    head_rows = (feature(16), ((16, flat), f32))
    fold = (pl.BlockSpec((width, 128), lambda r, *s: (0, 0)), ((width, 128), f32))
    state = (state_spec, ((rows, STATE_ROWS, 2 * HEAD_DIM), f32))
    grid = (rows,)

    batch_place = lax.axis_index("batch").astype(jnp.int32)
    scalars = jnp.stack(
        [batch_place & 1, (batch_place >> 1) & 1, lax.axis_index("seq").astype(jnp.int32)]
    )
    order = Order(scalars)

    def run(kernel, ins, outs, scratch, *args, **more):
        return order.call(kernel, grid, ins, outs, scratch, args, **more)

    def column(v):
        return v[:, None]

    table, tok_t, k_t, v_t, key, value, sig_k, state_a, state_b = run(
        project_kernel,
        [token_major, whole, whole],
        [(table_spec, ((rows, 8, toks), f32))]
        + [wide_low] * 3
        + [tok_low] * 2
        + [wide_low]
        + [state] * 2,
        [pltpu.VMEM((2, width, width), bf16)],
        tokens,
        w_key,
        w_value,
        extra=(doc_lengths,),
    )
    begins = first_begins(doc_lengths, shards, toks)
    if shards == 4:
        weights = jnp.stack(weights_of(begins, toks, False) + weights_of(begins, toks, True))
        later = 8
    else:
        weights = [weights_of(begins, toks, False), weights_of(begins, toks, True)]
        later = 1
    states = entering(order, (state_a, state_b), weights, 0)
    next(states)
    part = ff // rows
    q_t, sig_q, numer, denom_loc, w_out_t, w_in_t, w_back_t = run(
        local_kernel,
        [
            table_spec,
            feature(width),
            token_major,
            feature(width),
            whole,
            whole,
            pl.BlockSpec((width, part), lambda r, *s: (0, r)),
            pl.BlockSpec((part, width), lambda r, *s: (r, 0)),
        ],
        [
            wide_low,
            wide_low,
            wide_full,
            head_rows,
            (pl.BlockSpec((width, width), lambda r, *s: (0, 0)), ((width, width), bf16)),
            (pl.BlockSpec((part, width), lambda r, *s: (r, 0)), ((ff, width), bf16)),
            (pl.BlockSpec((width, part), lambda r, *s: (0, r)), ((width, ff), bf16)),
        ],
        [pltpu.VMEM((width, width), bf16)],
        table,
        tok_t,
        key,
        v_t,
        w_query,
        w_out,
        w_in,
        w_back,
    )
    next(states)
    in_a, in_b = next(states)
    (
        layer_out,
        att_t,
        first_t,
        active_t,
        grad_second,
        grad_hidden,
        grad_base,
        grad_branch,
        grad_numer,
        grad_denom,
        small,
        out_a,
        out_b,
    ) = run(
        layer_kernel,
        [
            table_spec,
            feature(width),
            feature(width),
            feature(16),
            state_spec,
            state_spec,
            feature(width),
            token_major,
        ]
        + [whole] * 10,
        [
            tok_low,
            wide_low,
            wide_low,
            ff_low,
            wide_low,
            ff_low,
            wide_full,
            wide_low,
            wide_low,
            head_rows,
            fold,
            state,
            state,
        ],
        [
            pltpu.VMEM((ff, toks), bf16),
            pltpu.VMEM((width, toks), f32),
            pltpu.VMEM((width, toks), f32),
            pltpu.VMEM((16, toks), f32),
            pltpu.VMEM((width, toks), f32),
        ]
        + [pltpu.VMEM((width, 128), f32)] * 4,
        table,
        q_t,
        numer,
        denom_loc,
        in_a,
        in_b,
        tok_t,
        cotangent,
        w_out_t,
        w_in_t,
        w_back_t,
        w_out,
        w_in,
        w_back,
        column(gain_one),
        column(shift_one),
        column(gain_two),
        column(shift_two),
        near=range(8, 14),
        limit=LAYER_LIMIT,
    )

    back_states = entering(order, (out_a, out_b), weights, later)
    next(back_states)
    pieces, made = {}, {}

    def begin(name, product, widths):
        pieces[name] = reduced(order, *product, widths)
        next(pieces[name])

    def local_back():
        made["query"], made["key"], made["value"] = run(
            local_back_kernel,
            [
                table_spec,
                feature(width),
                feature(width),
                token_major,
                token_major,
                feature(width),
                feature(width),
                feature(16),
                state_spec,
                state_spec,
            ],
            [wide_low, wide_full, wide_full],
            [],
            table,
            q_t,
            k_t,
            key,
            value,
            sig_q,
            grad_numer,
            grad_denom,
            in_a,
            in_b,
        )

    def tail():
        back_a, back_b = made["states"]
        (made["kv"],) = run(
            tail_kernel,
            [table_spec]
            + [feature(width)] * 3
            + [state_spec] * 2
            + [feature(width)] * 2,
            [(pl.BlockSpec((2, width, toks), lambda r, *s: (0, 0, r)), ((2, width, flat), bf16))],
            [],
            table,
            k_t,
            v_t,
            sig_k,
            back_a,
            back_b,
            made["key"],
            made["value"],
        )

    def token_grads():
        (made["tokens"],) = run(
            token_kernel,
            [
                feature(width),
                pl.BlockSpec((2, width, toks), lambda r, *s: (0, 0, r)),
                feature(width),
            ]
            + [whole] * 3,
            [(token_major, ((rows, toks, width), f32))],
            [],
            made["query"],
            made["kv"],
            grad_base,
            w_query,
            w_key,
            w_value,
        )

    def states_on():
        made["states"] = next(back_states)

    steps = {
        "back_product": lambda: begin("back", tall_product(order, active_t, grad_second), (width,)),
        "in_product": lambda: begin("in", wide_product(order, first_t, grad_hidden), (ff,)),
        "mixed_product": lambda: begin(
            "mixed",
            twin_product(order, att_t, (grad_branch[None], 0), tok_t, (made["query"][None], 0), small),
            (width, width, 128),
        ),
        "last_product": lambda: begin(
            "last",
            twin_product(order, tok_t, (made["kv"], 0), tok_t, (made["kv"], 1)),
            (width, width),
        ),
        "states": states_on,
        "local": local_back,
        "tail": tail,
        "tokens": token_grads,
    }
    ends = {}

    def step(name):
        value = next(pieces[name])
        if value is not None:
            ends[name] = value

    for name in SCHEDULE:
        if name in steps:
            steps[name]()
        elif name not in ends:
            step(name)
    while len(ends) < len(pieces):
        for name in pieces:
            if name not in ends:
                step(name)
    (total_back,), (total_in,) = ends["back"], ends["in"]
    total_out, total_query, vectors = ends["mixed"]
    total_key, total_value = ends["last"]
    grad_tokens = made["tokens"]
    return (
        layer_out,
        grad_tokens,
        total_query,
        total_key,
        total_value,
        total_out,
        total_in,
        total_back,
        vectors[:, 0],
        vectors[:, 1],
        vectors[:, 2],
        vectors[:, 3],
    )


def solution(mesh):
    in_specs = (
        P("batch", "seq", None),
        P("batch", "seq", None),
        P("batch", None),
        P(),
        P(),
        P(),
        P(),
        P(),
        P(),
        P(),
        P(),
        P(),
        P(),
    )
    out_specs = (
        P("batch", "seq", None),
        P("batch", "seq", None),
        P("seq", None),
        P("seq", None),
        P("seq", None),
        P("seq", None),
        P("seq", None),
        P("seq", None),
        P("seq"),
        P("seq"),
        P("seq"),
        P("seq"),
    )
    return jax.shard_map(body, mesh=mesh, in_specs=in_specs, out_specs=out_specs, check_vma=False)
```

```python
from functools import partial

import jax
import jax.numpy as jnp
from jax import lax
from jax.experimental import pallas as pl
from jax.experimental.pallas import tpu as pltpu
from jax.sharding import PartitionSpec as P

HEADS = 12
HEAD_DIM = 64
PAIRS = HEADS // 2
HALF_HEADS = HEADS // 2
STATE_ROWS = HALF_HEADS * HEAD_DIM + 8

f32 = jnp.float32
bf16 = jnp.bfloat16
half_pi = 1.5707963267948966
norm_eps = 1e-05
VMEM_LIMIT = 30 * 1024 * 1024
SMALL_LIMIT = 16 * 1024 * 1024
LAYER_LIMIT = 38 * 1024 * 1024

NN = (((1,), (0,)), ((), ()))
NT = (((1,), (1,)), ((), ()))
TN = (((0,), (0,)), ((), ()))


def mm(a, b, dims=NN):
    return lax.dot_general(a, b, dims, preferred_element_type=f32)


COS, SIN, BEGIN, COS_READ, SIN_READ, COS_TAIL, SIN_TAIL = range(7)


def make_table(place, lens_ref, row, tok_count):
    pos = place + lax.broadcasted_iota(jnp.int32, (8, tok_count), 1)
    last = place + tok_count - 1
    start = jnp.int32(0)
    begin = jnp.zeros((8, tok_count), jnp.int32)
    span = jnp.ones((8, tok_count), jnp.int32)
    last_begin = jnp.int32(0)
    for d in range(lens_ref.shape[1]):
        length = lens_ref[row, d]
        inside = pos >= start
        begin = jnp.where(inside, start, begin)
        span = jnp.where(inside, length, span)
        last_begin = jnp.where(start <= last, start, last_begin)
        start = start + length
    angle = half_pi * (pos - begin).astype(f32) / span.astype(f32)
    cos, sin = jnp.cos(angle), jnp.sin(angle)
    reader = (begin < place).astype(f32)
    tail = (begin == last_begin).astype(f32)
    which = lax.broadcasted_iota(jnp.int32, (8, tok_count), 0)
    table = jnp.zeros((8, tok_count), f32)
    for index, value in (
        (COS, cos),
        (SIN, sin),
        (BEGIN, begin.astype(f32)),
        (COS_READ, cos * reader),
        (SIN_READ, sin * reader),
        (COS_TAIL, cos * tail),
        (SIN_TAIL, sin * tail),
    ):
        table = jnp.where(which == index, value, table)
    return table


def blend_of(table):
    columns = table.T
    tok_count = table.shape[1]
    source = lax.broadcasted_iota(jnp.int32, (tok_count, tok_count), 0)
    reader = lax.broadcasted_iota(jnp.int32, (tok_count, tok_count), 1)
    same = (columns[:, BEGIN : BEGIN + 1] == table[BEGIN : BEGIN + 1]) & (source <= reader)
    value = (
        columns[:, COS : COS + 1] * table[COS : COS + 1]
        + columns[:, SIN : SIN + 1] * table[SIN : SIN + 1]
    )
    return jnp.where(same, value, 0.0)


def trig_rows(head_rows, cos, sin):
    wide = head_rows.astype(f32)
    return jnp.concatenate([(wide * cos).astype(bf16), (wide * sin).astype(bf16)], axis=0)


def with_row(rows, extra):
    which = lax.broadcasted_iota(jnp.int32, (16, rows.shape[1]), 0)
    return jnp.concatenate([rows, jnp.where(which == 0, extra, 0.0).astype(bf16)], axis=0)


def head_slice(h):
    return slice(h * HEAD_DIM, (h + 1) * HEAD_DIM)


def put_state(state_refs, h, value):
    ref = state_refs[h // HALF_HEADS]
    place = h % HALF_HEADS
    ref[0, head_slice(place), :] = value[:HEAD_DIM]
    ref[0, HALF_HEADS * HEAD_DIM + place : HALF_HEADS * HEAD_DIM + place + 1, :] = value[
        HEAD_DIM : HEAD_DIM + 1
    ]


def take_state(state_refs, h):
    ref = state_refs[h // HALF_HEADS]
    place = h % HALF_HEADS
    mats = ref[0, head_slice(place), :].astype(bf16)
    sums = ref[0, HALF_HEADS * HEAD_DIM + place : HALF_HEADS * HEAD_DIM + place + 1, :]
    return with_row(mats, sums)


def clear_pad(state_refs):
    for ref in state_refs:
        ref[0, HALF_HEADS * HEAD_DIM :, :] = jnp.zeros((8, 2 * HEAD_DIM), f32)


def softplus_sigmoid(v):
    small = jnp.exp(-jnp.abs(v))
    soft = jnp.maximum(v, 0.0) + jnp.log1p(small)
    inverse = 1.0 / (1.0 + small)
    return soft, jnp.where(v >= 0, inverse, small * inverse)


def project_kernel(
    s_ref,
    lens_ref,
    tok_ref,
    wk_ref,
    wv_ref,
    tab_ref,
    tok_t_ref,
    k_t_ref,
    v_t_ref,
    k_ref,
    v_ref,
    sig_k_ref,
    state_a,
    state_b,
    w_t,
):
    row = pl.program_id(0)

    @pl.when(row == 0)
    def _():
        w_t[0] = wk_ref[...].T
        w_t[1] = wv_ref[...].T

    tok_t = tok_ref[0].T
    tok_t_ref[...] = tok_t
    table = make_table(s_ref[PLACE] * tok_t.shape[1], lens_ref, row, tok_t.shape[1])
    tab_ref[0] = table
    soft, sig = softplus_sigmoid(mm(w_t[0], tok_t))
    key_t = soft.astype(bf16)
    k_t_ref[...] = key_t
    k_ref[0] = key_t.T
    sig_k_ref[...] = sig.astype(bf16)
    value_t = mm(w_t[1], tok_t).astype(bf16)
    v_t_ref[...] = value_t
    v_ref[0] = value_t.T
    states = (state_a, state_b)
    clear_pad(states)
    cos, sin = table[COS_TAIL : COS_TAIL + 1], table[SIN_TAIL : SIN_TAIL + 1]
    for h in range(HEADS):
        keys = trig_rows(k_t_ref[head_slice(h), :], cos, sin)
        values = with_row(v_t_ref[head_slice(h), :], 1.0)
        put_state(states, h, mm(values, keys, NT))


def pair_rows(ref, pair):
    first = ref[head_slice(2 * pair), :]
    second = ref[head_slice(2 * pair + 1), :]
    nothing = jnp.zeros_like(first)
    return jnp.concatenate(
        [
            jnp.concatenate([first, nothing], axis=1),
            jnp.concatenate([nothing, second], axis=1),
        ],
        axis=0,
    )


def two_parts(v):
    high = v.astype(bf16)
    return high, (v - high.astype(f32)).astype(bf16)


def local_kernel(
    s_ref,
    tab_ref,
    tok_t_ref,
    k_ref,
    v_t_ref,
    wq_ref,
    w_out_ref,
    w_in_ref,
    w_back_ref,
    q_t_ref,
    sig_q_ref,
    numer_ref,
    denom_ref,
    w_out_t,
    w_in_t,
    w_back_t,
    w_t,
):
    @pl.when(pl.program_id(0) == 0)
    def _():
        w_t[...] = wq_ref[...].T
        w_out_t[...] = w_out_ref[...].T

    w_in_t[...] = w_in_ref[...].T
    w_back_t[...] = w_back_ref[...].T

    soft, sig = softplus_sigmoid(mm(w_t[...], tok_t_ref[...]))
    q_t_ref[...] = soft.astype(bf16)
    sig_q_ref[...] = sig.astype(bf16)
    blend = blend_of(tab_ref[0])
    tok_count = blend.shape[0]
    denom_ref[...] = jnp.zeros_like(denom_ref)
    for pair in range(PAIRS):
        lanes = slice(pair * 2 * HEAD_DIM, (pair + 1) * 2 * HEAD_DIM)
        both = mm(k_ref[0, :, lanes], pair_rows(q_t_ref, pair))
        for side in range(2):
            h = 2 * pair + side
            high, low = two_parts(both[:, side * tok_count : (side + 1) * tok_count] * blend)
            values = with_row(v_t_ref[head_slice(h), :], 1.0)
            out = mm(values, high) + mm(values, low)
            numer_ref[head_slice(h), :] = out[:HEAD_DIM]
            denom_ref[h : h + 1, :] = out[HEAD_DIM : HEAD_DIM + 1]


def mean_rows(v):
    return jnp.sum(v, axis=0, keepdims=True) * (1.0 / v.shape[0])


def fold_lanes(v):
    total = v[:, :128]
    for at in range(128, v.shape[1], 128):
        total = total + v[:, at : at + 128]
    return total


def add_to(ref, value):
    first = pl.program_id(0) == 0

    @pl.when(first)
    def _():
        ref[...] = value

    @pl.when(jnp.logical_not(first))
    def _():
        ref[...] += value


def norm_back(grad_norm, normed, inv_scale):
    return inv_scale * (grad_norm - mean_rows(grad_norm) - normed * mean_rows(grad_norm * normed))


def lane_total(ref):
    return jnp.sum(ref[...], axis=1, keepdims=True)


def layer_kernel(
    s_ref,
    tab_ref,
    q_t_ref,
    numer_ref,
    denom_loc_ref,
    state_a,
    state_b,
    tok_t_ref,
    cot_ref,
    w_out_t,
    w_in_t,
    w_back_t,
    w_out_ref,
    w_in_ref,
    w_back_ref,
    gain_one_ref,
    shift_one_ref,
    gain_two_ref,
    shift_two_ref,
    layer_ref,
    att_t_ref,
    first_t_ref,
    active_t_ref,
    grad_second_ref,
    grad_hidden_ref,
    grad_base_ref,
    grad_branch_ref,
    grad_numer_ref,
    grad_denom_ref,
    small_ref,
    out_a,
    out_b,
    slope,
    normed_one,
    attended,
    inverse_denom,
    total,
    fold_gain_one,
    fold_shift_one,
    fold_gain_two,
    fold_shift_two,
):
    ff = w_in_ref.shape[1]
    step = 768
    table = tab_ref[0]
    cos, sin = table[COS_READ : COS_READ + 1], table[SIN_READ : SIN_READ + 1]
    states = (state_a, state_b)
    for h in range(HEADS):
        reads = trig_rows(q_t_ref[head_slice(h), :], cos, sin)
        more = mm(take_state(states, h), reads)
        numer = numer_ref[head_slice(h), :] + more[:HEAD_DIM]
        inverse = 1.0 / (denom_loc_ref[h : h + 1, :] + more[HEAD_DIM : HEAD_DIM + 1])
        inverse_denom[h : h + 1, :] = inverse
        value = numer * inverse
        attended[head_slice(h), :] = value
        att_t_ref[head_slice(h), :] = value.astype(bf16)
    summed = tok_t_ref[...].astype(f32) + mm(w_out_t[...], att_t_ref[...])
    centered = summed - mean_rows(summed)
    scale_one = lax.rsqrt(mean_rows(centered * centered) + norm_eps)
    normed = centered * scale_one
    normed_one[...] = normed
    first_out = normed * gain_one_ref[...] + shift_one_ref[...]
    total[...] = first_out
    first_low = first_out.astype(bf16)
    first_t_ref[...] = first_low
    for at in range(0, ff, step):
        hidden = mm(w_in_t[at : at + step, :], first_low)
        half = 0.5 * (1.0 + lax.erf(hidden * 0.7071067811865476))
        bell = jnp.exp(hidden * hidden * -0.5) * 0.3989422804014327
        active = (hidden * half).astype(bf16)
        active_t_ref[at : at + step, :] = active
        slope[at : at + step, :] = (half + hidden * bell).astype(bf16)
        total[...] += mm(w_back_t[:, at : at + step], active)
    summed = total[...]
    centered = summed - mean_rows(summed)
    scale_two = lax.rsqrt(mean_rows(centered * centered) + norm_eps)
    normed = centered * scale_two
    layer_ref[0] = (normed * gain_two_ref[...] + shift_two_ref[...]).T.astype(bf16)
    grad_top = cot_ref[0].T.astype(f32)
    add_to(fold_gain_two, fold_lanes(grad_top * normed))
    add_to(fold_shift_two, fold_lanes(grad_top))
    grad_mid = norm_back(grad_top * gain_two_ref[...], normed, scale_two)
    total[...] = grad_mid
    grad_second = grad_mid.astype(bf16)
    grad_second_ref[...] = grad_second
    for at in range(0, ff, step):
        grad_active = mm(w_back_ref[at : at + step, :], grad_second)
        low = (grad_active * slope[at : at + step, :].astype(f32)).astype(bf16)
        grad_hidden_ref[at : at + step, :] = low
        total[...] += mm(w_in_ref[:, at : at + step], low)
    grad_first = total[...]
    normed = normed_one[...]
    add_to(fold_gain_one, fold_lanes(grad_first * normed))
    add_to(fold_shift_one, fold_lanes(grad_first))
    grad_base = norm_back(grad_first * gain_one_ref[...], normed, scale_one)
    grad_base_ref[...] = grad_base
    grad_branch = grad_base.astype(bf16)
    grad_branch_ref[...] = grad_branch
    total[...] = mm(w_out_ref[...], grad_branch)
    outs = (out_a, out_b)
    clear_pad(outs)
    grad_denom_ref[...] = jnp.zeros_like(grad_denom_ref)
    for h in range(HEADS):
        rows = head_slice(h)
        grad_numer = (total[rows, :] * inverse_denom[h : h + 1, :]).astype(bf16)
        grad_denom = -jnp.sum(grad_numer.astype(f32) * attended[rows, :], axis=0, keepdims=True)
        grad_denom_ref[h : h + 1, :] = grad_denom
        grad_numer_ref[rows, :] = grad_numer
        reads = trig_rows(q_t_ref[rows, :], cos, sin)
        put_state(outs, h, mm(with_row(grad_numer, grad_denom), reads, NT))

    @pl.when(pl.program_id(0) == pl.num_programs(0) - 1)
    def _():
        lane = lax.broadcasted_iota(jnp.int32, small_ref.shape, 1)
        value = jnp.zeros(small_ref.shape, f32)
        for i, ref in enumerate((fold_gain_one, fold_shift_one, fold_gain_two, fold_shift_two)):
            value = jnp.where(lane == i, lane_total(ref), value)
        small_ref[...] = value


def local_back_kernel(
    s_ref,
    tab_ref,
    q_t_ref,
    k_t_ref,
    k_ref,
    v_ref,
    sig_q_ref,
    grad_numer_ref,
    grad_denom_ref,
    state_a,
    state_b,
    grad_q_ref,
    grad_k_ref,
    grad_v_ref,
):
    table = tab_ref[0]
    blend = blend_of(table)
    tok_count = blend.shape[0]
    cos, sin = table[COS_READ : COS_READ + 1], table[SIN_READ : SIN_READ + 1]
    states = (state_a, state_b)
    for pair in range(PAIRS):
        lanes = slice(pair * 2 * HEAD_DIM, (pair + 1) * 2 * HEAD_DIM)
        both = mm(k_ref[0, :, lanes], pair_rows(q_t_ref, pair))
        grads = mm(v_ref[0, :, lanes], pair_rows(grad_numer_ref, pair))
        for side in range(2):
            h = 2 * pair + side
            rows = head_slice(h)
            part = slice(side * tok_count, (side + 1) * tok_count)
            grad_denom = grad_denom_ref[h : h + 1, :]
            scores = (both[:, part] * blend).astype(bf16)
            grad_scores, rest = two_parts((grads[:, part] + grad_denom) * blend)
            grad_numer = grad_numer_ref[rows, :]
            grad_v_ref[rows, :] = mm(grad_numer, scores, NT)
            grad_k_ref[rows, :] = mm(q_t_ref[rows, :], grad_scores, NT)
            reads = mm(take_state(states, h), with_row(grad_numer, grad_denom), TN)
            grad_q = (
                mm(k_t_ref[rows, :], grad_scores)
                + mm(k_t_ref[rows, :], rest)
                + cos * reads[:HEAD_DIM]
                + sin * reads[HEAD_DIM:]
            )
            grad_q_ref[rows, :] = (grad_q * sig_q_ref[rows, :].astype(f32)).astype(bf16)


def tail_kernel(
    s_ref,
    tab_ref,
    k_t_ref,
    v_t_ref,
    sig_k_ref,
    state_a,
    state_b,
    grad_k_in,
    grad_v_in,
    grad_kv_ref,
):
    table = tab_ref[0]
    cos, sin = table[COS_TAIL : COS_TAIL + 1], table[SIN_TAIL : SIN_TAIL + 1]
    states = (state_a, state_b)
    for h in range(HEADS):
        rows = head_slice(h)
        state = take_state(states, h)
        inner = mm(state, with_row(v_t_ref[rows, :], 1.0), TN)
        grad_k = grad_k_in[rows, :] + cos * inner[:HEAD_DIM] + sin * inner[HEAD_DIM:]
        grad_kv_ref[0, rows, :] = (grad_k * sig_k_ref[rows, :].astype(f32)).astype(bf16)
        keys = trig_rows(k_t_ref[rows, :], cos, sin)
        grad_kv_ref[1, rows, :] = (grad_v_in[rows, :] + mm(state[:HEAD_DIM], keys)).astype(bf16)


def token_kernel(s_ref, gq_ref, gkv_ref, base_ref, wq_ref, wk_ref, wv_ref, out_ref):
    total = base_ref[...] + mm(wq_ref[...], gq_ref[...])
    total = total + mm(wk_ref[...], gkv_ref[0])
    total = total + mm(wv_ref[...], gkv_ref[1])
    out_ref[0] = total.T


def spec(block, index):
    return pl.BlockSpec(block, index)


NEAR = pl.BlockSpec(memory_space=pltpu.VMEM)

CORE, ODD, PLACE = range(3)


class Order:
    def __init__(self, scalars):
        self.scalars = scalars
        self.last = None

    def call(
        self, kernel, grid, ins, outs, scratch, args, extra=(), free=(), near=(), near_out=(), limit=VMEM_LIMIT
    ):
        count = 1 + len(extra)
        before = () if self.last is None else (pltpu.with_memory_space_constraint(*self.last),)
        at = count + len(ins)

        def stepped(*refs):
            kernel(*refs[:at], *refs[at + len(before) :])

        values = pl.pallas_call(
            stepped,
            grid_spec=pltpu.PrefetchScalarGridSpec(
                num_scalar_prefetch=count,
                grid=grid,
                in_specs=list(ins) + [pl.BlockSpec(memory_space=pl.ANY) for _ in before],
                out_specs=[o for o, _ in outs],
                scratch_shapes=scratch,
            ),
            out_shape=[
                (pltpu.VMEM if i in near_out else pltpu.HBM)(shape, kind)
                for i, (_, (shape, kind)) in enumerate(outs)
            ],
            compiler_params=pltpu.CompilerParams(
                dimension_semantics=("arbitrary",) * len(grid), vmem_limit_bytes=limit
            ),
            cost_estimate=pl.CostEstimate(flops=10**12, bytes_accessed=1, transcendentals=0),
        )(
            self.scalars,
            *extra,
            *[
                v
                if i in free
                else pltpu.with_memory_space_constraint(v, pltpu.VMEM if i in near else pltpu.HBM)
                for i, v in enumerate(args)
            ],
            *before,
        )
        at, value = min(reversed(list(enumerate(values))), key=lambda v: v[1].size * v[1].dtype.itemsize)
        self.last = value, pltpu.VMEM if at in near_out else pltpu.HBM
        return values


def pick_halves(core, value):
    cut = value.shape[1] // 2
    low, high = value[:, :cut], value[:, cut:]
    return jnp.where(core == 0, high, low), jnp.where(core == 0, low, high)


def tall_kernel(s_ref, a_ref, b_ref, away_ref, keep_ref):
    away_ref[...], keep_ref[...] = pick_halves(s_ref[CORE], mm(a_ref[...], b_ref[...], NT))


def tall_product(order, a, b):
    count, flat = a.shape
    tile, cut = count // 4, b.shape[0] // 2
    out = (spec((tile, cut), lambda i, *s: (i, 0)), ((count, cut), f32))
    ins = [spec((tile, flat), lambda i, *s: (i, 0)), spec(b.shape, lambda i, *s: (0, 0))]
    return order.call(tall_kernel, (4,), ins, [out, out], [], (a, b))


def wide_kernel(s_ref, a_ref, b_ref, away_ref, keep_ref):
    value = mm(a_ref[...], b_ref[...], NT)
    first = pl.program_id(0) < pl.num_programs(0) // 2

    @pl.when(first)
    def _():
        away_ref[...] = value

    @pl.when(jnp.logical_not(first))
    def _():
        keep_ref[...] = value


def wide_product(order, a, b):
    count, flat = a.shape
    cut = b.shape[0] // 2
    tile = 512
    half = cut // tile

    def source(i, s):
        return jnp.where(i < half, (1 - s[CORE]) * half + i, s[CORE] * half + i - half), 0

    outs = [
        (spec((count, tile), lambda i, s: (0, jnp.minimum(i, half - 1))), ((count, cut), f32)),
        (spec((count, tile), lambda i, s: (0, jnp.maximum(i - half, 0))), ((count, cut), f32)),
    ]
    ins = [spec(a.shape, lambda i, s: (0, 0)), spec((tile, flat), source)]
    return order.call(wide_kernel, (2 * half,), ins, outs, [], (a, b))


def twin_kernel(s_ref, a_ref, b_ref, c_ref, d_ref, *refs):
    core = s_ref[CORE]
    away_ref, keep_ref = refs[-2:]
    at = 0
    for left, right in ((a_ref, b_ref[0]), (c_ref, d_ref[0])):
        away, keep = pick_halves(core, mm(left[...], right, NT))
        away_ref[:, at : at + away.shape[1]] = away
        keep_ref[:, at : at + keep.shape[1]] = keep
        at += away.shape[1]
    if len(refs) == 3:
        value = refs[0][...]
        away_ref[:, at:] = jnp.where(core == 0, 0.0, value)
        keep_ref[:, at:] = jnp.where(core == 0, value, 0.0)


def twin_product(order, a, b, c, d, small=None):
    count, flat = a.shape
    tile = count // 2
    columns = count + (0 if small is None else small.shape[1])
    rows = spec((tile, flat), lambda i, s: (i, 0))
    ins, args = [], []
    for left, (right, group) in ((a, b), (c, d)):
        ins += [rows, spec((1, count, flat), lambda i, s, g=group: (g, 0, 0))]
        args += [left, right]
    if small is not None:
        ins.append(spec((tile, small.shape[1]), lambda i, s: (i, 0)))
        args.append(small)
    out = (spec((tile, columns), lambda i, s: (i, 0)), ((count, columns), f32))
    return order.call(twin_kernel, (2,), ins, [out, out], [], args)


def route_kernel(s_ref, *refs):
    for i in range(4):
        refs[8 + i][...] = refs[2 * i][...] + refs[2 * i + 1][...]


def route(order, left, right, low_bit, high_bit):
    (a, b), (c, d) = left, right
    shards, rows, columns = a.shape
    same = a is c
    if same:
        rows //= 2
    lower = 1 if same else 0
    half = shards // 2

    def by_low(flip):
        def index(i, s):
            mine = (s[PLACE] >> low_bit) & 1
            return 2 * i + ((1 - mine) if flip else mine), 0, 0

        return index

    def by_high(flip):
        def index(i, s):
            mine = (s[PLACE] >> high_bit) & 1
            return i + ((1 - mine) if flip else mine) * half, lower, 0

        return index

    block = (1, rows, columns)
    maps = [by_low(True), by_low(False), by_high(True), by_high(False)]
    ins = [spec(block, m) for m in maps for _ in range(2)]
    out = (spec(block, lambda i, s: (i, 0, 0)), ((half, rows, columns), f32))
    return order.call(route_kernel, (half,), ins, [out] * 4, [], (a, b, a, b, c, d, c, d))


def choose_kernel(s_ref, a_ref, b_ref, c_ref, d_ref, away_ref, kept_ref):
    upper, lower = a_ref[0] + b_ref[0], c_ref[0] + d_ref[0]
    odd = s_ref[ODD] == 1
    away_ref[...] = jnp.where(odd, upper, lower)
    kept_ref[...] = jnp.where(odd, lower, upper)


def choose(order, left, right):
    shape = left[0].shape[1:]
    return order.call(
        choose_kernel,
        (1,),
        [NEAR] * 4,
        [(NEAR, (shape, f32))] * 2,
        [],
        (*left, *right),
        free=range(4),
        near_out=range(2),
        limit=SMALL_LIMIT,
    )


def add_kernel(s_ref, a_ref, b_ref, out_ref):
    out_ref[...] = a_ref[...] + b_ref[...]


def add(order, a, b):
    outs = [(NEAR, (a.shape, f32))]
    return order.call(
        add_kernel, (1,), [NEAR] * 2, outs, [], (a, b), near=range(2), near_out=range(1), limit=SMALL_LIMIT
    )[0]


def merge_kernel(s_ref, kept_ref, got_ref, out_ref):
    odd = s_ref[ODD] == 1
    rows = kept_ref.shape[0]
    kept, got = kept_ref[...], got_ref[...]
    out_ref[:rows, :] = jnp.where(odd, got, kept)
    out_ref[rows:, :] = jnp.where(odd, kept, got)


def merge(order, kept, got):
    rows, columns = kept.shape
    outs = [(NEAR, ((2 * rows, columns), f32))]
    return order.call(
        merge_kernel,
        (1,),
        [NEAR] * 2,
        outs,
        [],
        (kept, got),
        near=range(2),
        near_out=range(1),
        limit=SMALL_LIMIT,
    )[0]


def side_kernel(s_ref, mine_ref, other_ref, *outs):
    first = s_ref[CORE] == 0
    at = 0
    for out in outs:
        cut = out.shape[1] // 2
        if cut < 128:
            out[...] = jnp.where(first, mine_ref[:, at:], other_ref[:, at:])
            break
        mine, other = mine_ref[:, at : at + cut], other_ref[:, at : at + cut]
        out[:, :cut] = jnp.where(first, mine, other)
        out[:, cut:] = jnp.where(first, other, mine)
        at += cut


def side(order, mine, other, widths):
    rows = mine.shape[0]
    outs = [(spec((rows, w), lambda i, s: (0, 0)), ((rows, w), f32)) for w in widths]
    return order.call(
        side_kernel, (1,), [NEAR] * 2, outs, [], (mine, other), near=range(2), limit=SMALL_LIMIT
    )


def mix_kernel(first, s_ref, w_ref, *refs):
    row = pl.program_id(0)
    for i in range(2):
        own, other = (w_ref[first + 2 * i + j, row] for j in range(2))
        refs[4 + i][...] = own * refs[2 * i][...] + other * refs[2 * i + 1][...]


def mix(order, weights, first, *parts):
    shape = parts[0].shape
    block = spec((1,) + shape[1:], lambda r, *s: (r, 0, 0))
    return order.call(
        partial(mix_kernel, first),
        (shape[0],),
        [block] * 4,
        [(block, (shape, f32))] * 2,
        [],
        parts,
        (weights,),
        free=range(4),
        limit=SMALL_LIMIT,
    )


def first_begins(lengths, count, tok_count):
    slots = lengths.shape[1]
    order = jnp.arange(slots)
    before = (order[:, None] > order[None, :]).astype(jnp.int32)
    starts = jnp.sum(lengths[:, None, :] * before[None], axis=-1)
    firsts = jnp.arange(count, dtype=jnp.int32) * tok_count
    reached = starts[:, None, :] <= firsts[None, :, None]
    return jnp.max(jnp.where(reached, starts[:, None, :], 0), axis=-1)


def pick(index, values):
    out = values[0]
    for i in range(1, len(values)):
        out = jnp.where(index == i, values[i], out)
    return out


def weights_of(begin_first, tok_count, reverse):
    count = lax.axis_size("seq")
    place = lax.axis_index("seq")

    def covers(i, j):
        low, high = (count - 1 - j, count - 1 - i) if reverse else (i, j)
        return (begin_first[:, high] < (low + 1) * tok_count).astype(f32)

    if count != 4:
        spots = jnp.arange(count)
        mine = begin_first.T if reverse else begin_first[:, place][None]
        reach = (place if reverse else spots[:, None]) + 1
        ahead = (spots > place) if reverse else (spots < place)
        return ((mine < reach * tok_count) & ahead[:, None]).astype(f32)
    index = count - 1 - place if reverse else place
    zero = jnp.zeros_like(begin_first[:, 0], f32)
    one = zero + 1.0
    m02, m03, m13 = covers(0, 2), covers(0, 3), covers(1, 3)
    onward = [
        pick(index, [m02, m13, zero, zero]),
        pick(index, [one, m03, zero, zero]),
        pick(index, [one, zero, one, zero]),
        pick(index, [zero, zero, m03, one]),
    ]
    final = [
        pick(index, [zero, one, zero, one]),
        pick(index, [zero, zero, one, one]),
        pick(index, [zero, zero, m02, m13]),
        pick(index, [zero, one, one, one]),
    ]
    return onward + final


def entering(order, parts, weights, first):
    if lax.axis_size("seq") != 4:
        gathered = [lax.all_gather(p, "seq") for p in parts]
        yield
        yield
        yield tuple(jnp.sum(g * weights[first][:, :, None, None], axis=0) for g in gathered)
    part_a, part_b = parts
    got_a, got_b = swap(part_a, "seq", 1), swap(part_b, "seq", 2)
    yield
    next_a, next_b = mix(order, weights, first, part_a, got_a, part_b, got_b)
    last_a, last_b = swap(next_a, "seq", 2), swap(next_b, "seq", 1)
    yield
    yield mix(order, weights, first + 4, got_a, last_a, got_b, last_b)


def swap(value, axis, distance):
    count = lax.axis_size(axis)
    return lax.ppermute(value, axis, [(i, i ^ distance) for i in range(count)])


def reduced(order, away, keep, widths):
    count = lax.axis_size("batch")
    shards = lax.axis_size("seq")
    bits = shards.bit_length() - 1
    shape = (shards, keep.shape[0] // shards, keep.shape[1])
    got = swap(away, "batch", 1).reshape(shape)
    yield
    left = right = (keep.reshape(shape), got)
    for step in range(bits):
        high = bits - 1 - step
        away_l, keep_l, away_r, keep_r = route(order, left, right, step, high)
        left = keep_l, swap(away_l, "seq", 1 << step)
        right = keep_r, swap(away_r, "seq", 1 << high)
        yield
    away, kept = choose(order, left, right)
    got = swap(away, "batch", 2)
    distance = 4
    while distance < count:
        yield
        kept = add(order, kept, got)
        got = swap(kept, "batch", distance)
        distance *= 2
    yield
    kept = add(order, kept, got)
    got = swap(kept, "batch", 2)
    yield
    merged = merge(order, kept, got)
    other = swap(merged, "batch", 1)
    yield
    yield side(order, merged, other, widths)


SCHEDULE = (
    "in_product", "states", "back_product", "in", "states", "back",
    "local", "mixed_product", "tail", "in", "back", "in",
    "mixed", "back", "mixed", "back", "last_product", "mixed",
    "last", "in", "back", "last", "mixed", "last",
    "in", "back", "last", "tokens", "mixed", "back",
    "last", "in", "mixed", "last", "in", "mixed",
    "last",
)


def body(
    tokens,
    cotangent,
    doc_lengths,
    w_query,
    w_key,
    w_value,
    w_out,
    w_in,
    w_back,
    gain_one,
    shift_one,
    gain_two,
    shift_two,
):
    rows, toks, width = tokens.shape
    ff = w_in.shape[1]
    flat = rows * toks
    shards = lax.axis_size("seq")
    whole = pl.BlockSpec(memory_space=pltpu.VMEM)
    token_major = pl.BlockSpec((1, toks, width), lambda r, *s: (r, 0, 0))
    table_spec = pl.BlockSpec((1, 8, toks), lambda r, *s: (r, 0, 0))
    state_spec = pl.BlockSpec((1, STATE_ROWS, 2 * HEAD_DIM), lambda r, *s: (r, 0, 0))

    def feature(count):
        return pl.BlockSpec((count, toks), lambda r, *s: (0, r))

    tok_low = (token_major, ((rows, toks, width), bf16))
    wide_low = (feature(width), ((width, flat), bf16))
    wide_full = (feature(width), ((width, flat), f32))
    ff_low = (feature(ff), ((ff, flat), bf16))
    head_rows = (feature(16), ((16, flat), f32))
    fold = (pl.BlockSpec((width, 128), lambda r, *s: (0, 0)), ((width, 128), f32))
    state = (state_spec, ((rows, STATE_ROWS, 2 * HEAD_DIM), f32))
    grid = (rows,)

    batch_place = lax.axis_index("batch").astype(jnp.int32)
    scalars = jnp.stack(
        [batch_place & 1, (batch_place >> 1) & 1, lax.axis_index("seq").astype(jnp.int32)]
    )
    order = Order(scalars)

    def run(kernel, ins, outs, scratch, *args, **more):
        return order.call(kernel, grid, ins, outs, scratch, args, **more)

    def column(v):
        return v[:, None]

    table, tok_t, k_t, v_t, key, value, sig_k, state_a, state_b = run(
        project_kernel,
        [token_major, whole, whole],
        [(table_spec, ((rows, 8, toks), f32))]
        + [wide_low] * 3
        + [tok_low] * 2
        + [wide_low]
        + [state] * 2,
        [pltpu.VMEM((2, width, width), bf16)],
        tokens,
        w_key,
        w_value,
        extra=(doc_lengths,),
    )
    begins = first_begins(doc_lengths, shards, toks)
    if shards == 4:
        weights = jnp.stack(weights_of(begins, toks, False) + weights_of(begins, toks, True))
        later = 8
    else:
        weights = [weights_of(begins, toks, False), weights_of(begins, toks, True)]
        later = 1
    states = entering(order, (state_a, state_b), weights, 0)
    next(states)
    part = ff // rows
    q_t, sig_q, numer, denom_loc, w_out_t, w_in_t, w_back_t = run(
        local_kernel,
        [
            table_spec,
            feature(width),
            token_major,
            feature(width),
            whole,
            whole,
            pl.BlockSpec((width, part), lambda r, *s: (0, r)),
            pl.BlockSpec((part, width), lambda r, *s: (r, 0)),
        ],
        [
            wide_low,
            wide_low,
            wide_full,
            head_rows,
            (pl.BlockSpec((width, width), lambda r, *s: (0, 0)), ((width, width), bf16)),
            (pl.BlockSpec((part, width), lambda r, *s: (r, 0)), ((ff, width), bf16)),
            (pl.BlockSpec((width, part), lambda r, *s: (0, r)), ((width, ff), bf16)),
        ],
        [pltpu.VMEM((width, width), bf16)],
        table,
        tok_t,
        key,
        v_t,
        w_query,
        w_out,
        w_in,
        w_back,
    )
    next(states)
    in_a, in_b = next(states)
    (
        layer_out,
        att_t,
        first_t,
        active_t,
        grad_second,
        grad_hidden,
        grad_base,
        grad_branch,
        grad_numer,
        grad_denom,
        small,
        out_a,
        out_b,
    ) = run(
        layer_kernel,
        [
            table_spec,
            feature(width),
            feature(width),
            feature(16),
            state_spec,
            state_spec,
            feature(width),
            token_major,
        ]
        + [whole] * 10,
        [
            tok_low,
            wide_low,
            wide_low,
            ff_low,
            wide_low,
            ff_low,
            wide_full,
            wide_low,
            wide_low,
            head_rows,
            fold,
            state,
            state,
        ],
        [
            pltpu.VMEM((ff, toks), bf16),
            pltpu.VMEM((width, toks), f32),
            pltpu.VMEM((width, toks), f32),
            pltpu.VMEM((16, toks), f32),
            pltpu.VMEM((width, toks), f32),
        ]
        + [pltpu.VMEM((width, 128), f32)] * 4,
        table,
        q_t,
        numer,
        denom_loc,
        in_a,
        in_b,
        tok_t,
        cotangent,
        w_out_t,
        w_in_t,
        w_back_t,
        w_out,
        w_in,
        w_back,
        column(gain_one),
        column(shift_one),
        column(gain_two),
        column(shift_two),
        near=range(8, 14),
        limit=LAYER_LIMIT,
    )

    back_states = entering(order, (out_a, out_b), weights, later)
    next(back_states)
    pieces, made = {}, {}

    def begin(name, product, widths):
        pieces[name] = reduced(order, *product, widths)
        next(pieces[name])

    def local_back():
        made["query"], made["key"], made["value"] = run(
            local_back_kernel,
            [
                table_spec,
                feature(width),
                feature(width),
                token_major,
                token_major,
                feature(width),
                feature(width),
                feature(16),
                state_spec,
                state_spec,
            ],
            [wide_low, wide_full, wide_full],
            [],
            table,
            q_t,
            k_t,
            key,
            value,
            sig_q,
            grad_numer,
            grad_denom,
            in_a,
            in_b,
        )

    def tail():
        back_a, back_b = made["states"]
        (made["kv"],) = run(
            tail_kernel,
            [table_spec]
            + [feature(width)] * 3
            + [state_spec] * 2
            + [feature(width)] * 2,
            [(pl.BlockSpec((2, width, toks), lambda r, *s: (0, 0, r)), ((2, width, flat), bf16))],
            [],
            table,
            k_t,
            v_t,
            sig_k,
            back_a,
            back_b,
            made["key"],
            made["value"],
        )

    def token_grads():
        (made["tokens"],) = run(
            token_kernel,
            [
                feature(width),
                pl.BlockSpec((2, width, toks), lambda r, *s: (0, 0, r)),
                feature(width),
            ]
            + [whole] * 3,
            [(token_major, ((rows, toks, width), f32))],
            [],
            made["query"],
            made["kv"],
            grad_base,
            w_query,
            w_key,
            w_value,
        )

    def states_on():
        made["states"] = next(back_states)

    steps = {
        "back_product": lambda: begin("back", tall_product(order, active_t, grad_second), (width,)),
        "in_product": lambda: begin("in", wide_product(order, first_t, grad_hidden), (ff,)),
        "mixed_product": lambda: begin(
            "mixed",
            twin_product(order, att_t, (grad_branch[None], 0), tok_t, (made["query"][None], 0), small),
            (width, width, 128),
        ),
        "last_product": lambda: begin(
            "last",
            twin_product(order, tok_t, (made["kv"], 0), tok_t, (made["kv"], 1)),
            (width, width),
        ),
        "states": states_on,
        "local": local_back,
        "tail": tail,
        "tokens": token_grads,
    }
    ends = {}

    def step(name):
        value = next(pieces[name])
        if value is not None:
            ends[name] = value

    for name in SCHEDULE:
        if name in steps:
            steps[name]()
        elif name not in ends:
            step(name)
    while len(ends) < len(pieces):
        for name in pieces:
            if name not in ends:
                step(name)
    (total_back,), (total_in,) = ends["back"], ends["in"]
    total_out, total_query, vectors = ends["mixed"]
    total_key, total_value = ends["last"]
    grad_tokens = made["tokens"]
    return (
        layer_out,
        grad_tokens,
        total_query,
        total_key,
        total_value,
        total_out,
        total_in,
        total_back,
        vectors[:, 0],
        vectors[:, 1],
        vectors[:, 2],
        vectors[:, 3],
    )


def solution(mesh):
    in_specs = (
        P("batch", "seq", None),
        P("batch", "seq", None),
        P("batch", None),
        P(),
        P(),
        P(),
        P(),
        P(),
        P(),
        P(),
        P(),
        P(),
        P(),
    )
    out_specs = (
        P("batch", "seq", None),
        P("batch", "seq", None),
        P("seq", None),
        P("seq", None),
        P("seq", None),
        P("seq", None),
        P("seq", None),
        P("seq", None),
        P("seq"),
        P("seq"),
        P("seq"),
        P("seq"),
    )
    return jax.shard_map(body, mesh=mesh, in_specs=in_specs, out_specs=out_specs, check_vma=False)
```

```python
from functools import partial

import jax
import jax.numpy as jnp
from jax import lax
from jax.experimental import pallas as pl
from jax.experimental.pallas import tpu as pltpu
from jax.sharding import PartitionSpec as P

HEADS = 12
HEAD_DIM = 64
PAIRS = HEADS // 2
HALF_HEADS = HEADS // 2
STATE_ROWS = HALF_HEADS * HEAD_DIM + 8

f32 = jnp.float32
bf16 = jnp.bfloat16
half_pi = 1.5707963267948966
norm_eps = 1e-05
VMEM_LIMIT = 30 * 1024 * 1024
SMALL_LIMIT = 16 * 1024 * 1024
LAYER_LIMIT = 38 * 1024 * 1024

NN = (((1,), (0,)), ((), ()))
NT = (((1,), (1,)), ((), ()))
TN = (((0,), (0,)), ((), ()))


def mm(a, b, dims=NN):
    return lax.dot_general(a, b, dims, preferred_element_type=f32)


COS, SIN, BEGIN, COS_READ, SIN_READ, COS_TAIL, SIN_TAIL = range(7)


def make_table(place, lens_ref, row, tok_count):
    pos = place + lax.broadcasted_iota(jnp.int32, (8, tok_count), 1)
    last = place + tok_count - 1
    start = jnp.int32(0)
    begin = jnp.zeros((8, tok_count), jnp.int32)
    span = jnp.ones((8, tok_count), jnp.int32)
    last_begin = jnp.int32(0)
    for d in range(lens_ref.shape[1]):
        length = lens_ref[row, d]
        inside = pos >= start
        begin = jnp.where(inside, start, begin)
        span = jnp.where(inside, length, span)
        last_begin = jnp.where(start <= last, start, last_begin)
        start = start + length
    angle = half_pi * (pos - begin).astype(f32) / span.astype(f32)
    cos, sin = jnp.cos(angle), jnp.sin(angle)
    reader = (begin < place).astype(f32)
    tail = (begin == last_begin).astype(f32)
    which = lax.broadcasted_iota(jnp.int32, (8, tok_count), 0)
    table = jnp.zeros((8, tok_count), f32)
    for index, value in (
        (COS, cos),
        (SIN, sin),
        (BEGIN, begin.astype(f32)),
        (COS_READ, cos * reader),
        (SIN_READ, sin * reader),
        (COS_TAIL, cos * tail),
        (SIN_TAIL, sin * tail),
    ):
        table = jnp.where(which == index, value, table)
    return table


def blend_of(table):
    columns = table.T
    tok_count = table.shape[1]
    source = lax.broadcasted_iota(jnp.int32, (tok_count, tok_count), 0)
    reader = lax.broadcasted_iota(jnp.int32, (tok_count, tok_count), 1)
    same = (columns[:, BEGIN : BEGIN + 1] == table[BEGIN : BEGIN + 1]) & (source <= reader)
    value = (
        columns[:, COS : COS + 1] * table[COS : COS + 1]
        + columns[:, SIN : SIN + 1] * table[SIN : SIN + 1]
    )
    return jnp.where(same, value, 0.0)


def trig_rows(head_rows, cos, sin):
    wide = head_rows.astype(f32)
    return jnp.concatenate([(wide * cos).astype(bf16), (wide * sin).astype(bf16)], axis=0)


def with_row(rows, extra):
    which = lax.broadcasted_iota(jnp.int32, (16, rows.shape[1]), 0)
    return jnp.concatenate([rows, jnp.where(which == 0, extra, 0.0).astype(bf16)], axis=0)


def head_slice(h):
    return slice(h * HEAD_DIM, (h + 1) * HEAD_DIM)


def put_state(state_refs, h, value):
    ref = state_refs[h // HALF_HEADS]
    place = h % HALF_HEADS
    ref[0, head_slice(place), :] = value[:HEAD_DIM]
    ref[0, HALF_HEADS * HEAD_DIM + place : HALF_HEADS * HEAD_DIM + place + 1, :] = value[
        HEAD_DIM : HEAD_DIM + 1
    ]


def take_state(state_refs, h):
    ref = state_refs[h // HALF_HEADS]
    place = h % HALF_HEADS
    mats = ref[0, head_slice(place), :].astype(bf16)
    sums = ref[0, HALF_HEADS * HEAD_DIM + place : HALF_HEADS * HEAD_DIM + place + 1, :]
    return with_row(mats, sums)


def clear_pad(state_refs):
    for ref in state_refs:
        ref[0, HALF_HEADS * HEAD_DIM :, :] = jnp.zeros((8, 2 * HEAD_DIM), f32)


def softplus_sigmoid(v):
    small = jnp.exp(-jnp.abs(v))
    soft = jnp.maximum(v, 0.0) + jnp.log1p(small)
    inverse = 1.0 / (1.0 + small)
    return soft, jnp.where(v >= 0, inverse, small * inverse)


def project_kernel(
    s_ref,
    lens_ref,
    tok_ref,
    wk_ref,
    wv_ref,
    tab_ref,
    tok_t_ref,
    k_t_ref,
    v_t_ref,
    k_ref,
    v_ref,
    sig_k_ref,
    state_a,
    state_b,
    w_t,
):
    row = pl.program_id(0)

    @pl.when(row == 0)
    def _():
        w_t[0] = wk_ref[...].T
        w_t[1] = wv_ref[...].T

    tok_t = tok_ref[0].T
    tok_t_ref[...] = tok_t
    table = make_table(s_ref[PLACE] * tok_t.shape[1], lens_ref, row, tok_t.shape[1])
    tab_ref[0] = table
    soft, sig = softplus_sigmoid(mm(w_t[0], tok_t))
    key_t = soft.astype(bf16)
    k_t_ref[...] = key_t
    k_ref[0] = key_t.T
    sig_k_ref[...] = sig.astype(bf16)
    value_t = mm(w_t[1], tok_t).astype(bf16)
    v_t_ref[...] = value_t
    v_ref[0] = value_t.T
    states = (state_a, state_b)
    clear_pad(states)
    cos, sin = table[COS_TAIL : COS_TAIL + 1], table[SIN_TAIL : SIN_TAIL + 1]
    for h in range(HEADS):
        keys = trig_rows(k_t_ref[head_slice(h), :], cos, sin)
        values = with_row(v_t_ref[head_slice(h), :], 1.0)
        put_state(states, h, mm(values, keys, NT))


def pair_rows(ref, pair):
    first = ref[head_slice(2 * pair), :]
    second = ref[head_slice(2 * pair + 1), :]
    nothing = jnp.zeros_like(first)
    return jnp.concatenate(
        [
            jnp.concatenate([first, nothing], axis=1),
            jnp.concatenate([nothing, second], axis=1),
        ],
        axis=0,
    )


def two_parts(v):
    high = v.astype(bf16)
    return high, (v - high.astype(f32)).astype(bf16)


def local_kernel(
    s_ref,
    tab_ref,
    tok_t_ref,
    k_ref,
    v_t_ref,
    wq_ref,
    w_out_ref,
    w_in_ref,
    w_back_ref,
    q_t_ref,
    sig_q_ref,
    numer_ref,
    denom_ref,
    w_out_t,
    w_in_t,
    w_back_t,
    w_t,
):
    @pl.when(pl.program_id(0) == 0)
    def _():
        w_t[...] = wq_ref[...].T
        w_out_t[...] = w_out_ref[...].T

    w_in_t[...] = w_in_ref[...].T
    w_back_t[...] = w_back_ref[...].T

    soft, sig = softplus_sigmoid(mm(w_t[...], tok_t_ref[...]))
    q_t_ref[...] = soft.astype(bf16)
    sig_q_ref[...] = sig.astype(bf16)
    blend = blend_of(tab_ref[0])
    tok_count = blend.shape[0]
    denom_ref[...] = jnp.zeros_like(denom_ref)
    for pair in range(PAIRS):
        lanes = slice(pair * 2 * HEAD_DIM, (pair + 1) * 2 * HEAD_DIM)
        both = mm(k_ref[0, :, lanes], pair_rows(q_t_ref, pair))
        for side in range(2):
            h = 2 * pair + side
            high, low = two_parts(both[:, side * tok_count : (side + 1) * tok_count] * blend)
            values = with_row(v_t_ref[head_slice(h), :], 1.0)
            out = mm(values, high) + mm(values, low)
            numer_ref[head_slice(h), :] = out[:HEAD_DIM]
            denom_ref[h : h + 1, :] = out[HEAD_DIM : HEAD_DIM + 1]


def mean_rows(v):
    return jnp.sum(v, axis=0, keepdims=True) * (1.0 / v.shape[0])


def fold_lanes(v):
    total = v[:, :128]
    for at in range(128, v.shape[1], 128):
        total = total + v[:, at : at + 128]
    return total


def add_to(ref, value):
    first = pl.program_id(0) == 0

    @pl.when(first)
    def _():
        ref[...] = value

    @pl.when(jnp.logical_not(first))
    def _():
        ref[...] += value


def norm_back(grad_norm, normed, inv_scale):
    return inv_scale * (grad_norm - mean_rows(grad_norm) - normed * mean_rows(grad_norm * normed))


def lane_total(ref):
    return jnp.sum(ref[...], axis=1, keepdims=True)


def layer_kernel(
    s_ref,
    tab_ref,
    q_t_ref,
    numer_ref,
    denom_loc_ref,
    state_a,
    state_b,
    tok_t_ref,
    cot_ref,
    w_out_t,
    w_in_t,
    w_back_t,
    w_out_ref,
    w_in_ref,
    w_back_ref,
    gain_one_ref,
    shift_one_ref,
    gain_two_ref,
    shift_two_ref,
    layer_ref,
    att_t_ref,
    first_t_ref,
    active_t_ref,
    grad_second_ref,
    grad_hidden_ref,
    grad_base_ref,
    grad_branch_ref,
    grad_numer_ref,
    grad_denom_ref,
    small_ref,
    out_a,
    out_b,
    slope,
    normed_one,
    attended,
    inverse_denom,
    total,
    fold_gain_one,
    fold_shift_one,
    fold_gain_two,
    fold_shift_two,
):
    ff = w_in_ref.shape[1]
    step = 768
    table = tab_ref[0]
    cos, sin = table[COS_READ : COS_READ + 1], table[SIN_READ : SIN_READ + 1]
    states = (state_a, state_b)
    for h in range(HEADS):
        reads = trig_rows(q_t_ref[head_slice(h), :], cos, sin)
        more = mm(take_state(states, h), reads)
        numer = numer_ref[head_slice(h), :] + more[:HEAD_DIM]
        inverse = 1.0 / (denom_loc_ref[h : h + 1, :] + more[HEAD_DIM : HEAD_DIM + 1])
        inverse_denom[h : h + 1, :] = inverse
        value = numer * inverse
        attended[head_slice(h), :] = value
        att_t_ref[head_slice(h), :] = value.astype(bf16)
    summed = tok_t_ref[...].astype(f32) + mm(w_out_t[...], att_t_ref[...])
    centered = summed - mean_rows(summed)
    scale_one = lax.rsqrt(mean_rows(centered * centered) + norm_eps)
    normed = centered * scale_one
    normed_one[...] = normed
    first_out = normed * gain_one_ref[...] + shift_one_ref[...]
    total[...] = first_out
    first_low = first_out.astype(bf16)
    first_t_ref[...] = first_low
    for at in range(0, ff, step):
        hidden = mm(w_in_t[at : at + step, :], first_low)
        half = 0.5 * (1.0 + lax.erf(hidden * 0.7071067811865476))
        bell = jnp.exp(hidden * hidden * -0.5) * 0.3989422804014327
        active = (hidden * half).astype(bf16)
        active_t_ref[at : at + step, :] = active
        slope[at : at + step, :] = (half + hidden * bell).astype(bf16)
        total[...] += mm(w_back_t[:, at : at + step], active)
    summed = total[...]
    centered = summed - mean_rows(summed)
    scale_two = lax.rsqrt(mean_rows(centered * centered) + norm_eps)
    normed = centered * scale_two
    layer_ref[0] = (normed * gain_two_ref[...] + shift_two_ref[...]).T.astype(bf16)
    grad_top = cot_ref[0].T.astype(f32)
    add_to(fold_gain_two, fold_lanes(grad_top * normed))
    add_to(fold_shift_two, fold_lanes(grad_top))
    grad_mid = norm_back(grad_top * gain_two_ref[...], normed, scale_two)
    total[...] = grad_mid
    grad_second = grad_mid.astype(bf16)
    grad_second_ref[...] = grad_second
    for at in range(0, ff, step):
        grad_active = mm(w_back_ref[at : at + step, :], grad_second)
        low = (grad_active * slope[at : at + step, :].astype(f32)).astype(bf16)
        grad_hidden_ref[at : at + step, :] = low
        total[...] += mm(w_in_ref[:, at : at + step], low)
    grad_first = total[...]
    normed = normed_one[...]
    add_to(fold_gain_one, fold_lanes(grad_first * normed))
    add_to(fold_shift_one, fold_lanes(grad_first))
    grad_base = norm_back(grad_first * gain_one_ref[...], normed, scale_one)
    grad_base_ref[...] = grad_base
    grad_branch = grad_base.astype(bf16)
    grad_branch_ref[...] = grad_branch
    total[...] = mm(w_out_ref[...], grad_branch)
    outs = (out_a, out_b)
    clear_pad(outs)
    grad_denom_ref[...] = jnp.zeros_like(grad_denom_ref)
    for h in range(HEADS):
        rows = head_slice(h)
        grad_numer = (total[rows, :] * inverse_denom[h : h + 1, :]).astype(bf16)
        grad_denom = -jnp.sum(grad_numer.astype(f32) * attended[rows, :], axis=0, keepdims=True)
        grad_denom_ref[h : h + 1, :] = grad_denom
        grad_numer_ref[rows, :] = grad_numer
        reads = trig_rows(q_t_ref[rows, :], cos, sin)
        put_state(outs, h, mm(with_row(grad_numer, grad_denom), reads, NT))

    @pl.when(pl.program_id(0) == pl.num_programs(0) - 1)
    def _():
        lane = lax.broadcasted_iota(jnp.int32, small_ref.shape, 1)
        value = jnp.zeros(small_ref.shape, f32)
        for i, ref in enumerate((fold_gain_one, fold_shift_one, fold_gain_two, fold_shift_two)):
            value = jnp.where(lane == i, lane_total(ref), value)
        small_ref[...] = value


def local_back_kernel(
    s_ref,
    tab_ref,
    q_t_ref,
    k_t_ref,
    k_ref,
    v_ref,
    sig_q_ref,
    grad_numer_ref,
    grad_denom_ref,
    state_a,
    state_b,
    grad_q_ref,
    grad_k_ref,
    grad_v_ref,
):
    table = tab_ref[0]
    blend = blend_of(table)
    tok_count = blend.shape[0]
    cos, sin = table[COS_READ : COS_READ + 1], table[SIN_READ : SIN_READ + 1]
    states = (state_a, state_b)
    for pair in range(PAIRS):
        lanes = slice(pair * 2 * HEAD_DIM, (pair + 1) * 2 * HEAD_DIM)
        both = mm(k_ref[0, :, lanes], pair_rows(q_t_ref, pair))
        grads = mm(v_ref[0, :, lanes], pair_rows(grad_numer_ref, pair))
        for side in range(2):
            h = 2 * pair + side
            rows = head_slice(h)
            part = slice(side * tok_count, (side + 1) * tok_count)
            grad_denom = grad_denom_ref[h : h + 1, :]
            scores = (both[:, part] * blend).astype(bf16)
            grad_scores, rest = two_parts((grads[:, part] + grad_denom) * blend)
            grad_numer = grad_numer_ref[rows, :]
            grad_v_ref[rows, :] = mm(grad_numer, scores, NT)
            grad_k_ref[rows, :] = mm(q_t_ref[rows, :], grad_scores, NT)
            reads = mm(take_state(states, h), with_row(grad_numer, grad_denom), TN)
            grad_q = (
                mm(k_t_ref[rows, :], grad_scores)
                + mm(k_t_ref[rows, :], rest)
                + cos * reads[:HEAD_DIM]
                + sin * reads[HEAD_DIM:]
            )
            grad_q_ref[rows, :] = (grad_q * sig_q_ref[rows, :].astype(f32)).astype(bf16)


def tail_kernel(
    s_ref,
    tab_ref,
    k_t_ref,
    v_t_ref,
    sig_k_ref,
    state_a,
    state_b,
    grad_k_in,
    grad_v_in,
    grad_kv_ref,
):
    table = tab_ref[0]
    cos, sin = table[COS_TAIL : COS_TAIL + 1], table[SIN_TAIL : SIN_TAIL + 1]
    states = (state_a, state_b)
    for h in range(HEADS):
        rows = head_slice(h)
        state = take_state(states, h)
        inner = mm(state, with_row(v_t_ref[rows, :], 1.0), TN)
        grad_k = grad_k_in[rows, :] + cos * inner[:HEAD_DIM] + sin * inner[HEAD_DIM:]
        grad_kv_ref[0, rows, :] = (grad_k * sig_k_ref[rows, :].astype(f32)).astype(bf16)
        keys = trig_rows(k_t_ref[rows, :], cos, sin)
        grad_kv_ref[1, rows, :] = (grad_v_in[rows, :] + mm(state[:HEAD_DIM], keys)).astype(bf16)


def token_kernel(s_ref, gq_ref, gkv_ref, base_ref, wq_ref, wk_ref, wv_ref, out_ref):
    total = base_ref[...] + mm(wq_ref[...], gq_ref[...])
    total = total + mm(wk_ref[...], gkv_ref[0])
    total = total + mm(wv_ref[...], gkv_ref[1])
    out_ref[0] = total.T


def spec(block, index):
    return pl.BlockSpec(block, index)


NEAR = pl.BlockSpec(memory_space=pltpu.VMEM)

CORE, ODD, PLACE = range(3)


class Order:
    def __init__(self, scalars):
        self.scalars = scalars

    def call(
        self, kernel, grid, ins, outs, scratch, args, extra=(), free=(), near=(), near_out=(), limit=VMEM_LIMIT
    ):
        count = 1 + len(extra)
        placed = len(scratch)

        def stepped(*refs):
            s_ref, handed = refs[0], refs[len(refs) - placed - 1]
            rest = refs[: len(refs) - placed - 1] + refs[len(refs) - placed :]
            kernel(*rest)
            for i in range(s_ref.shape[0]):
                handed[i] = s_ref[i]

        *values, self.scalars = pl.pallas_call(
            stepped,
            grid_spec=pltpu.PrefetchScalarGridSpec(
                num_scalar_prefetch=count,
                grid=grid,
                in_specs=ins,
                out_specs=[o for o, _ in outs] + [pl.BlockSpec(memory_space=pltpu.SMEM)],
                scratch_shapes=scratch,
            ),
            out_shape=[
                (pltpu.VMEM if i in near_out else pltpu.HBM)(shape, kind)
                for i, (_, (shape, kind)) in enumerate(outs)
            ]
            + [jax.ShapeDtypeStruct(self.scalars.shape, jnp.int32)],
            compiler_params=pltpu.CompilerParams(
                dimension_semantics=("arbitrary",) * len(grid), vmem_limit_bytes=limit
            ),
            cost_estimate=pl.CostEstimate(flops=1000000000000, bytes_accessed=1, transcendentals=0),
        )(
            self.scalars,
            *extra,
            *[
                v
                if i in free
                else pltpu.with_memory_space_constraint(v, pltpu.VMEM if i in near else pltpu.HBM)
                for i, v in enumerate(args)
            ],
        )
        return values


def pick_halves(core, value):
    cut = value.shape[1] // 2
    low, high = value[:, :cut], value[:, cut:]
    return jnp.where(core == 0, high, low), jnp.where(core == 0, low, high)


def tall_kernel(s_ref, a_ref, b_ref, c_ref, d_ref, away_ref, keep_ref):
    count = a_ref.shape[0]
    for left, right, lines in (
        (a_ref, b_ref, slice(0, count)),
        (c_ref, d_ref, slice(count, away_ref.shape[0])),
    ):
        away_ref[lines, :], keep_ref[lines, :] = pick_halves(
            s_ref[CORE], mm(left[...], right[...], NT)
        )


def tall_product(order, a, b, c, d):
    shards = lax.axis_size("seq")
    flat = a.shape[1]
    tall, low, cut = a.shape[0] // shards, c.shape[0] // shards, b.shape[0] // 2
    rows = tall + low
    out = (spec((rows, cut), lambda i, *s: (i, 0)), ((shards * rows, cut), f32))
    ins = [
        spec((tall, flat), lambda i, *s: (i, 0)),
        spec(b.shape, lambda i, *s: (0, 0)),
        spec((low, flat), lambda i, *s: (i, 0)),
        spec(d.shape, lambda i, *s: (0, 0)),
    ]
    return order.call(tall_kernel, (shards,), ins, [out, out], [], (a, b, c, d))


def wide_kernel(s_ref, a_ref, b_ref, away_ref, keep_ref):
    value = mm(a_ref[...], b_ref[...], NT)
    first = pl.program_id(0) < pl.num_programs(0) // 2

    @pl.when(first)
    def _():
        away_ref[...] = value

    @pl.when(jnp.logical_not(first))
    def _():
        keep_ref[...] = value


def wide_product(order, a, b):
    count, flat = a.shape
    cut = b.shape[0] // 2
    tile = 512
    half = cut // tile

    def source(i, s):
        return jnp.where(i < half, (1 - s[CORE]) * half + i, s[CORE] * half + i - half), 0

    outs = [
        (spec((count, tile), lambda i, s: (0, jnp.minimum(i, half - 1))), ((count, cut), f32)),
        (spec((count, tile), lambda i, s: (0, jnp.maximum(i - half, 0))), ((count, cut), f32)),
    ]
    ins = [spec(a.shape, lambda i, s: (0, 0)), spec((tile, flat), source)]
    return order.call(wide_kernel, (2 * half,), ins, outs, [], (a, b))


def side_product_kernel(s_ref, a_ref, query_ref, kv_ref, small_ref, away_ref, keep_ref):
    core = s_ref[CORE]
    at = 0
    for right in (query_ref[...], kv_ref[0], kv_ref[1]):
        away, keep = pick_halves(core, mm(a_ref[...], right, NT))
        away_ref[:, at : at + away.shape[1]] = away
        keep_ref[:, at : at + keep.shape[1]] = keep
        at += away.shape[1]
    value = small_ref[...]
    away_ref[:, at:] = jnp.where(core == 0, 0.0, value)
    keep_ref[:, at:] = jnp.where(core == 0, value, 0.0)


def side_product(order, a, query, kv, small):
    count, flat = a.shape
    tile = count // 2
    columns = 3 * (count // 2) + small.shape[1]
    ins = [
        spec((tile, flat), lambda i, s: (i, 0)),
        spec(query.shape, lambda i, s: (0, 0)),
        spec(kv.shape, lambda i, s: (0, 0, 0)),
        spec((tile, small.shape[1]), lambda i, s: (i, 0)),
    ]
    out = (spec((tile, columns), lambda i, s: (i, 0)), ((count, columns), f32))
    return order.call(side_product_kernel, (2,), ins, [out, out], [], (a, query, kv, small))


def route_kernel(s_ref, *refs):
    for i in range(4):
        refs[8 + i][...] = refs[2 * i][...] + refs[2 * i + 1][...]


def route(order, left, right, low_bit, high_bit):
    (a, b), (c, d) = left, right
    shards, rows, columns = a.shape
    same = a is c
    if same:
        rows //= 2
    lower = 1 if same else 0
    half = shards // 2

    def by_low(flip):
        def index(i, s):
            mine = (s[PLACE] >> low_bit) & 1
            return 2 * i + ((1 - mine) if flip else mine), 0, 0

        return index

    def by_high(flip):
        def index(i, s):
            mine = (s[PLACE] >> high_bit) & 1
            return i + ((1 - mine) if flip else mine) * half, lower, 0

        return index

    block = (1, rows, columns)
    maps = [by_low(True), by_low(False), by_high(True), by_high(False)]
    ins = [spec(block, m) for m in maps for _ in range(2)]
    out = (spec(block, lambda i, s: (i, 0, 0)), ((half, rows, columns), f32))
    return order.call(route_kernel, (half,), ins, [out] * 4, [], (a, b, a, b, c, d, c, d))


def choose_kernel(s_ref, a_ref, b_ref, c_ref, d_ref, away_ref, kept_ref):
    upper, lower = a_ref[0] + b_ref[0], c_ref[0] + d_ref[0]
    odd = s_ref[ODD] == 1
    away_ref[...] = jnp.where(odd, upper, lower)
    kept_ref[...] = jnp.where(odd, lower, upper)


def choose(order, left, right):
    shape = left[0].shape[1:]
    return order.call(
        choose_kernel,
        (1,),
        [NEAR] * 4,
        [(NEAR, (shape, f32))] * 2,
        [],
        (*left, *right),
        free=range(4),
        near_out=range(2),
        limit=SMALL_LIMIT,
    )


def add_kernel(s_ref, a_ref, b_ref, out_ref):
    out_ref[...] = a_ref[...] + b_ref[...]


def add(order, a, b):
    outs = [(NEAR, (a.shape, f32))]
    return order.call(
        add_kernel, (1,), [NEAR] * 2, outs, [], (a, b), near=range(2), near_out=range(1), limit=SMALL_LIMIT
    )[0]


def merge_kernel(s_ref, kept_ref, got_ref, out_ref):
    odd = s_ref[ODD] == 1
    rows = kept_ref.shape[0]
    kept, got = kept_ref[...], got_ref[...]
    out_ref[:rows, :] = jnp.where(odd, got, kept)
    out_ref[rows:, :] = jnp.where(odd, kept, got)


def merge(order, kept, got):
    rows, columns = kept.shape
    outs = [(NEAR, ((2 * rows, columns), f32))]
    return order.call(
        merge_kernel,
        (1,),
        [NEAR] * 2,
        outs,
        [],
        (kept, got),
        near=range(2),
        near_out=range(1),
        limit=SMALL_LIMIT,
    )[0]


def side_kernel(s_ref, mine_ref, other_ref, *outs):
    first = s_ref[CORE] == 0
    at = 0
    for out in outs:
        cut = out.shape[1] // 2
        if cut < 128:
            out[...] = jnp.where(first, mine_ref[:, at:], other_ref[:, at:])
            break
        mine, other = mine_ref[:, at : at + cut], other_ref[:, at : at + cut]
        out[:, :cut] = jnp.where(first, mine, other)
        out[:, cut:] = jnp.where(first, other, mine)
        at += cut


def side(order, mine, other, widths):
    rows = mine.shape[0]
    outs = [(spec((rows, w), lambda i, s: (0, 0)), ((rows, w), f32)) for w in widths]
    return order.call(
        side_kernel, (1,), [NEAR] * 2, outs, [], (mine, other), near=range(2), limit=SMALL_LIMIT
    )


def mix_kernel(first, s_ref, w_ref, *refs):
    row = pl.program_id(0)
    for i in range(2):
        own, other = (w_ref[first + 2 * i + j, row] for j in range(2))
        refs[4 + i][...] = own * refs[2 * i][...] + other * refs[2 * i + 1][...]


def mix(order, weights, first, *parts):
    shape = parts[0].shape
    block = spec((1,) + shape[1:], lambda r, *s: (r, 0, 0))
    return order.call(
        partial(mix_kernel, first),
        (shape[0],),
        [block] * 4,
        [(block, (shape, f32))] * 2,
        [],
        parts,
        (weights,),
        free=range(4),
        limit=SMALL_LIMIT,
    )


def first_begins(lengths, count, tok_count):
    slots = lengths.shape[1]
    order = jnp.arange(slots)
    before = (order[:, None] > order[None, :]).astype(jnp.int32)
    starts = jnp.sum(lengths[:, None, :] * before[None], axis=-1)
    firsts = jnp.arange(count, dtype=jnp.int32) * tok_count
    reached = starts[:, None, :] <= firsts[None, :, None]
    return jnp.max(jnp.where(reached, starts[:, None, :], 0), axis=-1)


def pick(index, values):
    out = values[0]
    for i in range(1, len(values)):
        out = jnp.where(index == i, values[i], out)
    return out


def weights_of(begin_first, tok_count, reverse):
    count = lax.axis_size("seq")
    place = lax.axis_index("seq")

    def covers(i, j):
        low, high = (count - 1 - j, count - 1 - i) if reverse else (i, j)
        return (begin_first[:, high] < (low + 1) * tok_count).astype(f32)

    if count != 4:
        spots = jnp.arange(count)
        mine = begin_first.T if reverse else begin_first[:, place][None]
        reach = (place if reverse else spots[:, None]) + 1
        ahead = (spots > place) if reverse else (spots < place)
        return ((mine < reach * tok_count) & ahead[:, None]).astype(f32)
    index = count - 1 - place if reverse else place
    zero = jnp.zeros_like(begin_first[:, 0], f32)
    one = zero + 1.0
    m02, m03, m13 = covers(0, 2), covers(0, 3), covers(1, 3)
    onward = [
        pick(index, [m02, m13, zero, zero]),
        pick(index, [one, m03, zero, zero]),
        pick(index, [one, zero, one, zero]),
        pick(index, [zero, zero, m03, one]),
    ]
    final = [
        pick(index, [zero, one, zero, one]),
        pick(index, [zero, zero, one, one]),
        pick(index, [zero, zero, m02, m13]),
        pick(index, [zero, one, one, one]),
    ]
    return onward + final


def entering(order, parts, weights, first):
    if lax.axis_size("seq") != 4:
        gathered = [lax.all_gather(p, "seq") for p in parts]
        yield
        yield
        yield tuple(jnp.sum(g * weights[first][:, :, None, None], axis=0) for g in gathered)
    part_a, part_b = parts
    got_a, got_b = swap(part_a, "seq", 1), swap(part_b, "seq", 2)
    yield
    next_a, next_b = mix(order, weights, first, part_a, got_a, part_b, got_b)
    last_a, last_b = swap(next_a, "seq", 2), swap(next_b, "seq", 1)
    yield
    yield mix(order, weights, first + 4, got_a, last_a, got_b, last_b)


def swap(value, axis, distance):
    count = lax.axis_size(axis)
    return lax.ppermute(value, axis, [(i, i ^ distance) for i in range(count)])


def reduced(order, away, keep, widths):
    count = lax.axis_size("batch")
    shards = lax.axis_size("seq")
    bits = shards.bit_length() - 1
    shape = (shards, keep.shape[0] // shards, keep.shape[1])
    got = swap(away, "batch", 1).reshape(shape)
    yield
    left = right = (keep.reshape(shape), got)
    for step in range(bits):
        high = bits - 1 - step
        away_l, keep_l, away_r, keep_r = route(order, left, right, step, high)
        left = keep_l, swap(away_l, "seq", 1 << step)
        right = keep_r, swap(away_r, "seq", 1 << high)
        yield
    away, kept = choose(order, left, right)
    got = swap(away, "batch", 2)
    distance = 4
    while distance < count:
        yield
        kept = add(order, kept, got)
        got = swap(kept, "batch", distance)
        distance *= 2
    yield
    kept = add(order, kept, got)
    got = swap(kept, "batch", 2)
    yield
    merged = merge(order, kept, got)
    other = swap(merged, "batch", 1)
    yield
    yield side(order, merged, other, widths)


SCHEDULE = (
    "back_product", "in_product", "states", "back", "local", "states",
    "in", "back", "tail", "last_product", "in", "back",
    "last", "in", "back", "last", "in", "last",
    "back", "last", "tokens", "in", "last", "back",
    "in", "last", "back", "in", "last",
)


def body(
    tokens,
    cotangent,
    doc_lengths,
    w_query,
    w_key,
    w_value,
    w_out,
    w_in,
    w_back,
    gain_one,
    shift_one,
    gain_two,
    shift_two,
):
    rows, toks, width = tokens.shape
    ff = w_in.shape[1]
    flat = rows * toks
    shards = lax.axis_size("seq")
    whole = pl.BlockSpec(memory_space=pltpu.VMEM)
    token_major = pl.BlockSpec((1, toks, width), lambda r, *s: (r, 0, 0))
    table_spec = pl.BlockSpec((1, 8, toks), lambda r, *s: (r, 0, 0))
    state_spec = pl.BlockSpec((1, STATE_ROWS, 2 * HEAD_DIM), lambda r, *s: (r, 0, 0))

    def feature(count):
        return pl.BlockSpec((count, toks), lambda r, *s: (0, r))

    tok_low = (token_major, ((rows, toks, width), bf16))
    wide_low = (feature(width), ((width, flat), bf16))
    wide_full = (feature(width), ((width, flat), f32))
    ff_low = (feature(ff), ((ff, flat), bf16))
    head_rows = (feature(16), ((16, flat), f32))
    fold = (pl.BlockSpec((width, 128), lambda r, *s: (0, 0)), ((width, 128), f32))
    state = (state_spec, ((rows, STATE_ROWS, 2 * HEAD_DIM), f32))
    grid = (rows,)

    batch_place = lax.axis_index("batch").astype(jnp.int32)
    scalars = jnp.stack(
        [batch_place & 1, (batch_place >> 1) & 1, lax.axis_index("seq").astype(jnp.int32)]
    )
    order = Order(scalars)

    def run(kernel, ins, outs, scratch, *args, **more):
        return order.call(kernel, grid, ins, outs, scratch, args, **more)

    def column(v):
        return v[:, None]

    table, tok_t, k_t, v_t, key, value, sig_k, state_a, state_b = run(
        project_kernel,
        [token_major, whole, whole],
        [(table_spec, ((rows, 8, toks), f32))]
        + [wide_low] * 3
        + [tok_low] * 2
        + [wide_low]
        + [state] * 2,
        [pltpu.VMEM((2, width, width), bf16)],
        tokens,
        w_key,
        w_value,
        extra=(doc_lengths,),
    )
    begins = first_begins(doc_lengths, shards, toks)
    if shards == 4:
        weights = jnp.stack(weights_of(begins, toks, False) + weights_of(begins, toks, True))
        later = 8
    else:
        weights = [weights_of(begins, toks, False), weights_of(begins, toks, True)]
        later = 1
    states = entering(order, (state_a, state_b), weights, 0)
    next(states)
    part = ff // rows
    q_t, sig_q, numer, denom_loc, w_out_t, w_in_t, w_back_t = run(
        local_kernel,
        [
            table_spec,
            feature(width),
            token_major,
            feature(width),
            whole,
            whole,
            pl.BlockSpec((width, part), lambda r, *s: (0, r)),
            pl.BlockSpec((part, width), lambda r, *s: (r, 0)),
        ],
        [
            wide_low,
            wide_low,
            wide_full,
            head_rows,
            (pl.BlockSpec((width, width), lambda r, *s: (0, 0)), ((width, width), bf16)),
            (pl.BlockSpec((part, width), lambda r, *s: (r, 0)), ((ff, width), bf16)),
            (pl.BlockSpec((width, part), lambda r, *s: (0, r)), ((width, ff), bf16)),
        ],
        [pltpu.VMEM((width, width), bf16)],
        table,
        tok_t,
        key,
        v_t,
        w_query,
        w_out,
        w_in,
        w_back,
    )
    next(states)
    in_a, in_b = next(states)
    (
        layer_out,
        att_t,
        first_t,
        active_t,
        grad_second,
        grad_hidden,
        grad_base,
        grad_branch,
        grad_numer,
        grad_denom,
        small,
        out_a,
        out_b,
    ) = run(
        layer_kernel,
        [
            table_spec,
            feature(width),
            feature(width),
            feature(16),
            state_spec,
            state_spec,
            feature(width),
            token_major,
        ]
        + [whole] * 10,
        [
            tok_low,
            wide_low,
            wide_low,
            ff_low,
            wide_low,
            ff_low,
            wide_full,
            wide_low,
            wide_low,
            head_rows,
            fold,
            state,
            state,
        ],
        [
            pltpu.VMEM((ff, toks), bf16),
            pltpu.VMEM((width, toks), f32),
            pltpu.VMEM((width, toks), f32),
            pltpu.VMEM((16, toks), f32),
            pltpu.VMEM((width, toks), f32),
        ]
        + [pltpu.VMEM((width, 128), f32)] * 4,
        table,
        q_t,
        numer,
        denom_loc,
        in_a,
        in_b,
        tok_t,
        cotangent,
        w_out_t,
        w_in_t,
        w_back_t,
        w_out,
        w_in,
        w_back,
        column(gain_one),
        column(shift_one),
        column(gain_two),
        column(shift_two),
        near=range(8, 14),
        limit=LAYER_LIMIT,
    )

    back_states = entering(order, (out_a, out_b), weights, later)
    next(back_states)
    pieces, made = {}, {}

    def begin(name, product, widths):
        pieces[name] = reduced(order, *product, widths)
        next(pieces[name])

    def local_back():
        made["query"], made["key"], made["value"] = run(
            local_back_kernel,
            [
                table_spec,
                feature(width),
                feature(width),
                token_major,
                token_major,
                feature(width),
                feature(width),
                feature(16),
                state_spec,
                state_spec,
            ],
            [wide_low, wide_full, wide_full],
            [],
            table,
            q_t,
            k_t,
            key,
            value,
            sig_q,
            grad_numer,
            grad_denom,
            in_a,
            in_b,
        )

    def tail():
        back_a, back_b = made["states"]
        (made["kv"],) = run(
            tail_kernel,
            [table_spec]
            + [feature(width)] * 3
            + [state_spec] * 2
            + [feature(width)] * 2,
            [(pl.BlockSpec((2, width, toks), lambda r, *s: (0, 0, r)), ((2, width, flat), bf16))],
            [],
            table,
            k_t,
            v_t,
            sig_k,
            back_a,
            back_b,
            made["key"],
            made["value"],
        )

    def token_grads():
        (made["tokens"],) = run(
            token_kernel,
            [
                feature(width),
                pl.BlockSpec((2, width, toks), lambda r, *s: (0, 0, r)),
                feature(width),
            ]
            + [whole] * 3,
            [(token_major, ((rows, toks, width), f32))],
            [],
            made["query"],
            made["kv"],
            grad_base,
            w_query,
            w_key,
            w_value,
        )

    def states_on():
        made["states"] = next(back_states)

    steps = {
        "back_product": lambda: begin(
            "back", tall_product(order, active_t, grad_second, att_t, grad_branch), (width,)
        ),
        "in_product": lambda: begin("in", wide_product(order, first_t, grad_hidden), (ff,)),
        "last_product": lambda: begin(
            "last",
            side_product(order, tok_t, made["query"], made["kv"], small),
            (width, width, width, 128),
        ),
        "states": states_on,
        "local": local_back,
        "tail": tail,
        "tokens": token_grads,
    }
    ends = {}

    def step(name):
        value = next(pieces[name])
        if value is not None:
            ends[name] = value

    for name in SCHEDULE:
        if name in steps:
            steps[name]()
        elif name not in ends:
            step(name)
    while len(ends) < len(pieces):
        for name in pieces:
            if name not in ends:
                step(name)
    (above,), (total_in,) = ends["back"], ends["in"]
    total_back, total_out = above[: ff // shards], above[ff // shards :]
    total_query, total_key, total_value, vectors = ends["last"]
    grad_tokens = made["tokens"]
    return (
        layer_out,
        grad_tokens,
        total_query,
        total_key,
        total_value,
        total_out,
        total_in,
        total_back,
        vectors[:, 0],
        vectors[:, 1],
        vectors[:, 2],
        vectors[:, 3],
    )


def solution(mesh):
    in_specs = (
        P("batch", "seq", None),
        P("batch", "seq", None),
        P("batch", None),
        P(),
        P(),
        P(),
        P(),
        P(),
        P(),
        P(),
        P(),
        P(),
        P(),
    )
    out_specs = (
        P("batch", "seq", None),
        P("batch", "seq", None),
        P("seq", None),
        P("seq", None),
        P("seq", None),
        P("seq", None),
        P("seq", None),
        P("seq", None),
        P("seq"),
        P("seq"),
        P("seq"),
        P("seq"),
    )
    return jax.shard_map(body, mesh=mesh, in_specs=in_specs, out_specs=out_specs, check_vma=False)
```

```python
from functools import partial

import jax
import jax.numpy as jnp
from jax import lax
from jax.experimental import pallas as pl
from jax.experimental.pallas import tpu as pltpu
from jax.sharding import PartitionSpec as P

HEADS = 12
HEAD_DIM = 64
PAIRS = HEADS // 2
HALF_HEADS = HEADS // 2
STATE_ROWS = HALF_HEADS * HEAD_DIM + 8

f32 = jnp.float32
bf16 = jnp.bfloat16
half_pi = 1.5707963267948966
norm_eps = 1e-05
VMEM_LIMIT = 30 * 1024 * 1024
SMALL_LIMIT = 16 * 1024 * 1024
LAYER_LIMIT = 38 * 1024 * 1024

NN = (((1,), (0,)), ((), ()))
NT = (((1,), (1,)), ((), ()))
TN = (((0,), (0,)), ((), ()))


def mm(a, b, dims=NN):
    return lax.dot_general(a, b, dims, preferred_element_type=f32)


COS, SIN, BEGIN, COS_READ, SIN_READ, COS_TAIL, SIN_TAIL = range(7)


def make_table(place, lens_ref, row, tok_count):
    pos = place + lax.broadcasted_iota(jnp.int32, (8, tok_count), 1)
    last = place + tok_count - 1
    start = jnp.int32(0)
    begin = jnp.zeros((8, tok_count), jnp.int32)
    span = jnp.ones((8, tok_count), jnp.int32)
    last_begin = jnp.int32(0)
    for d in range(lens_ref.shape[1]):
        length = lens_ref[row, d]
        inside = pos >= start
        begin = jnp.where(inside, start, begin)
        span = jnp.where(inside, length, span)
        last_begin = jnp.where(start <= last, start, last_begin)
        start = start + length
    angle = half_pi * (pos - begin).astype(f32) / span.astype(f32)
    cos, sin = jnp.cos(angle), jnp.sin(angle)
    reader = (begin < place).astype(f32)
    tail = (begin == last_begin).astype(f32)
    which = lax.broadcasted_iota(jnp.int32, (8, tok_count), 0)
    table = jnp.zeros((8, tok_count), f32)
    for index, value in (
        (COS, cos),
        (SIN, sin),
        (BEGIN, begin.astype(f32)),
        (COS_READ, cos * reader),
        (SIN_READ, sin * reader),
        (COS_TAIL, cos * tail),
        (SIN_TAIL, sin * tail),
    ):
        table = jnp.where(which == index, value, table)
    return table


def blend_of(table):
    columns = table.T
    tok_count = table.shape[1]
    source = lax.broadcasted_iota(jnp.int32, (tok_count, tok_count), 0)
    reader = lax.broadcasted_iota(jnp.int32, (tok_count, tok_count), 1)
    same = (columns[:, BEGIN : BEGIN + 1] == table[BEGIN : BEGIN + 1]) & (source <= reader)
    value = (
        columns[:, COS : COS + 1] * table[COS : COS + 1]
        + columns[:, SIN : SIN + 1] * table[SIN : SIN + 1]
    )
    return jnp.where(same, value, 0.0)


def trig_rows(head_rows, cos, sin):
    wide = head_rows.astype(f32)
    return jnp.concatenate([(wide * cos).astype(bf16), (wide * sin).astype(bf16)], axis=0)


def with_row(rows, extra):
    which = lax.broadcasted_iota(jnp.int32, (16, rows.shape[1]), 0)
    return jnp.concatenate([rows, jnp.where(which == 0, extra, 0.0).astype(bf16)], axis=0)


def head_slice(h):
    return slice(h * HEAD_DIM, (h + 1) * HEAD_DIM)


def put_state(state_refs, h, value):
    ref = state_refs[h // HALF_HEADS]
    place = h % HALF_HEADS
    ref[0, head_slice(place), :] = value[:HEAD_DIM]
    ref[0, HALF_HEADS * HEAD_DIM + place : HALF_HEADS * HEAD_DIM + place + 1, :] = value[
        HEAD_DIM : HEAD_DIM + 1
    ]


def take_state(state_refs, h):
    ref = state_refs[h // HALF_HEADS]
    place = h % HALF_HEADS
    mats = ref[0, head_slice(place), :].astype(bf16)
    sums = ref[0, HALF_HEADS * HEAD_DIM + place : HALF_HEADS * HEAD_DIM + place + 1, :]
    return with_row(mats, sums)


def clear_pad(state_refs):
    for ref in state_refs:
        ref[0, HALF_HEADS * HEAD_DIM :, :] = jnp.zeros((8, 2 * HEAD_DIM), f32)


def softplus_sigmoid(v):
    small = jnp.exp(-jnp.abs(v))
    soft = jnp.maximum(v, 0.0) + jnp.log1p(small)
    inverse = 1.0 / (1.0 + small)
    return soft, jnp.where(v >= 0, inverse, small * inverse)


def project_kernel(
    s_ref,
    lens_ref,
    tok_ref,
    wk_ref,
    wv_ref,
    tab_ref,
    tok_t_ref,
    k_t_ref,
    v_t_ref,
    k_ref,
    v_ref,
    sig_k_ref,
    state_a,
    state_b,
    w_t,
):
    row = pl.program_id(0)

    @pl.when(row == 0)
    def _():
        w_t[0] = wk_ref[...].T
        w_t[1] = wv_ref[...].T

    tok_t = tok_ref[0].T
    tok_t_ref[...] = tok_t
    table = make_table(s_ref[PLACE] * tok_t.shape[1], lens_ref, row, tok_t.shape[1])
    tab_ref[0] = table
    soft, sig = softplus_sigmoid(mm(w_t[0], tok_t))
    key_t = soft.astype(bf16)
    k_t_ref[...] = key_t
    k_ref[0] = key_t.T
    sig_k_ref[...] = sig.astype(bf16)
    value_t = mm(w_t[1], tok_t).astype(bf16)
    v_t_ref[...] = value_t
    v_ref[0] = value_t.T
    states = (state_a, state_b)
    clear_pad(states)
    cos, sin = table[COS_TAIL : COS_TAIL + 1], table[SIN_TAIL : SIN_TAIL + 1]
    for h in range(HEADS):
        keys = trig_rows(k_t_ref[head_slice(h), :], cos, sin)
        values = with_row(v_t_ref[head_slice(h), :], 1.0)
        put_state(states, h, mm(values, keys, NT))


def pair_rows(ref, pair):
    first = ref[head_slice(2 * pair), :]
    second = ref[head_slice(2 * pair + 1), :]
    nothing = jnp.zeros_like(first)
    return jnp.concatenate(
        [
            jnp.concatenate([first, nothing], axis=1),
            jnp.concatenate([nothing, second], axis=1),
        ],
        axis=0,
    )


def two_parts(v):
    high = v.astype(bf16)
    return high, (v - high.astype(f32)).astype(bf16)


def local_kernel(
    s_ref,
    tab_ref,
    tok_t_ref,
    k_ref,
    v_t_ref,
    wq_ref,
    w_out_ref,
    w_in_ref,
    w_back_ref,
    q_t_ref,
    sig_q_ref,
    numer_ref,
    denom_ref,
    w_out_t,
    w_in_t,
    w_back_t,
    w_t,
):
    @pl.when(pl.program_id(0) == 0)
    def _():
        w_t[...] = wq_ref[...].T
        w_out_t[...] = w_out_ref[...].T

    w_in_t[...] = w_in_ref[...].T
    w_back_t[...] = w_back_ref[...].T

    soft, sig = softplus_sigmoid(mm(w_t[...], tok_t_ref[...]))
    q_t_ref[...] = soft.astype(bf16)
    sig_q_ref[...] = sig.astype(bf16)
    blend = blend_of(tab_ref[0])
    tok_count = blend.shape[0]
    denom_ref[...] = jnp.zeros_like(denom_ref)
    for pair in range(PAIRS):
        lanes = slice(pair * 2 * HEAD_DIM, (pair + 1) * 2 * HEAD_DIM)
        both = mm(k_ref[0, :, lanes], pair_rows(q_t_ref, pair))
        for side in range(2):
            h = 2 * pair + side
            high, low = two_parts(both[:, side * tok_count : (side + 1) * tok_count] * blend)
            values = with_row(v_t_ref[head_slice(h), :], 1.0)
            out = mm(values, high) + mm(values, low)
            numer_ref[head_slice(h), :] = out[:HEAD_DIM]
            denom_ref[h : h + 1, :] = out[HEAD_DIM : HEAD_DIM + 1]


def fold_lanes(v):
    total = v[:, :128]
    for at in range(128, v.shape[1], 128):
        total = total + v[:, at : at + 128]
    return total


def chunks_of(ref):
    return [slice(at, at + 128) for at in range(0, ref.shape[0], 128)]


def fold_rows(v):
    return jnp.sum(v.reshape(v.shape[0] // 8, 8, v.shape[1]), axis=0)


def mean_of(fold, count):
    return jnp.sum(fold, axis=0, keepdims=True) * (1.0 / count)


def center(ref, more=None):
    width, lanes = ref.shape
    fold = jnp.zeros((8, lanes), f32)
    for c in chunks_of(ref):
        value = ref[c, :]
        if more is not None:
            value = value + more[c, :].astype(f32)
            ref[c, :] = value
        fold = fold + fold_rows(value)
    mean = mean_of(fold, width)
    fold = jnp.zeros((8, lanes), f32)
    for c in chunks_of(ref):
        value = ref[c, :] - mean
        ref[c, :] = value
        fold = fold + fold_rows(value * value)
    return lax.rsqrt(mean_of(fold, width) + norm_eps)


def lane_total(ref):
    return jnp.sum(ref[...], axis=1, keepdims=True)


def layer_kernel(
    s_ref,
    tab_ref,
    q_t_ref,
    numer_ref,
    denom_loc_ref,
    state_a,
    state_b,
    tok_t_ref,
    cot_ref,
    w_out_t,
    w_in_t,
    w_back_t,
    w_out_ref,
    w_in_ref,
    w_back_ref,
    gain_one_ref,
    shift_one_ref,
    gain_two_ref,
    shift_two_ref,
    layer_ref,
    att_t_ref,
    first_t_ref,
    active_t_ref,
    grad_second_ref,
    grad_hidden_ref,
    grad_base_ref,
    grad_branch_ref,
    grad_numer_ref,
    grad_denom_ref,
    small_ref,
    out_a,
    out_b,
    slope,
    normed_one,
    attended,
    inverse_denom,
    total,
    fold_gain_one,
    fold_shift_one,
    fold_gain_two,
    fold_shift_two,
    work,
):
    ff = w_in_ref.shape[1]
    step = 768

    @pl.when(pl.program_id(0) == 0)
    def _():
        for ref in (fold_gain_one, fold_shift_one, fold_gain_two, fold_shift_two):
            ref[...] = jnp.zeros_like(ref)

    table = tab_ref[0]
    cos, sin = table[COS_READ : COS_READ + 1], table[SIN_READ : SIN_READ + 1]
    states = (state_a, state_b)
    for h in range(HEADS):
        reads = trig_rows(q_t_ref[head_slice(h), :], cos, sin)
        more = mm(take_state(states, h), reads)
        numer = numer_ref[head_slice(h), :] + more[:HEAD_DIM]
        inverse = 1.0 / (denom_loc_ref[h : h + 1, :] + more[HEAD_DIM : HEAD_DIM + 1])
        inverse_denom[h : h + 1, :] = inverse
        value = numer * inverse
        attended[head_slice(h), :] = value
        att_t_ref[head_slice(h), :] = value.astype(bf16)
    total[...] = mm(w_out_t[...], att_t_ref[...])
    scale_one = center(total, tok_t_ref)
    for c in chunks_of(total):
        normed = total[c, :] * scale_one
        normed_one[c, :] = normed
        first_out = normed * gain_one_ref[c, :] + shift_one_ref[c, :]
        total[c, :] = first_out
        first_t_ref[c, :] = first_out.astype(bf16)
    first_low = first_t_ref[...]
    for at in range(0, ff, step):
        hidden = mm(w_in_t[at : at + step, :], first_low)
        half = 0.5 * (1.0 + lax.erf(hidden * 0.7071067811865476))
        bell = jnp.exp(hidden * hidden * -0.5) * 0.3989422804014327
        active = (hidden * half).astype(bf16)
        active_t_ref[at : at + step, :] = active
        slope[at : at + step, :] = (half + hidden * bell).astype(bf16)
        total[...] += mm(w_back_t[:, at : at + step], active)
    scale_two = center(total)
    fold_one = fold_two = jnp.zeros((8, total.shape[1]), f32)
    for c in chunks_of(total):
        normed = total[c, :] * scale_two
        total[c, :] = normed
        layer_ref[0, :, c] = (normed * gain_two_ref[c, :] + shift_two_ref[c, :]).T.astype(bf16)
        grad_top = cot_ref[0, :, c].T.astype(f32)
        fold_gain_two[c, :] += fold_lanes(grad_top * normed)
        fold_shift_two[c, :] += fold_lanes(grad_top)
        grad_norm = grad_top * gain_two_ref[c, :]
        work[c, :] = grad_norm
        fold_one = fold_one + fold_rows(grad_norm)
        fold_two = fold_two + fold_rows(grad_norm * normed)
    mean_one, mean_two = mean_of(fold_one, total.shape[0]), mean_of(fold_two, total.shape[0])
    for c in chunks_of(total):
        grad_mid = scale_two * (work[c, :] - mean_one - total[c, :] * mean_two)
        total[c, :] = grad_mid
        grad_second_ref[c, :] = grad_mid.astype(bf16)
    grad_second = grad_second_ref[...]
    for at in range(0, ff, step):
        grad_active = mm(w_back_ref[at : at + step, :], grad_second)
        low = (grad_active * slope[at : at + step, :].astype(f32)).astype(bf16)
        grad_hidden_ref[at : at + step, :] = low
        total[...] += mm(w_in_ref[:, at : at + step], low)
    fold_one = fold_two = jnp.zeros((8, total.shape[1]), f32)
    for c in chunks_of(total):
        grad_first, normed = total[c, :], normed_one[c, :]
        fold_gain_one[c, :] += fold_lanes(grad_first * normed)
        fold_shift_one[c, :] += fold_lanes(grad_first)
        grad_norm = grad_first * gain_one_ref[c, :]
        work[c, :] = grad_norm
        fold_one = fold_one + fold_rows(grad_norm)
        fold_two = fold_two + fold_rows(grad_norm * normed)
    mean_one, mean_two = mean_of(fold_one, total.shape[0]), mean_of(fold_two, total.shape[0])
    for c in chunks_of(total):
        grad_base = scale_one * (work[c, :] - mean_one - normed_one[c, :] * mean_two)
        grad_base_ref[c, :] = grad_base
        grad_branch_ref[c, :] = grad_base.astype(bf16)
    grad_branch = grad_branch_ref[...]
    total[...] = mm(w_out_ref[...], grad_branch)
    outs = (out_a, out_b)
    clear_pad(outs)
    grad_denom_ref[...] = jnp.zeros_like(grad_denom_ref)
    for h in range(HEADS):
        rows = head_slice(h)
        grad_numer = (total[rows, :] * inverse_denom[h : h + 1, :]).astype(bf16)
        grad_denom = -jnp.sum(grad_numer.astype(f32) * attended[rows, :], axis=0, keepdims=True)
        grad_denom_ref[h : h + 1, :] = grad_denom
        grad_numer_ref[rows, :] = grad_numer
        reads = trig_rows(q_t_ref[rows, :], cos, sin)
        put_state(outs, h, mm(with_row(grad_numer, grad_denom), reads, NT))

    @pl.when(pl.program_id(0) == pl.num_programs(0) - 1)
    def _():
        lane = lax.broadcasted_iota(jnp.int32, small_ref.shape, 1)
        value = jnp.zeros(small_ref.shape, f32)
        for i, ref in enumerate((fold_gain_one, fold_shift_one, fold_gain_two, fold_shift_two)):
            value = jnp.where(lane == i, lane_total(ref), value)
        small_ref[...] = value


def local_back_kernel(
    s_ref,
    tab_ref,
    q_t_ref,
    k_t_ref,
    k_ref,
    v_ref,
    sig_q_ref,
    grad_numer_ref,
    grad_denom_ref,
    state_a,
    state_b,
    grad_q_ref,
    grad_k_ref,
    grad_v_ref,
):
    table = tab_ref[0]
    blend = blend_of(table)
    tok_count = blend.shape[0]
    cos, sin = table[COS_READ : COS_READ + 1], table[SIN_READ : SIN_READ + 1]
    states = (state_a, state_b)
    for pair in range(PAIRS):
        lanes = slice(pair * 2 * HEAD_DIM, (pair + 1) * 2 * HEAD_DIM)
        both = mm(k_ref[0, :, lanes], pair_rows(q_t_ref, pair))
        grads = mm(v_ref[0, :, lanes], pair_rows(grad_numer_ref, pair))
        for side in range(2):
            h = 2 * pair + side
            rows = head_slice(h)
            part = slice(side * tok_count, (side + 1) * tok_count)
            grad_denom = grad_denom_ref[h : h + 1, :]
            scores = (both[:, part] * blend).astype(bf16)
            grad_scores, rest = two_parts((grads[:, part] + grad_denom) * blend)
            grad_numer = grad_numer_ref[rows, :]
            grad_v_ref[rows, :] = mm(grad_numer, scores, NT)
            grad_k_ref[rows, :] = mm(q_t_ref[rows, :], grad_scores, NT)
            reads = mm(take_state(states, h), with_row(grad_numer, grad_denom), TN)
            grad_q = (
                mm(k_t_ref[rows, :], grad_scores)
                + mm(k_t_ref[rows, :], rest)
                + cos * reads[:HEAD_DIM]
                + sin * reads[HEAD_DIM:]
            )
            grad_q_ref[rows, :] = (grad_q * sig_q_ref[rows, :].astype(f32)).astype(bf16)


def tail_kernel(
    s_ref,
    tab_ref,
    k_t_ref,
    v_t_ref,
    sig_k_ref,
    state_a,
    state_b,
    grad_k_in,
    grad_v_in,
    grad_kv_ref,
):
    table = tab_ref[0]
    cos, sin = table[COS_TAIL : COS_TAIL + 1], table[SIN_TAIL : SIN_TAIL + 1]
    states = (state_a, state_b)
    for h in range(HEADS):
        rows = head_slice(h)
        state = take_state(states, h)
        inner = mm(state, with_row(v_t_ref[rows, :], 1.0), TN)
        grad_k = grad_k_in[rows, :] + cos * inner[:HEAD_DIM] + sin * inner[HEAD_DIM:]
        grad_kv_ref[0, rows, :] = (grad_k * sig_k_ref[rows, :].astype(f32)).astype(bf16)
        keys = trig_rows(k_t_ref[rows, :], cos, sin)
        grad_kv_ref[1, rows, :] = (grad_v_in[rows, :] + mm(state[:HEAD_DIM], keys)).astype(bf16)


def token_kernel(s_ref, gq_ref, gkv_ref, base_ref, wq_ref, wk_ref, wv_ref, out_ref):
    total = base_ref[...] + mm(wq_ref[...], gq_ref[...])
    total = total + mm(wk_ref[...], gkv_ref[0])
    total = total + mm(wv_ref[...], gkv_ref[1])
    out_ref[0] = total.T


def spec(block, index):
    return pl.BlockSpec(block, index)


NEAR = pl.BlockSpec(memory_space=pltpu.VMEM)

CORE, ODD, PLACE = range(3)


class Order:
    def __init__(self, scalars):
        self.scalars = scalars

    def call(
        self, kernel, grid, ins, outs, scratch, args, extra=(), free=(), near=(), near_out=(), limit=VMEM_LIMIT
    ):
        count = 1 + len(extra)
        placed = len(scratch)

        def stepped(*refs):
            s_ref, handed = refs[0], refs[len(refs) - placed - 1]
            rest = refs[: len(refs) - placed - 1] + refs[len(refs) - placed :]
            kernel(*rest)
            for i in range(s_ref.shape[0]):
                handed[i] = s_ref[i]

        *values, self.scalars = pl.pallas_call(
            stepped,
            grid_spec=pltpu.PrefetchScalarGridSpec(
                num_scalar_prefetch=count,
                grid=grid,
                in_specs=ins,
                out_specs=[o for o, _ in outs] + [pl.BlockSpec(memory_space=pltpu.SMEM)],
                scratch_shapes=scratch,
            ),
            out_shape=[
                (pltpu.VMEM if i in near_out else pltpu.HBM)(shape, kind)
                for i, (_, (shape, kind)) in enumerate(outs)
            ]
            + [jax.ShapeDtypeStruct(self.scalars.shape, jnp.int32)],
            compiler_params=pltpu.CompilerParams(
                dimension_semantics=("arbitrary",) * len(grid), vmem_limit_bytes=limit
            ),
            cost_estimate=pl.CostEstimate(flops=1000000000000, bytes_accessed=1, transcendentals=0),
        )(
            self.scalars,
            *extra,
            *[
                v
                if i in free
                else pltpu.with_memory_space_constraint(v, pltpu.VMEM if i in near else pltpu.HBM)
                for i, v in enumerate(args)
            ],
        )
        return values


def pick_halves(core, value):
    cut = value.shape[1] // 2
    low, high = value[:, :cut], value[:, cut:]
    return jnp.where(core == 0, high, low), jnp.where(core == 0, low, high)


def tall_kernel(s_ref, a_ref, b_ref, away_ref, keep_ref):
    away_ref[...], keep_ref[...] = pick_halves(s_ref[CORE], mm(a_ref[...], b_ref[...], NT))


def tall_product(order, a, b):
    count, flat = a.shape
    tile, cut = count // 4, b.shape[0] // 2
    out = (spec((tile, cut), lambda i, *s: (i, 0)), ((count, cut), f32))
    ins = [spec((tile, flat), lambda i, *s: (i, 0)), spec(b.shape, lambda i, *s: (0, 0))]
    return order.call(tall_kernel, (4,), ins, [out, out], [], (a, b))


def wide_kernel(s_ref, a_ref, b_ref, away_ref, keep_ref):
    value = mm(a_ref[...], b_ref[...], NT)
    first = pl.program_id(0) < pl.num_programs(0) // 2

    @pl.when(first)
    def _():
        away_ref[...] = value

    @pl.when(jnp.logical_not(first))
    def _():
        keep_ref[...] = value


def wide_product(order, a, b):
    count, flat = a.shape
    cut = b.shape[0] // 2
    tile = 512
    half = cut // tile

    def source(i, s):
        return jnp.where(i < half, (1 - s[CORE]) * half + i, s[CORE] * half + i - half), 0

    outs = [
        (spec((count, tile), lambda i, s: (0, jnp.minimum(i, half - 1))), ((count, cut), f32)),
        (spec((count, tile), lambda i, s: (0, jnp.maximum(i - half, 0))), ((count, cut), f32)),
    ]
    ins = [spec(a.shape, lambda i, s: (0, 0)), spec((tile, flat), source)]
    return order.call(wide_kernel, (2 * half,), ins, outs, [], (a, b))


def twin_kernel(s_ref, a_ref, b_ref, c_ref, d_ref, *refs):
    core = s_ref[CORE]
    away_ref, keep_ref = refs[-2:]
    at = 0
    for left, right in ((a_ref, b_ref[0]), (c_ref, d_ref[0])):
        away, keep = pick_halves(core, mm(left[...], right, NT))
        away_ref[:, at : at + away.shape[1]] = away
        keep_ref[:, at : at + keep.shape[1]] = keep
        at += away.shape[1]
    if len(refs) == 3:
        value = refs[0][...]
        away_ref[:, at:] = jnp.where(core == 0, 0.0, value)
        keep_ref[:, at:] = jnp.where(core == 0, value, 0.0)


def twin_product(order, a, b, c, d, small=None):
    count, flat = a.shape
    tile = count // 2
    columns = count + (0 if small is None else small.shape[1])
    rows = spec((tile, flat), lambda i, s: (i, 0))
    ins, args = [], []
    for left, (right, group) in ((a, b), (c, d)):
        ins += [rows, spec((1, count, flat), lambda i, s, g=group: (g, 0, 0))]
        args += [left, right]
    if small is not None:
        ins.append(spec((tile, small.shape[1]), lambda i, s: (i, 0)))
        args.append(small)
    out = (spec((tile, columns), lambda i, s: (i, 0)), ((count, columns), f32))
    return order.call(twin_kernel, (2,), ins, [out, out], [], args)


def route_kernel(s_ref, *refs):
    for i in range(4):
        refs[8 + i][...] = refs[2 * i][...] + refs[2 * i + 1][...]


def route(order, left, right, low_bit, high_bit):
    (a, b), (c, d) = left, right
    shards, rows, columns = a.shape
    same = a is c
    if same:
        rows //= 2
    lower = 1 if same else 0
    half = shards // 2

    def by_low(flip):
        def index(i, s):
            mine = (s[PLACE] >> low_bit) & 1
            return 2 * i + ((1 - mine) if flip else mine), 0, 0

        return index

    def by_high(flip):
        def index(i, s):
            mine = (s[PLACE] >> high_bit) & 1
            return i + ((1 - mine) if flip else mine) * half, lower, 0

        return index

    block = (1, rows, columns)
    maps = [by_low(True), by_low(False), by_high(True), by_high(False)]
    ins = [spec(block, m) for m in maps for _ in range(2)]
    out = (spec(block, lambda i, s: (i, 0, 0)), ((half, rows, columns), f32))
    return order.call(route_kernel, (half,), ins, [out] * 4, [], (a, b, a, b, c, d, c, d))


def choose_kernel(s_ref, a_ref, b_ref, c_ref, d_ref, away_ref, kept_ref):
    upper, lower = a_ref[0] + b_ref[0], c_ref[0] + d_ref[0]
    odd = s_ref[ODD] == 1
    away_ref[...] = jnp.where(odd, upper, lower)
    kept_ref[...] = jnp.where(odd, lower, upper)


def choose(order, left, right):
    shape = left[0].shape[1:]
    return order.call(
        choose_kernel,
        (1,),
        [NEAR] * 4,
        [(NEAR, (shape, f32))] * 2,
        [],
        (*left, *right),
        free=range(4),
        near_out=range(2),
        limit=SMALL_LIMIT,
    )


def add_kernel(s_ref, a_ref, b_ref, out_ref):
    out_ref[...] = a_ref[...] + b_ref[...]


def add(order, a, b):
    outs = [(NEAR, (a.shape, f32))]
    return order.call(
        add_kernel, (1,), [NEAR] * 2, outs, [], (a, b), near=range(2), near_out=range(1), limit=SMALL_LIMIT
    )[0]


def merge_kernel(s_ref, kept_ref, got_ref, out_ref):
    odd = s_ref[ODD] == 1
    rows = kept_ref.shape[0]
    kept, got = kept_ref[...], got_ref[...]
    out_ref[:rows, :] = jnp.where(odd, got, kept)
    out_ref[rows:, :] = jnp.where(odd, kept, got)


def merge(order, kept, got):
    rows, columns = kept.shape
    outs = [(NEAR, ((2 * rows, columns), f32))]
    return order.call(
        merge_kernel,
        (1,),
        [NEAR] * 2,
        outs,
        [],
        (kept, got),
        near=range(2),
        near_out=range(1),
        limit=SMALL_LIMIT,
    )[0]


def side_kernel(s_ref, mine_ref, other_ref, *outs):
    first = s_ref[CORE] == 0
    at = 0
    for out in outs:
        cut = out.shape[1] // 2
        if cut < 128:
            out[...] = jnp.where(first, mine_ref[:, at:], other_ref[:, at:])
            break
        mine, other = mine_ref[:, at : at + cut], other_ref[:, at : at + cut]
        out[:, :cut] = jnp.where(first, mine, other)
        out[:, cut:] = jnp.where(first, other, mine)
        at += cut


def side(order, mine, other, widths):
    rows = mine.shape[0]
    outs = [(spec((rows, w), lambda i, s: (0, 0)), ((rows, w), f32)) for w in widths]
    return order.call(
        side_kernel, (1,), [NEAR] * 2, outs, [], (mine, other), near=range(2), limit=SMALL_LIMIT
    )


def mix_kernel(first, s_ref, w_ref, *refs):
    for row in range(refs[0].shape[0]):
        for i in range(2):
            own, other = (w_ref[first + 2 * i + j, row] for j in range(2))
            refs[4 + i][row] = own * refs[2 * i][row] + other * refs[2 * i + 1][row]


def mix(order, weights, first, last, *parts):
    shape = parts[0].shape
    out = spec(shape, lambda i, *s: (0, 0, 0)) if last else NEAR
    return order.call(
        partial(mix_kernel, first),
        (1,),
        [NEAR] * 4,
        [(out, (shape, f32))] * 2,
        [],
        parts,
        (weights,),
        near=range(4),
        near_out=() if last else range(2),
        limit=SMALL_LIMIT,
    )


def first_begins(lengths, count, tok_count):
    slots = lengths.shape[1]
    order = jnp.arange(slots)
    before = (order[:, None] > order[None, :]).astype(jnp.int32)
    starts = jnp.sum(lengths[:, None, :] * before[None], axis=-1)
    firsts = jnp.arange(count, dtype=jnp.int32) * tok_count
    reached = starts[:, None, :] <= firsts[None, :, None]
    return jnp.max(jnp.where(reached, starts[:, None, :], 0), axis=-1)


def pick(index, values):
    out = values[0]
    for i in range(1, len(values)):
        out = jnp.where(index == i, values[i], out)
    return out


def weights_of(begin_first, tok_count, reverse):
    count = lax.axis_size("seq")
    place = lax.axis_index("seq")

    def covers(i, j):
        low, high = (count - 1 - j, count - 1 - i) if reverse else (i, j)
        return (begin_first[:, high] < (low + 1) * tok_count).astype(f32)

    if count != 4:
        spots = jnp.arange(count)
        mine = begin_first.T if reverse else begin_first[:, place][None]
        reach = (place if reverse else spots[:, None]) + 1
        ahead = (spots > place) if reverse else (spots < place)
        return ((mine < reach * tok_count) & ahead[:, None]).astype(f32)
    index = count - 1 - place if reverse else place
    zero = jnp.zeros_like(begin_first[:, 0], f32)
    one = zero + 1.0
    m02, m03, m13 = covers(0, 2), covers(0, 3), covers(1, 3)
    onward = [
        pick(index, [m02, m13, zero, zero]),
        pick(index, [one, m03, zero, zero]),
        pick(index, [one, zero, one, zero]),
        pick(index, [zero, zero, m03, one]),
    ]
    final = [
        pick(index, [zero, one, zero, one]),
        pick(index, [zero, zero, one, one]),
        pick(index, [zero, zero, m02, m13]),
        pick(index, [zero, one, one, one]),
    ]
    return onward + final


def entering(order, parts, weights, first):
    if lax.axis_size("seq") != 4:
        gathered = [lax.all_gather(p, "seq") for p in parts]
        yield
        yield
        yield tuple(jnp.sum(g * weights[first][:, :, None, None], axis=0) for g in gathered)
    part_a, part_b = parts
    got_a, got_b = swap(part_a, "seq", 1), swap(part_b, "seq", 2)
    yield
    next_a, next_b = mix(order, weights, first, False, part_a, got_a, part_b, got_b)
    last_a, last_b = swap(next_a, "seq", 2), swap(next_b, "seq", 1)
    yield
    yield mix(order, weights, first + 4, True, got_a, last_a, got_b, last_b)


def swap(value, axis, distance):
    count = lax.axis_size(axis)
    return lax.ppermute(value, axis, [(i, i ^ distance) for i in range(count)])


def reduced(order, away, keep, widths):
    count = lax.axis_size("batch")
    shards = lax.axis_size("seq")
    bits = shards.bit_length() - 1
    shape = (shards, keep.shape[0] // shards, keep.shape[1])
    got = swap(away, "batch", 1).reshape(shape)
    yield
    left = right = (keep.reshape(shape), got)
    for step in range(bits):
        high = bits - 1 - step
        away_l, keep_l, away_r, keep_r = route(order, left, right, step, high)
        left = keep_l, swap(away_l, "seq", 1 << step)
        right = keep_r, swap(away_r, "seq", 1 << high)
        yield
    away, kept = choose(order, left, right)
    got = swap(away, "batch", 2)
    distance = 4
    while distance < count:
        yield
        kept = add(order, kept, got)
        got = swap(kept, "batch", distance)
        distance *= 2
    yield
    kept = add(order, kept, got)
    got = swap(kept, "batch", 2)
    yield
    merged = merge(order, kept, got)
    other = swap(merged, "batch", 1)
    yield
    yield side(order, merged, other, widths)


SCHEDULE = (
    "in_product", "states", "back_product", "in", "states", "back",
    "local", "mixed_product", "tail", "in", "back", "in",
    "mixed", "back", "mixed", "back", "last_product", "mixed",
    "last", "in", "back", "last", "mixed", "last",
    "in", "back", "last", "tokens", "mixed", "back",
    "last", "in", "mixed", "last", "in", "mixed",
    "last",
)


def body(
    tokens,
    cotangent,
    doc_lengths,
    w_query,
    w_key,
    w_value,
    w_out,
    w_in,
    w_back,
    gain_one,
    shift_one,
    gain_two,
    shift_two,
):
    rows, toks, width = tokens.shape
    ff = w_in.shape[1]
    flat = rows * toks
    shards = lax.axis_size("seq")
    whole = pl.BlockSpec(memory_space=pltpu.VMEM)
    token_major = pl.BlockSpec((1, toks, width), lambda r, *s: (r, 0, 0))
    table_spec = pl.BlockSpec((1, 8, toks), lambda r, *s: (r, 0, 0))
    state_spec = pl.BlockSpec((1, STATE_ROWS, 2 * HEAD_DIM), lambda r, *s: (r, 0, 0))

    def feature(count):
        return pl.BlockSpec((count, toks), lambda r, *s: (0, r))

    tok_low = (token_major, ((rows, toks, width), bf16))
    wide_low = (feature(width), ((width, flat), bf16))
    wide_full = (feature(width), ((width, flat), f32))
    ff_low = (feature(ff), ((ff, flat), bf16))
    head_rows = (feature(16), ((16, flat), f32))
    fold = (pl.BlockSpec((width, 128), lambda r, *s: (0, 0)), ((width, 128), f32))
    state = (state_spec, ((rows, STATE_ROWS, 2 * HEAD_DIM), f32))
    grid = (rows,)

    batch_place = lax.axis_index("batch").astype(jnp.int32)
    scalars = jnp.stack(
        [batch_place & 1, (batch_place >> 1) & 1, lax.axis_index("seq").astype(jnp.int32)]
    )
    order = Order(scalars)

    def run(kernel, ins, outs, scratch, *args, **more):
        return order.call(kernel, grid, ins, outs, scratch, args, **more)

    def column(v):
        return v[:, None]

    table, tok_t, k_t, v_t, key, value, sig_k, state_a, state_b = run(
        project_kernel,
        [token_major, whole, whole],
        [(table_spec, ((rows, 8, toks), f32))]
        + [wide_low] * 3
        + [tok_low] * 2
        + [wide_low]
        + [state] * 2,
        [pltpu.VMEM((2, width, width), bf16)],
        tokens,
        w_key,
        w_value,
        extra=(doc_lengths,),
    )
    begins = first_begins(doc_lengths, shards, toks)
    if shards == 4:
        weights = jnp.stack(weights_of(begins, toks, False) + weights_of(begins, toks, True))
        later = 8
    else:
        weights = [weights_of(begins, toks, False), weights_of(begins, toks, True)]
        later = 1
    states = entering(order, (state_a, state_b), weights, 0)
    next(states)
    part = ff // rows
    q_t, sig_q, numer, denom_loc, w_out_t, w_in_t, w_back_t = run(
        local_kernel,
        [
            table_spec,
            feature(width),
            token_major,
            feature(width),
            whole,
            whole,
            pl.BlockSpec((width, part), lambda r, *s: (0, r)),
            pl.BlockSpec((part, width), lambda r, *s: (r, 0)),
        ],
        [
            wide_low,
            wide_low,
            wide_full,
            head_rows,
            (pl.BlockSpec((width, width), lambda r, *s: (0, 0)), ((width, width), bf16)),
            (pl.BlockSpec((part, width), lambda r, *s: (r, 0)), ((ff, width), bf16)),
            (pl.BlockSpec((width, part), lambda r, *s: (0, r)), ((width, ff), bf16)),
        ],
        [pltpu.VMEM((width, width), bf16)],
        table,
        tok_t,
        key,
        v_t,
        w_query,
        w_out,
        w_in,
        w_back,
    )
    next(states)
    in_a, in_b = next(states)
    (
        layer_out,
        att_t,
        first_t,
        active_t,
        grad_second,
        grad_hidden,
        grad_base,
        grad_branch,
        grad_numer,
        grad_denom,
        small,
        out_a,
        out_b,
    ) = run(
        layer_kernel,
        [
            table_spec,
            feature(width),
            feature(width),
            feature(16),
            state_spec,
            state_spec,
            feature(width),
            token_major,
        ]
        + [whole] * 10,
        [
            tok_low,
            wide_low,
            wide_low,
            ff_low,
            wide_low,
            ff_low,
            wide_full,
            wide_low,
            wide_low,
            head_rows,
            fold,
            state,
            state,
        ],
        [
            pltpu.VMEM((ff, toks), bf16),
            pltpu.VMEM((width, toks), f32),
            pltpu.VMEM((width, toks), f32),
            pltpu.VMEM((16, toks), f32),
            pltpu.VMEM((width, toks), f32),
        ]
        + [pltpu.VMEM((width, 128), f32)] * 4
        + [pltpu.VMEM((width, toks), f32)],
        table,
        q_t,
        numer,
        denom_loc,
        in_a,
        in_b,
        tok_t,
        cotangent,
        w_out_t,
        w_in_t,
        w_back_t,
        w_out,
        w_in,
        w_back,
        column(gain_one),
        column(shift_one),
        column(gain_two),
        column(shift_two),
        near=range(8, 14),
        limit=LAYER_LIMIT,
    )

    back_states = entering(order, (out_a, out_b), weights, later)
    next(back_states)
    pieces, made = {}, {}

    def begin(name, product, widths):
        pieces[name] = reduced(order, *product, widths)
        next(pieces[name])

    def local_back():
        made["query"], made["key"], made["value"] = run(
            local_back_kernel,
            [
                table_spec,
                feature(width),
                feature(width),
                token_major,
                token_major,
                feature(width),
                feature(width),
                feature(16),
                state_spec,
                state_spec,
            ],
            [wide_low, wide_full, wide_full],
            [],
            table,
            q_t,
            k_t,
            key,
            value,
            sig_q,
            grad_numer,
            grad_denom,
            in_a,
            in_b,
        )

    def tail():
        back_a, back_b = made["states"]
        (made["kv"],) = run(
            tail_kernel,
            [table_spec]
            + [feature(width)] * 3
            + [state_spec] * 2
            + [feature(width)] * 2,
            [(pl.BlockSpec((2, width, toks), lambda r, *s: (0, 0, r)), ((2, width, flat), bf16))],
            [],
            table,
            k_t,
            v_t,
            sig_k,
            back_a,
            back_b,
            made["key"],
            made["value"],
        )

    def token_grads():
        (made["tokens"],) = run(
            token_kernel,
            [
                feature(width),
                pl.BlockSpec((2, width, toks), lambda r, *s: (0, 0, r)),
                feature(width),
            ]
            + [whole] * 3,
            [(token_major, ((rows, toks, width), f32))],
            [],
            made["query"],
            made["kv"],
            grad_base,
            w_query,
            w_key,
            w_value,
        )

    def states_on():
        made["states"] = next(back_states)

    steps = {
        "back_product": lambda: begin("back", tall_product(order, active_t, grad_second), (width,)),
        "in_product": lambda: begin("in", wide_product(order, first_t, grad_hidden), (ff,)),
        "mixed_product": lambda: begin(
            "mixed",
            twin_product(order, att_t, (grad_branch[None], 0), tok_t, (made["query"][None], 0), small),
            (width, width, 128),
        ),
        "last_product": lambda: begin(
            "last",
            twin_product(order, tok_t, (made["kv"], 0), tok_t, (made["kv"], 1)),
            (width, width),
        ),
        "states": states_on,
        "local": local_back,
        "tail": tail,
        "tokens": token_grads,
    }
    ends = {}

    def step(name):
        value = next(pieces[name])
        if value is not None:
            ends[name] = value

    for name in SCHEDULE:
        if name in steps:
            steps[name]()
        elif name not in ends:
            step(name)
    while len(ends) < len(pieces):
        for name in pieces:
            if name not in ends:
                step(name)
    (total_back,), (total_in,) = ends["back"], ends["in"]
    total_out, total_query, vectors = ends["mixed"]
    total_key, total_value = ends["last"]
    grad_tokens = made["tokens"]
    return (
        layer_out,
        grad_tokens,
        total_query,
        total_key,
        total_value,
        total_out,
        total_in,
        total_back,
        vectors[:, 0],
        vectors[:, 1],
        vectors[:, 2],
        vectors[:, 3],
    )


def solution(mesh):
    in_specs = (
        P("batch", "seq", None),
        P("batch", "seq", None),
        P("batch", None),
        P(),
        P(),
        P(),
        P(),
        P(),
        P(),
        P(),
        P(),
        P(),
        P(),
    )
    out_specs = (
        P("batch", "seq", None),
        P("batch", "seq", None),
        P("seq", None),
        P("seq", None),
        P("seq", None),
        P("seq", None),
        P("seq", None),
        P("seq", None),
        P("seq"),
        P("seq"),
        P("seq"),
        P("seq"),
    )
    return jax.shard_map(body, mesh=mesh, in_specs=in_specs, out_specs=out_specs, check_vma=False)
```

```python
from functools import partial

import jax
import jax.numpy as jnp
from jax import lax
from jax.experimental import pallas as pl
from jax.experimental.pallas import tpu as pltpu
from jax.sharding import PartitionSpec as P

HEADS = 12
HEAD_DIM = 64
PAIRS = HEADS // 2
HALF_HEADS = HEADS // 2
STATE_ROWS = HALF_HEADS * HEAD_DIM + 8

f32 = jnp.float32
bf16 = jnp.bfloat16
half_pi = 1.5707963267948966
norm_eps = 1e-05
VMEM_LIMIT = 30 * 1024 * 1024
SMALL_LIMIT = 16 * 1024 * 1024
LAYER_LIMIT = 38 * 1024 * 1024

NN = (((1,), (0,)), ((), ()))
NT = (((1,), (1,)), ((), ()))
TN = (((0,), (0,)), ((), ()))


def mm(a, b, dims=NN):
    return lax.dot_general(a, b, dims, preferred_element_type=f32)


COS, SIN, BEGIN, COS_READ, SIN_READ, COS_TAIL, SIN_TAIL = range(7)


def make_table(place, lens_ref, row, tok_count):
    pos = place + lax.broadcasted_iota(jnp.int32, (8, tok_count), 1)
    last = place + tok_count - 1
    start = jnp.int32(0)
    begin = jnp.zeros((8, tok_count), jnp.int32)
    span = jnp.ones((8, tok_count), jnp.int32)
    last_begin = jnp.int32(0)
    for d in range(lens_ref.shape[1]):
        length = lens_ref[row, d]
        inside = pos >= start
        begin = jnp.where(inside, start, begin)
        span = jnp.where(inside, length, span)
        last_begin = jnp.where(start <= last, start, last_begin)
        start = start + length
    angle = half_pi * (pos - begin).astype(f32) / span.astype(f32)
    cos, sin = jnp.cos(angle), jnp.sin(angle)
    reader = (begin < place).astype(f32)
    tail = (begin == last_begin).astype(f32)
    which = lax.broadcasted_iota(jnp.int32, (8, tok_count), 0)
    table = jnp.zeros((8, tok_count), f32)
    for index, value in (
        (COS, cos),
        (SIN, sin),
        (BEGIN, begin.astype(f32)),
        (COS_READ, cos * reader),
        (SIN_READ, sin * reader),
        (COS_TAIL, cos * tail),
        (SIN_TAIL, sin * tail),
    ):
        table = jnp.where(which == index, value, table)
    return table


def blend_of(table):
    columns = table.T
    tok_count = table.shape[1]
    source = lax.broadcasted_iota(jnp.int32, (tok_count, tok_count), 0)
    reader = lax.broadcasted_iota(jnp.int32, (tok_count, tok_count), 1)
    same = (columns[:, BEGIN : BEGIN + 1] == table[BEGIN : BEGIN + 1]) & (source <= reader)
    value = (
        columns[:, COS : COS + 1] * table[COS : COS + 1]
        + columns[:, SIN : SIN + 1] * table[SIN : SIN + 1]
    )
    return jnp.where(same, value, 0.0)


def trig_rows(head_rows, cos, sin):
    wide = head_rows.astype(f32)
    return jnp.concatenate([(wide * cos).astype(bf16), (wide * sin).astype(bf16)], axis=0)


def with_row(rows, extra):
    which = lax.broadcasted_iota(jnp.int32, (16, rows.shape[1]), 0)
    return jnp.concatenate([rows, jnp.where(which == 0, extra, 0.0).astype(bf16)], axis=0)


def head_slice(h):
    return slice(h * HEAD_DIM, (h + 1) * HEAD_DIM)


def put_state(state_refs, h, value):
    ref = state_refs[h // HALF_HEADS]
    place = h % HALF_HEADS
    ref[0, head_slice(place), :] = value[:HEAD_DIM]
    ref[0, HALF_HEADS * HEAD_DIM + place : HALF_HEADS * HEAD_DIM + place + 1, :] = value[
        HEAD_DIM : HEAD_DIM + 1
    ]


def take_state(state_refs, h):
    ref = state_refs[h // HALF_HEADS]
    place = h % HALF_HEADS
    mats = ref[0, head_slice(place), :].astype(bf16)
    sums = ref[0, HALF_HEADS * HEAD_DIM + place : HALF_HEADS * HEAD_DIM + place + 1, :]
    return with_row(mats, sums)


def clear_pad(state_refs):
    for ref in state_refs:
        ref[0, HALF_HEADS * HEAD_DIM :, :] = jnp.zeros((8, 2 * HEAD_DIM), f32)


def softplus_sigmoid(v):
    small = jnp.exp(-jnp.abs(v))
    soft = jnp.maximum(v, 0.0) + jnp.log1p(small)
    inverse = 1.0 / (1.0 + small)
    return soft, jnp.where(v >= 0, inverse, small * inverse)


def project_kernel(
    s_ref,
    lens_ref,
    tok_ref,
    wk_ref,
    wv_ref,
    tab_ref,
    tok_t_ref,
    k_t_ref,
    v_t_ref,
    k_ref,
    v_ref,
    sig_k_ref,
    state_a,
    state_b,
    w_t,
):
    row = pl.program_id(0)

    @pl.when(row == 0)
    def _():
        w_t[0] = wk_ref[...].T
        w_t[1] = wv_ref[...].T

    tok_t = tok_ref[0].T
    tok_t_ref[...] = tok_t
    table = make_table(s_ref[PLACE] * tok_t.shape[1], lens_ref, row, tok_t.shape[1])
    tab_ref[0] = table
    soft, sig = softplus_sigmoid(mm(w_t[0], tok_t))
    key_t = soft.astype(bf16)
    k_t_ref[...] = key_t
    k_ref[0] = key_t.T
    sig_k_ref[...] = sig.astype(bf16)
    value_t = mm(w_t[1], tok_t).astype(bf16)
    v_t_ref[...] = value_t
    v_ref[0] = value_t.T
    states = (state_a, state_b)
    clear_pad(states)
    cos, sin = table[COS_TAIL : COS_TAIL + 1], table[SIN_TAIL : SIN_TAIL + 1]
    for h in range(HEADS):
        keys = trig_rows(k_t_ref[head_slice(h), :], cos, sin)
        values = with_row(v_t_ref[head_slice(h), :], 1.0)
        put_state(states, h, mm(values, keys, NT))


def pair_rows(ref, pair):
    first = ref[head_slice(2 * pair), :]
    second = ref[head_slice(2 * pair + 1), :]
    nothing = jnp.zeros_like(first)
    return jnp.concatenate(
        [
            jnp.concatenate([first, nothing], axis=1),
            jnp.concatenate([nothing, second], axis=1),
        ],
        axis=0,
    )


def two_parts(v):
    high = v.astype(bf16)
    return high, (v - high.astype(f32)).astype(bf16)


def local_kernel(
    s_ref,
    tab_ref,
    tok_t_ref,
    k_ref,
    v_t_ref,
    wq_ref,
    w_out_ref,
    w_in_ref,
    w_back_ref,
    q_t_ref,
    sig_q_ref,
    numer_ref,
    denom_ref,
    w_out_t,
    w_in_t,
    w_back_t,
    w_t,
):
    @pl.when(pl.program_id(0) == 0)
    def _():
        w_t[...] = wq_ref[...].T
        w_out_t[...] = w_out_ref[...].T

    w_in_t[...] = w_in_ref[...].T
    w_back_t[...] = w_back_ref[...].T

    soft, sig = softplus_sigmoid(mm(w_t[...], tok_t_ref[...]))
    q_t_ref[...] = soft.astype(bf16)
    sig_q_ref[...] = sig.astype(bf16)
    blend = blend_of(tab_ref[0])
    tok_count = blend.shape[0]
    denom_ref[...] = jnp.zeros_like(denom_ref)
    for pair in range(PAIRS):
        lanes = slice(pair * 2 * HEAD_DIM, (pair + 1) * 2 * HEAD_DIM)
        both = mm(k_ref[0, :, lanes], pair_rows(q_t_ref, pair))
        for side in range(2):
            h = 2 * pair + side
            high, low = two_parts(both[:, side * tok_count : (side + 1) * tok_count] * blend)
            values = with_row(v_t_ref[head_slice(h), :], 1.0)
            out = mm(values, high) + mm(values, low)
            numer_ref[head_slice(h), :] = out[:HEAD_DIM]
            denom_ref[h : h + 1, :] = out[HEAD_DIM : HEAD_DIM + 1]


def fold_lanes(v):
    total = v[:, :128]
    for at in range(128, v.shape[1], 128):
        total = total + v[:, at : at + 128]
    return total


def chunks_of(ref):
    return [slice(at, at + 128) for at in range(0, ref.shape[0], 128)]


def fold_rows(v):
    return jnp.sum(v.reshape(v.shape[0] // 8, 8, v.shape[1]), axis=0)


def mean_of(fold, count):
    return jnp.sum(fold, axis=0, keepdims=True) * (1.0 / count)


def center(ref, more=None):
    width, lanes = ref.shape
    fold = jnp.zeros((8, lanes), f32)
    for c in chunks_of(ref):
        value = ref[c, :]
        if more is not None:
            value = value + more[c, :].astype(f32)
            ref[c, :] = value
        fold = fold + fold_rows(value)
    mean = mean_of(fold, width)
    fold = jnp.zeros((8, lanes), f32)
    for c in chunks_of(ref):
        value = ref[c, :] - mean
        ref[c, :] = value
        fold = fold + fold_rows(value * value)
    return lax.rsqrt(mean_of(fold, width) + norm_eps)


def lane_total(ref):
    return jnp.sum(ref[...], axis=1, keepdims=True)


def layer_kernel(
    s_ref,
    tab_ref,
    q_t_ref,
    numer_ref,
    denom_loc_ref,
    state_a,
    state_b,
    tok_t_ref,
    cot_ref,
    w_out_t,
    w_in_t,
    w_back_t,
    w_out_ref,
    w_in_ref,
    w_back_ref,
    gain_one_ref,
    shift_one_ref,
    gain_two_ref,
    shift_two_ref,
    layer_ref,
    att_t_ref,
    first_t_ref,
    active_t_ref,
    grad_second_ref,
    grad_hidden_ref,
    grad_base_ref,
    grad_branch_ref,
    grad_numer_ref,
    grad_denom_ref,
    small_ref,
    out_a,
    out_b,
    slope,
    normed_one,
    attended,
    inverse_denom,
    total,
    fold_gain_one,
    fold_shift_one,
    fold_gain_two,
    fold_shift_two,
    work,
):
    ff = w_in_ref.shape[1]
    step = 768

    @pl.when(pl.program_id(0) == 0)
    def _():
        for ref in (fold_gain_one, fold_shift_one, fold_gain_two, fold_shift_two):
            ref[...] = jnp.zeros_like(ref)

    table = tab_ref[0]
    cos, sin = table[COS_READ : COS_READ + 1], table[SIN_READ : SIN_READ + 1]
    states = (state_a, state_b)
    for h in range(HEADS):
        reads = trig_rows(q_t_ref[head_slice(h), :], cos, sin)
        more = mm(take_state(states, h), reads)
        numer = numer_ref[head_slice(h), :] + more[:HEAD_DIM]
        inverse = 1.0 / (denom_loc_ref[h : h + 1, :] + more[HEAD_DIM : HEAD_DIM + 1])
        inverse_denom[h : h + 1, :] = inverse
        value = numer * inverse
        attended[head_slice(h), :] = value
        att_t_ref[head_slice(h), :] = value.astype(bf16)
    total[...] = mm(w_out_t[...], att_t_ref[...])
    scale_one = center(total, tok_t_ref)
    for c in chunks_of(total):
        normed = total[c, :] * scale_one
        normed_one[c, :] = normed
        first_out = normed * gain_one_ref[c, :] + shift_one_ref[c, :]
        total[c, :] = first_out
        first_t_ref[c, :] = first_out.astype(bf16)
    first_low = first_t_ref[...]
    for at in range(0, ff, step):
        hidden = mm(w_in_t[at : at + step, :], first_low)
        half = 0.5 * (1.0 + lax.erf(hidden * 0.7071067811865476))
        bell = jnp.exp(hidden * hidden * -0.5) * 0.3989422804014327
        active = (hidden * half).astype(bf16)
        active_t_ref[at : at + step, :] = active
        slope[at : at + step, :] = (half + hidden * bell).astype(bf16)
        total[...] += mm(w_back_t[:, at : at + step], active)
    scale_two = center(total)
    fold_one = fold_two = jnp.zeros((8, total.shape[1]), f32)
    for c in chunks_of(total):
        normed = total[c, :] * scale_two
        total[c, :] = normed
        layer_ref[0, :, c] = (normed * gain_two_ref[c, :] + shift_two_ref[c, :]).T.astype(bf16)
        grad_top = cot_ref[0, :, c].T.astype(f32)
        fold_gain_two[c, :] += fold_lanes(grad_top * normed)
        fold_shift_two[c, :] += fold_lanes(grad_top)
        grad_norm = grad_top * gain_two_ref[c, :]
        work[c, :] = grad_norm
        fold_one = fold_one + fold_rows(grad_norm)
        fold_two = fold_two + fold_rows(grad_norm * normed)
    mean_one, mean_two = mean_of(fold_one, total.shape[0]), mean_of(fold_two, total.shape[0])
    for c in chunks_of(total):
        grad_mid = scale_two * (work[c, :] - mean_one - total[c, :] * mean_two)
        total[c, :] = grad_mid
        grad_second_ref[c, :] = grad_mid.astype(bf16)
    grad_second = grad_second_ref[...]
    for at in range(0, ff, step):
        grad_active = mm(w_back_ref[at : at + step, :], grad_second)
        low = (grad_active * slope[at : at + step, :].astype(f32)).astype(bf16)
        grad_hidden_ref[at : at + step, :] = low
        total[...] += mm(w_in_ref[:, at : at + step], low)
    fold_one = fold_two = jnp.zeros((8, total.shape[1]), f32)
    for c in chunks_of(total):
        grad_first, normed = total[c, :], normed_one[c, :]
        fold_gain_one[c, :] += fold_lanes(grad_first * normed)
        fold_shift_one[c, :] += fold_lanes(grad_first)
        grad_norm = grad_first * gain_one_ref[c, :]
        work[c, :] = grad_norm
        fold_one = fold_one + fold_rows(grad_norm)
        fold_two = fold_two + fold_rows(grad_norm * normed)
    mean_one, mean_two = mean_of(fold_one, total.shape[0]), mean_of(fold_two, total.shape[0])
    for c in chunks_of(total):
        grad_base = scale_one * (work[c, :] - mean_one - normed_one[c, :] * mean_two)
        grad_base_ref[c, :] = grad_base
        grad_branch_ref[c, :] = grad_base.astype(bf16)
    grad_branch = grad_branch_ref[...]
    total[...] = mm(w_out_ref[...], grad_branch)
    outs = (out_a, out_b)
    clear_pad(outs)
    grad_denom_ref[...] = jnp.zeros_like(grad_denom_ref)
    for h in range(HEADS):
        rows = head_slice(h)
        grad_numer = (total[rows, :] * inverse_denom[h : h + 1, :]).astype(bf16)
        grad_denom = -jnp.sum(grad_numer.astype(f32) * attended[rows, :], axis=0, keepdims=True)
        grad_denom_ref[h : h + 1, :] = grad_denom
        grad_numer_ref[rows, :] = grad_numer
        reads = trig_rows(q_t_ref[rows, :], cos, sin)
        put_state(outs, h, mm(with_row(grad_numer, grad_denom), reads, NT))

    @pl.when(pl.program_id(0) == pl.num_programs(0) - 1)
    def _():
        lane = lax.broadcasted_iota(jnp.int32, small_ref.shape, 1)
        value = jnp.zeros(small_ref.shape, f32)
        for i, ref in enumerate((fold_gain_one, fold_shift_one, fold_gain_two, fold_shift_two)):
            value = jnp.where(lane == i, lane_total(ref), value)
        small_ref[...] = value


def local_back_kernel(
    s_ref,
    tab_ref,
    q_t_ref,
    k_t_ref,
    k_ref,
    v_ref,
    sig_q_ref,
    grad_numer_ref,
    grad_denom_ref,
    state_a,
    state_b,
    grad_q_ref,
    grad_k_ref,
    grad_v_ref,
):
    table = tab_ref[0]
    blend = blend_of(table)
    tok_count = blend.shape[0]
    cos, sin = table[COS_READ : COS_READ + 1], table[SIN_READ : SIN_READ + 1]
    states = (state_a, state_b)
    for pair in range(PAIRS):
        lanes = slice(pair * 2 * HEAD_DIM, (pair + 1) * 2 * HEAD_DIM)
        both = mm(k_ref[0, :, lanes], pair_rows(q_t_ref, pair))
        grads = mm(v_ref[0, :, lanes], pair_rows(grad_numer_ref, pair))
        for side in range(2):
            h = 2 * pair + side
            rows = head_slice(h)
            part = slice(side * tok_count, (side + 1) * tok_count)
            grad_denom = grad_denom_ref[h : h + 1, :]
            scores = (both[:, part] * blend).astype(bf16)
            grad_scores, rest = two_parts((grads[:, part] + grad_denom) * blend)
            grad_numer = grad_numer_ref[rows, :]
            grad_v_ref[rows, :] = mm(grad_numer, scores, NT)
            grad_k_ref[rows, :] = mm(q_t_ref[rows, :], grad_scores, NT)
            reads = mm(take_state(states, h), with_row(grad_numer, grad_denom), TN)
            grad_q = (
                mm(k_t_ref[rows, :], grad_scores)
                + mm(k_t_ref[rows, :], rest)
                + cos * reads[:HEAD_DIM]
                + sin * reads[HEAD_DIM:]
            )
            grad_q_ref[rows, :] = (grad_q * sig_q_ref[rows, :].astype(f32)).astype(bf16)


def tail_kernel(
    s_ref,
    tab_ref,
    k_t_ref,
    v_t_ref,
    sig_k_ref,
    state_a,
    state_b,
    grad_k_in,
    grad_v_in,
    grad_kv_ref,
):
    table = tab_ref[0]
    cos, sin = table[COS_TAIL : COS_TAIL + 1], table[SIN_TAIL : SIN_TAIL + 1]
    states = (state_a, state_b)
    for h in range(HEADS):
        rows = head_slice(h)
        state = take_state(states, h)
        inner = mm(state, with_row(v_t_ref[rows, :], 1.0), TN)
        grad_k = grad_k_in[rows, :] + cos * inner[:HEAD_DIM] + sin * inner[HEAD_DIM:]
        grad_kv_ref[0, rows, :] = (grad_k * sig_k_ref[rows, :].astype(f32)).astype(bf16)
        keys = trig_rows(k_t_ref[rows, :], cos, sin)
        grad_kv_ref[1, rows, :] = (grad_v_in[rows, :] + mm(state[:HEAD_DIM], keys)).astype(bf16)


def token_kernel(s_ref, gq_ref, gkv_ref, base_ref, wq_ref, wk_ref, wv_ref, out_ref):
    total = base_ref[...] + mm(wq_ref[...], gq_ref[...])
    total = total + mm(wk_ref[...], gkv_ref[0])
    total = total + mm(wv_ref[...], gkv_ref[1])
    out_ref[0] = total.T


def spec(block, index):
    return pl.BlockSpec(block, index)


NEAR = pl.BlockSpec(memory_space=pltpu.VMEM)

CORE, ODD, PLACE = range(3)


class Order:
    def __init__(self, scalars):
        self.scalars = scalars

    def call(
        self, kernel, grid, ins, outs, scratch, args, extra=(), free=(), near=(), near_out=(), limit=VMEM_LIMIT
    ):
        count = 1 + len(extra)
        placed = len(scratch)

        def stepped(*refs):
            s_ref, handed = refs[0], refs[len(refs) - placed - 1]
            rest = refs[: len(refs) - placed - 1] + refs[len(refs) - placed :]
            kernel(*rest)
            for i in range(s_ref.shape[0]):
                handed[i] = s_ref[i]

        *values, self.scalars = pl.pallas_call(
            stepped,
            grid_spec=pltpu.PrefetchScalarGridSpec(
                num_scalar_prefetch=count,
                grid=grid,
                in_specs=ins,
                out_specs=[o for o, _ in outs] + [pl.BlockSpec(memory_space=pltpu.SMEM)],
                scratch_shapes=scratch,
            ),
            out_shape=[
                (pltpu.VMEM if i in near_out else pltpu.HBM)(shape, kind)
                for i, (_, (shape, kind)) in enumerate(outs)
            ]
            + [jax.ShapeDtypeStruct(self.scalars.shape, jnp.int32)],
            compiler_params=pltpu.CompilerParams(
                dimension_semantics=("arbitrary",) * len(grid), vmem_limit_bytes=limit
            ),
            cost_estimate=pl.CostEstimate(flops=1000000000000, bytes_accessed=1, transcendentals=0),
        )(
            self.scalars,
            *extra,
            *[
                v
                if i in free
                else pltpu.with_memory_space_constraint(v, pltpu.VMEM if i in near else pltpu.HBM)
                for i, v in enumerate(args)
            ],
        )
        return values


def pick_halves(core, value):
    cut = value.shape[1] // 2
    low, high = value[:, :cut], value[:, cut:]
    return jnp.where(core == 0, high, low), jnp.where(core == 0, low, high)


def tall_kernel(s_ref, a_ref, b_ref, away_ref, keep_ref):
    away_ref[...], keep_ref[...] = pick_halves(s_ref[CORE], mm(a_ref[...], b_ref[...], NT))


def tall_product(order, a, b):
    count, flat = a.shape
    tile, cut = count // 4, b.shape[0] // 2
    out = (spec((tile, cut), lambda i, *s: (i, 0)), ((count, cut), f32))
    ins = [spec((tile, flat), lambda i, *s: (i, 0)), spec(b.shape, lambda i, *s: (0, 0))]
    return order.call(tall_kernel, (4,), ins, [out, out], [], (a, b))


def wide_kernel(s_ref, a_ref, b_ref, away_ref, keep_ref):
    value = mm(a_ref[...], b_ref[...], NT)
    first = pl.program_id(0) < pl.num_programs(0) // 2

    @pl.when(first)
    def _():
        away_ref[...] = value

    @pl.when(jnp.logical_not(first))
    def _():
        keep_ref[...] = value


def wide_product(order, a, b):
    count, flat = a.shape
    cut = b.shape[0] // 2
    tile = 512
    half = cut // tile

    def source(i, s):
        return jnp.where(i < half, (1 - s[CORE]) * half + i, s[CORE] * half + i - half), 0

    outs = [
        (spec((count, tile), lambda i, s: (0, jnp.minimum(i, half - 1))), ((count, cut), f32)),
        (spec((count, tile), lambda i, s: (0, jnp.maximum(i - half, 0))), ((count, cut), f32)),
    ]
    ins = [spec(a.shape, lambda i, s: (0, 0)), spec((tile, flat), source)]
    return order.call(wide_kernel, (2 * half,), ins, outs, [], (a, b))


def twin_kernel(s_ref, a_ref, b_ref, c_ref, d_ref, *refs):
    core = s_ref[CORE]
    away_ref, keep_ref = refs[-2:]
    at = 0
    for left, right in ((a_ref, b_ref[0]), (c_ref, d_ref[0])):
        away, keep = pick_halves(core, mm(left[...], right, NT))
        away_ref[:, at : at + away.shape[1]] = away
        keep_ref[:, at : at + keep.shape[1]] = keep
        at += away.shape[1]
    if len(refs) == 3:
        value = refs[0][...]
        away_ref[:, at:] = jnp.where(core == 0, 0.0, value)
        keep_ref[:, at:] = jnp.where(core == 0, value, 0.0)


def twin_product(order, a, b, c, d, small=None):
    count, flat = a.shape
    tile = count // 2
    columns = count + (0 if small is None else small.shape[1])
    rows = spec((tile, flat), lambda i, s: (i, 0))
    ins, args = [], []
    for left, (right, group) in ((a, b), (c, d)):
        ins += [rows, spec((1, count, flat), lambda i, s, g=group: (g, 0, 0))]
        args += [left, right]
    if small is not None:
        ins.append(spec((tile, small.shape[1]), lambda i, s: (i, 0)))
        args.append(small)
    out = (spec((tile, columns), lambda i, s: (i, 0)), ((count, columns), f32))
    return order.call(twin_kernel, (2,), ins, [out, out], [], args)


def route_kernel(s_ref, *refs):
    for i in range(4):
        refs[8 + i][...] = refs[2 * i][...] + refs[2 * i + 1][...]


def route(order, left, right, low_bit, high_bit):
    (a, b), (c, d) = left, right
    shards, rows, columns = a.shape
    same = a is c
    if same:
        rows //= 2
    lower = 1 if same else 0
    half = shards // 2

    def by_low(flip):
        def index(i, s):
            mine = (s[PLACE] >> low_bit) & 1
            return 2 * i + ((1 - mine) if flip else mine), 0, 0

        return index

    def by_high(flip):
        def index(i, s):
            mine = (s[PLACE] >> high_bit) & 1
            return i + ((1 - mine) if flip else mine) * half, lower, 0

        return index

    block = (1, rows, columns)
    maps = [by_low(True), by_low(False), by_high(True), by_high(False)]
    ins = [spec(block, m) for m in maps for _ in range(2)]
    out = (spec(block, lambda i, s: (i, 0, 0)), ((half, rows, columns), f32))
    return order.call(route_kernel, (half,), ins, [out] * 4, [], (a, b, a, b, c, d, c, d))


def choose_kernel(s_ref, a_ref, b_ref, c_ref, d_ref, away_ref, kept_ref):
    upper, lower = a_ref[0] + b_ref[0], c_ref[0] + d_ref[0]
    odd = s_ref[ODD] == 1
    away_ref[...] = jnp.where(odd, upper, lower)
    kept_ref[...] = jnp.where(odd, lower, upper)


def choose(order, left, right):
    shape = left[0].shape[1:]
    return order.call(
        choose_kernel,
        (1,),
        [NEAR] * 4,
        [(NEAR, (shape, f32))] * 2,
        [],
        (*left, *right),
        free=range(4),
        near_out=range(2),
        limit=SMALL_LIMIT,
    )


def add_kernel(s_ref, a_ref, b_ref, out_ref):
    out_ref[...] = a_ref[...] + b_ref[...]


def add(order, a, b):
    outs = [(NEAR, (a.shape, f32))]
    return order.call(
        add_kernel, (1,), [NEAR] * 2, outs, [], (a, b), near=range(2), near_out=range(1), limit=SMALL_LIMIT
    )[0]


def merge_kernel(s_ref, kept_ref, got_ref, out_ref):
    odd = s_ref[ODD] == 1
    rows = kept_ref.shape[0]
    kept, got = kept_ref[...], got_ref[...]
    out_ref[:rows, :] = jnp.where(odd, got, kept)
    out_ref[rows:, :] = jnp.where(odd, kept, got)


def merge(order, kept, got):
    rows, columns = kept.shape
    outs = [(NEAR, ((2 * rows, columns), f32))]
    return order.call(
        merge_kernel,
        (1,),
        [NEAR] * 2,
        outs,
        [],
        (kept, got),
        near=range(2),
        near_out=range(1),
        limit=SMALL_LIMIT,
    )[0]


def side_kernel(s_ref, mine_ref, other_ref, *outs):
    first = s_ref[CORE] == 0
    at = 0
    for out in outs:
        cut = out.shape[1] // 2
        if cut < 128:
            out[...] = jnp.where(first, mine_ref[:, at:], other_ref[:, at:])
            break
        mine, other = mine_ref[:, at : at + cut], other_ref[:, at : at + cut]
        out[:, :cut] = jnp.where(first, mine, other)
        out[:, cut:] = jnp.where(first, other, mine)
        at += cut


def side(order, mine, other, widths):
    rows = mine.shape[0]
    outs = [(spec((rows, w), lambda i, s: (0, 0)), ((rows, w), f32)) for w in widths]
    return order.call(
        side_kernel, (1,), [NEAR] * 2, outs, [], (mine, other), near=range(2), limit=SMALL_LIMIT
    )


def mix_kernel(first, s_ref, w_ref, *refs):
    for row in range(refs[0].shape[0]):
        for i in range(2):
            own, other = (w_ref[first + 2 * i + j, row] for j in range(2))
            refs[4 + i][row] = own * refs[2 * i][row] + other * refs[2 * i + 1][row]


def mix(order, weights, first, last, *parts):
    shape = parts[0].shape
    out = spec(shape, lambda i, *s: (0, 0, 0)) if last else NEAR
    return order.call(
        partial(mix_kernel, first),
        (1,),
        [NEAR] * 4,
        [(out, (shape, f32))] * 2,
        [],
        parts,
        (weights,),
        near=range(4),
        near_out=() if last else range(2),
        limit=SMALL_LIMIT,
    )


def first_begins(lengths, count, tok_count):
    slots = lengths.shape[1]
    order = jnp.arange(slots)
    before = (order[:, None] > order[None, :]).astype(jnp.int32)
    starts = jnp.sum(lengths[:, None, :] * before[None], axis=-1)
    firsts = jnp.arange(count, dtype=jnp.int32) * tok_count
    reached = starts[:, None, :] <= firsts[None, :, None]
    return jnp.max(jnp.where(reached, starts[:, None, :], 0), axis=-1)


def pick(index, values):
    out = values[0]
    for i in range(1, len(values)):
        out = jnp.where(index == i, values[i], out)
    return out


def weights_of(begin_first, tok_count, reverse):
    count = lax.axis_size("seq")
    place = lax.axis_index("seq")

    def covers(i, j):
        low, high = (count - 1 - j, count - 1 - i) if reverse else (i, j)
        return (begin_first[:, high] < (low + 1) * tok_count).astype(f32)

    if count != 4:
        spots = jnp.arange(count)
        mine = begin_first.T if reverse else begin_first[:, place][None]
        reach = (place if reverse else spots[:, None]) + 1
        ahead = (spots > place) if reverse else (spots < place)
        return ((mine < reach * tok_count) & ahead[:, None]).astype(f32)
    index = count - 1 - place if reverse else place
    zero = jnp.zeros_like(begin_first[:, 0], f32)
    one = zero + 1.0
    m02, m03, m13 = covers(0, 2), covers(0, 3), covers(1, 3)
    onward = [
        pick(index, [m02, m13, zero, zero]),
        pick(index, [one, m03, zero, zero]),
        pick(index, [one, zero, one, zero]),
        pick(index, [zero, zero, m03, one]),
    ]
    final = [
        pick(index, [zero, one, zero, one]),
        pick(index, [zero, zero, one, one]),
        pick(index, [zero, zero, m02, m13]),
        pick(index, [zero, one, one, one]),
    ]
    return onward + final


def entering(order, parts, weights, first):
    if lax.axis_size("seq") != 4:
        gathered = [lax.all_gather(p, "seq") for p in parts]
        yield
        yield
        yield tuple(jnp.sum(g * weights[first][:, :, None, None], axis=0) for g in gathered)
    part_a, part_b = parts
    got_a, got_b = swap(part_a, "seq", 1), swap(part_b, "seq", 2)
    yield
    next_a, next_b = mix(order, weights, first, False, part_a, got_a, part_b, got_b)
    last_a, last_b = swap(next_a, "seq", 2), swap(next_b, "seq", 1)
    yield
    yield mix(order, weights, first + 4, True, got_a, last_a, got_b, last_b)


def swap(value, axis, distance):
    count = lax.axis_size(axis)
    return lax.ppermute(value, axis, [(i, i ^ distance) for i in range(count)])


def reduced(order, away, keep, widths):
    count = lax.axis_size("batch")
    shards = lax.axis_size("seq")
    bits = shards.bit_length() - 1
    shape = (shards, keep.shape[0] // shards, keep.shape[1])
    got = swap(away, "batch", 1).reshape(shape)
    yield
    left = right = (keep.reshape(shape), got)
    for step in range(bits):
        high = bits - 1 - step
        away_l, keep_l, away_r, keep_r = route(order, left, right, step, high)
        left = keep_l, swap(away_l, "seq", 1 << step)
        right = keep_r, swap(away_r, "seq", 1 << high)
        yield
    away, kept = choose(order, left, right)
    got = swap(away, "batch", 2)
    distance = 4
    while distance < count:
        yield
        kept = add(order, kept, got)
        got = swap(kept, "batch", distance)
        distance *= 2
    yield
    kept = add(order, kept, got)
    got = swap(kept, "batch", 2)
    yield
    merged = merge(order, kept, got)
    other = swap(merged, "batch", 1)
    yield
    yield side(order, merged, other, widths)


SCHEDULE = (
    "back_product", "states", "back", "local", "in_product", "states",
    "back", "in", "mixed_product", "back", "mixed", "tail",
    "back", "mixed", "in", "mixed", "last_product", "in",
    "last", "mixed", "back", "in", "last", "tokens",
    "last", "back", "mixed", "last", "in", "mixed",
    "last", "in", "mixed", "last", "in", "back",
    "last",
)


def body(
    tokens,
    cotangent,
    doc_lengths,
    w_query,
    w_key,
    w_value,
    w_out,
    w_in,
    w_back,
    gain_one,
    shift_one,
    gain_two,
    shift_two,
):
    rows, toks, width = tokens.shape
    ff = w_in.shape[1]
    flat = rows * toks
    shards = lax.axis_size("seq")
    whole = pl.BlockSpec(memory_space=pltpu.VMEM)
    token_major = pl.BlockSpec((1, toks, width), lambda r, *s: (r, 0, 0))
    table_spec = pl.BlockSpec((1, 8, toks), lambda r, *s: (r, 0, 0))
    state_spec = pl.BlockSpec((1, STATE_ROWS, 2 * HEAD_DIM), lambda r, *s: (r, 0, 0))

    def feature(count):
        return pl.BlockSpec((count, toks), lambda r, *s: (0, r))

    tok_low = (token_major, ((rows, toks, width), bf16))
    wide_low = (feature(width), ((width, flat), bf16))
    wide_full = (feature(width), ((width, flat), f32))
    ff_low = (feature(ff), ((ff, flat), bf16))
    head_rows = (feature(16), ((16, flat), f32))
    fold = (pl.BlockSpec((width, 128), lambda r, *s: (0, 0)), ((width, 128), f32))
    state = (state_spec, ((rows, STATE_ROWS, 2 * HEAD_DIM), f32))
    grid = (rows,)

    batch_place = lax.axis_index("batch").astype(jnp.int32)
    scalars = jnp.stack(
        [batch_place & 1, (batch_place >> 1) & 1, lax.axis_index("seq").astype(jnp.int32)]
    )
    order = Order(scalars)

    def run(kernel, ins, outs, scratch, *args, **more):
        return order.call(kernel, grid, ins, outs, scratch, args, **more)

    def column(v):
        return v[:, None]

    table, tok_t, k_t, v_t, key, value, sig_k, state_a, state_b = run(
        project_kernel,
        [token_major, whole, whole],
        [(table_spec, ((rows, 8, toks), f32))]
        + [wide_low] * 3
        + [tok_low] * 2
        + [wide_low]
        + [state] * 2,
        [pltpu.VMEM((2, width, width), bf16)],
        tokens,
        w_key,
        w_value,
        extra=(doc_lengths,),
    )
    begins = first_begins(doc_lengths, shards, toks)
    if shards == 4:
        weights = jnp.stack(weights_of(begins, toks, False) + weights_of(begins, toks, True))
        later = 8
    else:
        weights = [weights_of(begins, toks, False), weights_of(begins, toks, True)]
        later = 1
    states = entering(order, (state_a, state_b), weights, 0)
    next(states)
    part = ff // rows
    q_t, sig_q, numer, denom_loc, w_out_t, w_in_t, w_back_t = run(
        local_kernel,
        [
            table_spec,
            feature(width),
            token_major,
            feature(width),
            whole,
            whole,
            pl.BlockSpec((width, part), lambda r, *s: (0, r)),
            pl.BlockSpec((part, width), lambda r, *s: (r, 0)),
        ],
        [
            wide_low,
            wide_low,
            wide_full,
            head_rows,
            (pl.BlockSpec((width, width), lambda r, *s: (0, 0)), ((width, width), bf16)),
            (pl.BlockSpec((part, width), lambda r, *s: (r, 0)), ((ff, width), bf16)),
            (pl.BlockSpec((width, part), lambda r, *s: (0, r)), ((width, ff), bf16)),
        ],
        [pltpu.VMEM((width, width), bf16)],
        table,
        tok_t,
        key,
        v_t,
        w_query,
        w_out,
        w_in,
        w_back,
    )
    next(states)
    in_a, in_b = next(states)
    (
        layer_out,
        att_t,
        first_t,
        active_t,
        grad_second,
        grad_hidden,
        grad_base,
        grad_branch,
        grad_numer,
        grad_denom,
        small,
        out_a,
        out_b,
    ) = run(
        layer_kernel,
        [
            table_spec,
            feature(width),
            feature(width),
            feature(16),
            state_spec,
            state_spec,
            feature(width),
            token_major,
        ]
        + [whole] * 10,
        [
            tok_low,
            wide_low,
            wide_low,
            ff_low,
            wide_low,
            ff_low,
            wide_full,
            wide_low,
            wide_low,
            head_rows,
            fold,
            state,
            state,
        ],
        [
            pltpu.VMEM((ff, toks), bf16),
            pltpu.VMEM((width, toks), f32),
            pltpu.VMEM((width, toks), f32),
            pltpu.VMEM((16, toks), f32),
            pltpu.VMEM((width, toks), f32),
        ]
        + [pltpu.VMEM((width, 128), f32)] * 4
        + [pltpu.VMEM((width, toks), f32)],
        table,
        q_t,
        numer,
        denom_loc,
        in_a,
        in_b,
        tok_t,
        cotangent,
        w_out_t,
        w_in_t,
        w_back_t,
        w_out,
        w_in,
        w_back,
        column(gain_one),
        column(shift_one),
        column(gain_two),
        column(shift_two),
        near=range(8, 14),
        limit=LAYER_LIMIT,
    )

    back_states = entering(order, (out_a, out_b), weights, later)
    next(back_states)
    pieces, made = {}, {}

    def begin(name, product, widths):
        pieces[name] = reduced(order, *product, widths)
        next(pieces[name])

    def local_back():
        made["query"], made["key"], made["value"] = run(
            local_back_kernel,
            [
                table_spec,
                feature(width),
                feature(width),
                token_major,
                token_major,
                feature(width),
                feature(width),
                feature(16),
                state_spec,
                state_spec,
            ],
            [wide_low, wide_full, wide_full],
            [],
            table,
            q_t,
            k_t,
            key,
            value,
            sig_q,
            grad_numer,
            grad_denom,
            in_a,
            in_b,
        )

    def tail():
        back_a, back_b = made["states"]
        (made["kv"],) = run(
            tail_kernel,
            [table_spec]
            + [feature(width)] * 3
            + [state_spec] * 2
            + [feature(width)] * 2,
            [(pl.BlockSpec((2, width, toks), lambda r, *s: (0, 0, r)), ((2, width, flat), bf16))],
            [],
            table,
            k_t,
            v_t,
            sig_k,
            back_a,
            back_b,
            made["key"],
            made["value"],
        )

    def token_grads():
        (made["tokens"],) = run(
            token_kernel,
            [
                feature(width),
                pl.BlockSpec((2, width, toks), lambda r, *s: (0, 0, r)),
                feature(width),
            ]
            + [whole] * 3,
            [(token_major, ((rows, toks, width), f32))],
            [],
            made["query"],
            made["kv"],
            grad_base,
            w_query,
            w_key,
            w_value,
        )

    def states_on():
        made["states"] = next(back_states)

    steps = {
        "back_product": lambda: begin("back", tall_product(order, active_t, grad_second), (width,)),
        "in_product": lambda: begin("in", wide_product(order, first_t, grad_hidden), (ff,)),
        "mixed_product": lambda: begin(
            "mixed",
            twin_product(order, att_t, (grad_branch[None], 0), tok_t, (made["query"][None], 0), small),
            (width, width, 128),
        ),
        "last_product": lambda: begin(
            "last",
            twin_product(order, tok_t, (made["kv"], 0), tok_t, (made["kv"], 1)),
            (width, width),
        ),
        "states": states_on,
        "local": local_back,
        "tail": tail,
        "tokens": token_grads,
    }
    ends = {}

    def step(name):
        value = next(pieces[name])
        if value is not None:
            ends[name] = value

    for name in SCHEDULE:
        if name in steps:
            steps[name]()
        elif name not in ends:
            step(name)
    while len(ends) < len(pieces):
        for name in pieces:
            if name not in ends:
                step(name)
    (total_back,), (total_in,) = ends["back"], ends["in"]
    total_out, total_query, vectors = ends["mixed"]
    total_key, total_value = ends["last"]
    grad_tokens = made["tokens"]
    return (
        layer_out,
        grad_tokens,
        total_query,
        total_key,
        total_value,
        total_out,
        total_in,
        total_back,
        vectors[:, 0],
        vectors[:, 1],
        vectors[:, 2],
        vectors[:, 3],
    )


def solution(mesh):
    in_specs = (
        P("batch", "seq", None),
        P("batch", "seq", None),
        P("batch", None),
        P(),
        P(),
        P(),
        P(),
        P(),
        P(),
        P(),
        P(),
        P(),
        P(),
    )
    out_specs = (
        P("batch", "seq", None),
        P("batch", "seq", None),
        P("seq", None),
        P("seq", None),
        P("seq", None),
        P("seq", None),
        P("seq", None),
        P("seq", None),
        P("seq"),
        P("seq"),
        P("seq"),
        P("seq"),
    )
    return jax.shard_map(body, mesh=mesh, in_specs=in_specs, out_specs=out_specs, check_vma=False)
```

```python
from functools import partial

import jax
import jax.numpy as jnp
from jax import lax
from jax.experimental import pallas as pl
from jax.experimental.pallas import tpu as pltpu
from jax.sharding import PartitionSpec as P

HEADS = 12
HEAD_DIM = 64
PAIRS = HEADS // 2
HALF_HEADS = HEADS // 2
STATE_ROWS = HALF_HEADS * HEAD_DIM + 8

f32 = jnp.float32
bf16 = jnp.bfloat16
half_pi = 1.5707963267948966
norm_eps = 1e-05
VMEM_LIMIT = 30 * 1024 * 1024
SMALL_LIMIT = 16 * 1024 * 1024
LAYER_LIMIT = 38 * 1024 * 1024

NN = (((1,), (0,)), ((), ()))
NT = (((1,), (1,)), ((), ()))
TN = (((0,), (0,)), ((), ()))


def mm(a, b, dims=NN):
    return lax.dot_general(a, b, dims, preferred_element_type=f32)


COS, SIN, BEGIN, COS_READ, SIN_READ, COS_TAIL, SIN_TAIL = range(7)


def make_table(place, lens_ref, row, tok_count):
    pos = place + lax.broadcasted_iota(jnp.int32, (8, tok_count), 1)
    last = place + tok_count - 1
    start = jnp.int32(0)
    begin = jnp.zeros((8, tok_count), jnp.int32)
    span = jnp.ones((8, tok_count), jnp.int32)
    last_begin = jnp.int32(0)
    for d in range(lens_ref.shape[1]):
        length = lens_ref[row, d]
        inside = pos >= start
        begin = jnp.where(inside, start, begin)
        span = jnp.where(inside, length, span)
        last_begin = jnp.where(start <= last, start, last_begin)
        start = start + length
    angle = half_pi * (pos - begin).astype(f32) / span.astype(f32)
    cos, sin = jnp.cos(angle), jnp.sin(angle)
    reader = (begin < place).astype(f32)
    tail = (begin == last_begin).astype(f32)
    which = lax.broadcasted_iota(jnp.int32, (8, tok_count), 0)
    table = jnp.zeros((8, tok_count), f32)
    for index, value in (
        (COS, cos),
        (SIN, sin),
        (BEGIN, begin.astype(f32)),
        (COS_READ, cos * reader),
        (SIN_READ, sin * reader),
        (COS_TAIL, cos * tail),
        (SIN_TAIL, sin * tail),
    ):
        table = jnp.where(which == index, value, table)
    return table


def blend_of(table):
    columns = table.T
    tok_count = table.shape[1]
    source = lax.broadcasted_iota(jnp.int32, (tok_count, tok_count), 0)
    reader = lax.broadcasted_iota(jnp.int32, (tok_count, tok_count), 1)
    same = (columns[:, BEGIN : BEGIN + 1] == table[BEGIN : BEGIN + 1]) & (source <= reader)
    value = (
        columns[:, COS : COS + 1] * table[COS : COS + 1]
        + columns[:, SIN : SIN + 1] * table[SIN : SIN + 1]
    )
    return jnp.where(same, value, 0.0)


def trig_rows(head_rows, cos, sin):
    wide = head_rows.astype(f32)
    return jnp.concatenate([(wide * cos).astype(bf16), (wide * sin).astype(bf16)], axis=0)


def with_row(rows, extra):
    which = lax.broadcasted_iota(jnp.int32, (16, rows.shape[1]), 0)
    return jnp.concatenate([rows, jnp.where(which == 0, extra, 0.0).astype(bf16)], axis=0)


def head_slice(h):
    return slice(h * HEAD_DIM, (h + 1) * HEAD_DIM)


def put_state(state_refs, h, value):
    ref = state_refs[h // HALF_HEADS]
    place = h % HALF_HEADS
    ref[0, head_slice(place), :] = value[:HEAD_DIM]
    ref[0, HALF_HEADS * HEAD_DIM + place : HALF_HEADS * HEAD_DIM + place + 1, :] = value[
        HEAD_DIM : HEAD_DIM + 1
    ]


def take_state(state_refs, h):
    ref = state_refs[h // HALF_HEADS]
    place = h % HALF_HEADS
    mats = ref[0, head_slice(place), :].astype(bf16)
    sums = ref[0, HALF_HEADS * HEAD_DIM + place : HALF_HEADS * HEAD_DIM + place + 1, :]
    return with_row(mats, sums)


def clear_pad(state_refs):
    for ref in state_refs:
        ref[0, HALF_HEADS * HEAD_DIM :, :] = jnp.zeros((8, 2 * HEAD_DIM), f32)


def softplus_sigmoid(v):
    small = jnp.exp(-jnp.abs(v))
    soft = jnp.maximum(v, 0.0) + jnp.log1p(small)
    inverse = 1.0 / (1.0 + small)
    return soft, jnp.where(v >= 0, inverse, small * inverse)


def project_kernel(
    s_ref,
    lens_ref,
    tok_ref,
    wk_ref,
    wv_ref,
    tab_ref,
    tok_t_ref,
    k_t_ref,
    v_t_ref,
    k_ref,
    v_ref,
    sig_k_ref,
    state_a,
    state_b,
    w_t,
):
    row = pl.program_id(0)

    @pl.when(row == 0)
    def _():
        w_t[0] = wk_ref[...].T
        w_t[1] = wv_ref[...].T

    tok_t = tok_ref[0].T
    tok_t_ref[...] = tok_t
    table = make_table(s_ref[PLACE] * tok_t.shape[1], lens_ref, row, tok_t.shape[1])
    tab_ref[0] = table
    soft, sig = softplus_sigmoid(mm(w_t[0], tok_t))
    key_t = soft.astype(bf16)
    k_t_ref[...] = key_t
    k_ref[0] = key_t.T
    sig_k_ref[...] = sig.astype(bf16)
    value_t = mm(w_t[1], tok_t).astype(bf16)
    v_t_ref[...] = value_t
    v_ref[0] = value_t.T
    states = (state_a, state_b)
    clear_pad(states)
    cos, sin = table[COS_TAIL : COS_TAIL + 1], table[SIN_TAIL : SIN_TAIL + 1]
    for h in range(HEADS):
        keys = trig_rows(k_t_ref[head_slice(h), :], cos, sin)
        values = with_row(v_t_ref[head_slice(h), :], 1.0)
        put_state(states, h, mm(values, keys, NT))


def pair_rows(ref, pair):
    first = ref[head_slice(2 * pair), :]
    second = ref[head_slice(2 * pair + 1), :]
    nothing = jnp.zeros_like(first)
    return jnp.concatenate(
        [
            jnp.concatenate([first, nothing], axis=1),
            jnp.concatenate([nothing, second], axis=1),
        ],
        axis=0,
    )


def two_parts(v):
    high = v.astype(bf16)
    return high, (v - high.astype(f32)).astype(bf16)


def local_kernel(
    s_ref,
    tab_ref,
    tok_t_ref,
    k_ref,
    v_t_ref,
    wq_ref,
    w_out_ref,
    w_in_ref,
    w_back_ref,
    q_t_ref,
    sig_q_ref,
    numer_ref,
    denom_ref,
    w_out_t,
    w_in_t,
    w_back_t,
    w_t,
):
    @pl.when(pl.program_id(0) == 0)
    def _():
        w_t[...] = wq_ref[...].T
        w_out_t[...] = w_out_ref[...].T

    w_in_t[...] = w_in_ref[...].T
    w_back_t[...] = w_back_ref[...].T

    soft, sig = softplus_sigmoid(mm(w_t[...], tok_t_ref[...]))
    q_t_ref[...] = soft.astype(bf16)
    sig_q_ref[...] = sig.astype(bf16)
    blend = blend_of(tab_ref[0])
    tok_count = blend.shape[0]
    denom_ref[...] = jnp.zeros_like(denom_ref)
    for pair in range(PAIRS):
        lanes = slice(pair * 2 * HEAD_DIM, (pair + 1) * 2 * HEAD_DIM)
        both = mm(k_ref[0, :, lanes], pair_rows(q_t_ref, pair))
        for side in range(2):
            h = 2 * pair + side
            high, low = two_parts(both[:, side * tok_count : (side + 1) * tok_count] * blend)
            values = with_row(v_t_ref[head_slice(h), :], 1.0)
            out = mm(values, high) + mm(values, low)
            numer_ref[head_slice(h), :] = out[:HEAD_DIM]
            denom_ref[h : h + 1, :] = out[HEAD_DIM : HEAD_DIM + 1]


def fold_lanes(v):
    total = v[:, :128]
    for at in range(128, v.shape[1], 128):
        total = total + v[:, at : at + 128]
    return total


def chunks_of(ref):
    return [slice(at, at + 128) for at in range(0, ref.shape[0], 128)]


def fold_rows(v):
    return jnp.sum(v.reshape(v.shape[0] // 8, 8, v.shape[1]), axis=0)


def mean_of(fold, count):
    return jnp.sum(fold, axis=0, keepdims=True) * (1.0 / count)


def center(ref, more=None):
    width, lanes = ref.shape
    fold = jnp.zeros((8, lanes), f32)
    for c in chunks_of(ref):
        value = ref[c, :]
        if more is not None:
            value = value + more[c, :].astype(f32)
            ref[c, :] = value
        fold = fold + fold_rows(value)
    mean = mean_of(fold, width)
    fold = jnp.zeros((8, lanes), f32)
    for c in chunks_of(ref):
        value = ref[c, :] - mean
        ref[c, :] = value
        fold = fold + fold_rows(value * value)
    return lax.rsqrt(mean_of(fold, width) + norm_eps)


def lane_total(ref):
    return jnp.sum(ref[...], axis=1, keepdims=True)


def layer_kernel(
    s_ref,
    tab_ref,
    q_t_ref,
    numer_ref,
    denom_loc_ref,
    state_a,
    state_b,
    tok_t_ref,
    cot_ref,
    w_out_t,
    w_in_t,
    w_back_t,
    w_out_ref,
    w_in_ref,
    w_back_ref,
    gain_one_ref,
    shift_one_ref,
    gain_two_ref,
    shift_two_ref,
    layer_ref,
    att_t_ref,
    first_t_ref,
    active_t_ref,
    grad_second_ref,
    grad_hidden_ref,
    grad_base_ref,
    grad_branch_ref,
    grad_numer_ref,
    grad_denom_ref,
    small_ref,
    out_a,
    out_b,
    slope,
    normed_one,
    attended,
    inverse_denom,
    total,
    fold_gain_one,
    fold_shift_one,
    fold_gain_two,
    fold_shift_two,
    work,
):
    ff = w_in_ref.shape[1]
    step = 768

    @pl.when(pl.program_id(0) == 0)
    def _():
        for ref in (fold_gain_one, fold_shift_one, fold_gain_two, fold_shift_two):
            ref[...] = jnp.zeros_like(ref)

    table = tab_ref[0]
    cos, sin = table[COS_READ : COS_READ + 1], table[SIN_READ : SIN_READ + 1]
    states = (state_a, state_b)
    for h in range(HEADS):
        reads = trig_rows(q_t_ref[head_slice(h), :], cos, sin)
        more = mm(take_state(states, h), reads)
        numer = numer_ref[head_slice(h), :] + more[:HEAD_DIM]
        inverse = 1.0 / (denom_loc_ref[h : h + 1, :] + more[HEAD_DIM : HEAD_DIM + 1])
        inverse_denom[h : h + 1, :] = inverse
        value = numer * inverse
        attended[head_slice(h), :] = value
        att_t_ref[head_slice(h), :] = value.astype(bf16)
    total[...] = mm(w_out_t[...], att_t_ref[...])
    scale_one = center(total, tok_t_ref)
    for c in chunks_of(total):
        normed = total[c, :] * scale_one
        normed_one[c, :] = normed
        first_out = normed * gain_one_ref[c, :] + shift_one_ref[c, :]
        total[c, :] = first_out
        first_t_ref[c, :] = first_out.astype(bf16)
    first_low = first_t_ref[...]
    for at in range(0, ff, step):
        hidden = mm(w_in_t[at : at + step, :], first_low)
        half = 0.5 * (1.0 + lax.erf(hidden * 0.7071067811865476))
        bell = jnp.exp(hidden * hidden * -0.5) * 0.3989422804014327
        active = (hidden * half).astype(bf16)
        active_t_ref[at : at + step, :] = active
        slope[at : at + step, :] = (half + hidden * bell).astype(bf16)
        total[...] += mm(w_back_t[:, at : at + step], active)
    scale_two = center(total)
    fold_one = fold_two = jnp.zeros((8, total.shape[1]), f32)
    for c in chunks_of(total):
        normed = total[c, :] * scale_two
        total[c, :] = normed
        layer_ref[0, :, c] = (normed * gain_two_ref[c, :] + shift_two_ref[c, :]).T.astype(bf16)
        grad_top = cot_ref[0, :, c].T.astype(f32)
        fold_gain_two[c, :] += fold_lanes(grad_top * normed)
        fold_shift_two[c, :] += fold_lanes(grad_top)
        grad_norm = grad_top * gain_two_ref[c, :]
        work[c, :] = grad_norm
        fold_one = fold_one + fold_rows(grad_norm)
        fold_two = fold_two + fold_rows(grad_norm * normed)
    mean_one, mean_two = mean_of(fold_one, total.shape[0]), mean_of(fold_two, total.shape[0])
    for c in chunks_of(total):
        grad_mid = scale_two * (work[c, :] - mean_one - total[c, :] * mean_two)
        total[c, :] = grad_mid
        grad_second_ref[c, :] = grad_mid.astype(bf16)
    grad_second = grad_second_ref[...]
    for at in range(0, ff, step):
        grad_active = mm(w_back_ref[at : at + step, :], grad_second)
        low = (grad_active * slope[at : at + step, :].astype(f32)).astype(bf16)
        grad_hidden_ref[at : at + step, :] = low
        total[...] += mm(w_in_ref[:, at : at + step], low)
    fold_one = fold_two = jnp.zeros((8, total.shape[1]), f32)
    for c in chunks_of(total):
        grad_first, normed = total[c, :], normed_one[c, :]
        fold_gain_one[c, :] += fold_lanes(grad_first * normed)
        fold_shift_one[c, :] += fold_lanes(grad_first)
        grad_norm = grad_first * gain_one_ref[c, :]
        work[c, :] = grad_norm
        fold_one = fold_one + fold_rows(grad_norm)
        fold_two = fold_two + fold_rows(grad_norm * normed)
    mean_one, mean_two = mean_of(fold_one, total.shape[0]), mean_of(fold_two, total.shape[0])
    for c in chunks_of(total):
        grad_base = scale_one * (work[c, :] - mean_one - normed_one[c, :] * mean_two)
        grad_base_ref[c, :] = grad_base
        grad_branch_ref[c, :] = grad_base.astype(bf16)
    grad_branch = grad_branch_ref[...]
    total[...] = mm(w_out_ref[...], grad_branch)
    outs = (out_a, out_b)
    clear_pad(outs)
    grad_denom_ref[...] = jnp.zeros_like(grad_denom_ref)
    for h in range(HEADS):
        rows = head_slice(h)
        grad_numer = (total[rows, :] * inverse_denom[h : h + 1, :]).astype(bf16)
        grad_denom = -jnp.sum(grad_numer.astype(f32) * attended[rows, :], axis=0, keepdims=True)
        grad_denom_ref[h : h + 1, :] = grad_denom
        grad_numer_ref[rows, :] = grad_numer
        reads = trig_rows(q_t_ref[rows, :], cos, sin)
        put_state(outs, h, mm(with_row(grad_numer, grad_denom), reads, NT))

    @pl.when(pl.program_id(0) == pl.num_programs(0) - 1)
    def _():
        lane = lax.broadcasted_iota(jnp.int32, small_ref.shape, 1)
        value = jnp.zeros(small_ref.shape, f32)
        for i, ref in enumerate((fold_gain_one, fold_shift_one, fold_gain_two, fold_shift_two)):
            value = jnp.where(lane == i, lane_total(ref), value)
        small_ref[...] = value


def local_back_kernel(
    s_ref,
    tab_ref,
    q_t_ref,
    k_t_ref,
    k_ref,
    v_ref,
    sig_q_ref,
    grad_numer_ref,
    grad_denom_ref,
    state_a,
    state_b,
    grad_q_ref,
    grad_k_ref,
    grad_v_ref,
):
    table = tab_ref[0]
    blend = blend_of(table)
    tok_count = blend.shape[0]
    cos, sin = table[COS_READ : COS_READ + 1], table[SIN_READ : SIN_READ + 1]
    states = (state_a, state_b)
    for pair in range(PAIRS):
        lanes = slice(pair * 2 * HEAD_DIM, (pair + 1) * 2 * HEAD_DIM)
        both = mm(k_ref[0, :, lanes], pair_rows(q_t_ref, pair))
        grads = mm(v_ref[0, :, lanes], pair_rows(grad_numer_ref, pair))
        for side in range(2):
            h = 2 * pair + side
            rows = head_slice(h)
            part = slice(side * tok_count, (side + 1) * tok_count)
            grad_denom = grad_denom_ref[h : h + 1, :]
            scores = (both[:, part] * blend).astype(bf16)
            grad_scores, rest = two_parts((grads[:, part] + grad_denom) * blend)
            grad_numer = grad_numer_ref[rows, :]
            grad_v_ref[rows, :] = mm(grad_numer, scores, NT)
            grad_k_ref[rows, :] = mm(q_t_ref[rows, :], grad_scores, NT)
            reads = mm(take_state(states, h), with_row(grad_numer, grad_denom), TN)
            grad_q = (
                mm(k_t_ref[rows, :], grad_scores)
                + mm(k_t_ref[rows, :], rest)
                + cos * reads[:HEAD_DIM]
                + sin * reads[HEAD_DIM:]
            )
            grad_q_ref[rows, :] = (grad_q * sig_q_ref[rows, :].astype(f32)).astype(bf16)


def tail_kernel(
    s_ref,
    tab_ref,
    k_t_ref,
    v_t_ref,
    sig_k_ref,
    state_a,
    state_b,
    grad_k_in,
    grad_v_in,
    grad_kv_ref,
):
    table = tab_ref[0]
    cos, sin = table[COS_TAIL : COS_TAIL + 1], table[SIN_TAIL : SIN_TAIL + 1]
    states = (state_a, state_b)
    for h in range(HEADS):
        rows = head_slice(h)
        state = take_state(states, h)
        inner = mm(state, with_row(v_t_ref[rows, :], 1.0), TN)
        grad_k = grad_k_in[rows, :] + cos * inner[:HEAD_DIM] + sin * inner[HEAD_DIM:]
        grad_kv_ref[0, rows, :] = (grad_k * sig_k_ref[rows, :].astype(f32)).astype(bf16)
        keys = trig_rows(k_t_ref[rows, :], cos, sin)
        grad_kv_ref[1, rows, :] = (grad_v_in[rows, :] + mm(state[:HEAD_DIM], keys)).astype(bf16)


def token_kernel(s_ref, gq_ref, gkv_ref, base_ref, wq_ref, wk_ref, wv_ref, out_ref):
    total = base_ref[...] + mm(wq_ref[...], gq_ref[...])
    total = total + mm(wk_ref[...], gkv_ref[0])
    total = total + mm(wv_ref[...], gkv_ref[1])
    out_ref[0] = total.T


def spec(block, index):
    return pl.BlockSpec(block, index)


NEAR = pl.BlockSpec(memory_space=pltpu.VMEM)

CORE, ODD, PLACE = range(3)


class Order:
    def __init__(self, scalars):
        self.scalars = scalars

    def call(
        self, kernel, grid, ins, outs, scratch, args, extra=(), free=(), near=(), near_out=(), limit=VMEM_LIMIT
    ):
        count = 1 + len(extra)
        placed = len(scratch)

        def stepped(*refs):
            s_ref, handed = refs[0], refs[len(refs) - placed - 1]
            rest = refs[: len(refs) - placed - 1] + refs[len(refs) - placed :]
            kernel(*rest)
            for i in range(s_ref.shape[0]):
                handed[i] = s_ref[i]

        *values, self.scalars = pl.pallas_call(
            stepped,
            grid_spec=pltpu.PrefetchScalarGridSpec(
                num_scalar_prefetch=count,
                grid=grid,
                in_specs=ins,
                out_specs=[o for o, _ in outs] + [pl.BlockSpec(memory_space=pltpu.SMEM)],
                scratch_shapes=scratch,
            ),
            out_shape=[
                (pltpu.VMEM if i in near_out else pltpu.HBM)(shape, kind)
                for i, (_, (shape, kind)) in enumerate(outs)
            ]
            + [jax.ShapeDtypeStruct(self.scalars.shape, jnp.int32)],
            compiler_params=pltpu.CompilerParams(
                dimension_semantics=("arbitrary",) * len(grid), vmem_limit_bytes=limit
            ),
            cost_estimate=pl.CostEstimate(flops=1000000000000, bytes_accessed=1, transcendentals=0),
        )(
            self.scalars,
            *extra,
            *[
                v
                if i in free
                else pltpu.with_memory_space_constraint(v, pltpu.VMEM if i in near else pltpu.HBM)
                for i, v in enumerate(args)
            ],
        )
        return values


def pick_halves(core, value):
    cut = value.shape[1] // 2
    low, high = value[:, :cut], value[:, cut:]
    return jnp.where(core == 0, high, low), jnp.where(core == 0, low, high)


def tall_kernel(s_ref, a_ref, b_ref, away_ref, keep_ref):
    away_ref[...], keep_ref[...] = pick_halves(s_ref[CORE], mm(a_ref[...], b_ref[...], NT))


def tall_product(order, a, b):
    count, flat = a.shape
    tile, cut = count // 4, b.shape[0] // 2
    out = (spec((tile, cut), lambda i, *s: (i, 0)), ((count, cut), f32))
    ins = [spec((tile, flat), lambda i, *s: (i, 0)), spec(b.shape, lambda i, *s: (0, 0))]
    return order.call(tall_kernel, (4,), ins, [out, out], [], (a, b))


def wide_kernel(s_ref, a_ref, b_ref, away_ref, keep_ref):
    value = mm(a_ref[...], b_ref[...], NT)
    first = pl.program_id(0) < pl.num_programs(0) // 2

    @pl.when(first)
    def _():
        away_ref[...] = value

    @pl.when(jnp.logical_not(first))
    def _():
        keep_ref[...] = value


def wide_product(order, a, b):
    count, flat = a.shape
    cut = b.shape[0] // 2
    tile = 512
    half = cut // tile

    def source(i, s):
        return jnp.where(i < half, (1 - s[CORE]) * half + i, s[CORE] * half + i - half), 0

    outs = [
        (spec((count, tile), lambda i, s: (0, jnp.minimum(i, half - 1))), ((count, cut), f32)),
        (spec((count, tile), lambda i, s: (0, jnp.maximum(i - half, 0))), ((count, cut), f32)),
    ]
    ins = [spec(a.shape, lambda i, s: (0, 0)), spec((tile, flat), source)]
    return order.call(wide_kernel, (2 * half,), ins, outs, [], (a, b))


def twin_kernel(s_ref, a_ref, b_ref, c_ref, d_ref, *refs):
    core = s_ref[CORE]
    away_ref, keep_ref = refs[-2:]
    at = 0
    for left, right in ((a_ref, b_ref[0]), (c_ref, d_ref[0])):
        away, keep = pick_halves(core, mm(left[...], right, NT))
        away_ref[:, at : at + away.shape[1]] = away
        keep_ref[:, at : at + keep.shape[1]] = keep
        at += away.shape[1]
    if len(refs) == 3:
        value = refs[0][...]
        away_ref[:, at:] = jnp.where(core == 0, 0.0, value)
        keep_ref[:, at:] = jnp.where(core == 0, value, 0.0)


def twin_product(order, a, b, c, d, small=None):
    count, flat = a.shape
    tile = count // 2
    columns = count + (0 if small is None else small.shape[1])
    rows = spec((tile, flat), lambda i, s: (i, 0))
    ins, args = [], []
    for left, (right, group) in ((a, b), (c, d)):
        ins += [rows, spec((1, count, flat), lambda i, s, g=group: (g, 0, 0))]
        args += [left, right]
    if small is not None:
        ins.append(spec((tile, small.shape[1]), lambda i, s: (i, 0)))
        args.append(small)
    out = (spec((tile, columns), lambda i, s: (i, 0)), ((count, columns), f32))
    return order.call(twin_kernel, (2,), ins, [out, out], [], args)


def route_kernel(s_ref, *refs):
    for i in range(4):
        refs[8 + i][...] = refs[2 * i][...] + refs[2 * i + 1][...]


def route(order, left, right, low_bit, high_bit):
    (a, b), (c, d) = left, right
    shards, rows, columns = a.shape
    same = a is c
    if same:
        rows //= 2
    lower = 1 if same else 0
    half = shards // 2

    def by_low(flip):
        def index(i, s):
            mine = (s[PLACE] >> low_bit) & 1
            return 2 * i + ((1 - mine) if flip else mine), 0, 0

        return index

    def by_high(flip):
        def index(i, s):
            mine = (s[PLACE] >> high_bit) & 1
            return i + ((1 - mine) if flip else mine) * half, lower, 0

        return index

    block = (1, rows, columns)
    maps = [by_low(True), by_low(False), by_high(True), by_high(False)]
    ins = [spec(block, m) for m in maps for _ in range(2)]
    out = (spec(block, lambda i, s: (i, 0, 0)), ((half, rows, columns), f32))
    return order.call(route_kernel, (half,), ins, [out] * 4, [], (a, b, a, b, c, d, c, d))


def last_route_kernel(low_bit, high_bit, s_ref, a_ref, b_ref, c_ref, d_ref, *outs):
    left, right = ((s_ref[PLACE] >> bit) & 1 for bit in (low_bit, high_bit))
    outs[0][0] = a_ref[1 - left] + b_ref[1 - left]
    outs[1][0] = a_ref[left] + b_ref[left]
    outs[2][0] = c_ref[1 - right] + d_ref[1 - right]
    outs[3][0] = c_ref[right] + d_ref[right]


def last_route(order, left, right, low_bit, high_bit):
    shape = (1,) + left[0].shape[1:]
    return order.call(
        partial(last_route_kernel, low_bit, high_bit),
        (1,),
        [NEAR] * 4,
        [(NEAR, (shape, f32))] * 4,
        [],
        (*left, *right),
        free=(0, 2),
        near=(1, 3),
        near_out=range(4),
        limit=SMALL_LIMIT,
    )


def choose_kernel(s_ref, a_ref, b_ref, c_ref, d_ref, away_ref, kept_ref):
    upper, lower = a_ref[0] + b_ref[0], c_ref[0] + d_ref[0]
    odd = s_ref[ODD] == 1
    away_ref[...] = jnp.where(odd, upper, lower)
    kept_ref[...] = jnp.where(odd, lower, upper)


def choose(order, left, right):
    shape = left[0].shape[1:]
    return order.call(
        choose_kernel,
        (1,),
        [NEAR] * 4,
        [(NEAR, (shape, f32))] * 2,
        [],
        (*left, *right),
        free=range(4),
        near_out=range(2),
        limit=SMALL_LIMIT,
    )


def add_kernel(s_ref, a_ref, b_ref, out_ref):
    out_ref[...] = a_ref[...] + b_ref[...]


def add(order, a, b):
    outs = [(NEAR, (a.shape, f32))]
    return order.call(
        add_kernel, (1,), [NEAR] * 2, outs, [], (a, b), near=range(2), near_out=range(1), limit=SMALL_LIMIT
    )[0]


def merge_kernel(s_ref, kept_ref, got_ref, out_ref):
    odd = s_ref[ODD] == 1
    rows = kept_ref.shape[0]
    kept, got = kept_ref[...], got_ref[...]
    out_ref[:rows, :] = jnp.where(odd, got, kept)
    out_ref[rows:, :] = jnp.where(odd, kept, got)


def merge(order, kept, got):
    rows, columns = kept.shape
    outs = [(NEAR, ((2 * rows, columns), f32))]
    return order.call(
        merge_kernel,
        (1,),
        [NEAR] * 2,
        outs,
        [],
        (kept, got),
        near=range(2),
        near_out=range(1),
        limit=SMALL_LIMIT,
    )[0]


def side_kernel(s_ref, mine_ref, other_ref, *outs):
    first = s_ref[CORE] == 0
    at = 0
    for out in outs:
        cut = out.shape[1] // 2
        if cut < 128:
            out[...] = jnp.where(first, mine_ref[:, at:], other_ref[:, at:])
            break
        mine, other = mine_ref[:, at : at + cut], other_ref[:, at : at + cut]
        out[:, :cut] = jnp.where(first, mine, other)
        out[:, cut:] = jnp.where(first, other, mine)
        at += cut


def side(order, mine, other, widths):
    rows = mine.shape[0]
    outs = [(spec((rows, w), lambda i, s: (0, 0)), ((rows, w), f32)) for w in widths]
    return order.call(
        side_kernel, (1,), [NEAR] * 2, outs, [], (mine, other), near=range(2), limit=SMALL_LIMIT
    )


def mix_kernel(first, s_ref, w_ref, *refs):
    for row in range(refs[0].shape[0]):
        for i in range(2):
            own, other = (w_ref[first + 2 * i + j, row] for j in range(2))
            refs[4 + i][row] = own * refs[2 * i][row] + other * refs[2 * i + 1][row]


def mix(order, weights, first, last, *parts):
    shape = parts[0].shape
    out = spec(shape, lambda i, *s: (0, 0, 0)) if last else NEAR
    return order.call(
        partial(mix_kernel, first),
        (1,),
        [NEAR] * 4,
        [(out, (shape, f32))] * 2,
        [],
        parts,
        (weights,),
        near=range(4),
        near_out=() if last else range(2),
        limit=SMALL_LIMIT,
    )


def first_begins(lengths, count, tok_count):
    slots = lengths.shape[1]
    order = jnp.arange(slots)
    before = (order[:, None] > order[None, :]).astype(jnp.int32)
    starts = jnp.sum(lengths[:, None, :] * before[None], axis=-1)
    firsts = jnp.arange(count, dtype=jnp.int32) * tok_count
    reached = starts[:, None, :] <= firsts[None, :, None]
    return jnp.max(jnp.where(reached, starts[:, None, :], 0), axis=-1)


def pick(index, values):
    out = values[0]
    for i in range(1, len(values)):
        out = jnp.where(index == i, values[i], out)
    return out


def weights_of(begin_first, tok_count, reverse):
    count = lax.axis_size("seq")
    place = lax.axis_index("seq")

    def covers(i, j):
        low, high = (count - 1 - j, count - 1 - i) if reverse else (i, j)
        return (begin_first[:, high] < (low + 1) * tok_count).astype(f32)

    if count != 4:
        spots = jnp.arange(count)
        mine = begin_first.T if reverse else begin_first[:, place][None]
        reach = (place if reverse else spots[:, None]) + 1
        ahead = (spots > place) if reverse else (spots < place)
        return ((mine < reach * tok_count) & ahead[:, None]).astype(f32)
    index = count - 1 - place if reverse else place
    zero = jnp.zeros_like(begin_first[:, 0], f32)
    one = zero + 1.0
    m02, m03, m13 = covers(0, 2), covers(0, 3), covers(1, 3)
    onward = [
        pick(index, [m02, m13, zero, zero]),
        pick(index, [one, m03, zero, zero]),
        pick(index, [one, zero, one, zero]),
        pick(index, [zero, zero, m03, one]),
    ]
    final = [
        pick(index, [zero, one, zero, one]),
        pick(index, [zero, zero, one, one]),
        pick(index, [zero, zero, m02, m13]),
        pick(index, [zero, one, one, one]),
    ]
    return onward + final


def entering(order, parts, weights, first):
    if lax.axis_size("seq") != 4:
        gathered = [lax.all_gather(p, "seq") for p in parts]
        yield
        yield
        yield tuple(jnp.sum(g * weights[first][:, :, None, None], axis=0) for g in gathered)
    part_a, part_b = parts
    got_a, got_b = swap(part_a, "seq", 1), swap(part_b, "seq", 2)
    yield
    next_a, next_b = mix(order, weights, first, False, part_a, got_a, part_b, got_b)
    last_a, last_b = swap(next_a, "seq", 2), swap(next_b, "seq", 1)
    yield
    yield mix(order, weights, first + 4, True, got_a, last_a, got_b, last_b)


def swap(value, axis, distance):
    count = lax.axis_size(axis)
    return lax.ppermute(value, axis, [(i, i ^ distance) for i in range(count)])


def reduced(order, away, keep, widths):
    count = lax.axis_size("batch")
    shards = lax.axis_size("seq")
    bits = shards.bit_length() - 1
    shape = (shards, keep.shape[0] // shards, keep.shape[1])
    got = swap(away, "batch", 1).reshape(shape)
    yield
    left = right = (keep.reshape(shape), got)
    for step in range(bits):
        high = bits - 1 - step
        part = last_route if 0 < step == bits - 1 else route
        away_l, keep_l, away_r, keep_r = part(order, left, right, step, high)
        left = keep_l, swap(away_l, "seq", 1 << step)
        right = keep_r, swap(away_r, "seq", 1 << high)
        yield
    away, kept = choose(order, left, right)
    got = swap(away, "batch", 2)
    distance = 4
    while distance < count:
        yield
        kept = add(order, kept, got)
        got = swap(kept, "batch", distance)
        distance *= 2
    yield
    kept = add(order, kept, got)
    got = swap(kept, "batch", 2)
    yield
    merged = merge(order, kept, got)
    other = swap(merged, "batch", 1)
    yield
    yield side(order, merged, other, widths)


SCHEDULE = (
    "back_product", "states", "back", "local", "in_product", "states",
    "back", "in", "mixed_product", "back", "mixed", "tail",
    "back", "mixed", "in", "mixed", "last_product", "in",
    "last", "mixed", "back", "in", "last", "tokens",
    "last", "back", "mixed", "last", "in", "mixed",
    "last", "back", "in", "mixed", "last", "in",
    "last",
)


def body(
    tokens,
    cotangent,
    doc_lengths,
    w_query,
    w_key,
    w_value,
    w_out,
    w_in,
    w_back,
    gain_one,
    shift_one,
    gain_two,
    shift_two,
):
    rows, toks, width = tokens.shape
    ff = w_in.shape[1]
    flat = rows * toks
    shards = lax.axis_size("seq")
    whole = pl.BlockSpec(memory_space=pltpu.VMEM)
    token_major = pl.BlockSpec((1, toks, width), lambda r, *s: (r, 0, 0))
    table_spec = pl.BlockSpec((1, 8, toks), lambda r, *s: (r, 0, 0))
    state_spec = pl.BlockSpec((1, STATE_ROWS, 2 * HEAD_DIM), lambda r, *s: (r, 0, 0))

    def feature(count):
        return pl.BlockSpec((count, toks), lambda r, *s: (0, r))

    tok_low = (token_major, ((rows, toks, width), bf16))
    wide_low = (feature(width), ((width, flat), bf16))
    wide_full = (feature(width), ((width, flat), f32))
    ff_low = (feature(ff), ((ff, flat), bf16))
    head_rows = (feature(16), ((16, flat), f32))
    fold = (pl.BlockSpec((width, 128), lambda r, *s: (0, 0)), ((width, 128), f32))
    state = (state_spec, ((rows, STATE_ROWS, 2 * HEAD_DIM), f32))
    grid = (rows,)

    batch_place = lax.axis_index("batch").astype(jnp.int32)
    scalars = jnp.stack(
        [batch_place & 1, (batch_place >> 1) & 1, lax.axis_index("seq").astype(jnp.int32)]
    )
    order = Order(scalars)

    def run(kernel, ins, outs, scratch, *args, **more):
        return order.call(kernel, grid, ins, outs, scratch, args, **more)

    def column(v):
        return v[:, None]

    table, tok_t, k_t, v_t, key, value, sig_k, state_a, state_b = run(
        project_kernel,
        [token_major, whole, whole],
        [(table_spec, ((rows, 8, toks), f32))]
        + [wide_low] * 3
        + [tok_low] * 2
        + [wide_low]
        + [state] * 2,
        [pltpu.VMEM((2, width, width), bf16)],
        tokens,
        w_key,
        w_value,
        extra=(doc_lengths,),
    )
    begins = first_begins(doc_lengths, shards, toks)
    if shards == 4:
        weights = jnp.stack(weights_of(begins, toks, False) + weights_of(begins, toks, True))
        later = 8
    else:
        weights = [weights_of(begins, toks, False), weights_of(begins, toks, True)]
        later = 1
    states = entering(order, (state_a, state_b), weights, 0)
    next(states)
    part = ff // rows
    q_t, sig_q, numer, denom_loc, w_out_t, w_in_t, w_back_t = run(
        local_kernel,
        [
            table_spec,
            feature(width),
            token_major,
            feature(width),
            whole,
            whole,
            pl.BlockSpec((width, part), lambda r, *s: (0, r)),
            pl.BlockSpec((part, width), lambda r, *s: (r, 0)),
        ],
        [
            wide_low,
            wide_low,
            wide_full,
            head_rows,
            (pl.BlockSpec((width, width), lambda r, *s: (0, 0)), ((width, width), bf16)),
            (pl.BlockSpec((part, width), lambda r, *s: (r, 0)), ((ff, width), bf16)),
            (pl.BlockSpec((width, part), lambda r, *s: (0, r)), ((width, ff), bf16)),
        ],
        [pltpu.VMEM((width, width), bf16)],
        table,
        tok_t,
        key,
        v_t,
        w_query,
        w_out,
        w_in,
        w_back,
    )
    next(states)
    in_a, in_b = next(states)
    (
        layer_out,
        att_t,
        first_t,
        active_t,
        grad_second,
        grad_hidden,
        grad_base,
        grad_branch,
        grad_numer,
        grad_denom,
        small,
        out_a,
        out_b,
    ) = run(
        layer_kernel,
        [
            table_spec,
            feature(width),
            feature(width),
            feature(16),
            state_spec,
            state_spec,
            feature(width),
            token_major,
        ]
        + [whole] * 10,
        [
            tok_low,
            wide_low,
            wide_low,
            ff_low,
            wide_low,
            ff_low,
            wide_full,
            wide_low,
            wide_low,
            head_rows,
            fold,
            state,
            state,
        ],
        [
            pltpu.VMEM((ff, toks), bf16),
            pltpu.VMEM((width, toks), f32),
            pltpu.VMEM((width, toks), f32),
            pltpu.VMEM((16, toks), f32),
            pltpu.VMEM((width, toks), f32),
        ]
        + [pltpu.VMEM((width, 128), f32)] * 4
        + [pltpu.VMEM((width, toks), f32)],
        table,
        q_t,
        numer,
        denom_loc,
        in_a,
        in_b,
        tok_t,
        cotangent,
        w_out_t,
        w_in_t,
        w_back_t,
        w_out,
        w_in,
        w_back,
        column(gain_one),
        column(shift_one),
        column(gain_two),
        column(shift_two),
        near=range(8, 14),
        limit=LAYER_LIMIT,
    )

    back_states = entering(order, (out_a, out_b), weights, later)
    next(back_states)
    pieces, made = {}, {}

    def begin(name, product, widths):
        pieces[name] = reduced(order, *product, widths)
        next(pieces[name])

    def local_back():
        made["query"], made["key"], made["value"] = run(
            local_back_kernel,
            [
                table_spec,
                feature(width),
                feature(width),
                token_major,
                token_major,
                feature(width),
                feature(width),
                feature(16),
                state_spec,
                state_spec,
            ],
            [wide_low, wide_full, wide_full],
            [],
            table,
            q_t,
            k_t,
            key,
            value,
            sig_q,
            grad_numer,
            grad_denom,
            in_a,
            in_b,
        )

    def tail():
        back_a, back_b = made["states"]
        (made["kv"],) = run(
            tail_kernel,
            [table_spec]
            + [feature(width)] * 3
            + [state_spec] * 2
            + [feature(width)] * 2,
            [(pl.BlockSpec((2, width, toks), lambda r, *s: (0, 0, r)), ((2, width, flat), bf16))],
            [],
            table,
            k_t,
            v_t,
            sig_k,
            back_a,
            back_b,
            made["key"],
            made["value"],
        )

    def token_grads():
        (made["tokens"],) = run(
            token_kernel,
            [
                feature(width),
                pl.BlockSpec((2, width, toks), lambda r, *s: (0, 0, r)),
                feature(width),
            ]
            + [whole] * 3,
            [(token_major, ((rows, toks, width), f32))],
            [],
            made["query"],
            made["kv"],
            grad_base,
            w_query,
            w_key,
            w_value,
        )

    def states_on():
        made["states"] = next(back_states)

    steps = {
        "back_product": lambda: begin("back", tall_product(order, active_t, grad_second), (width,)),
        "in_product": lambda: begin("in", wide_product(order, first_t, grad_hidden), (ff,)),
        "mixed_product": lambda: begin(
            "mixed",
            twin_product(order, att_t, (grad_branch[None], 0), tok_t, (made["query"][None], 0), small),
            (width, width, 128),
        ),
        "last_product": lambda: begin(
            "last",
            twin_product(order, tok_t, (made["kv"], 0), tok_t, (made["kv"], 1)),
            (width, width),
        ),
        "states": states_on,
        "local": local_back,
        "tail": tail,
        "tokens": token_grads,
    }
    ends = {}

    def step(name):
        value = next(pieces[name])
        if value is not None:
            ends[name] = value

    for name in SCHEDULE:
        if name in steps:
            steps[name]()
        elif name not in ends:
            step(name)
    while len(ends) < len(pieces):
        for name in pieces:
            if name not in ends:
                step(name)
    (total_back,), (total_in,) = ends["back"], ends["in"]
    total_out, total_query, vectors = ends["mixed"]
    total_key, total_value = ends["last"]
    grad_tokens = made["tokens"]
    return (
        layer_out,
        grad_tokens,
        total_query,
        total_key,
        total_value,
        total_out,
        total_in,
        total_back,
        vectors[:, 0],
        vectors[:, 1],
        vectors[:, 2],
        vectors[:, 3],
    )


def solution(mesh):
    in_specs = (
        P("batch", "seq", None),
        P("batch", "seq", None),
        P("batch", None),
        P(),
        P(),
        P(),
        P(),
        P(),
        P(),
        P(),
        P(),
        P(),
        P(),
    )
    out_specs = (
        P("batch", "seq", None),
        P("batch", "seq", None),
        P("seq", None),
        P("seq", None),
        P("seq", None),
        P("seq", None),
        P("seq", None),
        P("seq", None),
        P("seq"),
        P("seq"),
        P("seq"),
        P("seq"),
    )
    return jax.shard_map(body, mesh=mesh, in_specs=in_specs, out_specs=out_specs, check_vma=False)
```

```python
from functools import partial

import jax
import jax.numpy as jnp
from jax import lax
from jax.experimental import pallas as pl
from jax.experimental.pallas import tpu as pltpu
from jax.sharding import PartitionSpec as P

HEADS = 12
HEAD_DIM = 64
PAIRS = HEADS // 2
HALF_HEADS = HEADS // 2
STATE_ROWS = HALF_HEADS * HEAD_DIM + 8

f32 = jnp.float32
bf16 = jnp.bfloat16
half_pi = 1.5707963267948966
norm_eps = 1e-05
VMEM_LIMIT = 30 * 1024 * 1024
SMALL_LIMIT = 16 * 1024 * 1024
LAYER_LIMIT = 38 * 1024 * 1024

NN = (((1,), (0,)), ((), ()))
NT = (((1,), (1,)), ((), ()))
TN = (((0,), (0,)), ((), ()))


def mm(a, b, dims=NN):
    return lax.dot_general(a, b, dims, preferred_element_type=f32)


COS, SIN, BEGIN, COS_READ, SIN_READ, COS_TAIL, SIN_TAIL = range(7)


def make_table(place, lens_ref, row, tok_count):
    pos = place + lax.broadcasted_iota(jnp.int32, (8, tok_count), 1)
    last = place + tok_count - 1
    start = jnp.int32(0)
    begin = jnp.zeros((8, tok_count), jnp.int32)
    span = jnp.ones((8, tok_count), jnp.int32)
    last_begin = jnp.int32(0)
    for d in range(lens_ref.shape[1]):
        length = lens_ref[row, d]
        inside = pos >= start
        begin = jnp.where(inside, start, begin)
        span = jnp.where(inside, length, span)
        last_begin = jnp.where(start <= last, start, last_begin)
        start = start + length
    angle = half_pi * (pos - begin).astype(f32) / span.astype(f32)
    cos, sin = jnp.cos(angle), jnp.sin(angle)
    reader = (begin < place).astype(f32)
    tail = (begin == last_begin).astype(f32)
    which = lax.broadcasted_iota(jnp.int32, (8, tok_count), 0)
    table = jnp.zeros((8, tok_count), f32)
    for index, value in (
        (COS, cos),
        (SIN, sin),
        (BEGIN, begin.astype(f32)),
        (COS_READ, cos * reader),
        (SIN_READ, sin * reader),
        (COS_TAIL, cos * tail),
        (SIN_TAIL, sin * tail),
    ):
        table = jnp.where(which == index, value, table)
    return table


def blend_of(table):
    columns = table.T
    tok_count = table.shape[1]
    source = lax.broadcasted_iota(jnp.int32, (tok_count, tok_count), 0)
    reader = lax.broadcasted_iota(jnp.int32, (tok_count, tok_count), 1)
    same = (columns[:, BEGIN : BEGIN + 1] == table[BEGIN : BEGIN + 1]) & (source <= reader)
    value = (
        columns[:, COS : COS + 1] * table[COS : COS + 1]
        + columns[:, SIN : SIN + 1] * table[SIN : SIN + 1]
    )
    return jnp.where(same, value, 0.0)


def trig_rows(head_rows, cos, sin):
    wide = head_rows.astype(f32)
    return jnp.concatenate([(wide * cos).astype(bf16), (wide * sin).astype(bf16)], axis=0)


def with_row(rows, extra):
    which = lax.broadcasted_iota(jnp.int32, (16, rows.shape[1]), 0)
    return jnp.concatenate([rows, jnp.where(which == 0, extra, 0.0).astype(bf16)], axis=0)


def head_slice(h):
    return slice(h * HEAD_DIM, (h + 1) * HEAD_DIM)


def put_state(state_refs, h, value):
    ref = state_refs[h // HALF_HEADS]
    place = h % HALF_HEADS
    ref[0, head_slice(place), :] = value[:HEAD_DIM]
    ref[0, HALF_HEADS * HEAD_DIM + place : HALF_HEADS * HEAD_DIM + place + 1, :] = value[
        HEAD_DIM : HEAD_DIM + 1
    ]


def take_state(state_refs, h):
    ref = state_refs[h // HALF_HEADS]
    place = h % HALF_HEADS
    mats = ref[0, head_slice(place), :].astype(bf16)
    sums = ref[0, HALF_HEADS * HEAD_DIM + place : HALF_HEADS * HEAD_DIM + place + 1, :]
    return with_row(mats, sums)


def clear_pad(state_refs):
    for ref in state_refs:
        ref[0, HALF_HEADS * HEAD_DIM :, :] = jnp.zeros((8, 2 * HEAD_DIM), f32)


def softplus_sigmoid(v):
    small = jnp.exp(-jnp.abs(v))
    soft = jnp.maximum(v, 0.0) + jnp.log1p(small)
    inverse = 1.0 / (1.0 + small)
    return soft, jnp.where(v >= 0, inverse, small * inverse)


def project_kernel(
    s_ref,
    lens_ref,
    tok_ref,
    wk_ref,
    wv_ref,
    tab_ref,
    tok_t_ref,
    k_t_ref,
    v_t_ref,
    k_ref,
    v_ref,
    sig_k_ref,
    state_a,
    state_b,
    w_t,
):
    row = pl.program_id(0)

    @pl.when(row == 0)
    def _():
        w_t[0] = wk_ref[...].T
        w_t[1] = wv_ref[...].T

    tok_t = tok_ref[0].T
    tok_t_ref[...] = tok_t
    table = make_table(s_ref[PLACE] * tok_t.shape[1], lens_ref, row, tok_t.shape[1])
    tab_ref[0] = table
    soft, sig = softplus_sigmoid(mm(w_t[0], tok_t))
    key_t = soft.astype(bf16)
    k_t_ref[...] = key_t
    k_ref[0] = key_t.T
    sig_k_ref[...] = sig.astype(bf16)
    value_t = mm(w_t[1], tok_t).astype(bf16)
    v_t_ref[...] = value_t
    v_ref[0] = value_t.T
    states = (state_a, state_b)
    clear_pad(states)
    cos, sin = table[COS_TAIL : COS_TAIL + 1], table[SIN_TAIL : SIN_TAIL + 1]
    for h in range(HEADS):
        keys = trig_rows(k_t_ref[head_slice(h), :], cos, sin)
        values = with_row(v_t_ref[head_slice(h), :], 1.0)
        put_state(states, h, mm(values, keys, NT))


def pair_rows(ref, pair):
    first = ref[head_slice(2 * pair), :]
    second = ref[head_slice(2 * pair + 1), :]
    nothing = jnp.zeros_like(first)
    return jnp.concatenate(
        [
            jnp.concatenate([first, nothing], axis=1),
            jnp.concatenate([nothing, second], axis=1),
        ],
        axis=0,
    )


def two_parts(v):
    high = v.astype(bf16)
    return high, (v - high.astype(f32)).astype(bf16)


def local_kernel(
    s_ref,
    tab_ref,
    tok_t_ref,
    k_ref,
    v_t_ref,
    wq_ref,
    w_out_ref,
    w_in_ref,
    w_back_ref,
    q_t_ref,
    sig_q_ref,
    numer_ref,
    denom_ref,
    w_out_t,
    w_in_t,
    w_back_t,
    w_t,
):
    @pl.when(pl.program_id(0) == 0)
    def _():
        w_t[...] = wq_ref[...].T
        w_out_t[...] = w_out_ref[...].T

    w_in_t[...] = w_in_ref[...].T
    w_back_t[...] = w_back_ref[...].T

    soft, sig = softplus_sigmoid(mm(w_t[...], tok_t_ref[...]))
    q_t_ref[...] = soft.astype(bf16)
    sig_q_ref[...] = sig.astype(bf16)
    blend = blend_of(tab_ref[0])
    tok_count = blend.shape[0]
    denom_ref[...] = jnp.zeros_like(denom_ref)
    for pair in range(PAIRS):
        lanes = slice(pair * 2 * HEAD_DIM, (pair + 1) * 2 * HEAD_DIM)
        both = mm(k_ref[0, :, lanes], pair_rows(q_t_ref, pair))
        for side in range(2):
            h = 2 * pair + side
            high, low = two_parts(both[:, side * tok_count : (side + 1) * tok_count] * blend)
            values = with_row(v_t_ref[head_slice(h), :], 1.0)
            out = mm(values, high) + mm(values, low)
            numer_ref[head_slice(h), :] = out[:HEAD_DIM]
            denom_ref[h : h + 1, :] = out[HEAD_DIM : HEAD_DIM + 1]


def fold_lanes(v):
    total = v[:, :128]
    for at in range(128, v.shape[1], 128):
        total = total + v[:, at : at + 128]
    return total


def chunks_of(ref):
    return [slice(at, at + 128) for at in range(0, ref.shape[0], 128)]


def fold_rows(v):
    return jnp.sum(v.reshape(v.shape[0] // 8, 8, v.shape[1]), axis=0)


def mean_of(fold, count):
    return jnp.sum(fold, axis=0, keepdims=True) * (1.0 / count)


def center(ref, more=None):
    width, lanes = ref.shape
    fold = jnp.zeros((8, lanes), f32)
    for c in chunks_of(ref):
        value = ref[c, :]
        if more is not None:
            value = value + more[c, :].astype(f32)
            ref[c, :] = value
        fold = fold + fold_rows(value)
    mean = mean_of(fold, width)
    fold = jnp.zeros((8, lanes), f32)
    for c in chunks_of(ref):
        value = ref[c, :] - mean
        ref[c, :] = value
        fold = fold + fold_rows(value * value)
    return lax.rsqrt(mean_of(fold, width) + norm_eps)


def lane_total(ref):
    return jnp.sum(ref[...], axis=1, keepdims=True)


def layer_kernel(
    s_ref,
    tab_ref,
    q_t_ref,
    numer_ref,
    denom_loc_ref,
    state_a,
    state_b,
    tok_t_ref,
    cot_ref,
    w_out_t,
    w_in_t,
    w_back_t,
    w_out_ref,
    w_in_ref,
    w_back_ref,
    gain_one_ref,
    shift_one_ref,
    gain_two_ref,
    shift_two_ref,
    layer_ref,
    att_t_ref,
    first_t_ref,
    active_t_ref,
    grad_second_ref,
    grad_hidden_ref,
    grad_base_ref,
    grad_branch_ref,
    grad_numer_ref,
    grad_denom_ref,
    small_ref,
    out_a,
    out_b,
    slope,
    normed_one,
    attended,
    inverse_denom,
    total,
    fold_gain_one,
    fold_shift_one,
    fold_gain_two,
    fold_shift_two,
    work,
):
    ff = w_in_ref.shape[1]
    step = 768

    @pl.when(pl.program_id(0) == 0)
    def _():
        for ref in (fold_gain_one, fold_shift_one, fold_gain_two, fold_shift_two):
            ref[...] = jnp.zeros_like(ref)

    table = tab_ref[0]
    cos, sin = table[COS_READ : COS_READ + 1], table[SIN_READ : SIN_READ + 1]
    states = (state_a, state_b)
    for h in range(HEADS):
        reads = trig_rows(q_t_ref[head_slice(h), :], cos, sin)
        more = mm(take_state(states, h), reads)
        numer = numer_ref[head_slice(h), :] + more[:HEAD_DIM]
        inverse = 1.0 / (denom_loc_ref[h : h + 1, :] + more[HEAD_DIM : HEAD_DIM + 1])
        inverse_denom[h : h + 1, :] = inverse
        value = numer * inverse
        attended[head_slice(h), :] = value
        att_t_ref[head_slice(h), :] = value.astype(bf16)
    total[...] = mm(w_out_t[...], att_t_ref[...])
    scale_one = center(total, tok_t_ref)
    for c in chunks_of(total):
        normed = total[c, :] * scale_one
        normed_one[c, :] = normed
        first_out = normed * gain_one_ref[c, :] + shift_one_ref[c, :]
        total[c, :] = first_out
        first_t_ref[c, :] = first_out.astype(bf16)
    first_low = first_t_ref[...]
    for at in range(0, ff, step):
        hidden = mm(w_in_t[at : at + step, :], first_low)
        half = 0.5 * (1.0 + lax.erf(hidden * 0.7071067811865476))
        bell = jnp.exp(hidden * hidden * -0.5) * 0.3989422804014327
        active = (hidden * half).astype(bf16)
        active_t_ref[at : at + step, :] = active
        slope[at : at + step, :] = (half + hidden * bell).astype(bf16)
        total[...] += mm(w_back_t[:, at : at + step], active)
    scale_two = center(total)
    fold_one = fold_two = jnp.zeros((8, total.shape[1]), f32)
    for c in chunks_of(total):
        normed = total[c, :] * scale_two
        total[c, :] = normed
        layer_ref[0, :, c] = (normed * gain_two_ref[c, :] + shift_two_ref[c, :]).T.astype(bf16)
        grad_top = cot_ref[0, :, c].T.astype(f32)
        fold_gain_two[c, :] += fold_lanes(grad_top * normed)
        fold_shift_two[c, :] += fold_lanes(grad_top)
        grad_norm = grad_top * gain_two_ref[c, :]
        work[c, :] = grad_norm
        fold_one = fold_one + fold_rows(grad_norm)
        fold_two = fold_two + fold_rows(grad_norm * normed)
    mean_one, mean_two = mean_of(fold_one, total.shape[0]), mean_of(fold_two, total.shape[0])
    for c in chunks_of(total):
        grad_mid = scale_two * (work[c, :] - mean_one - total[c, :] * mean_two)
        total[c, :] = grad_mid
        grad_second_ref[c, :] = grad_mid.astype(bf16)
    grad_second = grad_second_ref[...]
    for at in range(0, ff, step):
        grad_active = mm(w_back_ref[at : at + step, :], grad_second)
        low = (grad_active * slope[at : at + step, :].astype(f32)).astype(bf16)
        grad_hidden_ref[at : at + step, :] = low
        total[...] += mm(w_in_ref[:, at : at + step], low)
    fold_one = fold_two = jnp.zeros((8, total.shape[1]), f32)
    for c in chunks_of(total):
        grad_first, normed = total[c, :], normed_one[c, :]
        fold_gain_one[c, :] += fold_lanes(grad_first * normed)
        fold_shift_one[c, :] += fold_lanes(grad_first)
        grad_norm = grad_first * gain_one_ref[c, :]
        work[c, :] = grad_norm
        fold_one = fold_one + fold_rows(grad_norm)
        fold_two = fold_two + fold_rows(grad_norm * normed)
    mean_one, mean_two = mean_of(fold_one, total.shape[0]), mean_of(fold_two, total.shape[0])
    for c in chunks_of(total):
        grad_base = scale_one * (work[c, :] - mean_one - normed_one[c, :] * mean_two)
        grad_base_ref[c, :] = grad_base
        grad_branch_ref[c, :] = grad_base.astype(bf16)
    grad_branch = grad_branch_ref[...]
    total[...] = mm(w_out_ref[...], grad_branch)
    outs = (out_a, out_b)
    clear_pad(outs)
    grad_denom_ref[...] = jnp.zeros_like(grad_denom_ref)
    for h in range(HEADS):
        rows = head_slice(h)
        grad_numer = (total[rows, :] * inverse_denom[h : h + 1, :]).astype(bf16)
        grad_denom = -jnp.sum(grad_numer.astype(f32) * attended[rows, :], axis=0, keepdims=True)
        grad_denom_ref[h : h + 1, :] = grad_denom
        grad_numer_ref[rows, :] = grad_numer
        reads = trig_rows(q_t_ref[rows, :], cos, sin)
        put_state(outs, h, mm(with_row(grad_numer, grad_denom), reads, NT))

    @pl.when(pl.program_id(0) == pl.num_programs(0) - 1)
    def _():
        lane = lax.broadcasted_iota(jnp.int32, small_ref.shape, 1)
        value = jnp.zeros(small_ref.shape, f32)
        for i, ref in enumerate((fold_gain_one, fold_shift_one, fold_gain_two, fold_shift_two)):
            value = jnp.where(lane == i, lane_total(ref), value)
        small_ref[...] = value


def local_back_kernel(
    s_ref,
    tab_ref,
    q_t_ref,
    k_t_ref,
    k_ref,
    v_ref,
    sig_q_ref,
    grad_numer_ref,
    grad_denom_ref,
    state_a,
    state_b,
    grad_q_ref,
    grad_k_ref,
    grad_v_ref,
):
    table = tab_ref[0]
    blend = blend_of(table)
    tok_count = blend.shape[0]
    cos, sin = table[COS_READ : COS_READ + 1], table[SIN_READ : SIN_READ + 1]
    states = (state_a, state_b)
    for pair in range(PAIRS):
        lanes = slice(pair * 2 * HEAD_DIM, (pair + 1) * 2 * HEAD_DIM)
        both = mm(k_ref[0, :, lanes], pair_rows(q_t_ref, pair))
        grads = mm(v_ref[0, :, lanes], pair_rows(grad_numer_ref, pair))
        for side in range(2):
            h = 2 * pair + side
            rows = head_slice(h)
            part = slice(side * tok_count, (side + 1) * tok_count)
            grad_denom = grad_denom_ref[h : h + 1, :]
            scores = (both[:, part] * blend).astype(bf16)
            grad_scores, rest = two_parts((grads[:, part] + grad_denom) * blend)
            grad_numer = grad_numer_ref[rows, :]
            grad_v_ref[rows, :] = mm(grad_numer, scores, NT)
            grad_k_ref[rows, :] = mm(q_t_ref[rows, :], grad_scores, NT)
            reads = mm(take_state(states, h), with_row(grad_numer, grad_denom), TN)
            grad_q = (
                mm(k_t_ref[rows, :], grad_scores)
                + mm(k_t_ref[rows, :], rest)
                + cos * reads[:HEAD_DIM]
                + sin * reads[HEAD_DIM:]
            )
            grad_q_ref[rows, :] = (grad_q * sig_q_ref[rows, :].astype(f32)).astype(bf16)


def tail_kernel(
    s_ref,
    tab_ref,
    k_t_ref,
    v_t_ref,
    sig_k_ref,
    state_a,
    state_b,
    grad_k_in,
    grad_v_in,
    grad_kv_ref,
):
    table = tab_ref[0]
    cos, sin = table[COS_TAIL : COS_TAIL + 1], table[SIN_TAIL : SIN_TAIL + 1]
    states = (state_a, state_b)
    for h in range(HEADS):
        rows = head_slice(h)
        state = take_state(states, h)
        inner = mm(state, with_row(v_t_ref[rows, :], 1.0), TN)
        grad_k = grad_k_in[rows, :] + cos * inner[:HEAD_DIM] + sin * inner[HEAD_DIM:]
        grad_kv_ref[0, rows, :] = (grad_k * sig_k_ref[rows, :].astype(f32)).astype(bf16)
        keys = trig_rows(k_t_ref[rows, :], cos, sin)
        grad_kv_ref[1, rows, :] = (grad_v_in[rows, :] + mm(state[:HEAD_DIM], keys)).astype(bf16)


def token_kernel(s_ref, gq_ref, gkv_ref, base_ref, wq_ref, wk_ref, wv_ref, out_ref):
    total = base_ref[...] + mm(wq_ref[...], gq_ref[...])
    total = total + mm(wk_ref[...], gkv_ref[0])
    total = total + mm(wv_ref[...], gkv_ref[1])
    out_ref[0] = total.T


def spec(block, index):
    return pl.BlockSpec(block, index)


NEAR = pl.BlockSpec(memory_space=pltpu.VMEM)

CORE, ODD, PLACE = range(3)


class Order:
    def __init__(self, scalars):
        self.scalars = scalars

    def call(
        self, kernel, grid, ins, outs, scratch, args, extra=(), free=(), near=(), near_out=(), limit=VMEM_LIMIT
    ):
        count = 1 + len(extra)
        placed = len(scratch)

        def stepped(*refs):
            s_ref, handed = refs[0], refs[len(refs) - placed - 1]
            rest = refs[: len(refs) - placed - 1] + refs[len(refs) - placed :]
            kernel(*rest)
            for i in range(s_ref.shape[0]):
                handed[i] = s_ref[i]

        *values, self.scalars = pl.pallas_call(
            stepped,
            grid_spec=pltpu.PrefetchScalarGridSpec(
                num_scalar_prefetch=count,
                grid=grid,
                in_specs=ins,
                out_specs=[o for o, _ in outs] + [pl.BlockSpec(memory_space=pltpu.SMEM)],
                scratch_shapes=scratch,
            ),
            out_shape=[
                (pltpu.VMEM if i in near_out else pltpu.HBM)(shape, kind)
                for i, (_, (shape, kind)) in enumerate(outs)
            ]
            + [jax.ShapeDtypeStruct(self.scalars.shape, jnp.int32)],
            compiler_params=pltpu.CompilerParams(
                dimension_semantics=("arbitrary",) * len(grid), vmem_limit_bytes=limit
            ),
            cost_estimate=pl.CostEstimate(flops=1000000000000, bytes_accessed=1, transcendentals=0),
        )(
            self.scalars,
            *extra,
            *[
                v
                if i in free
                else pltpu.with_memory_space_constraint(v, pltpu.VMEM if i in near else pltpu.HBM)
                for i, v in enumerate(args)
            ],
        )
        return values


def pick_halves(core, value):
    cut = value.shape[1] // 2
    low, high = value[:, :cut], value[:, cut:]
    return jnp.where(core == 0, high, low), jnp.where(core == 0, low, high)


def tall_kernel(s_ref, a_ref, b_ref, away_ref, keep_ref):
    away_ref[...], keep_ref[...] = pick_halves(s_ref[CORE], mm(a_ref[...], b_ref[...], NT))


def tall_product(order, a, b):
    count, flat = a.shape
    tile, cut = count // 2, b.shape[0] // 2
    out = (spec((tile, cut), lambda i, *s: (i, 0)), ((count, cut), f32))
    ins = [spec((tile, flat), lambda i, *s: (i, 0)), spec(b.shape, lambda i, *s: (0, 0))]
    return order.call(tall_kernel, (2,), ins, [out, out], [], (a, b))


def wide_kernel(s_ref, a_ref, b_ref, away_ref, keep_ref):
    value = mm(a_ref[...], b_ref[...], NT)
    first = pl.program_id(0) < pl.num_programs(0) // 2

    @pl.when(first)
    def _():
        away_ref[...] = value

    @pl.when(jnp.logical_not(first))
    def _():
        keep_ref[...] = value


def wide_product(order, a, b):
    count, flat = a.shape
    cut = b.shape[0] // 2
    tile = 768
    half = cut // tile

    def source(i, s):
        return jnp.where(i < half, (1 - s[CORE]) * half + i, s[CORE] * half + i - half), 0

    outs = [
        (spec((count, tile), lambda i, s: (0, jnp.minimum(i, half - 1))), ((count, cut), f32)),
        (spec((count, tile), lambda i, s: (0, jnp.maximum(i - half, 0))), ((count, cut), f32)),
    ]
    ins = [spec(a.shape, lambda i, s: (0, 0)), spec((tile, flat), source)]
    return order.call(wide_kernel, (2 * half,), ins, outs, [], (a, b))


def twin_kernel(s_ref, a_ref, b_ref, c_ref, d_ref, *refs):
    core = s_ref[CORE]
    away_ref, keep_ref = refs[-2:]
    at = 0
    for left, right in ((a_ref, b_ref[0]), (c_ref, d_ref[0])):
        away, keep = pick_halves(core, mm(left[...], right, NT))
        away_ref[:, at : at + away.shape[1]] = away
        keep_ref[:, at : at + keep.shape[1]] = keep
        at += away.shape[1]
    if len(refs) == 3:
        value = refs[0][...]
        away_ref[:, at:] = jnp.where(core == 0, 0.0, value)
        keep_ref[:, at:] = jnp.where(core == 0, value, 0.0)


def twin_product(order, a, b, c, d, small=None):
    count, flat = a.shape
    tile = count // 2
    columns = count + (0 if small is None else small.shape[1])
    rows = spec((tile, flat), lambda i, s: (i, 0))
    ins, args = [], []
    for left, (right, group) in ((a, b), (c, d)):
        ins += [rows, spec((1, count, flat), lambda i, s, g=group: (g, 0, 0))]
        args += [left, right]
    if small is not None:
        ins.append(spec((tile, small.shape[1]), lambda i, s: (i, 0)))
        args.append(small)
    out = (spec((tile, columns), lambda i, s: (i, 0)), ((count, columns), f32))
    return order.call(twin_kernel, (2,), ins, [out, out], [], args)


def route_kernel(s_ref, *refs):
    for i in range(4):
        refs[8 + i][...] = refs[2 * i][...] + refs[2 * i + 1][...]


def route(order, left, right, low_bit, high_bit):
    (a, b), (c, d) = left, right
    shards, rows, columns = a.shape
    same = a is c
    if same:
        rows //= 2
    lower = 1 if same else 0
    half = shards // 2

    def by_low(flip):
        def index(i, s):
            mine = (s[PLACE] >> low_bit) & 1
            return 2 * i + ((1 - mine) if flip else mine), 0, 0

        return index

    def by_high(flip):
        def index(i, s):
            mine = (s[PLACE] >> high_bit) & 1
            return i + ((1 - mine) if flip else mine) * half, lower, 0

        return index

    block = (1, rows, columns)
    maps = [by_low(True), by_low(False), by_high(True), by_high(False)]
    ins = [spec(block, m) for m in maps for _ in range(2)]
    out = (spec(block, lambda i, s: (i, 0, 0)), ((half, rows, columns), f32))
    return order.call(route_kernel, (half,), ins, [out] * 4, [], (a, b, a, b, c, d, c, d))


def last_route_kernel(low_bit, high_bit, s_ref, a_ref, b_ref, c_ref, d_ref, *outs):
    left, right = ((s_ref[PLACE] >> bit) & 1 for bit in (low_bit, high_bit))
    outs[0][0] = a_ref[1 - left] + b_ref[1 - left]
    outs[1][0] = a_ref[left] + b_ref[left]
    outs[2][0] = c_ref[1 - right] + d_ref[1 - right]
    outs[3][0] = c_ref[right] + d_ref[right]


def last_route(order, left, right, low_bit, high_bit):
    shape = (1,) + left[0].shape[1:]
    return order.call(
        partial(last_route_kernel, low_bit, high_bit),
        (1,),
        [NEAR] * 4,
        [(NEAR, (shape, f32))] * 4,
        [],
        (*left, *right),
        free=(0, 2),
        near=(1, 3),
        near_out=range(4),
        limit=SMALL_LIMIT,
    )


def choose_kernel(s_ref, a_ref, b_ref, c_ref, d_ref, away_ref, kept_ref):
    upper, lower = a_ref[0] + b_ref[0], c_ref[0] + d_ref[0]
    odd = s_ref[ODD] == 1
    away_ref[...] = jnp.where(odd, upper, lower)
    kept_ref[...] = jnp.where(odd, lower, upper)


def choose(order, left, right):
    shape = left[0].shape[1:]
    return order.call(
        choose_kernel,
        (1,),
        [NEAR] * 4,
        [(NEAR, (shape, f32))] * 2,
        [],
        (*left, *right),
        free=range(4),
        near_out=range(2),
        limit=SMALL_LIMIT,
    )


def add_kernel(s_ref, a_ref, b_ref, out_ref):
    out_ref[...] = a_ref[...] + b_ref[...]


def add(order, a, b):
    outs = [(NEAR, (a.shape, f32))]
    return order.call(
        add_kernel, (1,), [NEAR] * 2, outs, [], (a, b), near=range(2), near_out=range(1), limit=SMALL_LIMIT
    )[0]


def merge_kernel(s_ref, kept_ref, got_ref, out_ref):
    odd = s_ref[ODD] == 1
    rows = kept_ref.shape[0]
    kept, got = kept_ref[...], got_ref[...]
    out_ref[:rows, :] = jnp.where(odd, got, kept)
    out_ref[rows:, :] = jnp.where(odd, kept, got)


def merge(order, kept, got):
    rows, columns = kept.shape
    outs = [(NEAR, ((2 * rows, columns), f32))]
    return order.call(
        merge_kernel,
        (1,),
        [NEAR] * 2,
        outs,
        [],
        (kept, got),
        near=range(2),
        near_out=range(1),
        limit=SMALL_LIMIT,
    )[0]


def side_kernel(s_ref, mine_ref, other_ref, *outs):
    first = s_ref[CORE] == 0
    at = 0
    for out in outs:
        cut = out.shape[1] // 2
        if cut < 128:
            out[...] = jnp.where(first, mine_ref[:, at:], other_ref[:, at:])
            break
        mine, other = mine_ref[:, at : at + cut], other_ref[:, at : at + cut]
        out[:, :cut] = jnp.where(first, mine, other)
        out[:, cut:] = jnp.where(first, other, mine)
        at += cut


def side(order, mine, other, widths):
    rows = mine.shape[0]
    outs = [(spec((rows, w), lambda i, s: (0, 0)), ((rows, w), f32)) for w in widths]
    return order.call(
        side_kernel, (1,), [NEAR] * 2, outs, [], (mine, other), near=range(2), limit=SMALL_LIMIT
    )


def mix_kernel(first, s_ref, w_ref, *refs):
    for row in range(refs[0].shape[0]):
        for i in range(2):
            own, other = (w_ref[first + 2 * i + j, row] for j in range(2))
            refs[4 + i][row] = own * refs[2 * i][row] + other * refs[2 * i + 1][row]


def mix(order, weights, first, last, *parts):
    shape = parts[0].shape
    out = spec(shape, lambda i, *s: (0, 0, 0)) if last else NEAR
    return order.call(
        partial(mix_kernel, first),
        (1,),
        [NEAR] * 4,
        [(out, (shape, f32))] * 2,
        [],
        parts,
        (weights,),
        near=range(4),
        near_out=() if last else range(2),
        limit=SMALL_LIMIT,
    )


def first_begins(lengths, count, tok_count):
    slots = lengths.shape[1]
    order = jnp.arange(slots)
    before = (order[:, None] > order[None, :]).astype(jnp.int32)
    starts = jnp.sum(lengths[:, None, :] * before[None], axis=-1)
    firsts = jnp.arange(count, dtype=jnp.int32) * tok_count
    reached = starts[:, None, :] <= firsts[None, :, None]
    return jnp.max(jnp.where(reached, starts[:, None, :], 0), axis=-1)


def pick(index, values):
    out = values[0]
    for i in range(1, len(values)):
        out = jnp.where(index == i, values[i], out)
    return out


def weights_of(begin_first, tok_count, reverse):
    count = lax.axis_size("seq")
    place = lax.axis_index("seq")

    def covers(i, j):
        low, high = (count - 1 - j, count - 1 - i) if reverse else (i, j)
        return (begin_first[:, high] < (low + 1) * tok_count).astype(f32)

    if count != 4:
        spots = jnp.arange(count)
        mine = begin_first.T if reverse else begin_first[:, place][None]
        reach = (place if reverse else spots[:, None]) + 1
        ahead = (spots > place) if reverse else (spots < place)
        return ((mine < reach * tok_count) & ahead[:, None]).astype(f32)
    index = count - 1 - place if reverse else place
    zero = jnp.zeros_like(begin_first[:, 0], f32)
    one = zero + 1.0
    m02, m03, m13 = covers(0, 2), covers(0, 3), covers(1, 3)
    onward = [
        pick(index, [m02, m13, zero, zero]),
        pick(index, [one, m03, zero, zero]),
        pick(index, [one, zero, one, zero]),
        pick(index, [zero, zero, m03, one]),
    ]
    final = [
        pick(index, [zero, one, zero, one]),
        pick(index, [zero, zero, one, one]),
        pick(index, [zero, zero, m02, m13]),
        pick(index, [zero, one, one, one]),
    ]
    return onward + final


def entering(order, parts, weights, first):
    if lax.axis_size("seq") != 4:
        gathered = [lax.all_gather(p, "seq") for p in parts]
        yield
        yield
        yield tuple(jnp.sum(g * weights[first][:, :, None, None], axis=0) for g in gathered)
    part_a, part_b = parts
    got_a, got_b = swap(part_a, "seq", 1), swap(part_b, "seq", 2)
    yield
    next_a, next_b = mix(order, weights, first, False, part_a, got_a, part_b, got_b)
    last_a, last_b = swap(next_a, "seq", 2), swap(next_b, "seq", 1)
    yield
    yield mix(order, weights, first + 4, True, got_a, last_a, got_b, last_b)


def swap(value, axis, distance):
    count = lax.axis_size(axis)
    return lax.ppermute(value, axis, [(i, i ^ distance) for i in range(count)])


def reduced(order, away, keep, widths):
    count = lax.axis_size("batch")
    shards = lax.axis_size("seq")
    bits = shards.bit_length() - 1
    shape = (shards, keep.shape[0] // shards, keep.shape[1])
    got = swap(away, "batch", 1).reshape(shape)
    yield
    left = right = (keep.reshape(shape), got)
    for step in range(bits):
        high = bits - 1 - step
        part = last_route if 0 < step == bits - 1 else route
        away_l, keep_l, away_r, keep_r = part(order, left, right, step, high)
        left = keep_l, swap(away_l, "seq", 1 << step)
        right = keep_r, swap(away_r, "seq", 1 << high)
        yield
    away, kept = choose(order, left, right)
    got = swap(away, "batch", 2)
    distance = 4
    while distance < count:
        yield
        kept = add(order, kept, got)
        got = swap(kept, "batch", distance)
        distance *= 2
    yield
    kept = add(order, kept, got)
    got = swap(kept, "batch", 2)
    yield
    merged = merge(order, kept, got)
    other = swap(merged, "batch", 1)
    yield
    yield side(order, merged, other, widths)


SCHEDULE = (
    "back_product", "states", "back", "local", "in_product", "states",
    "back", "in", "mixed_product", "back", "mixed", "tail",
    "back", "mixed", "in", "mixed", "last_product", "in",
    "last", "mixed", "back", "in", "last", "tokens",
    "last", "back", "mixed", "last", "in", "mixed",
    "last", "back", "in", "mixed", "last", "in",
    "last",
)


def body(
    tokens,
    cotangent,
    doc_lengths,
    w_query,
    w_key,
    w_value,
    w_out,
    w_in,
    w_back,
    gain_one,
    shift_one,
    gain_two,
    shift_two,
):
    rows, toks, width = tokens.shape
    ff = w_in.shape[1]
    flat = rows * toks
    shards = lax.axis_size("seq")
    whole = pl.BlockSpec(memory_space=pltpu.VMEM)
    token_major = pl.BlockSpec((1, toks, width), lambda r, *s: (r, 0, 0))
    table_spec = pl.BlockSpec((1, 8, toks), lambda r, *s: (r, 0, 0))
    state_spec = pl.BlockSpec((1, STATE_ROWS, 2 * HEAD_DIM), lambda r, *s: (r, 0, 0))

    def feature(count):
        return pl.BlockSpec((count, toks), lambda r, *s: (0, r))

    tok_low = (token_major, ((rows, toks, width), bf16))
    wide_low = (feature(width), ((width, flat), bf16))
    wide_full = (feature(width), ((width, flat), f32))
    ff_low = (feature(ff), ((ff, flat), bf16))
    head_rows = (feature(16), ((16, flat), f32))
    fold = (pl.BlockSpec((width, 128), lambda r, *s: (0, 0)), ((width, 128), f32))
    state = (state_spec, ((rows, STATE_ROWS, 2 * HEAD_DIM), f32))
    grid = (rows,)

    batch_place = lax.axis_index("batch").astype(jnp.int32)
    scalars = jnp.stack(
        [batch_place & 1, (batch_place >> 1) & 1, lax.axis_index("seq").astype(jnp.int32)]
    )
    order = Order(scalars)

    def run(kernel, ins, outs, scratch, *args, **more):
        return order.call(kernel, grid, ins, outs, scratch, args, **more)

    def column(v):
        return v[:, None]

    table, tok_t, k_t, v_t, key, value, sig_k, state_a, state_b = run(
        project_kernel,
        [token_major, whole, whole],
        [(table_spec, ((rows, 8, toks), f32))]
        + [wide_low] * 3
        + [tok_low] * 2
        + [wide_low]
        + [state] * 2,
        [pltpu.VMEM((2, width, width), bf16)],
        tokens,
        w_key,
        w_value,
        extra=(doc_lengths,),
    )
    begins = first_begins(doc_lengths, shards, toks)
    if shards == 4:
        weights = jnp.stack(weights_of(begins, toks, False) + weights_of(begins, toks, True))
        later = 8
    else:
        weights = [weights_of(begins, toks, False), weights_of(begins, toks, True)]
        later = 1
    states = entering(order, (state_a, state_b), weights, 0)
    next(states)
    part = ff // rows
    q_t, sig_q, numer, denom_loc, w_out_t, w_in_t, w_back_t = run(
        local_kernel,
        [
            table_spec,
            feature(width),
            token_major,
            feature(width),
            whole,
            whole,
            pl.BlockSpec((width, part), lambda r, *s: (0, r)),
            pl.BlockSpec((part, width), lambda r, *s: (r, 0)),
        ],
        [
            wide_low,
            wide_low,
            wide_full,
            head_rows,
            (pl.BlockSpec((width, width), lambda r, *s: (0, 0)), ((width, width), bf16)),
            (pl.BlockSpec((part, width), lambda r, *s: (r, 0)), ((ff, width), bf16)),
            (pl.BlockSpec((width, part), lambda r, *s: (0, r)), ((width, ff), bf16)),
        ],
        [pltpu.VMEM((width, width), bf16)],
        table,
        tok_t,
        key,
        v_t,
        w_query,
        w_out,
        w_in,
        w_back,
    )
    next(states)
    in_a, in_b = next(states)
    (
        layer_out,
        att_t,
        first_t,
        active_t,
        grad_second,
        grad_hidden,
        grad_base,
        grad_branch,
        grad_numer,
        grad_denom,
        small,
        out_a,
        out_b,
    ) = run(
        layer_kernel,
        [
            table_spec,
            feature(width),
            feature(width),
            feature(16),
            state_spec,
            state_spec,
            feature(width),
            token_major,
        ]
        + [whole] * 10,
        [
            tok_low,
            wide_low,
            wide_low,
            ff_low,
            wide_low,
            ff_low,
            wide_full,
            wide_low,
            wide_low,
            head_rows,
            fold,
            state,
            state,
        ],
        [
            pltpu.VMEM((ff, toks), bf16),
            pltpu.VMEM((width, toks), f32),
            pltpu.VMEM((width, toks), f32),
            pltpu.VMEM((16, toks), f32),
            pltpu.VMEM((width, toks), f32),
        ]
        + [pltpu.VMEM((width, 128), f32)] * 4
        + [pltpu.VMEM((width, toks), f32)],
        table,
        q_t,
        numer,
        denom_loc,
        in_a,
        in_b,
        tok_t,
        cotangent,
        w_out_t,
        w_in_t,
        w_back_t,
        w_out,
        w_in,
        w_back,
        column(gain_one),
        column(shift_one),
        column(gain_two),
        column(shift_two),
        near=range(8, 14),
        limit=LAYER_LIMIT,
    )

    back_states = entering(order, (out_a, out_b), weights, later)
    next(back_states)
    pieces, made = {}, {}

    def begin(name, product, widths):
        pieces[name] = reduced(order, *product, widths)
        next(pieces[name])

    def local_back():
        made["query"], made["key"], made["value"] = run(
            local_back_kernel,
            [
                table_spec,
                feature(width),
                feature(width),
                token_major,
                token_major,
                feature(width),
                feature(width),
                feature(16),
                state_spec,
                state_spec,
            ],
            [wide_low, wide_full, wide_full],
            [],
            table,
            q_t,
            k_t,
            key,
            value,
            sig_q,
            grad_numer,
            grad_denom,
            in_a,
            in_b,
        )

    def tail():
        back_a, back_b = made["states"]
        (made["kv"],) = run(
            tail_kernel,
            [table_spec]
            + [feature(width)] * 3
            + [state_spec] * 2
            + [feature(width)] * 2,
            [(pl.BlockSpec((2, width, toks), lambda r, *s: (0, 0, r)), ((2, width, flat), bf16))],
            [],
            table,
            k_t,
            v_t,
            sig_k,
            back_a,
            back_b,
            made["key"],
            made["value"],
        )

    def token_grads():
        (made["tokens"],) = run(
            token_kernel,
            [
                feature(width),
                pl.BlockSpec((2, width, toks), lambda r, *s: (0, 0, r)),
                feature(width),
            ]
            + [whole] * 3,
            [(token_major, ((rows, toks, width), f32))],
            [],
            made["query"],
            made["kv"],
            grad_base,
            w_query,
            w_key,
            w_value,
        )

    def states_on():
        made["states"] = next(back_states)

    steps = {
        "back_product": lambda: begin("back", tall_product(order, active_t, grad_second), (width,)),
        "in_product": lambda: begin("in", wide_product(order, first_t, grad_hidden), (ff,)),
        "mixed_product": lambda: begin(
            "mixed",
            twin_product(order, att_t, (grad_branch[None], 0), tok_t, (made["query"][None], 0), small),
            (width, width, 128),
        ),
        "last_product": lambda: begin(
            "last",
            twin_product(order, tok_t, (made["kv"], 0), tok_t, (made["kv"], 1)),
            (width, width),
        ),
        "states": states_on,
        "local": local_back,
        "tail": tail,
        "tokens": token_grads,
    }
    ends = {}

    def step(name):
        value = next(pieces[name])
        if value is not None:
            ends[name] = value

    for name in SCHEDULE:
        if name in steps:
            steps[name]()
        elif name not in ends:
            step(name)
    while len(ends) < len(pieces):
        for name in pieces:
            if name not in ends:
                step(name)
    (total_back,), (total_in,) = ends["back"], ends["in"]
    total_out, total_query, vectors = ends["mixed"]
    total_key, total_value = ends["last"]
    grad_tokens = made["tokens"]
    return (
        layer_out,
        grad_tokens,
        total_query,
        total_key,
        total_value,
        total_out,
        total_in,
        total_back,
        vectors[:, 0],
        vectors[:, 1],
        vectors[:, 2],
        vectors[:, 3],
    )


def solution(mesh):
    in_specs = (
        P("batch", "seq", None),
        P("batch", "seq", None),
        P("batch", None),
        P(),
        P(),
        P(),
        P(),
        P(),
        P(),
        P(),
        P(),
        P(),
        P(),
    )
    out_specs = (
        P("batch", "seq", None),
        P("batch", "seq", None),
        P("seq", None),
        P("seq", None),
        P("seq", None),
        P("seq", None),
        P("seq", None),
        P("seq", None),
        P("seq"),
        P("seq"),
        P("seq"),
        P("seq"),
    )
    return jax.shard_map(body, mesh=mesh, in_specs=in_specs, out_specs=out_specs, check_vma=False)
```
